32 devices in a mesh: dp: 8 (over z, y), blk: 4 (over x, core).
Axes of the slice: x: 2, y: 2, z: 4, core: 2. Of those that a mesh axis runs over, the one named last changes fastest.
Arguments:
- inputs: bfloat16 [32, 1024, 768], P('dp', 'blk'), may hold values from -6 to 6
- lengths: int32 [32], P('dp'), may hold values from 512 to 1024, as said below
- out_grad: bfloat16 [32, 1024, 768], P('dp', 'blk'), may hold values from -6 to 6
- ln1_gain: bfloat16 [768], replicated, may hold values from 0.5 to 1.5
- ln1_bias: bfloat16 [768], replicated, may hold values from -1 to 1
- w_query: bfloat16 [768, 768], replicated, may hold values from -0.3125 to 0.3125
- b_query: bfloat16 [768], replicated, may hold values from -1 to 1
- w_key: bfloat16 [768, 768], replicated, may hold values from -0.3125 to 0.3125
- w_value: bfloat16 [768, 768], replicated, may hold values from -0.21875 to 0.21875
- b_value: bfloat16 [768], replicated, may hold values from -1 to 1
- w_output: bfloat16 [768, 768], replicated, may hold values from -0.875 to 0.875
- b_output: bfloat16 [768], replicated, may hold values from -1 to 1
- ln2_gain: bfloat16 [768], replicated, may hold values from 0.5 to 1.5
- ln2_bias: bfloat16 [768], replicated, may hold values from -1 to 1
- w_in: bfloat16 [768, 3072], replicated, may hold values from -0.21875 to 0.21875
- b_in: bfloat16 [3072], replicated, may hold values from -1 to 1
- w_out: bfloat16 [3072, 768], replicated, may hold values from -0.109375 to 0.109375
- b_out: bfloat16 [768], replicated, may hold values from -1 to 1
Outputs:
- output: bfloat16 [32, 1024, 768], P('dp', 'blk')
- input_grad: bfloat16 [32, 1024, 768], P('dp', 'blk')
- ln1_gain_grad: float32 [768], P(('dp', 'blk'))
- ln1_bias_grad: float32 [768], P(('dp', 'blk'))
- w_query_grad: float32 [768, 768], P(('dp', 'blk'))
- b_query_grad: float32 [768], P(('dp', 'blk'))
- w_key_grad: float32 [768, 768], P(('dp', 'blk'))
- w_value_grad: float32 [768, 768], P(('dp', 'blk'))
- b_value_grad: float32 [768], P(('dp', 'blk'))
- w_output_grad: float32 [768, 768], P(('dp', 'blk'))
- b_output_grad: float32 [768], P(('dp', 'blk'))
- ln2_gain_grad: float32 [768], P(('dp', 'blk'))
- ln2_bias_grad: float32 [768], P(('dp', 'blk'))
- w_in_grad: float32 [768, 3072], P(('dp', 'blk'))
- b_in_grad: float32 [3072], P(('dp', 'blk'))
- w_out_grad: float32 [3072, 768], P(('dp', 'blk'))
- b_out_grad: float32 [768], P(('dp', 'blk'))
The draws below stay inside these ranges and needn't reach their ends.
Inputs may be any that keep to these rules, and one draw needn't show every extreme that they name: `lengths`: every length is 512 or 1024; among the 4 sequences of one index of dp at least one has length 1024.
All inputs are finite; a program needn't handle non-finite values.
Results may differ from the reference program's by a relative error of at most 0.02.
Values may be sent and summed in bfloat16 or wider, within the bound.
A program may use at most 256 MiB of HBM per device.

```python
import jax
import jax.numpy as jnp
from jax import lax

D = 768
H = 12
HD = 64
FF = 3072
SEQ_DEV = 4
SEQ_LEN = 1024
SEQS = 32


def draw_lengths(key, part):
    key = jax.random.fold_in(key, 11)
    coin_key, chosen_key = jax.random.split(key)
    coin_flips = jax.random.randint(coin_key, (SEQS,), 0, 2)
    chosen_slot = jax.random.randint(chosen_key, (SEQS // SEQ_DEV,), 0, SEQ_DEV)
    slot_index = jnp.arange(SEQS) % SEQ_DEV
    forced_full = slot_index == jnp.repeat(chosen_slot, SEQ_DEV)
    full_length = jnp.logical_or(coin_flips == 1, forced_full)
    return jnp.where(full_length, SEQ_LEN, SEQ_LEN // 2).astype(jnp.int32)


def steps_of(own_key, extent, pieces, smallest, largest):
    def one(position, parts):
        steps = jax.random.uniform(jax.random.fold_in(jax.random.fold_in(own_key, 6), position), (parts,), jnp.float32, smallest / len(pieces), largest / len(pieces))
        return jnp.repeat(jnp.exp(steps), extent[position] // parts).reshape((-1,) + (1,) * (len(extent) - position - 1))

    gain = one(*pieces[0])
    for cut in pieces[1:]:
        gain = gain * one(*cut)
    return gain


def scatter_about(rng, extent, deviation, limit, cuts=(), held_as=jnp.bfloat16):
    values = jax.random.normal(rng, extent, jnp.float32) * deviation
    if len(cuts) > 0:
        values = steps_of(rng, extent, cuts, -0.22, 0.18) * values
    return jnp.clip(values, min=-limit, max=limit).astype(held_as)


def setup_inputs(seed: int = 0) -> dict:
    key_of = jax.random.split(jax.random.key(seed), 19)
    inputs = scatter_about(key_of[0], (SEQS, SEQ_LEN, D), 1.0, 6.0, ((0, 8), (1, 4)))
    lengths = draw_lengths(jax.random.fold_in(key_of[18], 71), 0)
    out_grad = scatter_about(key_of[2], (SEQS, SEQ_LEN, D), 1.0, 6.0, ((0, 8), (1, 4)))
    ln1_gain = jnp.clip(1.0 + 0.1 * jax.random.normal(key_of[3], (D,), jnp.float32), 0.5, 1.5).astype(jnp.bfloat16)
    ln1_bias = scatter_about(key_of[4], (D,), 0.2, 1.0)
    w_query = scatter_about(key_of[5], (D, D), (D // 2) ** -0.5, 0.3125)
    b_query = scatter_about(key_of[6], (D,), 0.2, 1.0)
    w_key = scatter_about(key_of[7], (D, D), (D // 2) ** -0.5, 0.3125)
    w_value = scatter_about(key_of[8], (D, D), D ** -0.5, 0.21875)
    b_value = scatter_about(key_of[9], (D,), 0.2, 1.0)
    w_output = scatter_about(key_of[10], (D, D), (D // 16) ** -0.5, 0.875)
    b_output = scatter_about(key_of[11], (D,), 0.2, 1.0)
    ln2_gain = jnp.clip(1.0 + 0.1 * jax.random.normal(key_of[12], (D,), jnp.float32), 0.5, 1.5).astype(jnp.bfloat16)
    ln2_bias = scatter_about(key_of[13], (D,), 0.2, 1.0)
    w_in = scatter_about(key_of[14], (D, FF), D ** -0.5, 0.21875)
    b_in = scatter_about(key_of[15], (FF,), 0.2, 1.0)
    w_out = scatter_about(key_of[16], (FF, D), FF ** -0.5, 0.109375)
    b_out = scatter_about(key_of[17], (D,), 0.2, 1.0)
    return {"inputs": inputs, "lengths": lengths, "out_grad": out_grad, "ln1_gain": ln1_gain, "ln1_bias": ln1_bias, "w_query": w_query, "b_query": b_query, "w_key": w_key, "w_value": w_value, "b_value": b_value, "w_output": w_output, "b_output": b_output, "ln2_gain": ln2_gain, "ln2_bias": ln2_bias, "w_in": w_in, "b_in": b_in, "w_out": w_out, "b_out": b_out}


epsilon = 1e-05

@jax.custom_vjp
def low(v):
    return lax.optimization_barrier(v.astype(jnp.bfloat16)).astype(jnp.float32)

@jax.custom_vjp
def low_back(v):
    return v

def low_keep(v):
    return (low(v), None)

def low_pass(kept, grad):
    return (grad,)

def back_keep(v):
    return (v, None)

def back_low(kept, grad):
    return (low(grad),)
low.defvjp(low_keep, low_pass)
low_back.defvjp(back_keep, back_low)

def normalize(values, gains, shifts):
    average = lax.optimization_barrier(jnp.mean(values, axis=-1, keepdims=True))
    centred = values - average
    variance = lax.optimization_barrier(jnp.mean(centred * centred, axis=-1, keepdims=True))
    return centred * lax.rsqrt(variance + epsilon) * gains + shifts

def product(left, right):
    return jnp.dot(left, right, precision=lax.Precision.HIGHEST, preferred_element_type=jnp.float32)

def attend(packed):
    query_heads, key_heads, value_heads, length = packed
    scores = low_back(jnp.einsum('qhd,khd->hqk', query_heads, key_heads, precision=lax.Precision.HIGHEST) * HD ** (-0.5))
    positions = jnp.arange(key_heads.shape[0])
    key_mask = positions < length
    masked = jnp.where(key_mask[None, None, :], scores, -1e+30)
    row_max = lax.optimization_barrier(jnp.max(masked, axis=-1, keepdims=True))
    expos = jnp.exp(masked - row_max)
    probabilities = low(expos / lax.optimization_barrier(jnp.sum(expos, axis=-1, keepdims=True)))
    return jnp.einsum('hqk,khd->qhd', probabilities, value_heads, precision=lax.Precision.HIGHEST)

def forward_group(inputs, group_lengths, params):
    ln1_gain, ln1_bias, w_query, b_query, w_key, w_value, b_value, w_output, b_output, ln2_gain, ln2_bias, w_in, b_in, w_out, b_out = params
    seq_count, seq_len, model_width = inputs.shape
    flat_rows = inputs.reshape(seq_count * seq_len, model_width)
    normed_one = low(normalize(flat_rows, ln1_gain, ln1_bias))
    queries = low_back(low(product(normed_one, w_query) + b_query))
    keys_all = low_back(low(product(normed_one, w_key)))
    values_all = low_back(low(product(normed_one, w_value) + b_value))
    head_shape = (seq_count, seq_len, H, HD)
    context = lax.map(jax.checkpoint(attend), (queries.reshape(head_shape), keys_all.reshape(head_shape), values_all.reshape(head_shape), group_lengths))
    context = low_back(low(context.reshape(seq_count * seq_len, model_width)))
    middle = flat_rows + low_back(product(context, w_output) + b_output)
    normed_two = low(normalize(middle, ln2_gain, ln2_bias))
    pre_gate = low_back(product(normed_two, w_in) + b_in)
    activated = low(jax.nn.gelu(pre_gate, approximate=False))
    result = middle + product(activated, w_out) + b_out
    return result.reshape(inputs.shape)

def reference(inputs, lengths, out_grad, ln1_gain, ln1_bias, w_query, b_query, w_key, w_value, b_value, w_output, b_output, ln2_gain, ln2_bias, w_in, b_in, w_out, b_out):
    params = tuple((weight_array.astype(jnp.float32) for weight_array in (ln1_gain, ln1_bias, w_query, b_query, w_key, w_value, b_value, w_output, b_output, ln2_gain, ln2_bias, w_in, b_in, w_out, b_out)))
    group_count = SEQS // SEQ_DEV
    grouped_inputs = inputs.astype(jnp.float32).reshape(group_count, SEQ_DEV, SEQ_LEN, D)
    grouped_lengths = lengths.reshape(group_count, SEQ_DEV)
    grouped_cot = out_grad.astype(jnp.float32).reshape(group_count, SEQ_DEV, SEQ_LEN, D)

    def group_step(totals, packed):
        group_inputs, group_lengths, group_cot = packed

        def apply_layer(layer_inputs, layer_params):
            return forward_group(layer_inputs, group_lengths, layer_params)
        result, pullback = jax.vjp(apply_layer, group_inputs, params)
        input_grads, param_grads = pullback(group_cot)
        totals = jax.tree.map(lambda left, right: left + right, totals, param_grads)
        return (totals, (result.astype(jnp.bfloat16), input_grads.astype(jnp.bfloat16)))
    starting = tuple((jnp.zeros_like(weight_array) for weight_array in params))
    totals, (outputs, input_grads) = lax.scan(group_step, starting, (grouped_inputs, grouped_lengths, grouped_cot))
    return (outputs.reshape(SEQS, SEQ_LEN, D), input_grads.reshape(SEQS, SEQ_LEN, D), totals[0], totals[1], totals[2], totals[3], totals[4], totals[5], totals[6], totals[7], totals[8], totals[9], totals[10], totals[11], totals[12], totals[13], totals[14])
```

```python
import functools

import jax
import jax.numpy as jnp
from jax import lax
from jax.experimental import pallas as pl
from jax.experimental.pallas import tpu as pltpu
from jax.sharding import PartitionSpec as P

H = 12
EPS = 1e-05
LOG2E = 1.4426950408889634
LN2 = 0.6931471805599453
INV_SQRT_2PI = 0.3989422804014327
F32 = jnp.float32
BF16 = jnp.bfloat16
VMEM_LIMIT = 56 * 2**20

NN = (((1,), (0,)), ((), ()))
NT = (((1,), (1,)), ((), ()))
TN = (((0,), (0,)), ((), ()))

TAIL_P = 0.28
TAIL_C = (
    0.116425338,
    0.068098667,
    0.267402196,
    -0.235117072,
    0.388714046,
    -0.105523175,
)


def dot(left, right, dims=NN):
    return lax.dot_general(left, right, dims, preferred_element_type=F32)


def params(**kw):
    return pltpu.CompilerParams(vmem_limit_bytes=VMEM_LIMIT, **kw)


def full(shape):
    return pl.BlockSpec(shape, lambda *_: (0,) * len(shape))


def center(v):
    mean = jnp.mean(v, axis=-1, keepdims=True)
    cent = v - mean
    var = jnp.mean(cent * cent, axis=-1, keepdims=True)
    rstd = lax.rsqrt(var + EPS)
    return cent * rstd, rstd


def gate(u):
    a = jnp.abs(u)
    den = 1.0 + TAIL_P * a
    t = pl.reciprocal(den, approx=True)
    t = t * (2.0 - den * t)
    e = jnp.exp2(u * u * (-0.5 * LOG2E))
    poly = TAIL_C[-1]
    for c in TAIL_C[-2::-1]:
        poly = poly * t + c
    tail = poly * t * e
    phi = jnp.where(u < 0.0, tail, 1.0 - tail)
    return phi, u * e * INV_SQRT_2PI


def qkv_kernel(scale, n_blk, *refs):
    xs = refs[:n_blk]
    gain, bias, wq, bq, wk, wv, bv, nt_ref, q_ref, k_ref, v_ref = refs[n_blk:]
    tok = xs[0].shape[0]

    @pl.when(pl.program_id(0) == 0)
    def _():
        for s in range(n_blk):
            n, _ = center(xs[s][...].astype(F32))
            n = n * gain[...] + bias[...]
            nt_ref[:, s * tok : (s + 1) * tok] = n.astype(BF16).T

    nt = nt_ref[...]
    q_ref[...] = ((dot(wq[...], nt, TN) + bq[...]) * scale).astype(BF16)
    k_ref[...] = dot(wk[...], nt, TN).astype(BF16)
    v_ref[...] = (dot(wv[...], nt, TN) + bv[...]).astype(BF16)


def attend_kernel(n_blk, live_ref, q_ref, k_ref, v_ref, c_ref, p_ref, il_ref):
    seq = q_ref.shape[1]
    tok = seq // n_blk
    s = dot(k_ref[...].T, q_ref[...])
    live = [live_ref[0, i] > 0 for i in range(n_blk)]
    m = None
    for i in range(n_blk):
        mi = jnp.max(s[i * tok : (i + 1) * tok], axis=0, keepdims=True)
        mi = jnp.where(live[i], mi, -1e30)
        m = mi if m is None else jnp.maximum(m, mi)
    total = None
    ps = []
    for i in range(n_blk):
        p = jnp.exp2(s[i * tok : (i + 1) * tok] - jnp.where(live[i], m, 1e30))
        li = jnp.sum(p, axis=0, keepdims=True)
        total = li if total is None else total + li
        pb = p.astype(BF16)
        p_ref[0, i * tok : (i + 1) * tok] = pb
        ps.append(pb)
    inv = 1.0 / total
    c_ref[...] = (dot(v_ref[...], jnp.concatenate(ps, axis=0)) * inv).astype(BF16)
    il_ref[0] = inv


def ffn_kernel(n_blk, *refs):
    xs = refs[:n_blk]
    gs = refs[n_blk : 2 * n_blk]
    (ct_ref, il_ref, wo_ref, bo_ref, gain_ref, bias_ref, win_ref, bin_ref, wout_ref, bout_ref) = refs[
        2 * n_blk : 2 * n_blk + 10
    ]
    rest = refs[2 * n_blk + 10 :]
    outs = rest[:n_blk]
    (gwout_ref, gwin_ref, gbin_ref, dmid_ref, dot_ref, gwo_ref, vec_ref) = rest[n_blk : n_blk + 7]
    mid, n2, n2t, g, acc_o, acc_d, act, dpre = rest[n_blk + 7 :]
    tok = xs[0].shape[0]
    j = pl.program_id(0)

    @pl.when(j == 0)
    def _():
        for s in range(n_blk):
            sl = slice(s * tok, (s + 1) * tok)
            m = xs[s][...].astype(F32) + dot(ct_ref[:, sl], wo_ref[...], TN) + bo_ref[...]
            mid[sl] = m
            acc_o[sl] = m + bout_ref[...]
            acc_d[sl] = jnp.zeros_like(m)
            n, _ = center(m)
            nb = (n * gain_ref[...] + bias_ref[...]).astype(BF16)
            n2[sl] = nb
            n2t[:, sl] = nb.T
            g[sl] = gs[s][...]

    bin_grad = None
    for s in range(n_blk):
        sl = slice(s * tok, (s + 1) * tok)
        pre = dot(n2[sl], win_ref[...]) + bin_ref[...]
        phi, slope = gate(pre)
        a = (pre * phi).astype(BF16)
        dact = dot(g[sl], wout_ref[...], NT)
        dp = (dact * (phi + slope)).astype(BF16)
        act[sl] = a
        dpre[sl] = dp
        col = jnp.sum(dp.astype(F32), axis=0, keepdims=True)
        bin_grad = col if bin_grad is None else bin_grad + col
        acc_o[sl] += dot(a, wout_ref[...])
        acc_d[sl] += dot(dp, win_ref[...], NT)
    gbin_ref[...] = bin_grad
    gwout_ref[...] = dot(act[...], g[...], TN).astype(BF16)
    gwin_ref[...] = dot(n2t[...], dpre[...]).astype(BF16)

    @pl.when(j == pl.num_programs(0) - 1)
    def _():
        head = wo_ref.shape[0] // H
        sums = [None] * 4
        for s in range(n_blk):
            sl = slice(s * tok, (s + 1) * tok)
            outs[s][...] = acc_o[sl].astype(BF16)
            n, rstd = center(mid[sl])
            e = acc_d[sl]
            gf = g[sl].astype(F32)
            f = e * gain_ref[...]
            dm = gf + rstd * (
                f - jnp.mean(f, axis=-1, keepdims=True) - n * jnp.mean(f * n, axis=-1, keepdims=True)
            )
            dmid_ref[sl] = dm
            db = dm.astype(BF16)
            n2[sl] = db
            for i, term in enumerate((gf, e * n, e, db.astype(F32))):
                col = jnp.sum(term, axis=0, keepdims=True)
                sums[i] = col if sums[i] is None else sums[i] + col
            dc = dot(wo_ref[...], db, NT)
            for h in range(H):
                hs = slice(h * head, (h + 1) * head)
                dot_ref[hs, sl] = (dc[hs] * il_ref[h, :, sl]).astype(BF16)
        for i in range(4):
            vec_ref[i : i + 1] = sums[i]
        gwo_ref[...] = dot(ct_ref[...], n2[...]).astype(BF16)


def attend_back_kernel(scale, p_ref, q_ref, k_ref, v_ref, do_ref, c_ref, dq_ref, dk_ref, dv_ref, ds):
    seq = q_ref.shape[1]
    do = do_ref[...]
    vh = v_ref[...].T
    delta = jnp.sum(do.astype(F32) * c_ref[...].astype(F32), axis=0, keepdims=True)
    step = seq // 2
    for c in range(2):
        sl = slice(c * step, (c + 1) * step)
        dp = dot(vh, do[:, sl])
        d = (p_ref[0, :, sl].astype(F32) * (dp - delta[:, sl])).astype(BF16)
        ds[:, sl] = d
        dq_ref[:, sl] = (dot(k_ref[...], d) * scale).astype(BF16)
    dv_ref[...] = dot(p_ref[0], do, NT).T.astype(BF16)
    dk_ref[...] = (dot(ds[...], q_ref[...], NT) * LN2).T.astype(BF16)


def input_kernel(n_blk, *refs):
    xs = refs[:n_blk]
    dmid_ref, gain_ref, dq_ref, dk_ref, dv_ref, wq_ref, wk_ref, wv_ref = refs[n_blk : n_blk + 8]
    outs = refs[n_blk + 8 : 2 * n_blk + 8]
    vec_ref = refs[2 * n_blk + 8]
    tok = xs[0].shape[0]
    sums = [None] * 2
    for s in range(n_blk):
        sl = slice(s * tok, (s + 1) * tok)
        et = dot(wq_ref[...], dq_ref[:, sl]) + dot(wk_ref[...], dk_ref[:, sl]) + dot(wv_ref[...], dv_ref[:, sl])
        e = et.T
        n, rstd = center(xs[s][...].astype(F32))
        f = e * gain_ref[...]
        dx = dmid_ref[sl] + rstd * (
            f - jnp.mean(f, axis=-1, keepdims=True) - n * jnp.mean(f * n, axis=-1, keepdims=True)
        )
        outs[s][...] = dx.astype(BF16)
        for i, term in enumerate((e * n, e)):
            col = jnp.sum(term, axis=0, keepdims=True)
            sums[i] = col if sums[i] is None else sums[i] + col
    for i in range(2):
        vec_ref[i : i + 1] = sums[i]


def qkv_grad_kernel(nt_ref, dq_ref, dk_ref, dv_ref, gq_ref, gk_ref, gv_ref, vec_ref):
    nt = nt_ref[...]
    ones = jnp.ones((8, nt.shape[1]), BF16)
    gq_ref[...] = dot(nt, dq_ref[...], NT).astype(BF16)
    gk_ref[...] = dot(nt, dk_ref[...], NT).astype(BF16)
    gv_ref[...] = dot(nt, dv_ref[...], NT).astype(BF16)
    vec_ref[0:1] = dot(ones, dq_ref[...], NT)[:1]
    vec_ref[1:2] = dot(ones, dv_ref[...], NT)[:1]


def body(
    inputs,
    lengths,
    out_grad,
    ln1_gain,
    ln1_bias,
    w_query,
    b_query,
    w_key,
    w_value,
    b_value,
    w_output,
    b_output,
    ln2_gain,
    ln2_bias,
    w_in,
    b_in,
    w_out,
    b_out,
):
    n_seq, tok, width = inputs.shape
    n_blk = lax.axis_size("blk")
    n_dp = lax.axis_size("dp")
    n_dev = n_blk * n_dp
    assert n_seq == n_blk
    seq = tok * n_blk
    hidden = w_in.shape[1]
    head = width // H
    scale = head ** (-0.5)
    blk = lax.axis_index("blk")
    me = lax.axis_index("dp") * n_blk + blk

    def swap(v, s):
        return lax.ppermute(v, "blk", [(i, i ^ s) for i in range(n_blk)])

    def spread(v):
        pick = [lax.dynamic_index_in_dim(v, blk ^ s, 0, keepdims=False) for s in range(n_blk)]
        return [pick[0]] + [swap(pick[s], s) for s in range(1, n_blk)]

    def collect(pieces):
        back = [pieces[0]] + [swap(pieces[s], s) for s in range(1, n_blk)]
        out = jnp.zeros((n_seq, tok, width), BF16)
        for s in range(n_blk):
            out = lax.dynamic_update_index_in_dim(out, back[s], blk ^ s, 0)
        return out

    row = lambda v: v.astype(F32).reshape(1, -1)
    column = lambda v: v.astype(F32).reshape(-1, 1)

    xs = spread(inputs)
    tied = lax.optimization_barrier((out_grad, xs))
    gs = spread(tied[0])
    xs = tied[1]
    live = ((blk ^ jnp.arange(n_blk)) * tok < lengths[blk]).astype(jnp.int32).reshape(1, n_blk)

    sds = jax.ShapeDtypeStruct
    piece = full((tok, width))
    wide = full((width, seq))
    n_col = 3
    cols = width // n_col
    strip = pl.BlockSpec((cols, seq), lambda j: (j, 0))
    nt, qt, kt, vt = pl.pallas_call(
        functools.partial(qkv_kernel, scale * LOG2E, n_blk),
        grid=(n_col,),
        in_specs=[piece] * n_blk
        + [full((1, width))] * 2
        + [pl.BlockSpec((width, cols), lambda j: (0, j)), pl.BlockSpec((cols, 1), lambda j: (j, 0))]
        + [pl.BlockSpec((width, cols), lambda j: (0, j))] * 2
        + [pl.BlockSpec((cols, 1), lambda j: (j, 0))],
        out_specs=[wide, strip, strip, strip],
        out_shape=[sds((width, seq), BF16)] * 4,
        compiler_params=params(),
        name="qkv",
    )(*xs, row(ln1_gain), row(ln1_bias), w_query, column(b_query), w_key, w_value, column(b_value))

    per_head = pl.BlockSpec((head, seq), lambda h: (h, 0))
    per_square = pl.BlockSpec((1, seq, seq), lambda h: (h, 0, 0))
    ct, probs, inv_total = pl.pallas_call(
        functools.partial(attend_kernel, n_blk),
        grid=(H,),
        in_specs=[pl.BlockSpec(memory_space=pltpu.SMEM), per_head, per_head, per_head],
        out_specs=[per_head, per_square, pl.BlockSpec((1, 1, seq), lambda h: (h, 0, 0))],
        out_shape=[sds((width, seq), BF16), sds((H, seq, seq), BF16), sds((H, 1, seq), F32)],
        compiler_params=params(),
        name="attend",
    )(live, qt, kt, vt)

    n_tile = 12
    tile = hidden // n_tile
    result = pl.pallas_call(
        functools.partial(ffn_kernel, n_blk),
        grid=(n_tile,),
        in_specs=[piece] * (2 * n_blk)
        + [
            wide,
            full((H, 1, seq)),
            full((width, width)),
            full((1, width)),
            full((1, width)),
            full((1, width)),
            pl.BlockSpec((width, tile), lambda j: (0, j)),
            pl.BlockSpec((1, tile), lambda j: (0, j)),
            pl.BlockSpec((tile, width), lambda j: (j, 0)),
            full((1, width)),
        ],
        out_specs=[piece] * n_blk
        + [
            pl.BlockSpec((tile, width), lambda j: (j, 0)),
            pl.BlockSpec((width, tile), lambda j: (0, j)),
            pl.BlockSpec((1, tile), lambda j: (0, j)),
            full((seq, width)),
            wide,
            full((width, width)),
            full((8, width)),
        ],
        out_shape=[sds((tok, width), BF16)] * n_blk
        + [
            sds((hidden, width), BF16),
            sds((width, hidden), BF16),
            sds((1, hidden), F32),
            sds((seq, width), F32),
            sds((width, seq), BF16),
            sds((width, width), BF16),
            sds((8, width), F32),
        ],
        scratch_shapes=[
            pltpu.VMEM((seq, width), F32),
            pltpu.VMEM((seq, width), BF16),
            pltpu.VMEM((width, seq), BF16),
            pltpu.VMEM((seq, width), BF16),
            pltpu.VMEM((seq, width), F32),
            pltpu.VMEM((seq, width), F32),
            pltpu.VMEM((seq, tile), BF16),
            pltpu.VMEM((seq, tile), BF16),
        ],
        compiler_params=params(),
        name="ffn",
    )(
        *xs,
        *gs,
        ct,
        inv_total,
        w_output,
        row(b_output),
        row(ln2_gain),
        row(ln2_bias),
        w_in,
        row(b_in),
        w_out,
        row(b_out),
    )
    out_pieces = result[:n_blk]
    g_wout, g_win, g_bin, dmid, dct, g_wo, vec2 = result[n_blk:]

    bits = (n_dev - 1).bit_length()
    assert n_dev == 1 << bits

    def scatter(grad, order, wire):
        share = grad.shape[0] // n_dev
        order = list(order) + [b for b in range(bits) if b not in order]
        axes = list(range(bits - 1, -1, -1))
        terms = [grad.reshape((2,) * bits + (share,) + grad.shape[1:])]
        for b in order:
            at = axes.index(b)
            axes.pop(at)
            mine = (me >> b) & 1
            send = None
            keep = []
            for t in terms:
                other = lax.dynamic_index_in_dim(t, 1 - mine, at, keepdims=False)
                send = other.astype(F32) if send is None else send + other.astype(F32)
                keep.append(lax.dynamic_index_in_dim(t, mine, at, keepdims=False))
            got = lax.ppermute(send.astype(wire), ("dp", "blk"), [(i, i ^ (1 << b)) for i in range(n_dev)])
            terms = keep + [got]
        total = terms[0].astype(F32)
        for t in terms[1:]:
            total = total + t.astype(F32)
        return total

    s_wout = scatter(g_wout, (0, 1, 2, 3, 4), BF16)
    s_win = scatter(g_win, (0, 2, 1, 3, 4), BF16)
    s_wo = scatter(g_wo, (0, 3, 4, 1, 2), BF16)
    output = collect(out_pieces)

    dqt, dkt, dvt = pl.pallas_call(
        functools.partial(attend_back_kernel, scale),
        grid=(H,),
        in_specs=[per_square] + [per_head] * 5,
        out_specs=[per_head] * 3,
        out_shape=[sds((width, seq), BF16)] * 3,
        scratch_shapes=[pltpu.VMEM((seq, seq), BF16)],
        compiler_params=params(),
        name="attend_back",
    )(probs, qt, kt, vt, dct, ct)

    result = pl.pallas_call(
        functools.partial(input_kernel, n_blk),
        in_specs=[piece] * n_blk
        + [full((seq, width)), full((1, width)), wide, wide, wide]
        + [full((width, width))] * 3,
        out_specs=[piece] * n_blk + [full((8, width))],
        out_shape=[sds((tok, width), BF16)] * n_blk + [sds((8, width), F32)],
        compiler_params=params(),
        name="input_grad",
    )(*xs, dmid, row(ln1_gain), dqt, dkt, dvt, w_query, w_key, w_value)
    input_grad = collect(result[:n_blk])
    vec1 = result[n_blk]

    col = pl.BlockSpec((width, cols), lambda j: (0, j))
    g_wq, g_wk, g_wv, vecq = pl.pallas_call(
        qkv_grad_kernel,
        grid=(n_col,),
        in_specs=[wide, strip, strip, strip],
        out_specs=[col, col, col, pl.BlockSpec((8, cols), lambda j: (0, j))],
        out_shape=[sds((width, width), BF16)] * 3 + [sds((8, width), F32)],
        compiler_params=params(),
        name="qkv_grad",
    )(nt, dqt, dkt, dvt)
    s_wq = scatter(g_wq, (0, 1, 2, 3, 4), BF16)
    s_wk = scatter(g_wk, (0, 2, 3, 4, 1), BF16)
    s_wv = scatter(g_wv, (0, 3, 4, 1, 2), BF16)

    vectors = [vec1[0], vec1[1], vecq[0], vecq[1], vec2[3], vec2[1], vec2[2], g_bin[0], vec2[0]]
    packed = jnp.concatenate([v.reshape(n_dev, -1) for v in vectors], axis=1)
    packed = scatter(packed, (0, 1, 2, 3, 4), F32).reshape(-1)
    parts = []
    at = 0
    for v in vectors:
        size = v.shape[0] // n_dev
        parts.append(packed[at : at + size])
        at += size
    p_ln1g, p_ln1b, p_bq, p_bv, p_bo, p_ln2g, p_ln2b, p_bin, p_bout = parts
    return (
        output,
        input_grad,
        p_ln1g,
        p_ln1b,
        s_wq,
        p_bq,
        s_wk,
        s_wv,
        p_bv,
        s_wo,
        p_bo,
        p_ln2g,
        p_ln2b,
        s_win,
        p_bin,
        s_wout,
        p_bout,
    )


def solution(mesh):
    whole = P(("dp", "blk"))
    rows = P(("dp", "blk"), None)
    tokens = P("dp", "blk", None)
    in_specs = (tokens, P("dp"), tokens) + (P(),) * 15
    out_specs = (
        tokens,
        tokens,
        whole,
        whole,
        rows,
        whole,
        rows,
        rows,
        whole,
        rows,
        whole,
        whole,
        whole,
        rows,
        whole,
        rows,
        whole,
    )
    return jax.shard_map(body, mesh=mesh, in_specs=in_specs, out_specs=out_specs, check_vma=False)
```

```python
import functools

import jax
import jax.numpy as jnp
from jax import lax
from jax.experimental import pallas as pl
from jax.experimental.pallas import tpu as pltpu
from jax.sharding import PartitionSpec as P

H = 12
EPS = 1e-05
LOG2E = 1.4426950408889634
LN2 = 0.6931471805599453
INV_SQRT_2PI = 0.3989422804014327
SQRT_HALF = 0.7071067811865476
F32 = jnp.float32
BF16 = jnp.bfloat16
VMEM_LIMIT = 56 * 2**20

NN = (((1,), (0,)), ((), ()))
NT = (((1,), (1,)), ((), ()))
TN = (((0,), (0,)), ((), ()))

def dot(left, right, dims=NN):
    return lax.dot_general(left, right, dims, preferred_element_type=F32)


def params(**kw):
    return pltpu.CompilerParams(vmem_limit_bytes=VMEM_LIMIT, **kw)


def cost(macs, nbytes, exps=0):
    return pl.CostEstimate(flops=2 * macs, bytes_accessed=nbytes, transcendentals=exps)


def full(shape):
    return pl.BlockSpec(shape, lambda *_: (0,) * len(shape))


def center(v):
    mean = jnp.mean(v, axis=-1, keepdims=True)
    cent = v - mean
    var = jnp.mean(cent * cent, axis=-1, keepdims=True)
    rstd = lax.rsqrt(var + EPS)
    return cent * rstd, rstd


def gate(u):
    phi = 0.5 + 0.5 * lax.erf(u * SQRT_HALF)
    e = jnp.exp2(u * u * (-0.5 * LOG2E))
    return phi, u * e * INV_SQRT_2PI


def attend_kernel(n_blk, live_ref, q_ref, k_ref, v_ref, c_ref, p_ref, il_ref):
    seq = q_ref.shape[1]
    tok = seq // n_blk
    s = dot(k_ref[...].T, q_ref[...])
    live = [live_ref[0, i] > 0 for i in range(n_blk)]
    m = None
    for i in range(n_blk):
        mi = jnp.max(s[i * tok : (i + 1) * tok], axis=0, keepdims=True)
        mi = jnp.where(live[i], mi, -1e30)
        m = mi if m is None else jnp.maximum(m, mi)
    total = None
    ps = []
    for i in range(n_blk):
        p = jnp.exp2(s[i * tok : (i + 1) * tok] - jnp.where(live[i], m, 1e30))
        li = jnp.sum(p, axis=0, keepdims=True)
        total = li if total is None else total + li
        pb = p.astype(BF16)
        p_ref[0, i * tok : (i + 1) * tok] = pb
        ps.append(pb)
    inv = 1.0 / total
    c_ref[...] = (dot(v_ref[...], jnp.concatenate(ps, axis=0)) * inv).astype(BF16)
    il_ref[0] = inv


MESH = pl.DeviceIdType.MESH


def greet(partners):
    barrier = pltpu.get_barrier_semaphore()
    for where in partners:
        pl.semaphore_signal(barrier, inc=1, device_id=where, device_id_type=MESH)
    pl.semaphore_wait(barrier, len(partners))


def qkv_spread_kernel(
    scale,
    n_blk,
    x_any,
    gain,
    bias,
    wq_any,
    bq,
    wk_any,
    wv_any,
    bv,
    xs_any,
    nt_any,
    q_any,
    k_any,
    v_any,
    xbuf,
    wbuf,
    wt,
    nt,
    qkv,
    send,
    recv,
    wsem,
    osem,
    xsem,
):
    tok, width = xbuf.shape[1:]
    dp = lax.axis_index("dp")
    blk = lax.axis_index("blk")
    own = pltpu.make_async_copy(x_any.at[blk], xbuf.at[0], xsem)
    own.start()
    loads = [
        pltpu.make_async_copy(w, wbuf.at[i], wsem.at[i]) for i, w in enumerate((wq_any, wk_any, wv_any))
    ]
    for load in loads:
        load.start()
    greet([(dp, blk ^ s) for s in range(1, n_blk)])
    order = list(range(n_blk - 1, 0, -1))
    copies = {}
    for s in order:
        copies[s] = pltpu.make_async_remote_copy(
            src_ref=x_any.at[blk ^ s],
            dst_ref=xbuf.at[s],
            send_sem=send.at[s - 1],
            recv_sem=recv.at[s - 1],
            device_id=(dp, blk ^ s),
            device_id_type=MESH,
        )
        copies[s].start()
    for i, load in enumerate(loads):
        load.wait()
        wt[i] = wbuf[i].T
    writes = []
    for s in range(n_blk):
        if s == 0:
            own.wait()
        else:
            copies[s].wait_recv()
        sl = slice(s * tok, (s + 1) * tok)
        n, _ = center(xbuf[s].astype(F32))
        n = (n * gain[...] + bias[...]).astype(BF16).T
        nt[:, sl] = n
        qkv[0, :, sl] = ((dot(wt[0], n) + bq[...]) * scale).astype(BF16)
        qkv[1, :, sl] = dot(wt[1], n).astype(BF16)
        qkv[2, :, sl] = (dot(wt[2], n) + bv[...]).astype(BF16)
        for i, (src, dst) in enumerate(
            (
                (xbuf.at[s], xs_any.at[s]),
                (nt.at[:, sl], nt_any.at[:, sl]),
                (qkv.at[0, :, sl], q_any.at[:, sl]),
                (qkv.at[1, :, sl], k_any.at[:, sl]),
                (qkv.at[2, :, sl], v_any.at[:, sl]),
            )
        ):
            write = pltpu.make_async_copy(src, dst, osem.at[s, i])
            write.start()
            writes.append(write)
    for s in order:
        copies[s].wait_send()
    for write in writes:
        write.wait()


def attend_spread_kernel(n_blk, live_ref, q_ref, k_ref, v_ref, g_any, c_ref, p_ref, il_ref, gs_any, send, recv, osem):
    h = pl.program_id(0)
    dp = lax.axis_index("dp")
    blk = lax.axis_index("blk")

    def copy(s):
        return pltpu.make_async_remote_copy(
            src_ref=g_any.at[blk ^ s],
            dst_ref=gs_any.at[s],
            send_sem=send.at[s - 1],
            recv_sem=recv.at[s - 1],
            device_id=(dp, blk ^ s),
            device_id_type=MESH,
        )

    own = pltpu.make_async_copy(g_any.at[blk], gs_any.at[0], osem)

    @pl.when(h == 0)
    def _():
        greet([(dp, blk ^ s) for s in range(1, n_blk)])
        own.start()
        for s in range(1, n_blk):
            copy(s).start()

    attend_kernel(n_blk, live_ref, q_ref, k_ref, v_ref, c_ref, p_ref, il_ref)

    @pl.when(h == pl.num_programs(0) - 1)
    def _():
        own.wait()
        for s in range(1, n_blk):
            copy(s).wait()


def ffn_kernel(n_blk, *refs):
    x_ref, g = refs[:2]
    (ct_ref, il_ref, wo_ref, bo_ref, gain_ref, bias_ref, win_ref, bin_ref, wout_ref, bout_ref) = refs[2:12]
    rest = refs[12:]
    outs = rest[:n_blk]
    (gwout_ref, gwin_ref, gbin_ref, dmid_ref, dot_ref, gwo_ref, vec_ref) = rest[n_blk : n_blk + 7]
    mid, n2, n2t, acc_o, acc_d, act, dpre = rest[n_blk + 7 :]
    tok = outs[0].shape[0]
    j = pl.program_id(0)

    @pl.when(j == 0)
    def _():
        for s in range(n_blk):
            sl = slice(s * tok, (s + 1) * tok)
            m = x_ref[sl].astype(F32) + dot(ct_ref[:, sl], wo_ref[...], TN) + bo_ref[...]
            mid[sl] = m
            acc_o[sl] = m + bout_ref[...]
            acc_d[sl] = jnp.zeros_like(m)
            n, _ = center(m)
            nb = (n * gain_ref[...] + bias_ref[...]).astype(BF16)
            n2[sl] = nb
            n2t[:, sl] = nb.T

    bin_grad = None
    for s in range(n_blk):
        sl = slice(s * tok, (s + 1) * tok)
        pre = dot(n2[sl], win_ref[...]) + bin_ref[...]
        phi, slope = gate(pre)
        a = (pre * phi).astype(BF16)
        dact = dot(g[sl], wout_ref[...], NT)
        dp = (dact * (phi + slope)).astype(BF16)
        act[sl] = a
        dpre[sl] = dp
        col = jnp.sum(dp.astype(F32), axis=0, keepdims=True)
        bin_grad = col if bin_grad is None else bin_grad + col
        acc_o[sl] += dot(a, wout_ref[...])
        acc_d[sl] += dot(dp, win_ref[...], NT)
    gbin_ref[...] = bin_grad
    gwout_ref[...] = dot(act[...], g[...], TN).astype(BF16)
    gwin_ref[...] = dot(n2t[...], dpre[...]).astype(BF16)

    @pl.when(j == pl.num_programs(0) - 1)
    def _():
        head = wo_ref.shape[0] // H
        sums = [None] * 4
        for s in range(n_blk):
            sl = slice(s * tok, (s + 1) * tok)
            outs[s][...] = acc_o[sl].astype(BF16)
            n, rstd = center(mid[sl])
            e = acc_d[sl]
            gf = g[sl].astype(F32)
            f = e * gain_ref[...]
            dm = gf + rstd * (
                f - jnp.mean(f, axis=-1, keepdims=True) - n * jnp.mean(f * n, axis=-1, keepdims=True)
            )
            dmid_ref[sl] = dm
            db = dm.astype(BF16)
            n2[sl] = db
            for i, term in enumerate((gf, e * n, e, db.astype(F32))):
                col = jnp.sum(term, axis=0, keepdims=True)
                sums[i] = col if sums[i] is None else sums[i] + col
            dc = dot(wo_ref[...], db, NT)
            for h in range(H):
                hs = slice(h * head, (h + 1) * head)
                dot_ref[hs, sl] = (dc[hs] * il_ref[h, :, sl]).astype(BF16)
        for i in range(4):
            vec_ref[i : i + 1] = sums[i]
        gwo_ref[...] = dot(ct_ref[...], n2[...]).astype(BF16)


def attend_back_kernel(scale, p_ref, q_ref, k_ref, v_ref, do_ref, c_ref, dq_ref, dk_ref, dv_ref, ds):
    seq = q_ref.shape[1]
    do = do_ref[...]
    vh = v_ref[...].T
    delta = jnp.sum(do.astype(F32) * c_ref[...].astype(F32), axis=0, keepdims=True)
    step = seq // 2
    for c in range(2):
        sl = slice(c * step, (c + 1) * step)
        dp = dot(vh, do[:, sl])
        d = (p_ref[0, :, sl].astype(F32) * (dp - delta[:, sl])).astype(BF16)
        ds[:, sl] = d
        dq_ref[:, sl] = (dot(k_ref[...], d) * scale).astype(BF16)
    dv_ref[...] = dot(p_ref[0], do, NT).T.astype(BF16)
    dk_ref[...] = (dot(ds[...], q_ref[...], NT) * LN2).T.astype(BF16)


def input_kernel(n_blk, x_ref, dmid_ref, gain_ref, dq_ref, dk_ref, dv_ref, wq_ref, wk_ref, wv_ref, *rest):
    outs = rest[:n_blk]
    vec_ref = rest[n_blk]
    tok = outs[0].shape[0]
    sums = [None] * 2
    for s in range(n_blk):
        sl = slice(s * tok, (s + 1) * tok)
        et = dot(wq_ref[...], dq_ref[:, sl]) + dot(wk_ref[...], dk_ref[:, sl]) + dot(wv_ref[...], dv_ref[:, sl])
        e = et.T
        n, rstd = center(x_ref[sl].astype(F32))
        f = e * gain_ref[...]
        dx = dmid_ref[sl] + rstd * (
            f - jnp.mean(f, axis=-1, keepdims=True) - n * jnp.mean(f * n, axis=-1, keepdims=True)
        )
        outs[s][...] = dx.astype(BF16)
        for i, term in enumerate((e * n, e)):
            col = jnp.sum(term, axis=0, keepdims=True)
            sums[i] = col if sums[i] is None else sums[i] + col
    for i in range(2):
        vec_ref[i : i + 1] = sums[i]


def qkv_grad_kernel(nt_ref, dq_ref, dk_ref, dv_ref, gq_ref, gk_ref, gv_ref, vec_ref):
    nt = nt_ref[...]
    ones = jnp.ones((8, nt.shape[1]), BF16)
    gq_ref[...] = dot(nt, dq_ref[...], NT).astype(BF16)
    gk_ref[...] = dot(nt, dk_ref[...], NT).astype(BF16)
    gv_ref[...] = dot(nt, dv_ref[...], NT).astype(BF16)
    vec_ref[0:1] = dot(ones, dq_ref[...], NT)[:1]
    vec_ref[1:2] = dot(ones, dv_ref[...], NT)[:1]


def body(
    inputs,
    lengths,
    out_grad,
    ln1_gain,
    ln1_bias,
    w_query,
    b_query,
    w_key,
    w_value,
    b_value,
    w_output,
    b_output,
    ln2_gain,
    ln2_bias,
    w_in,
    b_in,
    w_out,
    b_out,
):
    n_seq, tok, width = inputs.shape
    n_blk = lax.axis_size("blk")
    n_dp = lax.axis_size("dp")
    n_dev = n_blk * n_dp
    assert n_seq == n_blk
    seq = tok * n_blk
    hidden = w_in.shape[1]
    head = width // H
    scale = head ** (-0.5)
    blk = lax.axis_index("blk")
    me = lax.axis_index("dp") * n_blk + blk

    def swap(v, s):
        return lax.ppermute(v, "blk", [(i, i ^ s) for i in range(n_blk)])

    def collect(pieces):
        back = [pieces[0]] + [swap(pieces[s], s) for s in range(1, n_blk)]
        out = jnp.zeros((n_seq, tok, width), BF16)
        for s in range(n_blk):
            out = lax.dynamic_update_index_in_dim(out, back[s], blk ^ s, 0)
        return out

    row = lambda v: v.astype(F32).reshape(1, -1)
    column = lambda v: v.astype(F32).reshape(-1, 1)

    live = ((blk ^ jnp.arange(n_blk)) * tok < lengths[blk]).astype(jnp.int32).reshape(1, n_blk)

    sds = jax.ShapeDtypeStruct
    piece = full((tok, width))
    wide = full((width, seq))
    n_col = 3
    cols = width // n_col
    strip = pl.BlockSpec((cols, seq), lambda j: (j, 0))
    anywhere = pl.BlockSpec(memory_space=pl.ANY)
    vmem = pl.BlockSpec(memory_space=pltpu.VMEM)
    xs, nt, qt, kt, vt = pl.pallas_call(
        functools.partial(qkv_spread_kernel, scale * LOG2E, n_blk),
        in_specs=[anywhere, vmem, vmem, anywhere, vmem, anywhere, anywhere, vmem],
        out_specs=[anywhere] * 5,
        out_shape=[sds((n_blk, tok, width), BF16)] + [sds((width, seq), BF16)] * 4,
        scratch_shapes=[
            pltpu.VMEM((n_blk, tok, width), BF16),
            pltpu.VMEM((3, width, width), BF16),
            pltpu.VMEM((3, width, width), BF16),
            pltpu.VMEM((width, seq), BF16),
            pltpu.VMEM((3, width, seq), BF16),
            pltpu.SemaphoreType.DMA((n_blk - 1,)),
            pltpu.SemaphoreType.DMA((n_blk - 1,)),
            pltpu.SemaphoreType.DMA((3,)),
            pltpu.SemaphoreType.DMA((n_blk, 5)),
            pltpu.SemaphoreType.DMA,
        ],
        compiler_params=params(collective_id=0, has_side_effects=True),
        cost_estimate=cost(3 * seq * width * width, 14 * seq * width),
        name="qkv",
    )(inputs, row(ln1_gain), row(ln1_bias), w_query, column(b_query), w_key, w_value, column(b_value))

    per_head = pl.BlockSpec((head, seq), lambda h: (h, 0))
    per_square = pl.BlockSpec((1, seq, seq), lambda h: (h, 0, 0))
    ct, probs, inv_total, gs = pl.pallas_call(
        functools.partial(attend_spread_kernel, n_blk),
        grid=(H,),
        in_specs=[pl.BlockSpec(memory_space=pltpu.SMEM), per_head, per_head, per_head, anywhere],
        out_specs=[per_head, per_square, pl.BlockSpec((1, 1, seq), lambda h: (h, 0, 0)), anywhere],
        out_shape=[
            sds((width, seq), BF16),
            sds((H, seq, seq), BF16),
            sds((H, 1, seq), F32),
            sds((n_blk, tok, width), BF16),
        ],
        scratch_shapes=[
            pltpu.SemaphoreType.DMA((n_blk - 1,)),
            pltpu.SemaphoreType.DMA((n_blk - 1,)),
            pltpu.SemaphoreType.DMA,
        ],
        compiler_params=params(collective_id=1, has_side_effects=True),
        cost_estimate=cost(8 * seq * seq * width, 2 * H * seq * seq, H * seq * seq),
        name="attend",
    )(live, qt, kt, vt, out_grad)

    n_tile = 4
    tile = hidden // n_tile
    result = pl.pallas_call(
        functools.partial(ffn_kernel, n_blk),
        grid=(n_tile,),
        in_specs=[full((seq, width))] * 2
        + [
            wide,
            full((H, 1, seq)),
            full((width, width)),
            full((1, width)),
            full((1, width)),
            full((1, width)),
            pl.BlockSpec((width, tile), lambda j: (0, j)),
            pl.BlockSpec((1, tile), lambda j: (0, j)),
            pl.BlockSpec((tile, width), lambda j: (j, 0)),
            full((1, width)),
        ],
        out_specs=[piece] * n_blk
        + [
            pl.BlockSpec((tile, width), lambda j: (j, 0)),
            pl.BlockSpec((width, tile), lambda j: (0, j)),
            pl.BlockSpec((1, tile), lambda j: (0, j)),
            full((seq, width)),
            wide,
            full((width, width)),
            full((8, width)),
        ],
        out_shape=[sds((tok, width), BF16)] * n_blk
        + [
            sds((hidden, width), BF16),
            sds((width, hidden), BF16),
            sds((1, hidden), F32),
            sds((seq, width), F32),
            sds((width, seq), BF16),
            sds((width, width), BF16),
            sds((8, width), F32),
        ],
        scratch_shapes=[
            pltpu.VMEM((seq, width), F32),
            pltpu.VMEM((seq, width), BF16),
            pltpu.VMEM((width, seq), BF16),
            pltpu.VMEM((seq, width), F32),
            pltpu.VMEM((seq, width), F32),
            pltpu.VMEM((seq, tile), BF16),
            pltpu.VMEM((seq, tile), BF16),
        ],
        compiler_params=params(),
        cost_estimate=cost(8 * seq * width * hidden, 8 * width * hidden),
        name="ffn",
    )(
        xs.reshape(seq, width),
        gs.reshape(seq, width),
        ct,
        inv_total,
        w_output,
        row(b_output),
        row(ln2_gain),
        row(ln2_bias),
        w_in,
        row(b_in),
        w_out,
        row(b_out),
    )
    out_pieces = result[:n_blk]
    g_wout, g_win, g_bin, dmid, dct, g_wo, vec2 = result[n_blk:]

    bits = (n_dev - 1).bit_length()
    assert n_dev == 1 << bits

    def scatter(grad, order, wire):
        share = grad.shape[0] // n_dev
        order = list(order) + [b for b in range(bits) if b not in order]
        axes = list(range(bits - 1, -1, -1))
        terms = [grad.reshape((2,) * bits + (share,) + grad.shape[1:])]
        for b in order:
            at = axes.index(b)
            axes.pop(at)
            mine = (me >> b) & 1
            send = None
            keep = []
            for t in terms:
                other = lax.dynamic_index_in_dim(t, 1 - mine, at, keepdims=False)
                send = other.astype(F32) if send is None else send + other.astype(F32)
                keep.append(lax.dynamic_index_in_dim(t, mine, at, keepdims=False))
            got = lax.ppermute(send.astype(wire), ("dp", "blk"), [(i, i ^ (1 << b)) for i in range(n_dev)])
            terms = keep + [got]
        total = terms[0].astype(F32)
        for t in terms[1:]:
            total = total + t.astype(F32)
        return total

    s_wout = scatter(g_wout, (0, 1, 2, 3, 4), BF16)
    s_win = scatter(g_win, (0, 2, 1, 3, 4), BF16)
    s_wo = scatter(g_wo, (0, 3, 4, 1, 2), BF16)
    output = collect(out_pieces)

    dqt, dkt, dvt = pl.pallas_call(
        functools.partial(attend_back_kernel, scale),
        grid=(H,),
        in_specs=[per_square] + [per_head] * 5,
        out_specs=[per_head] * 3,
        out_shape=[sds((width, seq), BF16)] * 3,
        scratch_shapes=[pltpu.VMEM((seq, seq), BF16)],
        compiler_params=params(),
        cost_estimate=cost(10 * seq * seq * width, 2 * H * seq * seq),
        name="attend_back",
    )(probs, qt, kt, vt, dct, ct)

    result = pl.pallas_call(
        functools.partial(input_kernel, n_blk),
        in_specs=[full((seq, width))] * 2
        + [full((1, width)), wide, wide, wide]
        + [full((width, width))] * 3,
        out_specs=[piece] * n_blk + [full((8, width))],
        out_shape=[sds((tok, width), BF16)] * n_blk + [sds((8, width), F32)],
        compiler_params=params(),
        cost_estimate=cost(3 * seq * width * width, 14 * seq * width),
        name="input_grad",
    )(xs.reshape(seq, width), dmid, row(ln1_gain), dqt, dkt, dvt, w_query, w_key, w_value)
    input_grad = collect(result[:n_blk])
    vec1 = result[n_blk]

    col = pl.BlockSpec((width, cols), lambda j: (0, j))
    g_wq, g_wk, g_wv, vecq = pl.pallas_call(
        qkv_grad_kernel,
        grid=(n_col,),
        in_specs=[wide, strip, strip, strip],
        out_specs=[col, col, col, pl.BlockSpec((8, cols), lambda j: (0, j))],
        out_shape=[sds((width, width), BF16)] * 3 + [sds((8, width), F32)],
        compiler_params=params(),
        cost_estimate=cost(3 * seq * width * width, 14 * seq * width),
        name="qkv_grad",
    )(nt, dqt, dkt, dvt)
    s_wq = scatter(g_wq, (0, 1, 2, 3, 4), BF16)
    s_wk = scatter(g_wk, (0, 2, 3, 4, 1), BF16)
    s_wv = scatter(g_wv, (0, 3, 4, 1, 2), BF16)

    vectors = [vec1[0], vec1[1], vecq[0], vecq[1], vec2[3], vec2[1], vec2[2], g_bin[0], vec2[0]]
    packed = jnp.concatenate([v.reshape(n_dev, -1) for v in vectors], axis=1)
    packed = scatter(packed, (0, 1, 2, 3, 4), F32).reshape(-1)
    parts = []
    at = 0
    for v in vectors:
        size = v.shape[0] // n_dev
        parts.append(packed[at : at + size])
        at += size
    p_ln1g, p_ln1b, p_bq, p_bv, p_bo, p_ln2g, p_ln2b, p_bin, p_bout = parts
    return (
        output,
        input_grad,
        p_ln1g,
        p_ln1b,
        s_wq,
        p_bq,
        s_wk,
        s_wv,
        p_bv,
        s_wo,
        p_bo,
        p_ln2g,
        p_ln2b,
        s_win,
        p_bin,
        s_wout,
        p_bout,
    )


def solution(mesh):
    whole = P(("dp", "blk"))
    rows = P(("dp", "blk"), None)
    tokens = P("dp", "blk", None)
    in_specs = (tokens, P("dp"), tokens) + (P(),) * 15
    out_specs = (
        tokens,
        tokens,
        whole,
        whole,
        rows,
        whole,
        rows,
        rows,
        whole,
        rows,
        whole,
        whole,
        whole,
        rows,
        whole,
        rows,
        whole,
    )
    return jax.shard_map(body, mesh=mesh, in_specs=in_specs, out_specs=out_specs, check_vma=False)
```

```python
import functools

import jax
import jax.numpy as jnp
from jax import lax
from jax.experimental import pallas as pl
from jax.experimental.pallas import tpu as pltpu
from jax.sharding import PartitionSpec as P

H = 12
EPS = 1e-05
LOG2E = 1.4426950408889634
LN2 = 0.6931471805599453
INV_SQRT_2PI = 0.3989422804014327
SQRT_HALF = 0.7071067811865476
F32 = jnp.float32
BF16 = jnp.bfloat16
VMEM_LIMIT = 56 * 2**20

NN = (((1,), (0,)), ((), ()))
NT = (((1,), (1,)), ((), ()))
TN = (((0,), (0,)), ((), ()))

def dot(left, right, dims=NN):
    return lax.dot_general(left, right, dims, preferred_element_type=F32)


def params(**kw):
    return pltpu.CompilerParams(vmem_limit_bytes=VMEM_LIMIT, **kw)


def cost(macs, nbytes, exps=0):
    return pl.CostEstimate(flops=2 * macs, bytes_accessed=nbytes, transcendentals=exps)


def full(shape):
    return pl.BlockSpec(shape, lambda *_: (0,) * len(shape))


def as_row(ref):
    return ref[...].astype(F32)[None, :]


def center(v):
    mean = jnp.mean(v, axis=-1, keepdims=True)
    cent = v - mean
    var = jnp.mean(cent * cent, axis=-1, keepdims=True)
    rstd = lax.rsqrt(var + EPS)
    return cent * rstd, rstd


def gate(u):
    phi = 0.5 + 0.5 * lax.erf(u * SQRT_HALF)
    e = jnp.exp2(u * u * (-0.5 * LOG2E))
    return phi, u * e * INV_SQRT_2PI


def attend_kernel(n_blk, len_ref, q_ref, k_ref, v_ref, c_ref, p_ref, il_ref):
    seq = q_ref.shape[1]
    tok = seq // n_blk
    blk = lax.axis_index("blk")
    length = len_ref[blk]
    s = dot(k_ref[...].T, q_ref[...])
    live = [(blk ^ i) * tok < length for i in range(n_blk)]
    m = None
    for i in range(n_blk):
        mi = jnp.max(s[i * tok : (i + 1) * tok], axis=0, keepdims=True)
        mi = jnp.where(live[i], mi, -1e30)
        m = mi if m is None else jnp.maximum(m, mi)
    total = None
    ps = []
    for i in range(n_blk):
        p = jnp.exp2(s[i * tok : (i + 1) * tok] - jnp.where(live[i], m, 1e30))
        li = jnp.sum(p, axis=0, keepdims=True)
        total = li if total is None else total + li
        pb = p.astype(BF16)
        p_ref[0, i * tok : (i + 1) * tok] = pb
        ps.append(pb)
    inv = 1.0 / total
    c_ref[...] = (dot(v_ref[...], jnp.concatenate(ps, axis=0)) * inv).astype(BF16)
    il_ref[0] = inv


MESH = pl.DeviceIdType.MESH


def greet(partners):
    barrier = pltpu.get_barrier_semaphore()
    for where in partners:
        pl.semaphore_signal(barrier, inc=1, device_id=where, device_id_type=MESH)
    pl.semaphore_wait(barrier, len(partners))


def qkv_spread_kernel(
    scale,
    n_blk,
    x_any,
    gain,
    bias,
    wq_any,
    bq,
    wk_any,
    wv_any,
    bv,
    xs_any,
    nt_any,
    q_any,
    k_any,
    v_any,
    xbuf,
    wbuf,
    wt,
    nt,
    qkv,
    send,
    recv,
    wsem,
    osem,
    xsem,
):
    tok, width = xbuf.shape[1:]
    dp = lax.axis_index("dp")
    blk = lax.axis_index("blk")
    own = pltpu.make_async_copy(x_any.at[blk], xbuf.at[0], xsem)
    own.start()
    loads = [
        pltpu.make_async_copy(w, wbuf.at[i], wsem.at[i]) for i, w in enumerate((wq_any, wk_any, wv_any))
    ]
    for load in loads:
        load.start()
    greet([(dp, blk ^ s) for s in range(1, n_blk)])
    order = list(range(n_blk - 1, 0, -1))
    copies = {}
    for s in order:
        copies[s] = pltpu.make_async_remote_copy(
            src_ref=x_any.at[blk ^ s],
            dst_ref=xbuf.at[s],
            send_sem=send.at[s - 1],
            recv_sem=recv.at[s - 1],
            device_id=(dp, blk ^ s),
            device_id_type=MESH,
        )
        copies[s].start()
    for i, load in enumerate(loads):
        load.wait()
        wt[i] = wbuf[i].T
    cols = jnp.concatenate([as_row(bq), as_row(bv), jnp.zeros((6, width), F32)], axis=0).T
    writes = []
    for s in range(n_blk):
        if s == 0:
            own.wait()
        else:
            copies[s].wait_recv()
        sl = slice(s * tok, (s + 1) * tok)
        n, _ = center(xbuf[s].astype(F32))
        n = (n * as_row(gain) + as_row(bias)).astype(BF16).T
        nt[:, sl] = n
        qkv[0, :, sl] = ((dot(wt[0], n) + cols[:, :1]) * scale).astype(BF16)
        qkv[1, :, sl] = dot(wt[1], n).astype(BF16)
        qkv[2, :, sl] = (dot(wt[2], n) + cols[:, 1:2]).astype(BF16)
        for i, (src, dst) in enumerate(
            (
                (xbuf.at[s], xs_any.at[s]),
                (nt.at[:, sl], nt_any.at[:, sl]),
                (qkv.at[0, :, sl], q_any.at[:, sl]),
                (qkv.at[1, :, sl], k_any.at[:, sl]),
                (qkv.at[2, :, sl], v_any.at[:, sl]),
            )
        ):
            write = pltpu.make_async_copy(src, dst, osem.at[s, i])
            write.start()
            writes.append(write)
    for s in order:
        copies[s].wait_send()
    for write in writes:
        write.wait()


def attend_spread_kernel(n_blk, len_ref, q_ref, k_ref, v_ref, g_any, c_ref, p_ref, il_ref, gs_any, send, recv, osem):
    h = pl.program_id(0)
    dp = lax.axis_index("dp")
    blk = lax.axis_index("blk")

    def copy(s):
        return pltpu.make_async_remote_copy(
            src_ref=g_any.at[blk ^ s],
            dst_ref=gs_any.at[s],
            send_sem=send.at[s - 1],
            recv_sem=recv.at[s - 1],
            device_id=(dp, blk ^ s),
            device_id_type=MESH,
        )

    own = pltpu.make_async_copy(g_any.at[blk], gs_any.at[0], osem)

    @pl.when(h == 0)
    def _():
        greet([(dp, blk ^ s) for s in range(1, n_blk)])
        own.start()
        for s in range(1, n_blk):
            copy(s).start()

    attend_kernel(n_blk, len_ref, q_ref, k_ref, v_ref, c_ref, p_ref, il_ref)

    @pl.when(h == pl.num_programs(0) - 1)
    def _():
        own.wait()
        for s in range(1, n_blk):
            copy(s).wait()


def regroup(v, share):
    def slab(c, x, y):
        at = [(z * 8 + y * 4 + x * 2 + c) * share for z in range(4)]
        return jnp.concatenate([v[a : a + share] for a in at], axis=0)

    return [[[slab(c, x, y) for y in range(2)] for x in range(2)] for c in range(2)]


CXY = [(c, x, y) for c in range(2) for x in range(2) for y in range(2)]


class Scatter:
    def __init__(self, source, cols, share, first, out, bufs, place):
        self.source, self.cols, self.share, self.out = source, cols, share, out
        self.b = bufs
        dp, blk = place
        self.c, self.x, self.y, self.z = blk & 1, blk >> 1, dp & 1, dp >> 1
        self.first = first
        ids = {"x": (dp, blk ^ 2), "y": (dp ^ 1, blk)}
        self.mp = self.x if first == "x" else self.y
        self.mq = self.y if first == "x" else self.x
        self.core_id = (dp, blk ^ 1)
        self.p_id = ids[first]
        self.q_id = ids["y" if first == "x" else "x"]
        self.z_ids = [(((self.z + d) & 3) * 2 + self.y, blk) for d in (1, 2, 3)]
        self.chunk = share if share % 16 == 0 else 2 * share

    def remote(self, src, dst, i, where):
        return pltpu.make_async_remote_copy(
            src_ref=src,
            dst_ref=dst,
            send_sem=self.b["send"].at[i],
            recv_sem=self.b["recv"].at[i],
            device_id=where,
            device_id_type=MESH,
        )

    def part(self, c):
        if self.cols is None:
            return self.source.at[c]
        return self.source.at[c, :, :, :, self.cols]

    def core_copy(self):
        return self.remote(self.part(1 - self.c), self.b["r0"], 0, self.core_id)

    def load(self):
        return pltpu.make_async_copy(self.part(self.c), self.b["keep"], self.b["load"])

    def p_copy(self):
        return self.remote(self.b["t1"], self.b["r1"], 1, self.p_id)

    def q_copy(self):
        return self.remote(self.b["t2"], self.b["r2"], 2, self.q_id)

    def z_copies(self):
        return [self.remote(self.b["t3"].at[d], self.b["r3"].at[d], 3 + d, self.z_ids[d]) for d in range(3)]

    def pick(self, ref, a, b, rows):
        return (ref[a, b, rows] if self.first == "x" else ref[b, a, rows]).astype(F32)

    def base(self, a, b, rows):
        if "keep" in self.b:
            own = self.pick(self.b["keep"], a, b, rows)
        else:
            own = (
                self.source[self.c, a, b, rows] if self.first == "x" else self.source[self.c, b, a, rows]
            ).astype(F32)
        return own + self.pick(self.b["r0"], a, b, rows)

    def each(self, fn):
        rows = 4 * self.share

        def step(i, carry):
            fn(i, pl.ds(pl.multiple_of(i * self.chunk, self.chunk), self.chunk))
            return carry

        lax.fori_loop(0, rows // self.chunk, step, 0)

    def stage0(self):
        self.core_copy().start()
        if "keep" in self.b:
            self.load().start()

    def stage1(self):
        if "keep" in self.b:
            self.load().wait()
        self.core_copy().wait()
        for b in range(2):

            def fn(i, rows):
                self.b["t1"][b, rows] = self.base(1 - self.mp, b, rows).astype(BF16)

            self.each(fn)
        self.p_copy().start()

    def stage2(self):
        self.p_copy().wait()

        def fn(i, rows):
            v = self.base(self.mp, 1 - self.mq, rows) + self.b["r1"][1 - self.mq, rows].astype(F32)
            self.b["t2"][rows] = v.astype(BF16)

        self.each(fn)
        self.q_copy().start()

    def stage3(self):
        self.q_copy().wait()
        share = self.share
        per = self.chunk // share
        f = self.b["f"]

        def fn(i, rows):
            v = self.base(self.mp, self.mq, rows)
            v = v + self.b["r1"][self.mq, rows].astype(F32) + self.b["r2"][rows].astype(F32)
            for k in range(per):
                f[i * per + k] = v[k * share : (k + 1) * share]

        self.each(fn)
        pad = self.b["t3"].shape[1] - share
        for d in range(3):
            v = f[(self.z + d + 1) & 3]
            if pad:
                v = jnp.concatenate([v, jnp.zeros((pad, v.shape[1]), F32)], axis=0)
            self.b["t3"][d] = v.astype(BF16)
        for copy in self.z_copies():
            copy.start()

    def stage4(self):
        for copy in self.z_copies():
            copy.wait()
        v = self.b["f"][self.z]
        for d in range(3):
            v = v + self.b["r3"][d].astype(F32)[: self.share]
        self.out(v)


def scatter_scratch(share, cols, in_hbm):
    rows = 4 * share
    pad = -(-share // 16) * 16
    bufs = {
        "r0": pltpu.VMEM((2, 2, rows, cols), BF16),
        "t1": pltpu.VMEM((2, rows, cols), BF16),
        "r1": pltpu.VMEM((2, rows, cols), BF16),
        "t2": pltpu.VMEM((rows, cols), BF16),
        "r2": pltpu.VMEM((rows, cols), BF16),
        "t3": pltpu.VMEM((3, pad, cols), BF16),
        "r3": pltpu.VMEM((3, pad, cols), BF16),
        "f": pltpu.VMEM((4, share, cols), F32),
        "send": pltpu.SemaphoreType.DMA((6,)),
        "recv": pltpu.SemaphoreType.DMA((6,)),
    }
    if in_hbm:
        bufs["keep"] = pltpu.VMEM((2, 2, rows, cols), BF16)
        bufs["load"] = pltpu.SemaphoreType.DMA
    return bufs


def ffn_kernel(n_blk, *refs):
    x_ref, g = refs[:2]
    (ct_ref, il_ref, wo_ref, bo_ref, gain_ref, bias_ref, win_ref, bin_ref, wout_ref, bout_ref) = refs[2:12]
    rest = refs[12:]
    outs = rest[:n_blk]
    (gwout_ref, gwin_ref, gbin_ref, dmid_ref, dot_ref, gwo_ref, vec_ref) = rest[n_blk : n_blk + 7]
    mid, n2, n2t, acc_o, acc_d, act, dpre = rest[n_blk + 7 :]
    tok = outs[0].shape[0]
    j = pl.program_id(0)

    @pl.when(j == 0)
    def _():
        for s in range(n_blk):
            sl = slice(s * tok, (s + 1) * tok)
            m = x_ref[sl].astype(F32) + dot(ct_ref[:, sl], wo_ref[...], TN) + bo_ref[...]
            mid[sl] = m
            acc_o[sl] = m + bout_ref[...]
            acc_d[sl] = jnp.zeros_like(m)
            n, _ = center(m)
            nb = (n * gain_ref[...] + bias_ref[...]).astype(BF16)
            n2[sl] = nb
            n2t[:, sl] = nb.T

    bin_grad = None
    for s in range(n_blk):
        sl = slice(s * tok, (s + 1) * tok)
        pre = dot(n2[sl], win_ref[...]) + bin_ref[...]
        phi, slope = gate(pre)
        a = (pre * phi).astype(BF16)
        dact = dot(g[sl], wout_ref[...], NT)
        dp = (dact * (phi + slope)).astype(BF16)
        act[sl] = a
        dpre[sl] = dp
        col = jnp.sum(dp.astype(F32), axis=0, keepdims=True)
        bin_grad = col if bin_grad is None else bin_grad + col
        acc_o[sl] += dot(a, wout_ref[...])
        acc_d[sl] += dot(dp, win_ref[...], NT)
    gbin_ref[...] = bin_grad
    gwout_ref[...] = dot(act[...], g[...], TN).astype(BF16)
    gwin_ref[...] = dot(n2t[...], dpre[...]).astype(BF16)

    @pl.when(j == pl.num_programs(0) - 1)
    def _():
        head = wo_ref.shape[0] // H
        sums = [None] * 4
        for s in range(n_blk):
            sl = slice(s * tok, (s + 1) * tok)
            outs[s][...] = acc_o[sl].astype(BF16)
            n, rstd = center(mid[sl])
            e = acc_d[sl]
            gf = g[sl].astype(F32)
            f = e * gain_ref[...]
            dm = gf + rstd * (
                f - jnp.mean(f, axis=-1, keepdims=True) - n * jnp.mean(f * n, axis=-1, keepdims=True)
            )
            dmid_ref[sl] = dm
            db = dm.astype(BF16)
            n2[sl] = db
            for i, term in enumerate((gf, e * n, e, db.astype(F32))):
                col = jnp.sum(term, axis=0, keepdims=True)
                sums[i] = col if sums[i] is None else sums[i] + col
            dc = dot(wo_ref[...], db, NT)
            for h in range(H):
                hs = slice(h * head, (h + 1) * head)
                dot_ref[hs, sl] = (dc[hs] * il_ref[h, :, sl]).astype(BF16)
        for i in range(4):
            vec_ref[i : i + 1] = sums[i]
        gwo_ref[...] = dot(ct_ref[...], n2[...]).astype(BF16)


def attend_back_kernel(scale, p_ref, q_ref, k_ref, v_ref, do_ref, c_ref, dq_ref, dk_ref, dv_ref, ds):
    seq = q_ref.shape[1]
    do = do_ref[...]
    vh = v_ref[...].T
    delta = jnp.sum(do.astype(F32) * c_ref[...].astype(F32), axis=0, keepdims=True)
    step = seq // 2
    for c in range(2):
        sl = slice(c * step, (c + 1) * step)
        dp = dot(vh, do[:, sl])
        d = (p_ref[0, :, sl].astype(F32) * (dp - delta[:, sl])).astype(BF16)
        ds[:, sl] = d
        dq_ref[:, sl] = (dot(k_ref[...], d) * scale).astype(BF16)
    dv_ref[...] = dot(p_ref[0], do, NT).T.astype(BF16)
    dk_ref[...] = (dot(ds[...], q_ref[...], NT) * LN2).T.astype(BF16)


def input_kernel(n_blk, x_ref, dmid_ref, gain_ref, dq_ref, dk_ref, dv_ref, wq_ref, wk_ref, wv_ref, *rest):
    outs = rest[:n_blk]
    vec_ref = rest[n_blk]
    tok = outs[0].shape[0]
    sums = [None] * 2
    for s in range(n_blk):
        sl = slice(s * tok, (s + 1) * tok)
        et = dot(wq_ref[...], dq_ref[:, sl]) + dot(wk_ref[...], dk_ref[:, sl]) + dot(wv_ref[...], dv_ref[:, sl])
        e = et.T
        n, rstd = center(x_ref[sl].astype(F32))
        f = e * gain_ref[...]
        dx = dmid_ref[sl] + rstd * (
            f - jnp.mean(f, axis=-1, keepdims=True) - n * jnp.mean(f * n, axis=-1, keepdims=True)
        )
        outs[s][...] = dx.astype(BF16)
        for i, term in enumerate((e * n, e)):
            col = jnp.sum(term, axis=0, keepdims=True)
            sums[i] = col if sums[i] is None else sums[i] + col
    for i in range(2):
        vec_ref[i : i + 1] = sums[i]


def qkv_grad_kernel(nt_ref, dq_ref, dk_ref, dv_ref, gq_ref, gk_ref, gv_ref, vec_ref):
    nt = nt_ref[...]
    ones = jnp.ones((8, nt.shape[1]), BF16)
    gq_ref[...] = dot(nt, dq_ref[...], NT).astype(BF16)
    gk_ref[...] = dot(nt, dk_ref[...], NT).astype(BF16)
    gv_ref[...] = dot(nt, dv_ref[...], NT).astype(BF16)
    vec_ref[0:1] = dot(ones, dq_ref[...], NT)[:1]
    vec_ref[1:2] = dot(ones, dv_ref[...], NT)[:1]


def ffn_host_kernel(names, n_blk, *refs):
    r = dict(zip(names, refs))
    i = pl.program_id(0)
    j = i & 3
    dp = lax.axis_index("dp")
    blk = lax.axis_index("blk")
    core, y = blk & 1, dp & 1
    mid, acc, n2, n2t, act, gp, gw, r0, t1, r1 = [
        r[k] for k in ("mid", "acc", "n2", "n2t", "act", "gp", "gw", "r0", "t1", "r1")
    ]
    g, win, wout, ct = r["g"], r["win"], r["wout"], r["ct"]
    seq, width = mid.shape
    tok = seq // n_blk
    tile = act.shape[1]
    share_f = gw.shape[4]
    rows = [slice(s * tok, (s + 1) * tok) for s in range(n_blk)]

    def core_copy(plane):
        return pltpu.make_async_remote_copy(
            src_ref=gw.at[1 - core, :, :, plane],
            dst_ref=r0.at[:, :, plane],
            send_sem=r["csend"].at[plane],
            recv_sem=r["crecv"].at[plane],
            device_id=(dp, blk ^ 1),
            device_id_type=MESH,
        )

    def y_copy():
        return pltpu.make_async_remote_copy(
            src_ref=t1, dst_ref=r1, send_sem=r["ysend"], recv_sem=r["yrecv"], device_id=(dp ^ 1, blk), device_id_type=MESH
        )

    def out_copy(s):
        src, dst = r["obuf"].at[s], r["output"].at[blk]
        if s == 0:
            return pltpu.make_async_copy(src, dst, r["lsem"].at[0])
        return pltpu.make_async_remote_copy(
            src_ref=src,
            dst_ref=dst,
            send_sem=r["osend"].at[s - 1],
            recv_sem=r["orecv"].at[s - 1],
            device_id=(dp, blk ^ s),
            device_id_type=MESH,
        )

    @pl.when(i == 0)
    def _():
        greet([(dp, blk ^ 1), (dp, blk ^ 2), (dp, blk ^ 3), (dp ^ 1, blk)])
        bins = as_row(r["bin"])
        for k in range(4):
            r["bins"][k] = bins[:, k * tile : (k + 1) * tile]
        for sl in rows:
            m = r["x"][sl].astype(F32) + dot(ct[:, sl], r["wo"][...], TN) + as_row(r["bo"])
            mid[sl] = m
            acc[sl] = m + as_row(r["bout"])
            n, _ = center(m)
            nb = (n * as_row(r["gain"]) + as_row(r["bias"])).astype(BF16)
            n2[sl] = nb
            n2t[:, sl] = nb.T

    @pl.when(i < 4)
    def _():
        for sl in rows:
            pre = dot(n2[sl], win[...]) + r["bins"][j]
            phi, slope = gate(pre)
            a = (pre * phi).astype(BF16)
            act[sl] = a
            gp[j, sl] = (phi + slope).astype(BF16)
            acc[sl] += dot(a, wout[...])
        v = dot(act[...], g[...], TN)
        for c, x, yy in CXY:
            at = (yy * 4 + x * 2 + c) * share_f
            gw[c, x, yy, j] = v[at : at + share_f].astype(BF16)
        core_copy(j).start()

    @pl.when(i == 4)
    def _():
        for s in range(n_blk - 1, -1, -1):
            r["obuf"][s] = acc[rows[s]].astype(BF16)
            out_copy(s).start()
            acc[rows[s]] = jnp.zeros((tok, width), F32)

    @pl.when(i >= 4)
    def _():
        total = None
        for sl in rows:
            d = (dot(g[sl], wout[...], NT) * gp[j, sl].astype(F32)).astype(BF16)
            act[sl] = d
            col = jnp.sum(d.astype(F32), axis=0, keepdims=True)
            total = col if total is None else total + col
            acc[sl] += dot(d, win[...], NT)
        r["bing"][j] = total
        v = regroup(dot(n2t[...], act[...]), width // 32)
        for c, x, yy in CXY:
            r["gwin"][c, x, yy] = v[c][x][yy].astype(BF16)

    @pl.when(i == 4)
    def _():
        for k in range(4):
            core_copy(k).wait()

        def step(k, carry):
            for x in range(2):
                t1[x, k] = (gw[core, x, 1 - y, k].astype(F32) + r0[x, 1 - y, k].astype(F32)).astype(BF16)
            return carry

        lax.fori_loop(0, 4, step, 0)
        y_copy().start()

    @pl.when(i == 7)
    def _():
        head = width // H
        sums = [None] * 4
        for sl in rows:
            n, rstd = center(mid[sl])
            e = acc[sl]
            gf = g[sl].astype(F32)
            f = e * as_row(r["gain"])
            dm = gf + rstd * (
                f - jnp.mean(f, axis=-1, keepdims=True) - n * jnp.mean(f * n, axis=-1, keepdims=True)
            )
            mid[sl] = dm
            db = dm.astype(BF16)
            n2[sl] = db
            for k, term in enumerate((gf, e * n, e, db.astype(F32))):
                col = jnp.sum(term, axis=0, keepdims=True)
                sums[k] = col if sums[k] is None else sums[k] + col
            dc = dot(r["wo"][...], db, NT)
            for h in range(H):
                hs = slice(h * head, (h + 1) * head)
                r["dot"][hs, sl] = (dc[hs] * r["il"][h, :, sl]).astype(BF16)
        save = pltpu.make_async_copy(mid, r["dmid"], r["lsem"].at[1])
        save.start()
        vec = r["vec"]
        vec[...] = jnp.zeros_like(vec)
        for k in range(4):
            vec[4 + k : 5 + k] = sums[k]
            vec[8 + k : 9 + k] = r["bing"][k]
        v = regroup(dot(ct[...], n2[...]), width // 32)
        for c, x, yy in CXY:
            r["gwo"][c, x, yy] = v[c][x][yy].astype(BF16)
        y_copy().wait()

        def step(k, carry):
            for x in range(2):
                v = gw[core, x, y, k].astype(F32) + r0[x, y, k].astype(F32) + r1[x, k].astype(F32)
                t1[x, k] = v.astype(BF16)
            return carry

        lax.fori_loop(0, 4, step, 0)
        part = pltpu.make_async_copy(t1, r["part"], r["lsem"].at[2])
        part.start()
        for s in range(n_blk):
            out_copy(s).wait()
        save.wait()
        part.wait()


class Resume:
    def __init__(self, r, place):
        dp, blk = place
        self.r = r
        self.x, self.y, self.z = blk >> 1, dp & 1, dp >> 1
        self.ids = [(((self.z + d) & 3) * 2 + self.y, blk) for d in (1, 2, 3)] + [(dp, blk ^ 2)]

    def remote(self, src, dst, i):
        return pltpu.make_async_remote_copy(
            src_ref=src,
            dst_ref=dst,
            send_sem=self.r["w_send"].at[i],
            recv_sem=self.r["w_recv"].at[i],
            device_id=self.ids[i],
            device_id_type=MESH,
        )

    def z_copies(self):
        return [
            self.remote(self.r["part"].at[:, (self.z + d + 1) & 3], self.r["w_rz"].at[d], d) for d in range(3)
        ]

    def load(self):
        return pltpu.make_async_copy(self.r["part"].at[:, self.z], self.r["w_keep"], self.r["lsem"].at[0])

    def x_copy(self):
        return self.remote(self.r["w_t"], self.r["w_rx"], 3)

    def stage0(self):
        for copy in self.z_copies():
            copy.start()
        self.load().start()

    def stage1(self):
        self.load().wait()
        for copy in self.z_copies():
            copy.wait()
        for k in range(2):
            v = self.r["w_keep"][k].astype(F32)
            for d in range(3):
                v = v + self.r["w_rz"][d, k].astype(F32)
            self.r["w_f"][k] = v
        self.r["w_t"][...] = self.r["w_f"][1 - self.x].astype(BF16)
        self.x_copy().start()

    def stage2(self):
        self.x_copy().wait()
        self.r["s_wout"][...] = self.r["w_f"][self.x] + self.r["w_rx"][...].astype(F32)


def finish_kernel(n_big, *refs):
    src, vec = refs[:n_big], refs[n_big]
    dst, small = refs[n_big + 1 : 2 * n_big + 1], refs[2 * n_big + 1 :]
    for a, b in zip(src[:2], dst[:2]):
        b[...] = a[...]

    @pl.when(pl.program_id(0) == 0)
    def _():
        for a, b in zip(src[2:], dst[2:]):
            b[...] = a[...]
        me = lax.axis_index("dp") * lax.axis_size("blk") + lax.axis_index("blk")
        share = small[0].shape[0]
        wide = small[8].shape[0]
        width = vec.shape[1]
        moved = pltpu.roll(vec[:8], lax.rem(width - me * share, width), 1)
        for i, k in enumerate((0, 1, 2, 3, 7, 5, 6, 4)):
            small[i][...] = moved[k, :share]
        each = width // wide
        lines = vec[8:16]
        moved = pltpu.roll(lines, lax.rem(width - lax.rem(me, each) * wide, width), 1)
        row = lax.div(me, each)
        pick = lax.broadcasted_iota(jnp.int32, moved.shape, 0) == row
        small[8][...] = jnp.sum(jnp.where(pick, moved, 0.0), axis=0)[:wide]


def back_kernel(scale, names, tasks, plan, *refs):
    r = dict(zip(names, refs))
    h = pl.program_id(0)
    dp = lax.axis_index("dp")
    blk = lax.axis_index("blk")
    place = (dp, blk)
    n_blk, tok, width = r["xs"].shape
    seq = n_blk * tok
    head = width // H
    dcat, wcat, gq, vec = r["dcat"], r["wcat"], r["gq"], r["vec"]

    def put(ref, cols):
        def out(v):
            if cols is None:
                ref[...] = v
            else:
                ref[:, cols] = v

        return out

    jobs = {}
    for name, source, index, cols, share, first, out, out_cols in tasks:
        ref = r[source] if index is None else r[source].at[index]
        bufs = {k: r[name + "_" + k] for k in SCATTER_KEYS if name + "_" + k in r}
        if isinstance(out, tuple):
            outs = [put(r[o], out_cols) for o in out]

            def sink(v, outs=outs):
                each = v.shape[1] // len(outs)
                for i, o in enumerate(outs):
                    o(v[:, i * each : (i + 1) * each])

        else:
            sink = put(r[out], out_cols)
        jobs[name] = Scatter(ref, cols, share, first, sink, bufs, place)

    jobs["wout"] = Resume(r, place)

    def spread(src, dst, sems, s):
        return pltpu.make_async_remote_copy(
            src_ref=src.at[s],
            dst_ref=dst.at[blk],
            send_sem=sems[0].at[s - 1],
            recv_sem=sems[1].at[s - 1],
            device_id=(dp, blk ^ s),
            device_id_type=MESH,
        )

    def in_copy(s):
        if s == 0:
            return pltpu.make_async_copy(r["dx"].at[0], r["input_grad"].at[blk], r["lsem"].at[1])
        return spread(r["dx"], r["input_grad"], (r["isend"], r["irecv"]), s)

    def loads():
        pairs = [(r["xs"], r["xbuf"]), (r["dmid"], r["dmbuf"])]
        pairs += [(r[w], wcat.at[:, i * width : (i + 1) * width]) for i, w in enumerate(("wq", "wk", "wv"))]
        return [pltpu.make_async_copy(a, b, r["lsem"].at[2 + i]) for i, (a, b) in enumerate(pairs)]

    z, y = dp >> 1, dp & 1
    vec_ids = [[(dp, blk ^ 1)], [(dp, blk ^ 2)], [(dp ^ 1, blk)]]
    vec_ids.append([(((z + d) & 3) * 2 + y, blk) for d in (1, 2, 3)])

    def vec_copies(stage):
        return [
            pltpu.make_async_remote_copy(
                src_ref=vec,
                dst_ref=r["rvec"].at[stage + d],
                send_sem=r["vsend"].at[stage + d],
                recv_sem=r["vrecv"].at[stage + d],
                device_id=where,
                device_id_type=MESH,
            )
            for d, where in enumerate(vec_ids[stage])
        ]

    def vec_start(stage):
        for copy in vec_copies(stage):
            copy.start()

    def vec_end(stage):
        copies = vec_copies(stage)
        for copy in copies:
            copy.wait()
        for d in range(len(copies)):
            vec[...] += r["rvec"][stage + d]

    def input_piece(s, sums):
        sl = slice(s * tok, (s + 1) * tok)
        e = dot(wcat[...], dcat[:, sl]).T
        n, rstd = center(r["xbuf"][s].astype(F32))
        f = e * as_row(r["gain"])
        dx = r["dmbuf"][sl] + rstd * (
            f - jnp.mean(f, axis=-1, keepdims=True) - n * jnp.mean(f * n, axis=-1, keepdims=True)
        )
        r["dx"][s] = dx.astype(BF16)
        in_copy(s).start()
        new = [jnp.sum(t, axis=0, keepdims=True) for t in (e * n, e)]
        return new if sums is None else [a + b for a, b in zip(sums, new)]

    @pl.when(h == 0)
    def _():
        greet(
            [(dp, blk ^ 1), (dp, blk ^ 2), (dp, blk ^ 3), (dp ^ 1, blk)]
            + [(((z + d) & 3) * 2 + y, blk) for d in (1, 2, 3)]
        )
        for load in loads():
            load.start()
        vec[...] = r["vec_in"][...]

    def act(item):
        kind, what = item
        getattr(jobs[kind], "stage%d" % what)()

    for at in range(H):
        if plan.get(at):

            @pl.when(h == at)
            def _(at=at):
                for item in plan[at]:
                    act(item)

    @pl.when(h < H)
    def _():
        do = r["do"][...]
        vh = r["v"][...].T
        delta = jnp.sum(do.astype(F32) * r["ct"][...].astype(F32), axis=0, keepdims=True)
        step = seq // 2
        base = pl.multiple_of(h * head, head)
        for c in range(2):
            sl = slice(c * step, (c + 1) * step)
            dpr = dot(vh, do[:, sl])
            d = (r["p"][0, :, sl].astype(F32) * (dpr - delta[:, sl])).astype(BF16)
            r["ds"][:, sl] = d
            dcat[pl.ds(base, head), sl] = (dot(r["k"][...], d) * scale).astype(BF16)
        dcat[pl.ds(base + 2 * width, head)] = dot(r["p"][0], do, NT).T.astype(BF16)
        dcat[pl.ds(base + width, head)] = (dot(r["ds"][...], r["q"][...], NT) * LN2).T.astype(BF16)

    n_group = gq.shape[0]
    cols = width // n_group
    for gi in range(n_group):

        @pl.when(h == (gi + 1) * (H // n_group) - 1)
        def _(gi=gi):
            nt = r["nt"][...]
            ones = jnp.ones((8, seq), BF16)
            for t in range(3):
                part = dcat[t * width + gi * cols : t * width + (gi + 1) * cols]
                v = regroup(dot(nt, part, NT), width // 32)
                for c, x, y in CXY:
                    gq[gi, c, x, y, :, t * cols : (t + 1) * cols] = v[c][x][y].astype(BF16)
                if t != 1:
                    row = 2 if t == 0 else 3
                    vec[row : row + 1, gi * cols : (gi + 1) * cols] = dot(ones, part, NT)[:1]
            jobs["q%d" % gi].stage0()

    @pl.when(h == H)
    def _():
        sums = None
        for load in loads():
            load.wait()
        for item in plan["tail"]:
            kind, what = item
            if kind == "piece":
                sums = input_piece(what, sums)
                if what == 0:
                    vec[0:1] = sums[0]
                    vec[1:2] = sums[1]
            elif kind == "vec":
                if what > 0:
                    vec_end(what - 1)
                if what < 4:
                    vec_start(what)
            else:
                act(item)
        r["vec_out"][...] = vec[...]
        for s in range(n_blk):
            in_copy(s).wait()


PLAN = {
    0: [("wout", 0), ("wo", 0), ("a2", 0), ("b2", 0)],
    1: [("wo", 1)],
    2: [("a2", 1)],
    3: [("b2", 1)],
    5: [("q0", 1), ("wo", 2)],
    8: [("a2", 2), ("q0", 2)],
    9: [("q1", 1)],
    10: [("wout", 1)],
    11: [("wo", 3)],
    "tail": [
        ("piece", 3),
        ("b2", 2),
        ("piece", 2),
        ("q2", 1),
        ("piece", 1),
        ("a2", 3),
        ("q0", 3),
        ("piece", 0),
        ("vec", 0),
        ("q1", 2),
        ("wout", 2),
        ("vec", 1),
        ("b2", 3),
        ("q2", 2),
        ("vec", 2),
        ("wo", 4),
        ("q1", 3),
        ("vec", 3),
        ("q2", 3),
        ("a2", 4),
        ("q0", 4),
        ("vec", 4),
        ("b2", 4),
        ("q1", 4),
        ("q2", 4),
    ],
}

SCATTER_KEYS = ("r0", "t1", "r1", "t2", "r2", "t3", "r3", "f", "send", "recv", "keep", "load")


def body(
    inputs,
    lengths,
    out_grad,
    ln1_gain,
    ln1_bias,
    w_query,
    b_query,
    w_key,
    w_value,
    b_value,
    w_output,
    b_output,
    ln2_gain,
    ln2_bias,
    w_in,
    b_in,
    w_out,
    b_out,
):
    n_seq, tok, width = inputs.shape
    n_blk = lax.axis_size("blk")
    n_dp = lax.axis_size("dp")
    n_dev = n_blk * n_dp
    assert n_seq == n_blk
    seq = tok * n_blk
    hidden = w_in.shape[1]
    head = width // H
    scale = head ** (-0.5)
    blk = lax.axis_index("blk")
    me = lax.axis_index("dp") * n_blk + blk

    def swap(v, s):
        return lax.ppermute(v, "blk", [(i, i ^ s) for i in range(n_blk)])

    def collect(pieces):
        back = [pieces[0]] + [swap(pieces[s], s) for s in range(1, n_blk)]
        out = jnp.zeros((n_seq, tok, width), BF16)
        for s in range(n_blk):
            out = lax.dynamic_update_index_in_dim(out, back[s], blk ^ s, 0)
        return out

    row = lambda v: v.astype(F32).reshape(1, -1)


    sds = jax.ShapeDtypeStruct
    piece = full((tok, width))
    wide = full((width, seq))
    n_col = 3
    cols = width // n_col
    strip = pl.BlockSpec((cols, seq), lambda j: (j, 0))
    anywhere = pl.BlockSpec(memory_space=pl.ANY)
    vmem = pl.BlockSpec(memory_space=pltpu.VMEM)
    xs, nt, qt, kt, vt = pl.pallas_call(
        functools.partial(qkv_spread_kernel, scale * LOG2E, n_blk),
        in_specs=[anywhere, vmem, vmem, anywhere, vmem, anywhere, anywhere, vmem],
        out_specs=[anywhere] * 5,
        out_shape=[sds((n_blk, tok, width), BF16)] + [sds((width, seq), BF16)] * 4,
        scratch_shapes=[
            pltpu.VMEM((n_blk, tok, width), BF16),
            pltpu.VMEM((3, width, width), BF16),
            pltpu.VMEM((3, width, width), BF16),
            pltpu.VMEM((width, seq), BF16),
            pltpu.VMEM((3, width, seq), BF16),
            pltpu.SemaphoreType.DMA((n_blk - 1,)),
            pltpu.SemaphoreType.DMA((n_blk - 1,)),
            pltpu.SemaphoreType.DMA((3,)),
            pltpu.SemaphoreType.DMA((n_blk, 5)),
            pltpu.SemaphoreType.DMA,
        ],
        compiler_params=params(collective_id=0, has_side_effects=True),
        cost_estimate=cost(3 * seq * width * width, 14 * seq * width),
        name="qkv",
    )(inputs, ln1_gain, ln1_bias, w_query, b_query, w_key, w_value, b_value)

    per_head = pl.BlockSpec((head, seq), lambda h: (h, 0))
    per_square = pl.BlockSpec((1, seq, seq), lambda h: (h, 0, 0))
    ct, probs, inv_total, gs = pl.pallas_call(
        functools.partial(attend_spread_kernel, n_blk),
        grid=(H,),
        in_specs=[pl.BlockSpec(memory_space=pltpu.SMEM), per_head, per_head, per_head, anywhere],
        out_specs=[per_head, per_square, pl.BlockSpec((1, 1, seq), lambda h: (h, 0, 0)), anywhere],
        out_shape=[
            sds((width, seq), BF16),
            sds((H, seq, seq), BF16),
            sds((H, 1, seq), F32),
            sds((n_blk, tok, width), BF16),
        ],
        scratch_shapes=[
            pltpu.SemaphoreType.DMA((n_blk - 1,)),
            pltpu.SemaphoreType.DMA((n_blk - 1,)),
            pltpu.SemaphoreType.DMA,
        ],
        compiler_params=params(collective_id=1, has_side_effects=True),
        cost_estimate=cost(8 * seq * seq * width, 2 * H * seq * seq, H * seq * seq),
        name="attend",
    )(lengths, qt, kt, vt, out_grad)

    if n_dp == 8 and n_blk == 4 and width % 768 == 0 and hidden == 4 * width:
        share, share_f = width // n_dev, hidden // n_dev
        tile = hidden // 4
        once = lambda shape: pl.BlockSpec(shape, lambda i: (0,) * len(shape), pipeline_mode=pl.Buffered(1))
        vec_rows = 16
        ins = {
            "x": (xs.reshape(seq, width), once((seq, width))),
            "g": (gs.reshape(seq, width), once((seq, width))),
            "ct": (ct, once((width, seq))),
            "il": (inv_total, once((H, 1, seq))),
            "wo": (w_output, once((width, width))),
            "bo": (b_output, once((width,))),
            "gain": (ln2_gain, once((width,))),
            "bias": (ln2_bias, once((width,))),
            "bout": (b_out, once((width,))),
            "bin": (b_in, once((hidden,))),
            "win": (w_in, pl.BlockSpec((width, tile), lambda i: (0, i % 4))),
            "wout": (w_out, pl.BlockSpec((tile, width), lambda i: (i % 4, 0))),
        }
        outs = {
            "output": (sds((n_seq, tok, width), BF16), anywhere),
            "dmid": (sds((seq, width), F32), anywhere),
            "dot": (sds((width, seq), BF16), once((width, seq))),
            "gwin": (
                sds((2, 2, 2, 4 * share, hidden), BF16),
                pl.BlockSpec((2, 2, 2, 4 * share, tile), lambda i: (0, 0, 0, 0, jnp.maximum(i - 4, 0))),
            ),
            "gwo": (sds((2, 2, 2, 4 * share, width), BF16), once((2, 2, 2, 4 * share, width))),
            "part": (sds((2, 4, share_f, width), BF16), anywhere),
            "vec": (sds((vec_rows, width), F32), once((vec_rows, width))),
        }
        scratch = {
            "mid": pltpu.VMEM((seq, width), F32),
            "acc": pltpu.VMEM((seq, width), F32),
            "n2": pltpu.VMEM((seq, width), BF16),
            "n2t": pltpu.VMEM((width, seq), BF16),
            "act": pltpu.VMEM((seq, tile), BF16),
            "gp": pltpu.VMEM((4, seq, tile), BF16),
            "bins": pltpu.VMEM((4, 1, tile), F32),
            "bing": pltpu.VMEM((4, 1, tile), F32),
            "obuf": pltpu.VMEM((n_blk, tok, width), BF16),
            "gw": pltpu.VMEM((2, 2, 2, 4, share_f, width), BF16),
            "r0": pltpu.VMEM((2, 2, 4, share_f, width), BF16),
            "t1": pltpu.VMEM((2, 4, share_f, width), BF16),
            "r1": pltpu.VMEM((2, 4, share_f, width), BF16),
            "csend": pltpu.SemaphoreType.DMA((4,)),
            "crecv": pltpu.SemaphoreType.DMA((4,)),
            "ysend": pltpu.SemaphoreType.DMA,
            "yrecv": pltpu.SemaphoreType.DMA,
            "osend": pltpu.SemaphoreType.DMA((n_blk - 1,)),
            "orecv": pltpu.SemaphoreType.DMA((n_blk - 1,)),
            "lsem": pltpu.SemaphoreType.DMA((3,)),
        }
        names = tuple(ins) + tuple(outs) + tuple(scratch)
        ffn = pl.pallas_call(
            functools.partial(ffn_host_kernel, names, n_blk),
            grid=(8,),
            in_specs=[v[1] for v in ins.values()],
            out_specs=[v[1] for v in outs.values()],
            out_shape=[v[0] for v in outs.values()],
            scratch_shapes=list(scratch.values()),
            compiler_params=pltpu.CompilerParams(
                vmem_limit_bytes=62 * 2**20, collective_id=3, has_side_effects=True
            ),
            name="ffn",
        )(*[v[0] for v in ins.values()])
        ffn = dict(zip(outs, ffn))
        tasks = (
            ("a2", "gwin", None, slice(0, hidden // 2), share, "y", "s_win", slice(0, hidden // 2)),
            ("b2", "gwin", None, slice(hidden // 2, hidden), share, "y", "s_win", slice(hidden // 2, hidden)),
            ("wo", "gwo", None, None, share, "x", "s_wo", None),
        ) + tuple(
            (
                "q%d" % i,
                "gq",
                i,
                None,
                share,
                "xxy"[i],
                ("s_wq", "s_wk", "s_wv"),
                slice(i * cols, (i + 1) * cols),
            )
            for i in range(n_col)
        )
        sizes = {"a2": hidden // 2, "b2": hidden // 2, "wo": width}
        plan = PLAN
        last = lambda shape: pl.BlockSpec(shape, lambda h: (jnp.minimum(h, H - 1),) + (0,) * (len(shape) - 1))
        strip_h = last((head, seq))
        ins = {
            "p": (probs, last((1, seq, seq))),
            "q": (qt, strip_h),
            "k": (kt, strip_h),
            "v": (vt, strip_h),
            "do": (ffn["dot"], strip_h),
            "ct": (ct, strip_h),
            "nt": (nt, wide),
            "gain": (ln1_gain, full((width,))),
            "vec_in": (ffn["vec"], full((vec_rows, width))),
            "xs": (xs, anywhere),
            "dmid": (ffn["dmid"], anywhere),
            "wq": (w_query, anywhere),
            "wk": (w_key, anywhere),
            "wv": (w_value, anywhere),
            "part": (ffn["part"], anywhere),
            "gwin": (ffn["gwin"], anywhere),
            "gwo": (ffn["gwo"], anywhere),
        }
        outs = {
            "input_grad": (sds((n_seq, tok, width), BF16), anywhere),
            "s_wq": (sds((share, width), F32), full((share, width))),
            "s_wk": (sds((share, width), F32), full((share, width))),
            "s_wv": (sds((share, width), F32), full((share, width))),
            "s_wo": (sds((share, width), F32), full((share, width))),
            "s_win": (sds((share, hidden), F32), full((share, hidden))),
            "s_wout": (sds((share_f, width), F32), full((share_f, width))),
            "vec_out": (sds((vec_rows, width), F32), full((vec_rows, width))),
        }
        scratch = {
            "ds": pltpu.VMEM((seq, seq), BF16),
            "dcat": pltpu.VMEM((3 * width, seq), BF16),
            "wcat": pltpu.VMEM((width, 3 * width), BF16),
            "gq": pltpu.VMEM((n_col, 2, 2, 2, 4 * share, 3 * cols), BF16),
            "vec": pltpu.VMEM((vec_rows, width), F32),
            "rvec": pltpu.VMEM((6, vec_rows, width), F32),
            "xbuf": pltpu.VMEM((n_blk, tok, width), BF16),
            "dmbuf": pltpu.VMEM((seq, width), F32),
            "dx": pltpu.VMEM((n_blk, tok, width), BF16),
            "lsem": pltpu.SemaphoreType.DMA((7,)),
            "vsend": pltpu.SemaphoreType.DMA((6,)),
            "vrecv": pltpu.SemaphoreType.DMA((6,)),
            "w_keep": pltpu.VMEM((2, share_f, width), BF16),
            "w_rz": pltpu.VMEM((3, 2, share_f, width), BF16),
            "w_f": pltpu.VMEM((2, share_f, width), F32),
            "w_t": pltpu.VMEM((share_f, width), BF16),
            "w_rx": pltpu.VMEM((share_f, width), BF16),
            "w_send": pltpu.SemaphoreType.DMA((4,)),
            "w_recv": pltpu.SemaphoreType.DMA((4,)),
            "isend": pltpu.SemaphoreType.DMA((n_blk - 1,)),
            "irecv": pltpu.SemaphoreType.DMA((n_blk - 1,)),
        }
        for name, source, _, _, task_share, _, _, _ in tasks:
            for k, v in scatter_scratch(task_share, sizes.get(name, width), source != "gq").items():
                scratch[name + "_" + k] = v
        names = tuple(ins) + tuple(outs) + tuple(scratch)
        got = pl.pallas_call(
            functools.partial(back_kernel, scale, names, tasks, plan),
            grid=(H + 1,),
            in_specs=[v[1] for v in ins.values()],
            out_specs=[v[1] for v in outs.values()],
            out_shape=[v[0] for v in outs.values()],
            scratch_shapes=list(scratch.values()),
            compiler_params=pltpu.CompilerParams(
                vmem_limit_bytes=60 * 2**20, collective_id=2, has_side_effects=True
            ),
            name="back",
        )(*[v[0] for v in ins.values()])
        got = dict(zip(outs, got))
        big = [ffn["output"], got["input_grad"]] + [
            got[k] for k in ("s_wq", "s_wk", "s_wv", "s_wo", "s_win", "s_wout")
        ]
        part = pl.BlockSpec((1, tok, width), lambda i: (i, 0, 0))
        flat = [sds(v.shape, v.dtype) for v in big]
        fin = pl.pallas_call(
            functools.partial(finish_kernel, len(big)),
            grid=(n_blk,),
            in_specs=[part] * 2 + [full(v.shape) for v in big[2:]] + [full((vec_rows, width))],
            out_specs=[part] * 2 + [full(v.shape) for v in big[2:]] + [full((share,))] * 8 + [full((share_f,))],
            out_shape=flat + [sds((share,), F32)] * 8 + [sds((share_f,), F32)],
            name="finish",
        )(*big, got["vec_out"])
        output, input_grad, s_wq, s_wk, s_wv, s_wo, s_win, s_wout = fin[: len(big)]
        g1, b1, bq, bv, bo_sum, g2, b2, bout_sum, bin_sum = fin[len(big) :]
        return (
            output,
            input_grad,
            g1,
            b1,
            s_wq,
            bq,
            s_wk,
            s_wv,
            bv,
            s_wo,
            bo_sum,
            g2,
            b2,
            s_win,
            bin_sum,
            s_wout,
            bout_sum,
        )

    n_tile = 4
    tile = hidden // n_tile
    result = pl.pallas_call(
        functools.partial(ffn_kernel, n_blk),
        grid=(n_tile,),
        in_specs=[full((seq, width))] * 2
        + [
            wide,
            full((H, 1, seq)),
            full((width, width)),
            full((1, width)),
            full((1, width)),
            full((1, width)),
            pl.BlockSpec((width, tile), lambda j: (0, j)),
            pl.BlockSpec((1, tile), lambda j: (0, j)),
            pl.BlockSpec((tile, width), lambda j: (j, 0)),
            full((1, width)),
        ],
        out_specs=[piece] * n_blk
        + [
            pl.BlockSpec((tile, width), lambda j: (j, 0)),
            pl.BlockSpec((width, tile), lambda j: (0, j)),
            pl.BlockSpec((1, tile), lambda j: (0, j)),
            full((seq, width)),
            wide,
            full((width, width)),
            full((8, width)),
        ],
        out_shape=[sds((tok, width), BF16)] * n_blk
        + [
            sds((hidden, width), BF16),
            sds((width, hidden), BF16),
            sds((1, hidden), F32),
            sds((seq, width), F32),
            sds((width, seq), BF16),
            sds((width, width), BF16),
            sds((8, width), F32),
        ],
        scratch_shapes=[
            pltpu.VMEM((seq, width), F32),
            pltpu.VMEM((seq, width), BF16),
            pltpu.VMEM((width, seq), BF16),
            pltpu.VMEM((seq, width), F32),
            pltpu.VMEM((seq, width), F32),
            pltpu.VMEM((seq, tile), BF16),
            pltpu.VMEM((seq, tile), BF16),
        ],
        compiler_params=params(),
        cost_estimate=cost(8 * seq * width * hidden, 8 * width * hidden),
        name="ffn",
    )(
        xs.reshape(seq, width),
        gs.reshape(seq, width),
        ct,
        inv_total,
        w_output,
        row(b_output),
        row(ln2_gain),
        row(ln2_bias),
        w_in,
        row(b_in),
        w_out,
        row(b_out),
    )
    out_pieces = result[:n_blk]
    g_wout, g_win, g_bin, dmid, dct, g_wo, vec2 = result[n_blk:]

    bits = (n_dev - 1).bit_length()
    assert n_dev == 1 << bits

    def scatter(grad, order, wire):
        share = grad.shape[0] // n_dev
        order = list(order) + [b for b in range(bits) if b not in order]
        axes = list(range(bits - 1, -1, -1))
        terms = [grad.reshape((2,) * bits + (share,) + grad.shape[1:])]
        for b in order:
            at = axes.index(b)
            axes.pop(at)
            mine = (me >> b) & 1
            send = None
            keep = []
            for t in terms:
                other = lax.dynamic_index_in_dim(t, 1 - mine, at, keepdims=False)
                send = other.astype(F32) if send is None else send + other.astype(F32)
                keep.append(lax.dynamic_index_in_dim(t, mine, at, keepdims=False))
            got = lax.ppermute(send.astype(wire), ("dp", "blk"), [(i, i ^ (1 << b)) for i in range(n_dev)])
            terms = keep + [got]
        total = terms[0].astype(F32)
        for t in terms[1:]:
            total = total + t.astype(F32)
        return total

    s_wout = scatter(g_wout, (0, 1, 2, 3, 4), BF16)
    s_win = scatter(g_win, (0, 2, 1, 3, 4), BF16)
    s_wo = scatter(g_wo, (0, 3, 4, 1, 2), BF16)
    output = collect(out_pieces)

    dqt, dkt, dvt = pl.pallas_call(
        functools.partial(attend_back_kernel, scale),
        grid=(H,),
        in_specs=[per_square] + [per_head] * 5,
        out_specs=[per_head] * 3,
        out_shape=[sds((width, seq), BF16)] * 3,
        scratch_shapes=[pltpu.VMEM((seq, seq), BF16)],
        compiler_params=params(),
        cost_estimate=cost(10 * seq * seq * width, 2 * H * seq * seq),
        name="attend_back",
    )(probs, qt, kt, vt, dct, ct)

    result = pl.pallas_call(
        functools.partial(input_kernel, n_blk),
        in_specs=[full((seq, width))] * 2
        + [full((1, width)), wide, wide, wide]
        + [full((width, width))] * 3,
        out_specs=[piece] * n_blk + [full((8, width))],
        out_shape=[sds((tok, width), BF16)] * n_blk + [sds((8, width), F32)],
        compiler_params=params(),
        cost_estimate=cost(3 * seq * width * width, 14 * seq * width),
        name="input_grad",
    )(xs.reshape(seq, width), dmid, row(ln1_gain), dqt, dkt, dvt, w_query, w_key, w_value)
    input_grad = collect(result[:n_blk])
    vec1 = result[n_blk]

    col = pl.BlockSpec((width, cols), lambda j: (0, j))
    g_wq, g_wk, g_wv, vecq = pl.pallas_call(
        qkv_grad_kernel,
        grid=(n_col,),
        in_specs=[wide, strip, strip, strip],
        out_specs=[col, col, col, pl.BlockSpec((8, cols), lambda j: (0, j))],
        out_shape=[sds((width, width), BF16)] * 3 + [sds((8, width), F32)],
        compiler_params=params(),
        cost_estimate=cost(3 * seq * width * width, 14 * seq * width),
        name="qkv_grad",
    )(nt, dqt, dkt, dvt)
    s_wq = scatter(g_wq, (0, 1, 2, 3, 4), BF16)
    s_wk = scatter(g_wk, (0, 2, 3, 4, 1), BF16)
    s_wv = scatter(g_wv, (0, 3, 4, 1, 2), BF16)

    vectors = [vec1[0], vec1[1], vecq[0], vecq[1], vec2[3], vec2[1], vec2[2], g_bin[0], vec2[0]]
    packed = jnp.concatenate([v.reshape(n_dev, -1) for v in vectors], axis=1)
    packed = scatter(packed, (0, 1, 2, 3, 4), F32).reshape(-1)
    parts = []
    at = 0
    for v in vectors:
        size = v.shape[0] // n_dev
        parts.append(packed[at : at + size])
        at += size
    p_ln1g, p_ln1b, p_bq, p_bv, p_bo, p_ln2g, p_ln2b, p_bin, p_bout = parts
    return (
        output,
        input_grad,
        p_ln1g,
        p_ln1b,
        s_wq,
        p_bq,
        s_wk,
        s_wv,
        p_bv,
        s_wo,
        p_bo,
        p_ln2g,
        p_ln2b,
        s_win,
        p_bin,
        s_wout,
        p_bout,
    )


def solution(mesh):
    whole = P(("dp", "blk"))
    rows = P(("dp", "blk"), None)
    tokens = P("dp", "blk", None)
    in_specs = (tokens, P("dp"), tokens) + (P(),) * 15
    out_specs = (
        tokens,
        tokens,
        whole,
        whole,
        rows,
        whole,
        rows,
        rows,
        whole,
        rows,
        whole,
        whole,
        whole,
        rows,
        whole,
        rows,
        whole,
    )
    return jax.shard_map(body, mesh=mesh, in_specs=in_specs, out_specs=out_specs, check_vma=False)
```

```python
import functools

import jax
import jax.numpy as jnp
from jax import lax
from jax.experimental import pallas as pl
from jax.experimental.pallas import tpu as pltpu
from jax.sharding import PartitionSpec as P

H = 12
EPS = 1e-05
LOG2E = 1.4426950408889634
LN2 = 0.6931471805599453
INV_SQRT_2PI = 0.3989422804014327
SQRT_HALF = 0.7071067811865476
F32 = jnp.float32
BF16 = jnp.bfloat16
VMEM_LIMIT = 56 * 2**20

NN = (((1,), (0,)), ((), ()))
NT = (((1,), (1,)), ((), ()))
TN = (((0,), (0,)), ((), ()))

def dot(left, right, dims=NN):
    return lax.dot_general(left, right, dims, preferred_element_type=F32)


def params(**kw):
    return pltpu.CompilerParams(vmem_limit_bytes=VMEM_LIMIT, **kw)


def cost(macs, nbytes, exps=0):
    return pl.CostEstimate(flops=2 * macs, bytes_accessed=nbytes, transcendentals=exps)


def full(shape):
    return pl.BlockSpec(shape, lambda *_: (0,) * len(shape))


def as_row(ref):
    return ref[...].astype(F32)[None, :]


def center(v):
    mean = jnp.mean(v, axis=-1, keepdims=True)
    cent = v - mean
    var = jnp.mean(cent * cent, axis=-1, keepdims=True)
    rstd = lax.rsqrt(var + EPS)
    return cent * rstd, rstd


def gate(u):
    phi = 0.5 + 0.5 * lax.erf(u * SQRT_HALF)
    e = jnp.exp2(u * u * (-0.5 * LOG2E))
    return phi, u * e * INV_SQRT_2PI


def attend_kernel(n_blk, len_ref, q_ref, k_ref, v_ref, c_ref, p_ref, il_ref):
    seq = q_ref.shape[1]
    tok = seq // n_blk
    blk = lax.axis_index("blk")
    length = len_ref[blk]
    s = dot(k_ref[...].T, q_ref[...])
    live = [(blk ^ i) * tok < length for i in range(n_blk)]
    m = None
    for i in range(n_blk):
        mi = jnp.max(s[i * tok : (i + 1) * tok], axis=0, keepdims=True)
        mi = jnp.where(live[i], mi, -1e30)
        m = mi if m is None else jnp.maximum(m, mi)
    total = None
    ps = []
    for i in range(n_blk):
        p = jnp.exp2(s[i * tok : (i + 1) * tok] - jnp.where(live[i], m, 1e30))
        li = jnp.sum(p, axis=0, keepdims=True)
        total = li if total is None else total + li
        pb = p.astype(BF16)
        p_ref[0, i * tok : (i + 1) * tok] = pb
        ps.append(pb)
    inv = 1.0 / total
    c_ref[...] = (dot(v_ref[...], jnp.concatenate(ps, axis=0)) * inv).astype(BF16)
    il_ref[0] = inv


MESH = pl.DeviceIdType.MESH


def greet(partners):
    barrier = pltpu.get_barrier_semaphore()
    for where in partners:
        pl.semaphore_signal(barrier, inc=1, device_id=where, device_id_type=MESH)
    pl.semaphore_wait(barrier, len(partners))


def qkv_spread_kernel(
    scale,
    n_blk,
    x_any,
    gain,
    bias,
    wq_any,
    bq,
    wk_any,
    wv_any,
    bv,
    xs_any,
    nt_any,
    q_any,
    k_any,
    v_any,
    xbuf,
    wbuf,
    wt,
    nt,
    qkv,
    send,
    recv,
    wsem,
    osem,
    xsem,
):
    tok, width = xbuf.shape[1:]
    dp = lax.axis_index("dp")
    blk = lax.axis_index("blk")
    own = pltpu.make_async_copy(x_any.at[blk], xbuf.at[0], xsem)
    own.start()
    loads = [
        pltpu.make_async_copy(w, wbuf.at[i], wsem.at[i]) for i, w in enumerate((wq_any, wk_any, wv_any))
    ]
    for load in loads:
        load.start()
    greet([(dp, blk ^ s) for s in range(1, n_blk)])
    order = list(range(n_blk - 1, 0, -1))
    copies = {}
    for s in order:
        copies[s] = pltpu.make_async_remote_copy(
            src_ref=x_any.at[blk ^ s],
            dst_ref=xbuf.at[s],
            send_sem=send.at[s - 1],
            recv_sem=recv.at[s - 1],
            device_id=(dp, blk ^ s),
            device_id_type=MESH,
        )
        if s != 2:
            copies[s].start()
    for i, load in enumerate(loads):
        load.wait()
        wt[i] = wbuf[i].T
    cols = jnp.concatenate([as_row(bq), as_row(bv), jnp.zeros((6, width), F32)], axis=0).T
    writes = []
    for s in (0, 1, 3, 2):
        if s == 0:
            own.wait()
        else:
            if s == 3:
                copies[3].wait_send()
                copies[2].start()
            copies[s].wait_recv()
        sl = slice(s * tok, (s + 1) * tok)
        n, _ = center(xbuf[s].astype(F32))
        n = (n * as_row(gain) + as_row(bias)).astype(BF16).T
        nt[:, sl] = n
        qkv[0, :, sl] = ((dot(wt[0], n) + cols[:, :1]) * scale).astype(BF16)
        qkv[1, :, sl] = dot(wt[1], n).astype(BF16)
        qkv[2, :, sl] = (dot(wt[2], n) + cols[:, 1:2]).astype(BF16)
        for i, (src, dst) in enumerate(
            (
                (xbuf.at[s], xs_any.at[s]),
                (nt.at[:, sl], nt_any.at[:, sl]),
                (qkv.at[0, :, sl], q_any.at[:, sl]),
                (qkv.at[1, :, sl], k_any.at[:, sl]),
                (qkv.at[2, :, sl], v_any.at[:, sl]),
            )
        ):
            write = pltpu.make_async_copy(src, dst, osem.at[s, i])
            write.start()
            writes.append(write)
    for s in (1, 2):
        copies[s].wait_send()
    for write in writes:
        write.wait()


def attend_spread_kernel(n_blk, len_ref, q_ref, k_ref, v_ref, g_any, c_ref, p_ref, il_ref, gs_any, send, recv, osem):
    h = pl.program_id(0)
    dp = lax.axis_index("dp")
    blk = lax.axis_index("blk")

    def copy(s):
        return pltpu.make_async_remote_copy(
            src_ref=g_any.at[blk ^ s],
            dst_ref=gs_any.at[s],
            send_sem=send.at[s - 1],
            recv_sem=recv.at[s - 1],
            device_id=(dp, blk ^ s),
            device_id_type=MESH,
        )

    own = pltpu.make_async_copy(g_any.at[blk], gs_any.at[0], osem)

    @pl.when(h == 0)
    def _():
        greet([(dp, blk ^ s) for s in range(1, n_blk)])
        own.start()
        for s in range(1, n_blk):
            copy(s).start()

    attend_kernel(n_blk, len_ref, q_ref, k_ref, v_ref, c_ref, p_ref, il_ref)

    @pl.when(h == pl.num_programs(0) - 1)
    def _():
        own.wait()
        for s in range(1, n_blk):
            copy(s).wait()


def regroup(v, share):
    def slab(c, x, y):
        at = [(z * 8 + y * 4 + x * 2 + c) * share for z in range(4)]
        return jnp.concatenate([v[a : a + share] for a in at], axis=0)

    return [[[slab(c, x, y) for y in range(2)] for x in range(2)] for c in range(2)]


CXY = [(c, x, y) for c in range(2) for x in range(2) for y in range(2)]


class Scatter:
    def __init__(self, source, cols, share, first, out, bufs, place):
        self.source, self.cols, self.share, self.out = source, cols, share, out
        self.b = bufs
        dp, blk = place
        self.c, self.x, self.y, self.z = blk & 1, blk >> 1, dp & 1, dp >> 1
        self.first = first
        ids = {"x": (dp, blk ^ 2), "y": (dp ^ 1, blk)}
        self.mp = self.x if first == "x" else self.y
        self.mq = self.y if first == "x" else self.x
        self.core_id = (dp, blk ^ 1)
        self.p_id = ids[first]
        self.q_id = ids["y" if first == "x" else "x"]
        self.z_ids = [(((self.z + d) & 3) * 2 + self.y, blk) for d in (1, 2, 3)]
        self.chunk = share if share % 16 == 0 else 2 * share

    def remote(self, src, dst, i, where):
        return pltpu.make_async_remote_copy(
            src_ref=src,
            dst_ref=dst,
            send_sem=self.b["send"].at[i],
            recv_sem=self.b["recv"].at[i],
            device_id=where,
            device_id_type=MESH,
        )

    def part(self, c):
        if self.cols is None:
            return self.source.at[c]
        return self.source.at[c, :, :, :, self.cols]

    def core_copy(self):
        return self.remote(self.part(1 - self.c), self.b["r0"], 0, self.core_id)

    def load(self):
        return pltpu.make_async_copy(self.part(self.c), self.b["keep"], self.b["load"])

    def p_copy(self):
        return self.remote(self.b["t1"], self.b["r1"], 1, self.p_id)

    def q_copy(self):
        return self.remote(self.b["t2"], self.b["r2"], 2, self.q_id)

    def z_copies(self):
        return [self.remote(self.b["t3"].at[d], self.b["r3"].at[d], 3 + d, self.z_ids[d]) for d in range(3)]

    def pick(self, ref, a, b, rows):
        return (ref[a, b, rows] if self.first == "x" else ref[b, a, rows]).astype(F32)

    def base(self, a, b, rows):
        if "keep" in self.b:
            own = self.pick(self.b["keep"], a, b, rows)
        else:
            own = (
                self.source[self.c, a, b, rows] if self.first == "x" else self.source[self.c, b, a, rows]
            ).astype(F32)
        return own + self.pick(self.b["r0"], a, b, rows)

    def each(self, fn):
        rows = 4 * self.share

        def step(i, carry):
            fn(i, pl.ds(pl.multiple_of(i * self.chunk, self.chunk), self.chunk))
            return carry

        lax.fori_loop(0, rows // self.chunk, step, 0)

    def stage0(self):
        self.core_copy().start()
        if "keep" in self.b:
            self.load().start()

    def stage1(self):
        if "keep" in self.b:
            self.load().wait()
        self.core_copy().wait()
        for b in range(2):

            def fn(i, rows):
                self.b["t1"][b, rows] = self.base(1 - self.mp, b, rows).astype(BF16)

            self.each(fn)
        self.p_copy().start()

    def stage2(self):
        self.p_copy().wait()

        def fn(i, rows):
            v = self.base(self.mp, 1 - self.mq, rows) + self.b["r1"][1 - self.mq, rows].astype(F32)
            self.b["t2"][rows] = v.astype(BF16)

        self.each(fn)
        self.q_copy().start()

    def stage3(self):
        self.q_copy().wait()
        share = self.share
        per = self.chunk // share
        f = self.b["f"]

        def fn(i, rows):
            v = self.base(self.mp, self.mq, rows)
            v = v + self.b["r1"][self.mq, rows].astype(F32) + self.b["r2"][rows].astype(F32)
            for k in range(per):
                f[i * per + k] = v[k * share : (k + 1) * share]

        self.each(fn)
        half = f.shape[2] // 2
        for d in range(3):
            v = f[(self.z + d + 1) & 3]
            if per > 1:
                v = jnp.concatenate([v[:, :half], v[:, half:]], axis=0)
            self.b["t3"][d] = v.astype(BF16)
        for copy in self.z_copies():
            copy.start()

    def stage4(self):
        for copy in self.z_copies():
            copy.wait()
        v = self.b["f"][self.z]
        for d in range(3):
            w = self.b["r3"][d].astype(F32)
            if self.chunk > self.share:
                w = jnp.concatenate([w[: self.share], w[self.share :]], axis=1)
            v = v + w
        self.out(v)


class ScatterLate(Scatter):
    def x_copy(self):
        return self.remote(self.b["f2"].at[1 - self.x], self.b["rx"], 2, self.q_id)

    def stage2(self):
        self.p_copy().wait()
        share = self.share
        per = self.chunk // share
        f = self.b["f"]
        for x in range(2):

            def fn(i, rows, x=x):
                v = self.base(self.mp, x, rows) + self.b["r1"][x, rows].astype(F32)
                for k in range(per):
                    f[x, i * per + k] = v[k * share : (k + 1) * share]

            self.each(fn)
        for d in range(3):
            at = (self.z + d + 1) & 3
            self.b["t3"][d] = jnp.concatenate([f[0, at], f[1, at]], axis=0).astype(BF16)
        for copy in self.z_copies():
            copy.start()

    def stage3(self):
        for copy in self.z_copies():
            copy.wait()
        for x in range(2):
            v = self.b["f"][x, self.z]
            for d in range(3):
                v = v + self.b["r3"][d].astype(F32)[x * self.share : (x + 1) * self.share]
            self.b["f2"][x] = v
        self.x_copy().start()

    def stage4(self):
        self.x_copy().wait()
        self.out(self.b["f2"][self.x] + self.b["rx"][...])


def scatter_scratch(share, cols, in_hbm, late):
    rows = 4 * share
    slab = (share, cols) if share % 16 == 0 else (2 * share, cols // 2)
    bufs = {
        "r0": pltpu.VMEM((2, 2, rows, cols), BF16),
        "t1": pltpu.VMEM((2, rows, cols), BF16),
        "r1": pltpu.VMEM((2, rows, cols), BF16),
        "t2": pltpu.VMEM((rows, cols), BF16),
        "r2": pltpu.VMEM((rows, cols), BF16),
        "t3": pltpu.VMEM((3,) + slab, BF16),
        "r3": pltpu.VMEM((3,) + slab, BF16),
        "f": pltpu.VMEM((4, share, cols), F32),
        "send": pltpu.SemaphoreType.DMA((6,)),
        "recv": pltpu.SemaphoreType.DMA((6,)),
    }
    if late:
        del bufs["t2"], bufs["r2"]
        bufs["t3"] = pltpu.VMEM((3, 2 * share, cols), BF16)
        bufs["r3"] = pltpu.VMEM((3, 2 * share, cols), BF16)
        bufs["f"] = pltpu.VMEM((2, 4, share, cols), F32)
        bufs["f2"] = pltpu.VMEM((2, share, cols), F32)
        bufs["rx"] = pltpu.VMEM((share, cols), F32)
    if in_hbm:
        bufs["keep"] = pltpu.VMEM((2, 2, rows, cols), BF16)
        bufs["load"] = pltpu.SemaphoreType.DMA
    return bufs


def ffn_kernel(n_blk, *refs):
    x_ref, g = refs[:2]
    (ct_ref, il_ref, wo_ref, bo_ref, gain_ref, bias_ref, win_ref, bin_ref, wout_ref, bout_ref) = refs[2:12]
    rest = refs[12:]
    outs = rest[:n_blk]
    (gwout_ref, gwin_ref, gbin_ref, dmid_ref, dot_ref, gwo_ref, vec_ref) = rest[n_blk : n_blk + 7]
    mid, n2, n2t, acc_o, acc_d, act, dpre = rest[n_blk + 7 :]
    tok = outs[0].shape[0]
    j = pl.program_id(0)

    @pl.when(j == 0)
    def _():
        for s in range(n_blk):
            sl = slice(s * tok, (s + 1) * tok)
            m = x_ref[sl].astype(F32) + dot(ct_ref[:, sl], wo_ref[...], TN) + bo_ref[...]
            mid[sl] = m
            acc_o[sl] = m + bout_ref[...]
            acc_d[sl] = jnp.zeros_like(m)
            n, _ = center(m)
            nb = (n * gain_ref[...] + bias_ref[...]).astype(BF16)
            n2[sl] = nb
            n2t[:, sl] = nb.T

    bin_grad = None
    for s in range(n_blk):
        sl = slice(s * tok, (s + 1) * tok)
        pre = dot(n2[sl], win_ref[...]) + bin_ref[...]
        phi, slope = gate(pre)
        a = (pre * phi).astype(BF16)
        dact = dot(g[sl], wout_ref[...], NT)
        dp = (dact * (phi + slope)).astype(BF16)
        act[sl] = a
        dpre[sl] = dp
        col = jnp.sum(dp.astype(F32), axis=0, keepdims=True)
        bin_grad = col if bin_grad is None else bin_grad + col
        acc_o[sl] += dot(a, wout_ref[...])
        acc_d[sl] += dot(dp, win_ref[...], NT)
    gbin_ref[...] = bin_grad
    gwout_ref[...] = dot(act[...], g[...], TN).astype(BF16)
    gwin_ref[...] = dot(n2t[...], dpre[...]).astype(BF16)

    @pl.when(j == pl.num_programs(0) - 1)
    def _():
        head = wo_ref.shape[0] // H
        sums = [None] * 4
        for s in range(n_blk):
            sl = slice(s * tok, (s + 1) * tok)
            outs[s][...] = acc_o[sl].astype(BF16)
            n, rstd = center(mid[sl])
            e = acc_d[sl]
            gf = g[sl].astype(F32)
            f = e * gain_ref[...]
            dm = gf + rstd * (
                f - jnp.mean(f, axis=-1, keepdims=True) - n * jnp.mean(f * n, axis=-1, keepdims=True)
            )
            dmid_ref[sl] = dm
            db = dm.astype(BF16)
            n2[sl] = db
            for i, term in enumerate((gf, e * n, e, db.astype(F32))):
                col = jnp.sum(term, axis=0, keepdims=True)
                sums[i] = col if sums[i] is None else sums[i] + col
            dc = dot(wo_ref[...], db, NT)
            for h in range(H):
                hs = slice(h * head, (h + 1) * head)
                dot_ref[hs, sl] = (dc[hs] * il_ref[h, :, sl]).astype(BF16)
        for i in range(4):
            vec_ref[i : i + 1] = sums[i]
        gwo_ref[...] = dot(ct_ref[...], n2[...]).astype(BF16)


def attend_back_kernel(scale, p_ref, q_ref, k_ref, v_ref, do_ref, c_ref, dq_ref, dk_ref, dv_ref, ds):
    seq = q_ref.shape[1]
    do = do_ref[...]
    vh = v_ref[...].T
    delta = jnp.sum(do.astype(F32) * c_ref[...].astype(F32), axis=0, keepdims=True)
    step = seq // 2
    for c in range(2):
        sl = slice(c * step, (c + 1) * step)
        dp = dot(vh, do[:, sl])
        d = (p_ref[0, :, sl].astype(F32) * (dp - delta[:, sl])).astype(BF16)
        ds[:, sl] = d
        dq_ref[:, sl] = (dot(k_ref[...], d) * scale).astype(BF16)
    dv_ref[...] = dot(p_ref[0], do, NT).T.astype(BF16)
    dk_ref[...] = (dot(ds[...], q_ref[...], NT) * LN2).T.astype(BF16)


def input_kernel(n_blk, x_ref, dmid_ref, gain_ref, dq_ref, dk_ref, dv_ref, wq_ref, wk_ref, wv_ref, *rest):
    outs = rest[:n_blk]
    vec_ref = rest[n_blk]
    tok = outs[0].shape[0]
    sums = [None] * 2
    for s in range(n_blk):
        sl = slice(s * tok, (s + 1) * tok)
        et = dot(wq_ref[...], dq_ref[:, sl]) + dot(wk_ref[...], dk_ref[:, sl]) + dot(wv_ref[...], dv_ref[:, sl])
        e = et.T
        n, rstd = center(x_ref[sl].astype(F32))
        f = e * gain_ref[...]
        dx = dmid_ref[sl] + rstd * (
            f - jnp.mean(f, axis=-1, keepdims=True) - n * jnp.mean(f * n, axis=-1, keepdims=True)
        )
        outs[s][...] = dx.astype(BF16)
        for i, term in enumerate((e * n, e)):
            col = jnp.sum(term, axis=0, keepdims=True)
            sums[i] = col if sums[i] is None else sums[i] + col
    for i in range(2):
        vec_ref[i : i + 1] = sums[i]


def qkv_grad_kernel(nt_ref, dq_ref, dk_ref, dv_ref, gq_ref, gk_ref, gv_ref, vec_ref):
    nt = nt_ref[...]
    ones = jnp.ones((8, nt.shape[1]), BF16)
    gq_ref[...] = dot(nt, dq_ref[...], NT).astype(BF16)
    gk_ref[...] = dot(nt, dk_ref[...], NT).astype(BF16)
    gv_ref[...] = dot(nt, dv_ref[...], NT).astype(BF16)
    vec_ref[0:1] = dot(ones, dq_ref[...], NT)[:1]
    vec_ref[1:2] = dot(ones, dv_ref[...], NT)[:1]


def ffn_host_kernel(names, n_blk, *refs):
    r = dict(zip(names, refs))
    i = pl.program_id(0)
    j = i & 3
    dp = lax.axis_index("dp")
    blk = lax.axis_index("blk")
    core, y = blk & 1, dp & 1
    mid, acc, n2, n2t, act, gp, gw, r0, t1, r1 = [
        r[k] for k in ("mid", "acc", "n2", "n2t", "act", "gp", "gw", "r0", "t1", "r1")
    ]
    g, win, wout, ct = r["g"], r["win"], r["wout"], r["ct"]
    seq, width = mid.shape
    tok = seq // n_blk
    tile = act.shape[1]
    share_f = gw.shape[4]
    rows = [slice(s * tok, (s + 1) * tok) for s in range(n_blk)]

    def core_copy(plane):
        return pltpu.make_async_remote_copy(
            src_ref=gw.at[1 - core, :, :, plane],
            dst_ref=r0.at[:, :, plane],
            send_sem=r["csend"].at[plane],
            recv_sem=r["crecv"].at[plane],
            device_id=(dp, blk ^ 1),
            device_id_type=MESH,
        )

    def y_copy(plane):
        return pltpu.make_async_remote_copy(
            src_ref=t1.at[:, plane],
            dst_ref=r1.at[:, plane],
            send_sem=r["ysend"].at[plane],
            recv_sem=r["yrecv"].at[plane],
            device_id=(dp ^ 1, blk),
            device_id_type=MESH,
        )

    def y_start(plane):
        core_copy(plane).wait()
        for x in range(2):
            t1[x, plane] = (gw[core, x, 1 - y, plane].astype(F32) + r0[x, 1 - y, plane].astype(F32)).astype(BF16)
        y_copy(plane).start()

    def out_copy(s):
        src, dst = r["obuf"].at[s], r["output"].at[blk]
        if s == 0:
            return pltpu.make_async_copy(src, dst, r["lsem"].at[0])
        return pltpu.make_async_remote_copy(
            src_ref=src,
            dst_ref=dst,
            send_sem=r["osend"].at[s - 1],
            recv_sem=r["orecv"].at[s - 1],
            device_id=(dp, blk ^ s),
            device_id_type=MESH,
        )

    @pl.when(i == 0)
    def _():
        greet([(dp, blk ^ 1), (dp, blk ^ 2), (dp, blk ^ 3), (dp ^ 1, blk)])
        bins = as_row(r["bin"])
        for k in range(4):
            r["bins"][k] = bins[:, k * tile : (k + 1) * tile]
        for sl in rows:
            m = r["x"][sl].astype(F32) + dot(ct[:, sl], r["wo"][...], TN) + as_row(r["bo"])
            mid[sl] = m
            acc[sl] = m + as_row(r["bout"])
            n, _ = center(m)
            nb = (n * as_row(r["gain"]) + as_row(r["bias"])).astype(BF16)
            n2[sl] = nb
            n2t[:, sl] = nb.T

    @pl.when(i < 4)
    def _():
        for sl in rows:
            pre = dot(n2[sl], win[...]) + r["bins"][j]
            phi, slope = gate(pre)
            a = (pre * phi).astype(BF16)
            act[sl] = a
            gp[j, sl] = (phi + slope).astype(BF16)
            acc[sl] += dot(a, wout[...])

        @pl.when(i > 0)
        def _():
            y_start(j - 1)

        v = dot(act[...], g[...], TN)
        for c, x, yy in CXY:
            at = (yy * 4 + x * 2 + c) * share_f
            gw[c, x, yy, j] = v[at : at + share_f].astype(BF16)
        core_copy(j).start()

    @pl.when(i == 4)
    def _():
        for s in range(n_blk - 1, -1, -1):
            r["obuf"][s] = acc[rows[s]].astype(BF16)
            out_copy(s).start()
            acc[rows[s]] = jnp.zeros((tok, width), F32)

    @pl.when(i >= 4)
    def _():
        total = None
        for sl in rows:
            d = (dot(g[sl], wout[...], NT) * gp[j, sl].astype(F32)).astype(BF16)
            act[sl] = d
            col = jnp.sum(d.astype(F32), axis=0, keepdims=True)
            total = col if total is None else total + col
            acc[sl] += dot(d, win[...], NT)
        r["bing"][j] = total

        @pl.when(i == 4)
        def _():
            y_start(3)

        v = regroup(dot(n2t[...], act[...]), width // 32)
        for c, x, yy in CXY:
            r["gwin"][c, x, yy] = v[c][x][yy].astype(BF16)

    @pl.when(i == 7)
    def _():
        head = width // H
        sums = [None] * 4
        for sl in rows:
            n, rstd = center(mid[sl])
            e = acc[sl]
            gf = g[sl].astype(F32)
            f = e * as_row(r["gain"])
            dm = gf + rstd * (
                f - jnp.mean(f, axis=-1, keepdims=True) - n * jnp.mean(f * n, axis=-1, keepdims=True)
            )
            mid[sl] = dm
            db = dm.astype(BF16)
            n2[sl] = db
            for k, term in enumerate((gf, e * n, e, db.astype(F32))):
                col = jnp.sum(term, axis=0, keepdims=True)
                sums[k] = col if sums[k] is None else sums[k] + col
            dc = dot(r["wo"][...], db, NT)
            for h in range(H):
                hs = slice(h * head, (h + 1) * head)
                r["dot"][hs, sl] = (dc[hs] * r["il"][h, :, sl]).astype(BF16)
        save = pltpu.make_async_copy(mid, r["dmid"], r["lsem"].at[1])
        save.start()
        vec = r["vec"]
        for k in range(4):
            vec[k : k + 1] = sums[k]
            vec[4 + k : 5 + k] = r["bing"][k]
        v = regroup(dot(ct[...], n2[...]), width // 32)
        for c, x, yy in CXY:
            r["gwo"][c, x, yy] = v[c][x][yy].astype(BF16)
        for k in range(4):
            y_copy(k).wait()

        def step(k, carry):
            for x in range(2):
                v = gw[core, x, y, k].astype(F32) + r0[x, y, k].astype(F32) + r1[x, k].astype(F32)
                t1[x, k] = v.astype(BF16)
            return carry

        lax.fori_loop(0, 4, step, 0)
        part = pltpu.make_async_copy(t1, r["part"], r["lsem"].at[2])
        part.start()
        for s in range(n_blk):
            out_copy(s).wait()
        save.wait()
        part.wait()


class Resume:
    def __init__(self, r, place):
        dp, blk = place
        self.r = r
        self.x, self.y, self.z = blk >> 1, dp & 1, dp >> 1
        self.ids = [(((self.z + d) & 3) * 2 + self.y, blk) for d in (1, 2, 3)] + [(dp, blk ^ 2)]

    def remote(self, src, dst, i):
        return pltpu.make_async_remote_copy(
            src_ref=src,
            dst_ref=dst,
            send_sem=self.r["w_send"].at[i],
            recv_sem=self.r["w_recv"].at[i],
            device_id=self.ids[i],
            device_id_type=MESH,
        )

    def z_copies(self):
        return [
            self.remote(self.r["part"].at[:, (self.z + d + 1) & 3], self.r["w_rz"].at[d], d) for d in range(3)
        ]

    def load(self):
        return pltpu.make_async_copy(self.r["part"].at[:, self.z], self.r["w_keep"], self.r["lsem"].at[0])

    def x_copy(self):
        return self.remote(self.r["w_t"], self.r["w_rx"], 3)

    def stage0(self):
        for copy in self.z_copies():
            copy.start()
        self.load().start()

    def stage1(self):
        self.load().wait()
        for copy in self.z_copies():
            copy.wait()
        for k in range(2):
            v = self.r["w_keep"][k].astype(F32)
            for d in range(3):
                v = v + self.r["w_rz"][d, k].astype(F32)
            self.r["w_f"][k] = v
        self.r["w_t"][...] = self.r["w_f"][1 - self.x].astype(BF16)
        self.x_copy().start()

    def stage2(self):
        self.x_copy().wait()
        self.r["s_wout"][...] = self.r["w_f"][self.x] + self.r["w_rx"][...].astype(F32)


def finish_kernel(n_big, *refs):
    src, va, vb = refs[:n_big], refs[n_big], refs[n_big + 1]
    dst, small = refs[n_big + 2 : 2 * n_big + 2], refs[2 * n_big + 2 :]
    for a, b in zip(src[:2], dst[:2]):
        b[...] = a[...]

    @pl.when(pl.program_id(0) == 0)
    def _():
        for a, b in zip(src[2:], dst[2:]):
            b[...] = a[...]
        me = lax.axis_index("dp") * lax.axis_size("blk") + lax.axis_index("blk")
        share = small[0].shape[0]
        wide = small[8].shape[0]
        width = va.shape[1]
        shift = lax.rem(width - me * share, width)
        moved = pltpu.roll(va[...], shift, 1)
        for k in range(4):
            small[k][...] = moved[k, :share]
        lines = vb[...]
        moved = pltpu.roll(lines, shift, 1)
        for i, k in enumerate((3, 1, 2, 0)):
            small[4 + i][...] = moved[k, :share]
        each = width // wide
        moved = pltpu.roll(lines, lax.rem(width - lax.rem(me, each) * wide, width), 1)
        row = 4 + lax.div(me, each)
        pick = lax.broadcasted_iota(jnp.int32, moved.shape, 0) == row
        small[8][...] = jnp.sum(jnp.where(pick, moved, 0.0), axis=0)[:wide]


def back_kernel(scale, names, tasks, plan, *refs):
    r = dict(zip(names, refs))
    h = pl.program_id(0)
    dp = lax.axis_index("dp")
    blk = lax.axis_index("blk")
    place = (dp, blk)
    n_blk, tok, width = r["xs"].shape
    seq = n_blk * tok
    head = width // H
    dcat, wcat, gq, vec = r["dcat"], r["wcat"], r["gq"], r["va"]

    def put(ref, cols):
        def out(v):
            if cols is None:
                ref[...] = v
            else:
                ref[:, cols] = v

        return out

    jobs = {}
    for name, source, index, cols, share, first, out, out_cols in tasks:
        ref = r[source] if index is None else r[source].at[index]
        bufs = {k: r[name + "_" + k] for k in SCATTER_KEYS if name + "_" + k in r}
        if isinstance(out, tuple):
            outs = [put(r[o], out_cols) for o in out]

            def sink(v, outs=outs):
                each = v.shape[1] // len(outs)
                for i, o in enumerate(outs):
                    o(v[:, i * each : (i + 1) * each])

        else:
            sink = put(r[out], out_cols)
        kind = ScatterLate if first == "late" else Scatter
        jobs[name] = kind(ref, cols, share, "y" if first == "late" else first, sink, bufs, place)

    jobs["wout"] = Resume(r, place)

    def spread(src, dst, sems, s):
        return pltpu.make_async_remote_copy(
            src_ref=src.at[s],
            dst_ref=dst.at[blk],
            send_sem=sems[0].at[s - 1],
            recv_sem=sems[1].at[s - 1],
            device_id=(dp, blk ^ s),
            device_id_type=MESH,
        )

    def in_copy(s):
        if s == 0:
            return pltpu.make_async_copy(r["dx"].at[0], r["input_grad"].at[blk], r["lsem"].at[1])
        return spread(r["dx"], r["input_grad"], (r["isend"], r["irecv"]), s)

    def loads():
        pairs = [(r["xs"], r["xbuf"]), (r["dmid"], r["dmbuf"])]
        pairs += [(r[w], wcat.at[:, i * width : (i + 1) * width]) for i, w in enumerate(("wq", "wk", "wv"))]
        return [pltpu.make_async_copy(a, b, r["lsem"].at[2 + i]) for i, (a, b) in enumerate(pairs)]

    z, y = dp >> 1, dp & 1
    z_ids = [(((z + d) & 3) * 2 + y, blk) for d in (1, 2, 3)]
    vec_ids = [z_ids, [(dp ^ 1, blk)], [(dp, blk ^ 1), (dp, blk ^ 2), (dp, blk ^ 3)]]

    def vec_copies(name, stage):
        at = (0, 3, 4)[stage]
        return [
            pltpu.make_async_remote_copy(
                src_ref=r[name],
                dst_ref=r[name + "_r"].at[at + d],
                send_sem=r[name + "_send"].at[at + d],
                recv_sem=r[name + "_recv"].at[at + d],
                device_id=where,
                device_id_type=MESH,
            )
            for d, where in enumerate(vec_ids[stage])
        ]

    def vec_step(name, stage):
        if stage > 0:
            copies = vec_copies(name, stage - 1)
            for copy in copies:
                copy.wait()
            at = (0, 3, 4)[stage - 1]
            r[name][...] += sum(r[name + "_r"][at + d] for d in range(len(copies)))
        if stage < 3:
            for copy in vec_copies(name, stage):
                copy.start()

    def input_piece(s, sums):
        sl = slice(s * tok, (s + 1) * tok)
        e = r["ebuf"][s & 1].T
        n, rstd = center(r["xbuf"][s].astype(F32))
        f = e * as_row(r["gain"])
        dx = r["dmbuf"][sl] + rstd * (
            f - jnp.mean(f, axis=-1, keepdims=True) - n * jnp.mean(f * n, axis=-1, keepdims=True)
        )
        r["dx"][s] = dx.astype(BF16)
        in_copy(s).start()
        new = [jnp.sum(t, axis=0, keepdims=True) for t in (e * n, e)]
        return new if sums is None else [a + b for a, b in zip(sums, new)]

    @pl.when(h == 0)
    def _():
        greet(
            [(dp, blk ^ 1), (dp, blk ^ 2), (dp, blk ^ 3), (dp ^ 1, blk)]
            + [(((z + d) & 3) * 2 + y, blk) for d in (1, 2, 3)]
        )
        for load in loads():
            load.start()
        vec[...] = jnp.zeros_like(vec)
        r["vb"][...] = r["vec_in"][...]

    def act(item):
        kind, what = item
        if kind in ("va", "vb"):
            vec_step(kind, what)
        else:
            getattr(jobs[kind], "stage%d" % what)()

    for at in range(H):
        if plan.get(at):

            @pl.when(h == at)
            def _(at=at):
                for item in plan[at]:
                    act(item)

    @pl.when(h < H)
    def _():
        do = r["do"][...]
        vh = r["v"][...].T
        delta = jnp.sum(do.astype(F32) * r["ct"][...].astype(F32), axis=0, keepdims=True)
        step = seq // 2
        base = pl.multiple_of(h * head, head)
        for c in range(2):
            sl = slice(c * step, (c + 1) * step)
            dpr = dot(vh, do[:, sl])
            d = (r["p"][0, :, sl].astype(F32) * (dpr - delta[:, sl])).astype(BF16)
            r["ds"][:, sl] = d
            dcat[pl.ds(base, head), sl] = (dot(r["k"][...], d) * scale).astype(BF16)
        dcat[pl.ds(base + 2 * width, head)] = dot(r["p"][0], do, NT).T.astype(BF16)
        dcat[pl.ds(base + width, head)] = (dot(r["ds"][...], r["q"][...], NT) * LN2).T.astype(BF16)

    n_group = gq.shape[0]
    cols = width // n_group
    for gi in range(n_group):

        @pl.when(h == (gi + 1) * (H // n_group) - 1)
        def _(gi=gi):
            nt = r["nt"][...]
            ones = jnp.ones((8, seq), BF16)
            for t in range(3):
                part = dcat[t * width + gi * cols : t * width + (gi + 1) * cols]
                v = regroup(dot(nt, part, NT), width // 32)
                for c, x, y in CXY:
                    gq[gi, c, x, y, :, t * cols : (t + 1) * cols] = v[c][x][y].astype(BF16)
                if t != 1:
                    row = 2 if t == 0 else 3
                    vec[row : row + 1, gi * cols : (gi + 1) * cols] = dot(ones, part, NT)[:1]
            jobs["q%d" % gi].stage0()

    @pl.when(h == H)
    def _():
        sums = None
        for load in loads():
            load.wait()
        for item in plan["tail"]:
            kind, what = item
            if kind == "mul":
                r["ebuf"][what & 1] = dot(wcat[...], dcat[:, what * tok : (what + 1) * tok])
            elif kind == "piece":
                sums = input_piece(what, sums)
                if what == 0:
                    vec[0:1] = sums[0]
                    vec[1:2] = sums[1]
            else:
                act(item)
        r["va_out"][...] = vec[...]
        r["vb_out"][...] = r["vb"][...]
        for s in range(n_blk):
            in_copy(s).wait()


PLAN = {
    0: [("wout", 0), ("a2", 0), ("b2", 0), ("wo", 0)],
    2: [("a2", 1), ("b2", 1)],
    3: [("wo", 1)],
    5: [("q0", 1)],
    7: [("a2", 2), ("b2", 2)],
    9: [("q1", 1)],
    10: [("q0", 2), ("wo", 2)],
    11: [("a2", 3), ("b2", 3), ("wout", 1)],
    "tail": [
        ("mul", 3),
        ("mul", 2),
        ("piece", 3),
        ("q2", 1),
        ("mul", 1),
        ("piece", 2),
        ("mul", 0),
        ("piece", 1),
        ("piece", 0),
        ("vb", 0),
        ("va", 0),
        ("q2", 2),
        ("q1", 2),
        ("wo", 3),
        ("q0", 3),
        ("vb", 1),
        ("va", 1),
        ("wout", 2),
        ("a2", 4),
        ("vb", 2),
        ("va", 2),
        ("q1", 3),
        ("b2", 4),
        ("q2", 3),
        ("vb", 3),
        ("va", 3),
        ("wo", 4),
        ("q0", 4),
        ("q1", 4),
        ("q2", 4),
    ],
}

SCATTER_KEYS = ("f2", "rx", "r0", "t1", "r1", "t2", "r2", "t3", "r3", "f", "send", "recv", "keep", "load")


def body(
    inputs,
    lengths,
    out_grad,
    ln1_gain,
    ln1_bias,
    w_query,
    b_query,
    w_key,
    w_value,
    b_value,
    w_output,
    b_output,
    ln2_gain,
    ln2_bias,
    w_in,
    b_in,
    w_out,
    b_out,
):
    n_seq, tok, width = inputs.shape
    n_blk = lax.axis_size("blk")
    n_dp = lax.axis_size("dp")
    n_dev = n_blk * n_dp
    assert n_seq == n_blk
    seq = tok * n_blk
    hidden = w_in.shape[1]
    head = width // H
    scale = head ** (-0.5)
    blk = lax.axis_index("blk")
    me = lax.axis_index("dp") * n_blk + blk

    def swap(v, s):
        return lax.ppermute(v, "blk", [(i, i ^ s) for i in range(n_blk)])

    def collect(pieces):
        back = [pieces[0]] + [swap(pieces[s], s) for s in range(1, n_blk)]
        out = jnp.zeros((n_seq, tok, width), BF16)
        for s in range(n_blk):
            out = lax.dynamic_update_index_in_dim(out, back[s], blk ^ s, 0)
        return out

    row = lambda v: v.astype(F32).reshape(1, -1)


    sds = jax.ShapeDtypeStruct
    piece = full((tok, width))
    wide = full((width, seq))
    n_col = 3
    cols = width // n_col
    strip = pl.BlockSpec((cols, seq), lambda j: (j, 0))
    anywhere = pl.BlockSpec(memory_space=pl.ANY)
    vmem = pl.BlockSpec(memory_space=pltpu.VMEM)
    xs, nt, qt, kt, vt = pl.pallas_call(
        functools.partial(qkv_spread_kernel, scale * LOG2E, n_blk),
        in_specs=[anywhere, vmem, vmem, anywhere, vmem, anywhere, anywhere, vmem],
        out_specs=[anywhere] * 5,
        out_shape=[sds((n_blk, tok, width), BF16)] + [sds((width, seq), BF16)] * 4,
        scratch_shapes=[
            pltpu.VMEM((n_blk, tok, width), BF16),
            pltpu.VMEM((3, width, width), BF16),
            pltpu.VMEM((3, width, width), BF16),
            pltpu.VMEM((width, seq), BF16),
            pltpu.VMEM((3, width, seq), BF16),
            pltpu.SemaphoreType.DMA((n_blk - 1,)),
            pltpu.SemaphoreType.DMA((n_blk - 1,)),
            pltpu.SemaphoreType.DMA((3,)),
            pltpu.SemaphoreType.DMA((n_blk, 5)),
            pltpu.SemaphoreType.DMA,
        ],
        compiler_params=params(collective_id=0, has_side_effects=True),
        cost_estimate=cost(3 * seq * width * width, 14 * seq * width),
        name="qkv",
    )(inputs, ln1_gain, ln1_bias, w_query, b_query, w_key, w_value, b_value)

    per_head = pl.BlockSpec((head, seq), lambda h: (h, 0))
    per_square = pl.BlockSpec((1, seq, seq), lambda h: (h, 0, 0))
    ct, probs, inv_total, gs = pl.pallas_call(
        functools.partial(attend_spread_kernel, n_blk),
        grid=(H,),
        in_specs=[pl.BlockSpec(memory_space=pltpu.SMEM), per_head, per_head, per_head, anywhere],
        out_specs=[per_head, per_square, pl.BlockSpec((1, 1, seq), lambda h: (h, 0, 0)), anywhere],
        out_shape=[
            sds((width, seq), BF16),
            sds((H, seq, seq), BF16),
            sds((H, 1, seq), F32),
            sds((n_blk, tok, width), BF16),
        ],
        scratch_shapes=[
            pltpu.SemaphoreType.DMA((n_blk - 1,)),
            pltpu.SemaphoreType.DMA((n_blk - 1,)),
            pltpu.SemaphoreType.DMA,
        ],
        compiler_params=params(collective_id=1, has_side_effects=True),
        cost_estimate=cost(8 * seq * seq * width, 2 * H * seq * seq, H * seq * seq),
        name="attend",
    )(lengths, qt, kt, vt, out_grad)

    if n_dp == 8 and n_blk == 4 and width % 768 == 0 and hidden == 4 * width:
        share, share_f = width // n_dev, hidden // n_dev
        tile = hidden // 4
        once = lambda shape: pl.BlockSpec(shape, lambda i: (0,) * len(shape), pipeline_mode=pl.Buffered(1))
        vec_rows = 8
        ins = {
            "x": (xs.reshape(seq, width), once((seq, width))),
            "g": (gs.reshape(seq, width), once((seq, width))),
            "ct": (ct, once((width, seq))),
            "il": (inv_total, once((H, 1, seq))),
            "wo": (w_output, once((width, width))),
            "bo": (b_output, once((width,))),
            "gain": (ln2_gain, once((width,))),
            "bias": (ln2_bias, once((width,))),
            "bout": (b_out, once((width,))),
            "bin": (b_in, once((hidden,))),
            "win": (w_in, pl.BlockSpec((width, tile), lambda i: (0, i % 4))),
            "wout": (w_out, pl.BlockSpec((tile, width), lambda i: (i % 4, 0))),
        }
        outs = {
            "output": (sds((n_seq, tok, width), BF16), anywhere),
            "dmid": (sds((seq, width), F32), anywhere),
            "dot": (sds((width, seq), BF16), once((width, seq))),
            "gwin": (
                sds((2, 2, 2, 4 * share, hidden), BF16),
                pl.BlockSpec((2, 2, 2, 4 * share, tile), lambda i: (0, 0, 0, 0, jnp.maximum(i - 4, 0))),
            ),
            "gwo": (sds((2, 2, 2, 4 * share, width), BF16), once((2, 2, 2, 4 * share, width))),
            "part": (sds((2, 4, share_f, width), BF16), anywhere),
            "vec": (sds((vec_rows, width), F32), once((vec_rows, width))),
        }
        scratch = {
            "mid": pltpu.VMEM((seq, width), F32),
            "acc": pltpu.VMEM((seq, width), F32),
            "n2": pltpu.VMEM((seq, width), BF16),
            "n2t": pltpu.VMEM((width, seq), BF16),
            "act": pltpu.VMEM((seq, tile), BF16),
            "gp": pltpu.VMEM((4, seq, tile), BF16),
            "bins": pltpu.VMEM((4, 1, tile), F32),
            "bing": pltpu.VMEM((4, 1, tile), F32),
            "obuf": pltpu.VMEM((n_blk, tok, width), BF16),
            "gw": pltpu.VMEM((2, 2, 2, 4, share_f, width), BF16),
            "r0": pltpu.VMEM((2, 2, 4, share_f, width), BF16),
            "t1": pltpu.VMEM((2, 4, share_f, width), BF16),
            "r1": pltpu.VMEM((2, 4, share_f, width), BF16),
            "csend": pltpu.SemaphoreType.DMA((4,)),
            "crecv": pltpu.SemaphoreType.DMA((4,)),
            "ysend": pltpu.SemaphoreType.DMA((4,)),
            "yrecv": pltpu.SemaphoreType.DMA((4,)),
            "osend": pltpu.SemaphoreType.DMA((n_blk - 1,)),
            "orecv": pltpu.SemaphoreType.DMA((n_blk - 1,)),
            "lsem": pltpu.SemaphoreType.DMA((3,)),
        }
        names = tuple(ins) + tuple(outs) + tuple(scratch)
        ffn = pl.pallas_call(
            functools.partial(ffn_host_kernel, names, n_blk),
            grid=(8,),
            in_specs=[v[1] for v in ins.values()],
            out_specs=[v[1] for v in outs.values()],
            out_shape=[v[0] for v in outs.values()],
            scratch_shapes=list(scratch.values()),
            compiler_params=pltpu.CompilerParams(
                vmem_limit_bytes=62 * 2**20, collective_id=3, has_side_effects=True
            ),
            name="ffn",
        )(*[v[0] for v in ins.values()])
        ffn = dict(zip(outs, ffn))
        tasks = (
            ("a2", "gwin", None, slice(0, hidden // 2), share, "x", "s_win", slice(0, hidden // 2)),
            ("b2", "gwin", None, slice(hidden // 2, hidden), share, "y", "s_win", slice(hidden // 2, hidden)),
            ("wo", "gwo", None, None, share, "x", "s_wo", None),
        ) + tuple(
            (
                "q%d" % i,
                "gq",
                i,
                None,
                share,
                ("y", "x", "late")[i],
                ("s_wq", "s_wk", "s_wv"),
                slice(i * cols, (i + 1) * cols),
            )
            for i in range(n_col)
        )
        sizes = {"a2": hidden // 2, "b2": hidden // 2, "wo": width}
        plan = PLAN
        last = lambda shape: pl.BlockSpec(shape, lambda h: (jnp.minimum(h, H - 1),) + (0,) * (len(shape) - 1))
        strip_h = last((head, seq))
        ins = {
            "p": (probs, last((1, seq, seq))),
            "q": (qt, strip_h),
            "k": (kt, strip_h),
            "v": (vt, strip_h),
            "do": (ffn["dot"], strip_h),
            "ct": (ct, strip_h),
            "nt": (nt, wide),
            "gain": (ln1_gain, full((width,))),
            "vec_in": (ffn["vec"], full((vec_rows, width))),
            "xs": (xs, anywhere),
            "dmid": (ffn["dmid"], anywhere),
            "wq": (w_query, anywhere),
            "wk": (w_key, anywhere),
            "wv": (w_value, anywhere),
            "part": (ffn["part"], anywhere),
            "gwin": (ffn["gwin"], anywhere),
            "gwo": (ffn["gwo"], anywhere),
        }
        outs = {
            "input_grad": (sds((n_seq, tok, width), BF16), anywhere),
            "s_wq": (sds((share, width), F32), full((share, width))),
            "s_wk": (sds((share, width), F32), full((share, width))),
            "s_wv": (sds((share, width), F32), full((share, width))),
            "s_wo": (sds((share, width), F32), full((share, width))),
            "s_win": (sds((share, hidden), F32), full((share, hidden))),
            "s_wout": (sds((share_f, width), F32), full((share_f, width))),
            "va_out": (sds((8, width), F32), full((8, width))),
            "vb_out": (sds((8, width), F32), full((8, width))),
        }
        scratch = {
            "ds": pltpu.VMEM((seq, seq), BF16),
            "dcat": pltpu.VMEM((3 * width, seq), BF16),
            "wcat": pltpu.VMEM((width, 3 * width), BF16),
            "gq": pltpu.VMEM((n_col, 2, 2, 2, 4 * share, 3 * cols), BF16),
            "va": pltpu.VMEM((8, width), F32),
            "vb": pltpu.VMEM((8, width), F32),
            "va_r": pltpu.VMEM((7, 8, width), F32),
            "vb_r": pltpu.VMEM((7, 8, width), F32),
            "ebuf": pltpu.VMEM((2, width, tok), F32),
            "xbuf": pltpu.VMEM((n_blk, tok, width), BF16),
            "dmbuf": pltpu.VMEM((seq, width), F32),
            "dx": pltpu.VMEM((n_blk, tok, width), BF16),
            "lsem": pltpu.SemaphoreType.DMA((7,)),
            "va_send": pltpu.SemaphoreType.DMA((7,)),
            "va_recv": pltpu.SemaphoreType.DMA((7,)),
            "vb_send": pltpu.SemaphoreType.DMA((7,)),
            "vb_recv": pltpu.SemaphoreType.DMA((7,)),
            "w_keep": pltpu.VMEM((2, share_f, width), BF16),
            "w_rz": pltpu.VMEM((3, 2, share_f, width), BF16),
            "w_f": pltpu.VMEM((2, share_f, width), F32),
            "w_t": pltpu.VMEM((share_f, width), BF16),
            "w_rx": pltpu.VMEM((share_f, width), BF16),
            "w_send": pltpu.SemaphoreType.DMA((4,)),
            "w_recv": pltpu.SemaphoreType.DMA((4,)),
            "isend": pltpu.SemaphoreType.DMA((n_blk - 1,)),
            "irecv": pltpu.SemaphoreType.DMA((n_blk - 1,)),
        }
        for name, source, _, _, task_share, first, _, _ in tasks:
            for k, v in scatter_scratch(task_share, sizes.get(name, width), source != "gq", first == "late").items():
                scratch[name + "_" + k] = v
        names = tuple(ins) + tuple(outs) + tuple(scratch)
        got = pl.pallas_call(
            functools.partial(back_kernel, scale, names, tasks, plan),
            grid=(H + 1,),
            in_specs=[v[1] for v in ins.values()],
            out_specs=[v[1] for v in outs.values()],
            out_shape=[v[0] for v in outs.values()],
            scratch_shapes=list(scratch.values()),
            compiler_params=pltpu.CompilerParams(
                vmem_limit_bytes=60 * 2**20, collective_id=2, has_side_effects=True
            ),
            name="back",
        )(*[v[0] for v in ins.values()])
        got = dict(zip(outs, got))
        big = [ffn["output"], got["input_grad"]] + [
            got[k] for k in ("s_wq", "s_wk", "s_wv", "s_wo", "s_win", "s_wout")
        ]
        part = pl.BlockSpec((1, tok, width), lambda i: (i, 0, 0))
        flat = [sds(v.shape, v.dtype) for v in big]
        fin = pl.pallas_call(
            functools.partial(finish_kernel, len(big)),
            grid=(n_blk,),
            in_specs=[part] * 2 + [full(v.shape) for v in big[2:]] + [full((8, width))] * 2,
            out_specs=[part] * 2 + [full(v.shape) for v in big[2:]] + [full((share,))] * 8 + [full((share_f,))],
            out_shape=flat + [sds((share,), F32)] * 8 + [sds((share_f,), F32)],
            name="finish",
        )(*big, got["va_out"], got["vb_out"])
        output, input_grad, s_wq, s_wk, s_wv, s_wo, s_win, s_wout = fin[: len(big)]
        g1, b1, bq, bv, bo_sum, g2, b2, bout_sum, bin_sum = fin[len(big) :]
        return (
            output,
            input_grad,
            g1,
            b1,
            s_wq,
            bq,
            s_wk,
            s_wv,
            bv,
            s_wo,
            bo_sum,
            g2,
            b2,
            s_win,
            bin_sum,
            s_wout,
            bout_sum,
        )

    n_tile = 4
    tile = hidden // n_tile
    result = pl.pallas_call(
        functools.partial(ffn_kernel, n_blk),
        grid=(n_tile,),
        in_specs=[full((seq, width))] * 2
        + [
            wide,
            full((H, 1, seq)),
            full((width, width)),
            full((1, width)),
            full((1, width)),
            full((1, width)),
            pl.BlockSpec((width, tile), lambda j: (0, j)),
            pl.BlockSpec((1, tile), lambda j: (0, j)),
            pl.BlockSpec((tile, width), lambda j: (j, 0)),
            full((1, width)),
        ],
        out_specs=[piece] * n_blk
        + [
            pl.BlockSpec((tile, width), lambda j: (j, 0)),
            pl.BlockSpec((width, tile), lambda j: (0, j)),
            pl.BlockSpec((1, tile), lambda j: (0, j)),
            full((seq, width)),
            wide,
            full((width, width)),
            full((8, width)),
        ],
        out_shape=[sds((tok, width), BF16)] * n_blk
        + [
            sds((hidden, width), BF16),
            sds((width, hidden), BF16),
            sds((1, hidden), F32),
            sds((seq, width), F32),
            sds((width, seq), BF16),
            sds((width, width), BF16),
            sds((8, width), F32),
        ],
        scratch_shapes=[
            pltpu.VMEM((seq, width), F32),
            pltpu.VMEM((seq, width), BF16),
            pltpu.VMEM((width, seq), BF16),
            pltpu.VMEM((seq, width), F32),
            pltpu.VMEM((seq, width), F32),
            pltpu.VMEM((seq, tile), BF16),
            pltpu.VMEM((seq, tile), BF16),
        ],
        compiler_params=params(),
        cost_estimate=cost(8 * seq * width * hidden, 8 * width * hidden),
        name="ffn",
    )(
        xs.reshape(seq, width),
        gs.reshape(seq, width),
        ct,
        inv_total,
        w_output,
        row(b_output),
        row(ln2_gain),
        row(ln2_bias),
        w_in,
        row(b_in),
        w_out,
        row(b_out),
    )
    out_pieces = result[:n_blk]
    g_wout, g_win, g_bin, dmid, dct, g_wo, vec2 = result[n_blk:]

    bits = (n_dev - 1).bit_length()
    assert n_dev == 1 << bits

    def scatter(grad, order, wire):
        share = grad.shape[0] // n_dev
        order = list(order) + [b for b in range(bits) if b not in order]
        axes = list(range(bits - 1, -1, -1))
        terms = [grad.reshape((2,) * bits + (share,) + grad.shape[1:])]
        for b in order:
            at = axes.index(b)
            axes.pop(at)
            mine = (me >> b) & 1
            send = None
            keep = []
            for t in terms:
                other = lax.dynamic_index_in_dim(t, 1 - mine, at, keepdims=False)
                send = other.astype(F32) if send is None else send + other.astype(F32)
                keep.append(lax.dynamic_index_in_dim(t, mine, at, keepdims=False))
            got = lax.ppermute(send.astype(wire), ("dp", "blk"), [(i, i ^ (1 << b)) for i in range(n_dev)])
            terms = keep + [got]
        total = terms[0].astype(F32)
        for t in terms[1:]:
            total = total + t.astype(F32)
        return total

    s_wout = scatter(g_wout, (0, 1, 2, 3, 4), BF16)
    s_win = scatter(g_win, (0, 2, 1, 3, 4), BF16)
    s_wo = scatter(g_wo, (0, 3, 4, 1, 2), BF16)
    output = collect(out_pieces)

    dqt, dkt, dvt = pl.pallas_call(
        functools.partial(attend_back_kernel, scale),
        grid=(H,),
        in_specs=[per_square] + [per_head] * 5,
        out_specs=[per_head] * 3,
        out_shape=[sds((width, seq), BF16)] * 3,
        scratch_shapes=[pltpu.VMEM((seq, seq), BF16)],
        compiler_params=params(),
        cost_estimate=cost(10 * seq * seq * width, 2 * H * seq * seq),
        name="attend_back",
    )(probs, qt, kt, vt, dct, ct)

    result = pl.pallas_call(
        functools.partial(input_kernel, n_blk),
        in_specs=[full((seq, width))] * 2
        + [full((1, width)), wide, wide, wide]
        + [full((width, width))] * 3,
        out_specs=[piece] * n_blk + [full((8, width))],
        out_shape=[sds((tok, width), BF16)] * n_blk + [sds((8, width), F32)],
        compiler_params=params(),
        cost_estimate=cost(3 * seq * width * width, 14 * seq * width),
        name="input_grad",
    )(xs.reshape(seq, width), dmid, row(ln1_gain), dqt, dkt, dvt, w_query, w_key, w_value)
    input_grad = collect(result[:n_blk])
    vec1 = result[n_blk]

    col = pl.BlockSpec((width, cols), lambda j: (0, j))
    g_wq, g_wk, g_wv, vecq = pl.pallas_call(
        qkv_grad_kernel,
        grid=(n_col,),
        in_specs=[wide, strip, strip, strip],
        out_specs=[col, col, col, pl.BlockSpec((8, cols), lambda j: (0, j))],
        out_shape=[sds((width, width), BF16)] * 3 + [sds((8, width), F32)],
        compiler_params=params(),
        cost_estimate=cost(3 * seq * width * width, 14 * seq * width),
        name="qkv_grad",
    )(nt, dqt, dkt, dvt)
    s_wq = scatter(g_wq, (0, 1, 2, 3, 4), BF16)
    s_wk = scatter(g_wk, (0, 2, 3, 4, 1), BF16)
    s_wv = scatter(g_wv, (0, 3, 4, 1, 2), BF16)

    vectors = [vec1[0], vec1[1], vecq[0], vecq[1], vec2[3], vec2[1], vec2[2], g_bin[0], vec2[0]]
    packed = jnp.concatenate([v.reshape(n_dev, -1) for v in vectors], axis=1)
    packed = scatter(packed, (0, 1, 2, 3, 4), F32).reshape(-1)
    parts = []
    at = 0
    for v in vectors:
        size = v.shape[0] // n_dev
        parts.append(packed[at : at + size])
        at += size
    p_ln1g, p_ln1b, p_bq, p_bv, p_bo, p_ln2g, p_ln2b, p_bin, p_bout = parts
    return (
        output,
        input_grad,
        p_ln1g,
        p_ln1b,
        s_wq,
        p_bq,
        s_wk,
        s_wv,
        p_bv,
        s_wo,
        p_bo,
        p_ln2g,
        p_ln2b,
        s_win,
        p_bin,
        s_wout,
        p_bout,
    )


def solution(mesh):
    whole = P(("dp", "blk"))
    rows = P(("dp", "blk"), None)
    tokens = P("dp", "blk", None)
    in_specs = (tokens, P("dp"), tokens) + (P(),) * 15
    out_specs = (
        tokens,
        tokens,
        whole,
        whole,
        rows,
        whole,
        rows,
        rows,
        whole,
        rows,
        whole,
        whole,
        whole,
        rows,
        whole,
        rows,
        whole,
    )
    return jax.shard_map(body, mesh=mesh, in_specs=in_specs, out_specs=out_specs, check_vma=False)
```

```python
import functools

import jax
import jax.numpy as jnp
from jax import lax
from jax.experimental import pallas as pl
from jax.experimental.pallas import tpu as pltpu
from jax.sharding import PartitionSpec as P

H = 12
EPS = 1e-05
LOG2E = 1.4426950408889634
LN2 = 0.6931471805599453
INV_SQRT_2PI = 0.3989422804014327
SQRT_HALF = 0.7071067811865476
F32 = jnp.float32
BF16 = jnp.bfloat16
VMEM_LIMIT = 56 * 2**20

NN = (((1,), (0,)), ((), ()))
NT = (((1,), (1,)), ((), ()))
TN = (((0,), (0,)), ((), ()))

def dot(left, right, dims=NN):
    return lax.dot_general(left, right, dims, preferred_element_type=F32)


def params(**kw):
    return pltpu.CompilerParams(vmem_limit_bytes=VMEM_LIMIT, **kw)


def cost(macs, nbytes, exps=0):
    return pl.CostEstimate(flops=2 * macs, bytes_accessed=nbytes, transcendentals=exps)


def full(shape):
    return pl.BlockSpec(shape, lambda *_: (0,) * len(shape))


def as_row(ref):
    return ref[...].astype(F32)[None, :]


def center(v):
    mean = jnp.mean(v, axis=-1, keepdims=True)
    cent = v - mean
    var = jnp.mean(cent * cent, axis=-1, keepdims=True)
    rstd = lax.rsqrt(var + EPS)
    return cent * rstd, rstd


def gate(u):
    phi = 0.5 + 0.5 * lax.erf(u * SQRT_HALF)
    e = jnp.exp2(u * u * (-0.5 * LOG2E))
    return phi, u * e * INV_SQRT_2PI


def attend_kernel(n_blk, len_ref, q_ref, k_ref, v_ref, c_ref, p_ref, il_ref, f_ref):
    seq = q_ref.shape[1]
    tok = seq // n_blk
    blk = lax.axis_index("blk")
    length = len_ref[blk]
    live = [(blk ^ i) * tok < length for i in range(n_blk)]
    keys, q, v = k_ref[...].T, q_ref[...], v_ref[...]
    m = jnp.full((1, seq), -1e30, F32)
    total = summed = None
    tops = []
    ahead = dot(keys[:tok], q)
    for i in range(n_blk):
        s = ahead
        if i + 1 < n_blk:
            ahead = dot(keys[(i + 1) * tok : (i + 2) * tok], q)
        new = jnp.maximum(m, jnp.where(live[i], jnp.max(s, axis=0, keepdims=True), -1e30))
        p = jnp.exp2(s - jnp.where(live[i], new, 1e30))
        part = jnp.sum(p, axis=0, keepdims=True)
        p = p.astype(BF16)
        p_ref[0, i * tok : (i + 1) * tok] = p
        o = dot(v[:, i * tok : (i + 1) * tok], p)
        if i == 0:
            summed, total = o, part
        else:
            shrink = jnp.exp2(m - new)
            summed, total = summed * shrink + o, total * shrink + part
        m = new
        tops.append(m)
    inv = 1.0 / total
    c_ref[...] = (summed * inv).astype(BF16)
    il_ref[0] = inv
    for i in range(n_blk):
        f_ref[0, i : i + 1] = jnp.exp2(tops[i] - m)


def attend_back_head(scale, n_blk, p_ref, q, k, v, do, ct, f_ref, ds, doi):
    seq = q.shape[1]
    tok = seq // n_blk
    vh = v.T
    do = do.astype(F32)
    delta = jnp.sum(do * ct.astype(F32), axis=0, keepdims=True)
    for i in range(n_blk):
        sl = slice(i * tok, (i + 1) * tok)
        f = f_ref[0, i : i + 1]
        d = (do * f).astype(BF16)
        doi[i] = d
        ds[sl] = (p_ref[0, sl].astype(F32) * (dot(vh[sl], d) - delta * f)).astype(BF16)
    dq = (dot(k, ds[...]) * scale).astype(BF16)
    dv = [dot(p_ref[0, i * tok : (i + 1) * tok], doi[i], NT).T.astype(BF16) for i in range(n_blk)]
    dk = (dot(ds[...], q, NT) * LN2).T.astype(BF16)
    return dq, dk, jnp.concatenate(dv, axis=1)


MESH = pl.DeviceIdType.MESH


def greet(partners):
    barrier = pltpu.get_barrier_semaphore()
    for where in partners:
        pl.semaphore_signal(barrier, inc=1, device_id=where, device_id_type=MESH)
    pl.semaphore_wait(barrier, len(partners))


def qkv_spread_kernel(
    scale,
    n_blk,
    x_any,
    gain,
    bias,
    wq_any,
    bq,
    wk_any,
    wv_any,
    bv,
    xs_any,
    nt_any,
    q_any,
    k_any,
    v_any,
    xbuf,
    wbuf,
    wt,
    nt,
    qkv,
    send,
    recv,
    wsem,
    osem,
    xsem,
):
    tok, width = xbuf.shape[1:]
    dp = lax.axis_index("dp")
    blk = lax.axis_index("blk")
    own = pltpu.make_async_copy(x_any.at[blk], xbuf.at[0], xsem)
    own.start()
    loads = [
        pltpu.make_async_copy(w, wbuf.at[i], wsem.at[i]) for i, w in enumerate((wq_any, wk_any, wv_any))
    ]
    for load in loads:
        load.start()
    greet([(dp, blk ^ s) for s in range(1, n_blk)])
    order = list(range(n_blk - 1, 0, -1))
    copies = {}
    for s in order:
        copies[s] = pltpu.make_async_remote_copy(
            src_ref=x_any.at[blk ^ s],
            dst_ref=xbuf.at[s],
            send_sem=send.at[s - 1],
            recv_sem=recv.at[s - 1],
            device_id=(dp, blk ^ s),
            device_id_type=MESH,
        )
        if s != 2:
            copies[s].start()
    for i, load in enumerate(loads):
        load.wait()
        wt[i] = wbuf[i].T
    cols = jnp.concatenate([as_row(bq), as_row(bv), jnp.zeros((6, width), F32)], axis=0).T
    writes = []
    for s in (0, 1, 3, 2):
        if s == 0:
            own.wait()
        else:
            if s == 3:
                copies[3].wait_send()
                copies[2].start()
            copies[s].wait_recv()
        sl = slice(s * tok, (s + 1) * tok)
        n, _ = center(xbuf[s].astype(F32))
        n = (n * as_row(gain) + as_row(bias)).astype(BF16).T
        nt[:, sl] = n
        qkv[0, :, sl] = ((dot(wt[0], n) + cols[:, :1]) * scale).astype(BF16)
        qkv[1, :, sl] = dot(wt[1], n).astype(BF16)
        qkv[2, :, sl] = (dot(wt[2], n) + cols[:, 1:2]).astype(BF16)
        for i, (src, dst) in enumerate(
            (
                (xbuf.at[s], xs_any.at[s]),
                (nt.at[:, sl], nt_any.at[:, sl]),
                (qkv.at[0, :, sl], q_any.at[:, sl]),
                (qkv.at[1, :, sl], k_any.at[:, sl]),
                (qkv.at[2, :, sl], v_any.at[:, sl]),
            )
        ):
            write = pltpu.make_async_copy(src, dst, osem.at[s, i])
            write.start()
            writes.append(write)
    for s in (1, 2):
        copies[s].wait_send()
    for write in writes:
        write.wait()


def attend_spread_kernel(n_blk, len_ref, q_ref, k_ref, v_ref, g_any, c_ref, p_ref, il_ref, f_ref, gs_any, send, recv, osem):
    h = pl.program_id(0)
    dp = lax.axis_index("dp")
    blk = lax.axis_index("blk")

    def copy(s):
        return pltpu.make_async_remote_copy(
            src_ref=g_any.at[blk ^ s],
            dst_ref=gs_any.at[s],
            send_sem=send.at[s - 1],
            recv_sem=recv.at[s - 1],
            device_id=(dp, blk ^ s),
            device_id_type=MESH,
        )

    own = pltpu.make_async_copy(g_any.at[blk], gs_any.at[0], osem)

    @pl.when(h == 0)
    def _():
        greet([(dp, blk ^ s) for s in range(1, n_blk)])
        own.start()
        for s in range(1, n_blk):
            copy(s).start()

    attend_kernel(n_blk, len_ref, q_ref, k_ref, v_ref, c_ref, p_ref, il_ref, f_ref)

    @pl.when(h == pl.num_programs(0) - 1)
    def _():
        own.wait()
        for s in range(1, n_blk):
            copy(s).wait()


def regroup(v, share):
    def slab(c, x, y):
        at = [(z * 8 + y * 4 + x * 2 + c) * share for z in range(4)]
        return jnp.concatenate([v[a : a + share] for a in at], axis=0)

    return [[[slab(c, x, y) for y in range(2)] for x in range(2)] for c in range(2)]


CXY = [(c, x, y) for c in range(2) for x in range(2) for y in range(2)]


class Scatter:
    def __init__(self, source, cols, share, first, out, bufs, place):
        self.source, self.cols, self.share, self.out = source, cols, share, out
        self.b = bufs
        dp, blk = place
        self.c, self.x, self.y, self.z = blk & 1, blk >> 1, dp & 1, dp >> 1
        self.first = first
        ids = {"x": (dp, blk ^ 2), "y": (dp ^ 1, blk)}
        self.mp = self.x if first == "x" else self.y
        self.mq = self.y if first == "x" else self.x
        self.core_id = (dp, blk ^ 1)
        self.p_id = ids[first]
        self.q_id = ids["y" if first == "x" else "x"]
        self.z_ids = [(((self.z + d) & 3) * 2 + self.y, blk) for d in (1, 2, 3)]
        self.chunk = share if share % 16 == 0 else 2 * share

    def remote(self, src, dst, i, where):
        return pltpu.make_async_remote_copy(
            src_ref=src,
            dst_ref=dst,
            send_sem=self.b["send"].at[i],
            recv_sem=self.b["recv"].at[i],
            device_id=where,
            device_id_type=MESH,
        )

    def part(self, c):
        if self.cols is None:
            return self.source.at[c]
        return self.source.at[c, :, :, :, self.cols]

    def core_copy(self):
        return self.remote(self.part(1 - self.c), self.b["r0"], 0, self.core_id)

    def load(self):
        return pltpu.make_async_copy(self.part(self.c), self.b["keep"], self.b["load"])

    def p_copy(self):
        return self.remote(self.b["t1"], self.b["r1"], 1, self.p_id)

    def q_copy(self):
        return self.remote(self.b["t2"], self.b["r2"], 2, self.q_id)

    def z_copies(self):
        return [self.remote(self.b["t3"].at[d], self.b["r3"].at[d], 3 + d, self.z_ids[d]) for d in range(3)]

    def pick(self, ref, a, b, rows):
        return (ref[a, b, rows] if self.first == "x" else ref[b, a, rows]).astype(F32)

    def two(self, a, b, rows):
        own = self.b["keep"] if "keep" in self.b else self.source.at[self.c]
        a, b = (a, b) if self.first == "x" else (b, a)
        return own[a, b, rows] + self.b["r0"][a, b, rows]

    def base(self, a, b, rows):
        if "keep" in self.b:
            own = self.pick(self.b["keep"], a, b, rows)
        else:
            own = (
                self.source[self.c, a, b, rows] if self.first == "x" else self.source[self.c, b, a, rows]
            ).astype(F32)
        return own + self.pick(self.b["r0"], a, b, rows)

    def each(self, fn):
        rows = 4 * self.share

        def step(i, carry):
            fn(i, pl.ds(pl.multiple_of(i * self.chunk, self.chunk), self.chunk))
            return carry

        lax.fori_loop(0, rows // self.chunk, step, 0)

    def stage0(self):
        self.core_copy().start()
        if "keep" in self.b:
            self.load().start()

    def stage1(self):
        if "keep" in self.b:
            self.load().wait()
        self.core_copy().wait()
        for b in range(2):

            def fn(i, rows):
                self.b["t1"][b, rows] = self.two(1 - self.mp, b, rows)

            self.each(fn)
        self.p_copy().start()

    def stage2(self):
        self.p_copy().wait()

        def fn(i, rows):
            v = self.base(self.mp, 1 - self.mq, rows) + self.b["r1"][1 - self.mq, rows].astype(F32)
            self.b["t2"][rows] = v.astype(BF16)

        self.each(fn)
        self.q_copy().start()

    def stage3(self):
        self.q_copy().wait()
        share = self.share
        per = self.chunk // share
        f = self.b["f"]

        def fn(i, rows):
            v = self.base(self.mp, self.mq, rows)
            v = v + self.b["r1"][self.mq, rows].astype(F32) + self.b["r2"][rows].astype(F32)
            for k in range(per):
                f[i * per + k] = v[k * share : (k + 1) * share]

        self.each(fn)
        half = f.shape[2] // 2
        for d in range(3):
            v = f[(self.z + d + 1) & 3]
            if per > 1:
                v = jnp.concatenate([v[:, :half], v[:, half:]], axis=0)
            self.b["t3"][d] = v.astype(BF16)
        for copy in self.z_copies():
            copy.start()

    def stage4(self):
        for copy in self.z_copies():
            copy.wait()
        v = self.b["f"][self.z]
        for d in range(3):
            w = self.b["r3"][d].astype(F32)
            if self.chunk > self.share:
                w = jnp.concatenate([w[: self.share], w[self.share :]], axis=1)
            v = v + w
        self.out(v)


class ScatterLate(Scatter):
    def x_copy(self):
        return self.remote(self.b["f2"].at[1 - self.x], self.b["rx"], 2, self.q_id)

    def stage2(self):
        self.p_copy().wait()
        share = self.share
        per = self.chunk // share
        f = self.b["f"]
        for x in range(2):

            def fn(i, rows, x=x):
                v = self.base(self.mp, x, rows) + self.b["r1"][x, rows].astype(F32)
                for k in range(per):
                    f[x, i * per + k] = v[k * share : (k + 1) * share]

            self.each(fn)
        for d in range(3):
            at = (self.z + d + 1) & 3
            self.b["t3"][d] = jnp.concatenate([f[0, at], f[1, at]], axis=0).astype(BF16)
        for copy in self.z_copies():
            copy.start()

    def stage3(self):
        for copy in self.z_copies():
            copy.wait()
        for x in range(2):
            v = self.b["f"][x, self.z]
            for d in range(3):
                v = v + self.b["r3"][d].astype(F32)[x * self.share : (x + 1) * self.share]
            self.b["f2"][x] = v
        self.x_copy().start()

    def stage4(self):
        self.x_copy().wait()
        self.out(self.b["f2"][self.x] + self.b["rx"][...])


def scatter_scratch(share, cols, in_hbm, late):
    rows = 4 * share
    slab = (share, cols) if share % 16 == 0 else (2 * share, cols // 2)
    bufs = {
        "r0": pltpu.VMEM((2, 2, rows, cols), BF16),
        "t1": pltpu.VMEM((2, rows, cols), BF16),
        "r1": pltpu.VMEM((2, rows, cols), BF16),
        "t2": pltpu.VMEM((rows, cols), BF16),
        "r2": pltpu.VMEM((rows, cols), BF16),
        "t3": pltpu.VMEM((3,) + slab, BF16),
        "r3": pltpu.VMEM((3,) + slab, BF16),
        "f": pltpu.VMEM((4, share, cols), F32),
        "send": pltpu.SemaphoreType.DMA((6,)),
        "recv": pltpu.SemaphoreType.DMA((6,)),
    }
    if late:
        del bufs["t2"], bufs["r2"]
        bufs["t3"] = pltpu.VMEM((3, 2 * share, cols), BF16)
        bufs["r3"] = pltpu.VMEM((3, 2 * share, cols), BF16)
        bufs["f"] = pltpu.VMEM((2, 4, share, cols), F32)
        bufs["f2"] = pltpu.VMEM((2, share, cols), F32)
        bufs["rx"] = pltpu.VMEM((share, cols), F32)
    if in_hbm:
        bufs["keep"] = pltpu.VMEM((2, 2, rows, cols), BF16)
        bufs["load"] = pltpu.SemaphoreType.DMA
    return bufs


def ffn_kernel(n_blk, *refs):
    x_ref, g = refs[:2]
    (ct_ref, il_ref, wo_ref, bo_ref, gain_ref, bias_ref, win_ref, bin_ref, wout_ref, bout_ref) = refs[2:12]
    rest = refs[12:]
    outs = rest[:n_blk]
    (gwout_ref, gwin_ref, gbin_ref, dmid_ref, dot_ref, gwo_ref, vec_ref) = rest[n_blk : n_blk + 7]
    mid, n2, n2t, acc_o, acc_d, act, dpre = rest[n_blk + 7 :]
    tok = outs[0].shape[0]
    j = pl.program_id(0)

    @pl.when(j == 0)
    def _():
        for s in range(n_blk):
            sl = slice(s * tok, (s + 1) * tok)
            m = x_ref[sl].astype(F32) + dot(ct_ref[:, sl], wo_ref[...], TN) + bo_ref[...]
            mid[sl] = m
            acc_o[sl] = m + bout_ref[...]
            acc_d[sl] = jnp.zeros_like(m)
            n, _ = center(m)
            nb = (n * gain_ref[...] + bias_ref[...]).astype(BF16)
            n2[sl] = nb
            n2t[:, sl] = nb.T

    bin_grad = None
    for s in range(n_blk):
        sl = slice(s * tok, (s + 1) * tok)
        pre = dot(n2[sl], win_ref[...]) + bin_ref[...]
        phi, slope = gate(pre)
        a = (pre * phi).astype(BF16)
        dact = dot(g[sl], wout_ref[...], NT)
        dp = (dact * (phi + slope)).astype(BF16)
        act[sl] = a
        dpre[sl] = dp
        col = jnp.sum(dp.astype(F32), axis=0, keepdims=True)
        bin_grad = col if bin_grad is None else bin_grad + col
        acc_o[sl] += dot(a, wout_ref[...])
        acc_d[sl] += dot(dp, win_ref[...], NT)
    gbin_ref[...] = bin_grad
    gwout_ref[...] = dot(act[...], g[...], TN).astype(BF16)
    gwin_ref[...] = dot(n2t[...], dpre[...]).astype(BF16)

    @pl.when(j == pl.num_programs(0) - 1)
    def _():
        head = wo_ref.shape[0] // H
        sums = [None] * 4
        for s in range(n_blk):
            sl = slice(s * tok, (s + 1) * tok)
            outs[s][...] = acc_o[sl].astype(BF16)
            n, rstd = center(mid[sl])
            e = acc_d[sl]
            gf = g[sl].astype(F32)
            f = e * gain_ref[...]
            dm = gf + rstd * (
                f - jnp.mean(f, axis=-1, keepdims=True) - n * jnp.mean(f * n, axis=-1, keepdims=True)
            )
            dmid_ref[sl] = dm
            db = dm.astype(BF16)
            n2[sl] = db
            for i, term in enumerate((gf, e * n, e, db.astype(F32))):
                col = jnp.sum(term, axis=0, keepdims=True)
                sums[i] = col if sums[i] is None else sums[i] + col
            dc = dot(wo_ref[...], db, NT)
            for h in range(H):
                hs = slice(h * head, (h + 1) * head)
                dot_ref[hs, sl] = (dc[hs] * il_ref[h, :, sl]).astype(BF16)
        for i in range(4):
            vec_ref[i : i + 1] = sums[i]
        gwo_ref[...] = dot(ct_ref[...], n2[...]).astype(BF16)


def attend_back_kernel(
    scale, n_blk, p_ref, q_ref, k_ref, v_ref, do_ref, c_ref, f_ref, dq_ref, dk_ref, dv_ref, ds, doi
):
    dq_ref[...], dk_ref[...], dv_ref[...] = attend_back_head(
        scale, n_blk, p_ref, q_ref[...], k_ref[...], v_ref[...], do_ref[...], c_ref[...], f_ref, ds, doi
    )


def input_kernel(n_blk, x_ref, dmid_ref, gain_ref, dq_ref, dk_ref, dv_ref, wq_ref, wk_ref, wv_ref, *rest):
    outs = rest[:n_blk]
    vec_ref = rest[n_blk]
    tok = outs[0].shape[0]
    sums = [None] * 2
    for s in range(n_blk):
        sl = slice(s * tok, (s + 1) * tok)
        et = dot(wq_ref[...], dq_ref[:, sl]) + dot(wk_ref[...], dk_ref[:, sl]) + dot(wv_ref[...], dv_ref[:, sl])
        e = et.T
        n, rstd = center(x_ref[sl].astype(F32))
        f = e * gain_ref[...]
        dx = dmid_ref[sl] + rstd * (
            f - jnp.mean(f, axis=-1, keepdims=True) - n * jnp.mean(f * n, axis=-1, keepdims=True)
        )
        outs[s][...] = dx.astype(BF16)
        for i, term in enumerate((e * n, e)):
            col = jnp.sum(term, axis=0, keepdims=True)
            sums[i] = col if sums[i] is None else sums[i] + col
    for i in range(2):
        vec_ref[i : i + 1] = sums[i]


def qkv_grad_kernel(nt_ref, dq_ref, dk_ref, dv_ref, gq_ref, gk_ref, gv_ref, vec_ref):
    nt = nt_ref[...]
    ones = jnp.ones((8, nt.shape[1]), BF16)
    gq_ref[...] = dot(nt, dq_ref[...], NT).astype(BF16)
    gk_ref[...] = dot(nt, dk_ref[...], NT).astype(BF16)
    gv_ref[...] = dot(nt, dv_ref[...], NT).astype(BF16)
    vec_ref[0:1] = dot(ones, dq_ref[...], NT)[:1]
    vec_ref[1:2] = dot(ones, dv_ref[...], NT)[:1]


def ffn_host_kernel(names, n_blk, *refs):
    r = dict(zip(names, refs))
    i = pl.program_id(0)
    j = i & 3
    dp = lax.axis_index("dp")
    blk = lax.axis_index("blk")
    core, y = blk & 1, dp & 1
    mid, acc, n2, n2t, act, gp, gw, r0, t1, r1 = [
        r[k] for k in ("mid", "acc", "n2", "n2t", "act", "gp", "gw", "r0", "t1", "r1")
    ]
    g, win, wout, ct = r["g"], r["win"], r["wout"], r["ct"]
    seq, width = mid.shape
    tok = seq // n_blk
    tile = act.shape[1]
    share_f = gw.shape[4]
    rows = [slice(s * tok, (s + 1) * tok) for s in range(n_blk)]

    def core_copy(plane):
        return pltpu.make_async_remote_copy(
            src_ref=gw.at[1 - core, :, :, plane],
            dst_ref=r0.at[:, :, plane],
            send_sem=r["csend"].at[plane],
            recv_sem=r["crecv"].at[plane],
            device_id=(dp, blk ^ 1),
            device_id_type=MESH,
        )

    def y_copy(plane):
        return pltpu.make_async_remote_copy(
            src_ref=t1.at[:, plane],
            dst_ref=r1.at[:, plane],
            send_sem=r["ysend"].at[plane],
            recv_sem=r["yrecv"].at[plane],
            device_id=(dp ^ 1, blk),
            device_id_type=MESH,
        )

    def y_start(plane):
        core_copy(plane).wait()
        for x in range(2):
            t1[x, plane] = gw[core, x, 1 - y, plane] + r0[x, 1 - y, plane]
        y_copy(plane).start()

    def out_copy(s):
        src, dst = r["obuf"].at[s], r["output"].at[blk]
        if s == 0:
            return pltpu.make_async_copy(src, dst, r["lsem"].at[0])
        return pltpu.make_async_remote_copy(
            src_ref=src,
            dst_ref=dst,
            send_sem=r["osend"].at[s - 1],
            recv_sem=r["orecv"].at[s - 1],
            device_id=(dp, blk ^ s),
            device_id_type=MESH,
        )

    @pl.when(i == 0)
    def _():
        greet([(dp, blk ^ 1), (dp, blk ^ 2), (dp, blk ^ 3), (dp ^ 1, blk)])
        bins = as_row(r["bin"])
        for k in range(4):
            r["bins"][k] = bins[:, k * tile : (k + 1) * tile]
        for sl in rows:
            m = r["x"][sl].astype(F32) + dot(ct[:, sl], r["wo"][...], TN) + as_row(r["bo"])
            mid[sl] = m
            acc[sl] = m + as_row(r["bout"])
            n, _ = center(m)
            nb = (n * as_row(r["gain"]) + as_row(r["bias"])).astype(BF16)
            n2[sl] = nb
            n2t[:, sl] = nb.T

    @pl.when(i < 4)
    def _():
        ahead = dot(n2[rows[0]], win[...])
        for s, sl in enumerate(rows):
            pre = ahead + r["bins"][j]
            if s + 1 < n_blk:
                ahead = dot(n2[rows[s + 1]], win[...])
            phi, slope = gate(pre)
            a = (pre * phi).astype(BF16)
            act[sl] = a
            gp[j, sl] = (phi + slope).astype(BF16)
            acc[sl] += dot(a, wout[...])

        @pl.when(i > 0)
        def _():
            y_start(j - 1)

        v = dot(act[...], g[...], TN)
        for c, x, yy in CXY:
            at = (yy * 4 + x * 2 + c) * share_f
            gw[c, x, yy, j] = v[at : at + share_f].astype(BF16)
        core_copy(j).start()

    @pl.when(i == 4)
    def _():
        for s in range(n_blk - 1, -1, -1):
            r["obuf"][s] = acc[rows[s]].astype(BF16)
            out_copy(s).start()
            acc[rows[s]] = jnp.zeros((tok, width), F32)

    @pl.when(i >= 4)
    def _():
        total = None
        ahead = dot(g[rows[0]], wout[...], NT)
        for s, sl in enumerate(rows):
            d = (ahead * gp[j, sl].astype(F32)).astype(BF16)
            if s + 1 < n_blk:
                ahead = dot(g[rows[s + 1]], wout[...], NT)
            act[sl] = d
            col = jnp.sum(d.astype(F32), axis=0, keepdims=True)
            total = col if total is None else total + col
            acc[sl] += dot(d, win[...], NT)
        r["bing"][j] = total

        @pl.when(i == 4)
        def _():
            y_start(3)

        v = regroup(dot(n2t[...], act[...]), width // 32)
        for c, x, yy in CXY:
            r["gwin"][c, x, yy] = v[c][x][yy].astype(BF16)

    @pl.when(i == 7)
    def _():
        head = width // H
        sums = [None] * 4
        for sl in rows:
            n, rstd = center(mid[sl])
            e = acc[sl]
            gf = g[sl].astype(F32)
            f = e * as_row(r["gain"])
            dm = gf + rstd * (
                f - jnp.mean(f, axis=-1, keepdims=True) - n * jnp.mean(f * n, axis=-1, keepdims=True)
            )
            mid[sl] = dm
            db = dm.astype(BF16)
            n2[sl] = db
            for k, term in enumerate((gf, e * n, e, db.astype(F32))):
                col = jnp.sum(term, axis=0, keepdims=True)
                sums[k] = col if sums[k] is None else sums[k] + col
            dc = dot(r["wo"][...], db, NT)
            for h in range(H):
                hs = slice(h * head, (h + 1) * head)
                r["dot"][hs, sl] = (dc[hs] * r["il"][h, :, sl]).astype(BF16)
        save = pltpu.make_async_copy(mid, r["dmid"], r["lsem"].at[1])
        save.start()
        vec = r["vec"]
        for k in range(4):
            vec[k : k + 1] = sums[k]
            vec[4 + k : 5 + k] = r["bing"][k]
        v = regroup(dot(ct[...], n2[...]), width // 32)
        for c, x, yy in CXY:
            r["gwo"][c, x, yy] = v[c][x][yy].astype(BF16)
        for k in range(4):
            y_copy(k).wait()

        def step(k, carry):
            for x in range(2):
                v = gw[core, x, y, k].astype(F32) + r0[x, y, k].astype(F32) + r1[x, k].astype(F32)
                t1[x, k] = v.astype(BF16)
            return carry

        lax.fori_loop(0, 4, step, 0)
        part = pltpu.make_async_copy(t1, r["part"], r["lsem"].at[2])
        part.start()
        for s in range(n_blk):
            out_copy(s).wait()
        save.wait()
        part.wait()


class Resume:
    def __init__(self, r, place):
        dp, blk = place
        self.r = r
        self.x, self.y, self.z = blk >> 1, dp & 1, dp >> 1
        self.ids = [(((self.z + d) & 3) * 2 + self.y, blk) for d in (1, 2, 3)] + [(dp, blk ^ 2)]

    def remote(self, src, dst, i):
        return pltpu.make_async_remote_copy(
            src_ref=src,
            dst_ref=dst,
            send_sem=self.r["w_send"].at[i],
            recv_sem=self.r["w_recv"].at[i],
            device_id=self.ids[i],
            device_id_type=MESH,
        )

    def z_copies(self):
        return [
            self.remote(self.r["part"].at[:, (self.z + d + 1) & 3], self.r["w_rz"].at[d], d) for d in range(3)
        ]

    def load(self):
        return pltpu.make_async_copy(self.r["part"].at[:, self.z], self.r["w_keep"], self.r["lsem"].at[0])

    def x_copy(self):
        return self.remote(self.r["w_t"], self.r["w_rx"], 3)

    def stage0(self):
        for copy in self.z_copies():
            copy.start()
        self.load().start()

    def stage1(self):
        self.load().wait()
        for copy in self.z_copies():
            copy.wait()
        for k in range(2):
            v = self.r["w_keep"][k].astype(F32)
            for d in range(3):
                v = v + self.r["w_rz"][d, k].astype(F32)
            self.r["w_f"][k] = v
        self.r["w_t"][...] = self.r["w_f"][1 - self.x].astype(BF16)
        self.x_copy().start()

    def stage2(self):
        self.x_copy().wait()
        self.r["s_wout"][...] = self.r["w_f"][self.x] + self.r["w_rx"][...].astype(F32)


def finish_kernel(n_big, *refs):
    src, va, vb = refs[:n_big], refs[n_big], refs[n_big + 1]
    dst, small = refs[n_big + 2 : 2 * n_big + 2], refs[2 * n_big + 2 :]
    for a, b in zip(src[:2], dst[:2]):
        b[...] = a[...]

    @pl.when(pl.program_id(0) == 0)
    def _():
        for a, b in zip(src[2:], dst[2:]):
            b[...] = a[...]
        me = lax.axis_index("dp") * lax.axis_size("blk") + lax.axis_index("blk")
        share = small[0].shape[0]
        wide = small[8].shape[0]
        width = va.shape[1]
        shift = lax.rem(width - me * share, width)
        moved = pltpu.roll(va[...], shift, 1)
        for k in range(4):
            small[k][...] = moved[k, :share]
        lines = vb[...]
        moved = pltpu.roll(lines, shift, 1)
        for i, k in enumerate((3, 1, 2, 0)):
            small[4 + i][...] = moved[k, :share]
        each = width // wide
        moved = pltpu.roll(lines, lax.rem(width - lax.rem(me, each) * wide, width), 1)
        row = 4 + lax.div(me, each)
        pick = lax.broadcasted_iota(jnp.int32, moved.shape, 0) == row
        small[8][...] = jnp.sum(jnp.where(pick, moved, 0.0), axis=0)[:wide]


def back_kernel(scale, names, tasks, plan, *refs):
    r = dict(zip(names, refs))
    h = pl.program_id(0)
    dp = lax.axis_index("dp")
    blk = lax.axis_index("blk")
    place = (dp, blk)
    n_blk, tok, width = r["xs"].shape
    seq = n_blk * tok
    head = width // H
    dcat, wcat, gq, vec = r["dcat"], r["wcat"], r["gq"], r["va"]

    def put(ref, cols):
        def out(v):
            if cols is None:
                ref[...] = v
            else:
                ref[:, cols] = v

        return out

    jobs = {}
    for name, source, index, cols, share, first, out, out_cols in tasks:
        ref = r[source] if index is None else r[source].at[index]
        bufs = {k: r[name + "_" + k] for k in SCATTER_KEYS if name + "_" + k in r}
        if isinstance(out, tuple):
            outs = [put(r[o], out_cols) for o in out]

            def sink(v, outs=outs):
                each = v.shape[1] // len(outs)
                for i, o in enumerate(outs):
                    o(v[:, i * each : (i + 1) * each])

        else:
            sink = put(r[out], out_cols)
        kind = ScatterLate if first == "late" else Scatter
        jobs[name] = kind(ref, cols, share, "y" if first == "late" else first, sink, bufs, place)

    jobs["wout"] = Resume(r, place)

    def spread(src, dst, sems, s):
        return pltpu.make_async_remote_copy(
            src_ref=src.at[s],
            dst_ref=dst.at[blk],
            send_sem=sems[0].at[s - 1],
            recv_sem=sems[1].at[s - 1],
            device_id=(dp, blk ^ s),
            device_id_type=MESH,
        )

    def in_copy(s):
        if s == 0:
            return pltpu.make_async_copy(r["dx"].at[0], r["input_grad"].at[blk], r["lsem"].at[1])
        return spread(r["dx"], r["input_grad"], (r["isend"], r["irecv"]), s)

    def loads():
        pairs = [(r["xs"], r["xbuf"]), (r["dmid"], r["dmbuf"])]
        pairs += [(r[w], wcat.at[:, i * width : (i + 1) * width]) for i, w in enumerate(("wq", "wk", "wv"))]
        return [pltpu.make_async_copy(a, b, r["lsem"].at[2 + i]) for i, (a, b) in enumerate(pairs)]

    z, y = dp >> 1, dp & 1
    z_ids = [(((z + d) & 3) * 2 + y, blk) for d in (1, 2, 3)]
    vec_ids = [z_ids, [(dp ^ 1, blk)], [(dp, blk ^ 1), (dp, blk ^ 2), (dp, blk ^ 3)]]

    def vec_copies(name, stage):
        at = (0, 3, 4)[stage]
        return [
            pltpu.make_async_remote_copy(
                src_ref=r[name],
                dst_ref=r[name + "_r"].at[at + d],
                send_sem=r[name + "_send"].at[at + d],
                recv_sem=r[name + "_recv"].at[at + d],
                device_id=where,
                device_id_type=MESH,
            )
            for d, where in enumerate(vec_ids[stage])
        ]

    def vec_step(name, stage):
        if stage > 0:
            copies = vec_copies(name, stage - 1)
            for copy in copies:
                copy.wait()
            at = (0, 3, 4)[stage - 1]
            r[name][...] += sum(r[name + "_r"][at + d] for d in range(len(copies)))
        if stage < 3:
            for copy in vec_copies(name, stage):
                copy.start()

    def input_piece(s, sums):
        sl = slice(s * tok, (s + 1) * tok)
        e = r["ebuf"][s & 1].T
        n, rstd = center(r["xbuf"][s].astype(F32))
        f = e * as_row(r["gain"])
        dx = r["dmbuf"][sl] + rstd * (
            f - jnp.mean(f, axis=-1, keepdims=True) - n * jnp.mean(f * n, axis=-1, keepdims=True)
        )
        r["dx"][s] = dx.astype(BF16)
        in_copy(s).start()
        new = [jnp.sum(t, axis=0, keepdims=True) for t in (e * n, e)]
        return new if sums is None else [a + b for a, b in zip(sums, new)]

    @pl.when(h == 0)
    def _():
        greet(
            [(dp, blk ^ 1), (dp, blk ^ 2), (dp, blk ^ 3), (dp ^ 1, blk)]
            + [(((z + d) & 3) * 2 + y, blk) for d in (1, 2, 3)]
        )
        for load in loads():
            load.start()
        vec[...] = jnp.zeros_like(vec)
        r["vb"][...] = r["vec_in"][...]

    def act(item):
        kind, what = item
        if kind in ("va", "vb"):
            vec_step(kind, what)
        else:
            getattr(jobs[kind], "stage%d" % what)()

    for at in range(H):
        if plan.get(at):

            @pl.when(h == at)
            def _(at=at):
                for item in plan[at]:
                    act(item)

    @pl.when(h < H)
    def _():
        base = pl.multiple_of(h * head, head)
        dq, dk, dv = attend_back_head(
            scale,
            n_blk,
            r["p"],
            r["q"][...],
            r["k"][...],
            r["v"][...],
            r["do"][...],
            r["ct"][...],
            r["tops"],
            r["ds"],
            r["doi"],
        )
        dcat[pl.ds(base, head)] = dq
        dcat[pl.ds(base + width, head)] = dk
        dcat[pl.ds(base + 2 * width, head)] = dv

    n_group = gq.shape[0]
    cols = width // n_group
    for gi in range(n_group):

        @pl.when(h == (gi + 1) * (H // n_group) - 1)
        def _(gi=gi):
            nt = r["nt"][...]
            ones = jnp.ones((8, seq), BF16)
            for t in range(3):
                part = dcat[t * width + gi * cols : t * width + (gi + 1) * cols]
                v = regroup(dot(nt, part, NT), width // 32)
                for c, x, y in CXY:
                    gq[gi, c, x, y, :, t * cols : (t + 1) * cols] = v[c][x][y].astype(BF16)
                if t != 1:
                    row = 2 if t == 0 else 3
                    vec[row : row + 1, gi * cols : (gi + 1) * cols] = dot(ones, part, NT)[:1]
            jobs["q%d" % gi].stage0()

    @pl.when(h == H)
    def _():
        sums = None
        for load in loads():
            load.wait()
        for item in plan["tail"]:
            kind, what = item
            if kind == "mul":
                r["ebuf"][what & 1] = dot(wcat[...], dcat[:, what * tok : (what + 1) * tok])
            elif kind == "piece":
                sums = input_piece(what, sums)
                if what == 0:
                    vec[0:1] = sums[0]
                    vec[1:2] = sums[1]
            else:
                act(item)
        r["va_out"][...] = vec[...]
        r["vb_out"][...] = r["vb"][...]
        for s in range(n_blk):
            in_copy(s).wait()


PLAN = {
    0: [("wout", 0), ("a2", 0), ("b2", 0), ("wo", 0)],
    2: [("a2", 1), ("b2", 1)],
    3: [("wo", 1)],
    5: [("q0", 1)],
    7: [("a2", 2), ("b2", 2)],
    9: [("q1", 1)],
    10: [("q0", 2), ("wo", 2)],
    11: [("a2", 3), ("b2", 3), ("wout", 1)],
    "tail": [
        ("mul", 3),
        ("mul", 2),
        ("piece", 3),
        ("q2", 1),
        ("mul", 1),
        ("piece", 2),
        ("mul", 0),
        ("piece", 1),
        ("piece", 0),
        ("vb", 0),
        ("va", 0),
        ("q2", 2),
        ("q1", 2),
        ("wo", 3),
        ("q0", 3),
        ("vb", 1),
        ("va", 1),
        ("wout", 2),
        ("a2", 4),
        ("vb", 2),
        ("va", 2),
        ("q1", 3),
        ("b2", 4),
        ("q2", 3),
        ("vb", 3),
        ("va", 3),
        ("wo", 4),
        ("q0", 4),
        ("q1", 4),
        ("q2", 4),
    ],
}

SCATTER_KEYS = ("f2", "rx", "r0", "t1", "r1", "t2", "r2", "t3", "r3", "f", "send", "recv", "keep", "load")


def body(
    inputs,
    lengths,
    out_grad,
    ln1_gain,
    ln1_bias,
    w_query,
    b_query,
    w_key,
    w_value,
    b_value,
    w_output,
    b_output,
    ln2_gain,
    ln2_bias,
    w_in,
    b_in,
    w_out,
    b_out,
):
    n_seq, tok, width = inputs.shape
    n_blk = lax.axis_size("blk")
    n_dp = lax.axis_size("dp")
    n_dev = n_blk * n_dp
    assert n_seq == n_blk
    seq = tok * n_blk
    hidden = w_in.shape[1]
    head = width // H
    scale = head ** (-0.5)
    blk = lax.axis_index("blk")
    me = lax.axis_index("dp") * n_blk + blk

    def swap(v, s):
        return lax.ppermute(v, "blk", [(i, i ^ s) for i in range(n_blk)])

    def collect(pieces):
        back = [pieces[0]] + [swap(pieces[s], s) for s in range(1, n_blk)]
        out = jnp.zeros((n_seq, tok, width), BF16)
        for s in range(n_blk):
            out = lax.dynamic_update_index_in_dim(out, back[s], blk ^ s, 0)
        return out

    row = lambda v: v.astype(F32).reshape(1, -1)


    sds = jax.ShapeDtypeStruct
    piece = full((tok, width))
    wide = full((width, seq))
    n_col = 3
    cols = width // n_col
    strip = pl.BlockSpec((cols, seq), lambda j: (j, 0))
    anywhere = pl.BlockSpec(memory_space=pl.ANY)
    vmem = pl.BlockSpec(memory_space=pltpu.VMEM)
    xs, nt, qt, kt, vt = pl.pallas_call(
        functools.partial(qkv_spread_kernel, scale * LOG2E, n_blk),
        in_specs=[anywhere, vmem, vmem, anywhere, vmem, anywhere, anywhere, vmem],
        out_specs=[anywhere] * 5,
        out_shape=[sds((n_blk, tok, width), BF16)] + [sds((width, seq), BF16)] * 4,
        scratch_shapes=[
            pltpu.VMEM((n_blk, tok, width), BF16),
            pltpu.VMEM((3, width, width), BF16),
            pltpu.VMEM((3, width, width), BF16),
            pltpu.VMEM((width, seq), BF16),
            pltpu.VMEM((3, width, seq), BF16),
            pltpu.SemaphoreType.DMA((n_blk - 1,)),
            pltpu.SemaphoreType.DMA((n_blk - 1,)),
            pltpu.SemaphoreType.DMA((3,)),
            pltpu.SemaphoreType.DMA((n_blk, 5)),
            pltpu.SemaphoreType.DMA,
        ],
        compiler_params=params(collective_id=0, has_side_effects=True),
        cost_estimate=cost(3 * seq * width * width, 14 * seq * width),
        name="qkv",
    )(inputs, ln1_gain, ln1_bias, w_query, b_query, w_key, w_value, b_value)

    per_head = pl.BlockSpec((head, seq), lambda h: (h, 0))
    per_square = pl.BlockSpec((1, seq, seq), lambda h: (h, 0, 0))
    per_block = pl.BlockSpec((1, n_blk, seq), lambda h: (h, 0, 0))
    ct, probs, inv_total, tops, gs = pl.pallas_call(
        functools.partial(attend_spread_kernel, n_blk),
        grid=(H,),
        in_specs=[pl.BlockSpec(memory_space=pltpu.SMEM), per_head, per_head, per_head, anywhere],
        out_specs=[per_head, per_square, pl.BlockSpec((1, 1, seq), lambda h: (h, 0, 0)), per_block, anywhere],
        out_shape=[
            sds((width, seq), BF16),
            sds((H, seq, seq), BF16),
            sds((H, 1, seq), F32),
            sds((H, n_blk, seq), F32),
            sds((n_blk, tok, width), BF16),
        ],
        scratch_shapes=[
            pltpu.SemaphoreType.DMA((n_blk - 1,)),
            pltpu.SemaphoreType.DMA((n_blk - 1,)),
            pltpu.SemaphoreType.DMA,
        ],
        compiler_params=params(collective_id=1, has_side_effects=True),
        cost_estimate=cost(8 * seq * seq * width, 2 * H * seq * seq, H * seq * seq),
        name="attend",
    )(lengths, qt, kt, vt, out_grad)

    if n_dp == 8 and n_blk == 4 and width % 768 == 0 and hidden == 4 * width:
        share, share_f = width // n_dev, hidden // n_dev
        tile = hidden // 4
        once = lambda shape: pl.BlockSpec(shape, lambda i: (0,) * len(shape), pipeline_mode=pl.Buffered(1))
        vec_rows = 8
        ins = {
            "x": (xs.reshape(seq, width), once((seq, width))),
            "g": (gs.reshape(seq, width), once((seq, width))),
            "ct": (ct, once((width, seq))),
            "il": (inv_total, once((H, 1, seq))),
            "wo": (w_output, once((width, width))),
            "bo": (b_output, once((width,))),
            "gain": (ln2_gain, once((width,))),
            "bias": (ln2_bias, once((width,))),
            "bout": (b_out, once((width,))),
            "bin": (b_in, once((hidden,))),
            "win": (w_in, pl.BlockSpec((width, tile), lambda i: (0, i % 4))),
            "wout": (w_out, pl.BlockSpec((tile, width), lambda i: (i % 4, 0))),
        }
        outs = {
            "output": (sds((n_seq, tok, width), BF16), anywhere),
            "dmid": (sds((seq, width), F32), anywhere),
            "dot": (sds((width, seq), BF16), once((width, seq))),
            "gwin": (
                sds((2, 2, 2, 4 * share, hidden), BF16),
                pl.BlockSpec((2, 2, 2, 4 * share, tile), lambda i: (0, 0, 0, 0, jnp.maximum(i - 4, 0))),
            ),
            "gwo": (sds((2, 2, 2, 4 * share, width), BF16), once((2, 2, 2, 4 * share, width))),
            "part": (sds((2, 4, share_f, width), BF16), anywhere),
            "vec": (sds((vec_rows, width), F32), once((vec_rows, width))),
        }
        scratch = {
            "mid": pltpu.VMEM((seq, width), F32),
            "acc": pltpu.VMEM((seq, width), F32),
            "n2": pltpu.VMEM((seq, width), BF16),
            "n2t": pltpu.VMEM((width, seq), BF16),
            "act": pltpu.VMEM((seq, tile), BF16),
            "gp": pltpu.VMEM((4, seq, tile), BF16),
            "bins": pltpu.VMEM((4, 1, tile), F32),
            "bing": pltpu.VMEM((4, 1, tile), F32),
            "obuf": pltpu.VMEM((n_blk, tok, width), BF16),
            "gw": pltpu.VMEM((2, 2, 2, 4, share_f, width), BF16),
            "r0": pltpu.VMEM((2, 2, 4, share_f, width), BF16),
            "t1": pltpu.VMEM((2, 4, share_f, width), BF16),
            "r1": pltpu.VMEM((2, 4, share_f, width), BF16),
            "csend": pltpu.SemaphoreType.DMA((4,)),
            "crecv": pltpu.SemaphoreType.DMA((4,)),
            "ysend": pltpu.SemaphoreType.DMA((4,)),
            "yrecv": pltpu.SemaphoreType.DMA((4,)),
            "osend": pltpu.SemaphoreType.DMA((n_blk - 1,)),
            "orecv": pltpu.SemaphoreType.DMA((n_blk - 1,)),
            "lsem": pltpu.SemaphoreType.DMA((3,)),
        }
        names = tuple(ins) + tuple(outs) + tuple(scratch)
        ffn = pl.pallas_call(
            functools.partial(ffn_host_kernel, names, n_blk),
            grid=(8,),
            in_specs=[v[1] for v in ins.values()],
            out_specs=[v[1] for v in outs.values()],
            out_shape=[v[0] for v in outs.values()],
            scratch_shapes=list(scratch.values()),
            compiler_params=pltpu.CompilerParams(
                vmem_limit_bytes=62 * 2**20, collective_id=3, has_side_effects=True
            ),
            name="ffn",
        )(*[v[0] for v in ins.values()])
        ffn = dict(zip(outs, ffn))
        tasks = (
            ("a2", "gwin", None, slice(0, hidden // 2), share, "x", "s_win", slice(0, hidden // 2)),
            ("b2", "gwin", None, slice(hidden // 2, hidden), share, "y", "s_win", slice(hidden // 2, hidden)),
            ("wo", "gwo", None, None, share, "x", "s_wo", None),
        ) + tuple(
            (
                "q%d" % i,
                "gq",
                i,
                None,
                share,
                ("y", "x", "late")[i],
                ("s_wq", "s_wk", "s_wv"),
                slice(i * cols, (i + 1) * cols),
            )
            for i in range(n_col)
        )
        sizes = {"a2": hidden // 2, "b2": hidden // 2, "wo": width}
        plan = PLAN
        last = lambda shape: pl.BlockSpec(shape, lambda h: (jnp.minimum(h, H - 1),) + (0,) * (len(shape) - 1))
        strip_h = last((head, seq))
        ins = {
            "p": (probs, last((1, seq, seq))),
            "q": (qt, strip_h),
            "k": (kt, strip_h),
            "v": (vt, strip_h),
            "do": (ffn["dot"], strip_h),
            "ct": (ct, strip_h),
            "tops": (tops, last((1, n_blk, seq))),
            "nt": (nt, wide),
            "gain": (ln1_gain, full((width,))),
            "vec_in": (ffn["vec"], full((vec_rows, width))),
            "xs": (xs, anywhere),
            "dmid": (ffn["dmid"], anywhere),
            "wq": (w_query, anywhere),
            "wk": (w_key, anywhere),
            "wv": (w_value, anywhere),
            "part": (ffn["part"], anywhere),
            "gwin": (ffn["gwin"], anywhere),
            "gwo": (ffn["gwo"], anywhere),
        }
        outs = {
            "input_grad": (sds((n_seq, tok, width), BF16), anywhere),
            "s_wq": (sds((share, width), F32), full((share, width))),
            "s_wk": (sds((share, width), F32), full((share, width))),
            "s_wv": (sds((share, width), F32), full((share, width))),
            "s_wo": (sds((share, width), F32), full((share, width))),
            "s_win": (sds((share, hidden), F32), full((share, hidden))),
            "s_wout": (sds((share_f, width), F32), full((share_f, width))),
            "va_out": (sds((8, width), F32), full((8, width))),
            "vb_out": (sds((8, width), F32), full((8, width))),
        }
        scratch = {
            "ds": pltpu.VMEM((seq, seq), BF16),
            "doi": pltpu.VMEM((n_blk, head, seq), BF16),
            "dcat": pltpu.VMEM((3 * width, seq), BF16),
            "wcat": pltpu.VMEM((width, 3 * width), BF16),
            "gq": pltpu.VMEM((n_col, 2, 2, 2, 4 * share, 3 * cols), BF16),
            "va": pltpu.VMEM((8, width), F32),
            "vb": pltpu.VMEM((8, width), F32),
            "va_r": pltpu.VMEM((7, 8, width), F32),
            "vb_r": pltpu.VMEM((7, 8, width), F32),
            "ebuf": pltpu.VMEM((2, width, tok), F32),
            "xbuf": pltpu.VMEM((n_blk, tok, width), BF16),
            "dmbuf": pltpu.VMEM((seq, width), F32),
            "dx": pltpu.VMEM((n_blk, tok, width), BF16),
            "lsem": pltpu.SemaphoreType.DMA((7,)),
            "va_send": pltpu.SemaphoreType.DMA((7,)),
            "va_recv": pltpu.SemaphoreType.DMA((7,)),
            "vb_send": pltpu.SemaphoreType.DMA((7,)),
            "vb_recv": pltpu.SemaphoreType.DMA((7,)),
            "w_keep": pltpu.VMEM((2, share_f, width), BF16),
            "w_rz": pltpu.VMEM((3, 2, share_f, width), BF16),
            "w_f": pltpu.VMEM((2, share_f, width), F32),
            "w_t": pltpu.VMEM((share_f, width), BF16),
            "w_rx": pltpu.VMEM((share_f, width), BF16),
            "w_send": pltpu.SemaphoreType.DMA((4,)),
            "w_recv": pltpu.SemaphoreType.DMA((4,)),
            "isend": pltpu.SemaphoreType.DMA((n_blk - 1,)),
            "irecv": pltpu.SemaphoreType.DMA((n_blk - 1,)),
        }
        for name, source, _, _, task_share, first, _, _ in tasks:
            for k, v in scatter_scratch(task_share, sizes.get(name, width), source != "gq", first == "late").items():
                scratch[name + "_" + k] = v
        names = tuple(ins) + tuple(outs) + tuple(scratch)
        got = pl.pallas_call(
            functools.partial(back_kernel, scale, names, tasks, plan),
            grid=(H + 1,),
            in_specs=[v[1] for v in ins.values()],
            out_specs=[v[1] for v in outs.values()],
            out_shape=[v[0] for v in outs.values()],
            scratch_shapes=list(scratch.values()),
            compiler_params=pltpu.CompilerParams(
                vmem_limit_bytes=60 * 2**20, collective_id=2, has_side_effects=True
            ),
            name="back",
        )(*[v[0] for v in ins.values()])
        got = dict(zip(outs, got))
        big = [ffn["output"], got["input_grad"]] + [
            got[k] for k in ("s_wq", "s_wk", "s_wv", "s_wo", "s_win", "s_wout")
        ]
        part = pl.BlockSpec((1, tok, width), lambda i: (i, 0, 0))
        flat = [sds(v.shape, v.dtype) for v in big]
        fin = pl.pallas_call(
            functools.partial(finish_kernel, len(big)),
            grid=(n_blk,),
            in_specs=[part] * 2 + [full(v.shape) for v in big[2:]] + [full((8, width))] * 2,
            out_specs=[part] * 2 + [full(v.shape) for v in big[2:]] + [full((share,))] * 8 + [full((share_f,))],
            out_shape=flat + [sds((share,), F32)] * 8 + [sds((share_f,), F32)],
            name="finish",
        )(*big, got["va_out"], got["vb_out"])
        output, input_grad, s_wq, s_wk, s_wv, s_wo, s_win, s_wout = fin[: len(big)]
        g1, b1, bq, bv, bo_sum, g2, b2, bout_sum, bin_sum = fin[len(big) :]
        return (
            output,
            input_grad,
            g1,
            b1,
            s_wq,
            bq,
            s_wk,
            s_wv,
            bv,
            s_wo,
            bo_sum,
            g2,
            b2,
            s_win,
            bin_sum,
            s_wout,
            bout_sum,
        )

    n_tile = 4
    tile = hidden // n_tile
    result = pl.pallas_call(
        functools.partial(ffn_kernel, n_blk),
        grid=(n_tile,),
        in_specs=[full((seq, width))] * 2
        + [
            wide,
            full((H, 1, seq)),
            full((width, width)),
            full((1, width)),
            full((1, width)),
            full((1, width)),
            pl.BlockSpec((width, tile), lambda j: (0, j)),
            pl.BlockSpec((1, tile), lambda j: (0, j)),
            pl.BlockSpec((tile, width), lambda j: (j, 0)),
            full((1, width)),
        ],
        out_specs=[piece] * n_blk
        + [
            pl.BlockSpec((tile, width), lambda j: (j, 0)),
            pl.BlockSpec((width, tile), lambda j: (0, j)),
            pl.BlockSpec((1, tile), lambda j: (0, j)),
            full((seq, width)),
            wide,
            full((width, width)),
            full((8, width)),
        ],
        out_shape=[sds((tok, width), BF16)] * n_blk
        + [
            sds((hidden, width), BF16),
            sds((width, hidden), BF16),
            sds((1, hidden), F32),
            sds((seq, width), F32),
            sds((width, seq), BF16),
            sds((width, width), BF16),
            sds((8, width), F32),
        ],
        scratch_shapes=[
            pltpu.VMEM((seq, width), F32),
            pltpu.VMEM((seq, width), BF16),
            pltpu.VMEM((width, seq), BF16),
            pltpu.VMEM((seq, width), F32),
            pltpu.VMEM((seq, width), F32),
            pltpu.VMEM((seq, tile), BF16),
            pltpu.VMEM((seq, tile), BF16),
        ],
        compiler_params=params(),
        cost_estimate=cost(8 * seq * width * hidden, 8 * width * hidden),
        name="ffn",
    )(
        xs.reshape(seq, width),
        gs.reshape(seq, width),
        ct,
        inv_total,
        w_output,
        row(b_output),
        row(ln2_gain),
        row(ln2_bias),
        w_in,
        row(b_in),
        w_out,
        row(b_out),
    )
    out_pieces = result[:n_blk]
    g_wout, g_win, g_bin, dmid, dct, g_wo, vec2 = result[n_blk:]

    bits = (n_dev - 1).bit_length()
    assert n_dev == 1 << bits

    def scatter(grad, order, wire):
        share = grad.shape[0] // n_dev
        order = list(order) + [b for b in range(bits) if b not in order]
        axes = list(range(bits - 1, -1, -1))
        terms = [grad.reshape((2,) * bits + (share,) + grad.shape[1:])]
        for b in order:
            at = axes.index(b)
            axes.pop(at)
            mine = (me >> b) & 1
            send = None
            keep = []
            for t in terms:
                other = lax.dynamic_index_in_dim(t, 1 - mine, at, keepdims=False)
                send = other.astype(F32) if send is None else send + other.astype(F32)
                keep.append(lax.dynamic_index_in_dim(t, mine, at, keepdims=False))
            got = lax.ppermute(send.astype(wire), ("dp", "blk"), [(i, i ^ (1 << b)) for i in range(n_dev)])
            terms = keep + [got]
        total = terms[0].astype(F32)
        for t in terms[1:]:
            total = total + t.astype(F32)
        return total

    s_wout = scatter(g_wout, (0, 1, 2, 3, 4), BF16)
    s_win = scatter(g_win, (0, 2, 1, 3, 4), BF16)
    s_wo = scatter(g_wo, (0, 3, 4, 1, 2), BF16)
    output = collect(out_pieces)

    dqt, dkt, dvt = pl.pallas_call(
        functools.partial(attend_back_kernel, scale, n_blk),
        grid=(H,),
        in_specs=[per_square] + [per_head] * 5 + [per_block],
        out_specs=[per_head] * 3,
        out_shape=[sds((width, seq), BF16)] * 3,
        scratch_shapes=[pltpu.VMEM((seq, seq), BF16), pltpu.VMEM((n_blk, head, seq), BF16)],
        compiler_params=params(),
        cost_estimate=cost(10 * seq * seq * width, 2 * H * seq * seq),
        name="attend_back",
    )(probs, qt, kt, vt, dct, ct, tops)

    result = pl.pallas_call(
        functools.partial(input_kernel, n_blk),
        in_specs=[full((seq, width))] * 2
        + [full((1, width)), wide, wide, wide]
        + [full((width, width))] * 3,
        out_specs=[piece] * n_blk + [full((8, width))],
        out_shape=[sds((tok, width), BF16)] * n_blk + [sds((8, width), F32)],
        compiler_params=params(),
        cost_estimate=cost(3 * seq * width * width, 14 * seq * width),
        name="input_grad",
    )(xs.reshape(seq, width), dmid, row(ln1_gain), dqt, dkt, dvt, w_query, w_key, w_value)
    input_grad = collect(result[:n_blk])
    vec1 = result[n_blk]

    col = pl.BlockSpec((width, cols), lambda j: (0, j))
    g_wq, g_wk, g_wv, vecq = pl.pallas_call(
        qkv_grad_kernel,
        grid=(n_col,),
        in_specs=[wide, strip, strip, strip],
        out_specs=[col, col, col, pl.BlockSpec((8, cols), lambda j: (0, j))],
        out_shape=[sds((width, width), BF16)] * 3 + [sds((8, width), F32)],
        compiler_params=params(),
        cost_estimate=cost(3 * seq * width * width, 14 * seq * width),
        name="qkv_grad",
    )(nt, dqt, dkt, dvt)
    s_wq = scatter(g_wq, (0, 1, 2, 3, 4), BF16)
    s_wk = scatter(g_wk, (0, 2, 3, 4, 1), BF16)
    s_wv = scatter(g_wv, (0, 3, 4, 1, 2), BF16)

    vectors = [vec1[0], vec1[1], vecq[0], vecq[1], vec2[3], vec2[1], vec2[2], g_bin[0], vec2[0]]
    packed = jnp.concatenate([v.reshape(n_dev, -1) for v in vectors], axis=1)
    packed = scatter(packed, (0, 1, 2, 3, 4), F32).reshape(-1)
    parts = []
    at = 0
    for v in vectors:
        size = v.shape[0] // n_dev
        parts.append(packed[at : at + size])
        at += size
    p_ln1g, p_ln1b, p_bq, p_bv, p_bo, p_ln2g, p_ln2b, p_bin, p_bout = parts
    return (
        output,
        input_grad,
        p_ln1g,
        p_ln1b,
        s_wq,
        p_bq,
        s_wk,
        s_wv,
        p_bv,
        s_wo,
        p_bo,
        p_ln2g,
        p_ln2b,
        s_win,
        p_bin,
        s_wout,
        p_bout,
    )


def solution(mesh):
    whole = P(("dp", "blk"))
    rows = P(("dp", "blk"), None)
    tokens = P("dp", "blk", None)
    in_specs = (tokens, P("dp"), tokens) + (P(),) * 15
    out_specs = (
        tokens,
        tokens,
        whole,
        whole,
        rows,
        whole,
        rows,
        rows,
        whole,
        rows,
        whole,
        whole,
        whole,
        rows,
        whole,
        rows,
        whole,
    )
    return jax.shard_map(body, mesh=mesh, in_specs=in_specs, out_specs=out_specs, check_vma=False)
```

```python
import functools

import jax
import jax.numpy as jnp
from jax import lax
from jax.experimental import pallas as pl
from jax.experimental.pallas import tpu as pltpu
from jax.sharding import PartitionSpec as P

H = 12
EPS = 1e-05
LOG2E = 1.4426950408889634
LN2 = 0.6931471805599453
INV_SQRT_2PI = 0.3989422804014327
SQRT_HALF = 0.7071067811865476
F32 = jnp.float32
BF16 = jnp.bfloat16
VMEM_LIMIT = 56 * 2**20

NN = (((1,), (0,)), ((), ()))
NT = (((1,), (1,)), ((), ()))
TN = (((0,), (0,)), ((), ()))

def dot(left, right, dims=NN):
    return lax.dot_general(left, right, dims, preferred_element_type=F32)


def params(**kw):
    return pltpu.CompilerParams(vmem_limit_bytes=VMEM_LIMIT, **kw)


def cost(macs, nbytes, exps=0):
    return pl.CostEstimate(flops=2 * macs, bytes_accessed=nbytes, transcendentals=exps)


def full(shape):
    return pl.BlockSpec(shape, lambda *_: (0,) * len(shape))


def as_row(ref):
    return ref[...].astype(F32)[None, :]


def center(v):
    mean = jnp.mean(v, axis=-1, keepdims=True)
    cent = v - mean
    var = jnp.mean(cent * cent, axis=-1, keepdims=True)
    rstd = lax.rsqrt(var + EPS)
    return cent * rstd, rstd


def gate(u):
    phi = 0.5 + 0.5 * lax.erf(u * SQRT_HALF)
    e = jnp.exp2(u * u * (-0.5 * LOG2E))
    return phi, u * e * INV_SQRT_2PI


def attend_kernel(n_blk, len_ref, q_ref, k_ref, v_ref, c_ref, p_ref, il_ref, f_ref):
    seq = q_ref.shape[1]
    tok = seq // n_blk
    blk = lax.axis_index("blk")
    length = len_ref[blk]
    live = [(blk ^ i) * tok < length for i in range(n_blk)]
    keys, q, v = k_ref[...].T, q_ref[...], v_ref[...]
    m = jnp.full((1, seq), -1e30, F32)
    total = summed = None
    tops = []
    ahead = dot(keys[:tok], q)
    for i in range(n_blk):
        s = ahead
        if i + 1 < n_blk:
            ahead = dot(keys[(i + 1) * tok : (i + 2) * tok], q)
        new = jnp.maximum(m, jnp.where(live[i], jnp.max(s, axis=0, keepdims=True), -1e30))
        p = jnp.exp2(s - jnp.where(live[i], new, 1e30))
        part = jnp.sum(p, axis=0, keepdims=True)
        p = p.astype(BF16)
        p_ref[0, i * tok : (i + 1) * tok] = p
        o = dot(v[:, i * tok : (i + 1) * tok], p)
        if i == 0:
            summed, total = o, part
        else:
            shrink = jnp.exp2(m - new)
            summed, total = summed * shrink + o, total * shrink + part
        m = new
        tops.append(m)
    inv = 1.0 / total
    c_ref[...] = (summed * inv).astype(BF16)
    il_ref[0] = inv
    for i in range(n_blk):
        f_ref[0, i : i + 1] = jnp.exp2(tops[i] - m)


def attend_back_head(scale, n_blk, p_ref, q, k, v, do, ct, f_ref, ds, doi):
    seq = q.shape[1]
    tok = seq // n_blk
    vh = v.T
    do = do.astype(F32)
    delta = jnp.sum(do * ct.astype(F32), axis=0, keepdims=True)
    for i in range(n_blk):
        sl = slice(i * tok, (i + 1) * tok)
        f = f_ref[0, i : i + 1]
        d = (do * f).astype(BF16)
        doi[i] = d
        ds[sl] = (p_ref[0, sl].astype(F32) * (dot(vh[sl], d) - delta * f)).astype(BF16)
    dq = (dot(k, ds[...]) * scale).astype(BF16)
    dv = [dot(p_ref[0, i * tok : (i + 1) * tok], doi[i], NT).T.astype(BF16) for i in range(n_blk)]
    dk = (dot(ds[...], q, NT) * LN2).T.astype(BF16)
    return dq, dk, jnp.concatenate(dv, axis=1)


MESH = pl.DeviceIdType.MESH


def greet(partners):
    barrier = pltpu.get_barrier_semaphore()
    for where in partners:
        pl.semaphore_signal(barrier, inc=1, device_id=where, device_id_type=MESH)
    pl.semaphore_wait(barrier, len(partners))


def qkv_spread_kernel(
    scale,
    n_blk,
    x_any,
    gain,
    bias,
    wq_any,
    bq,
    wk_any,
    wv_any,
    bv,
    xs_any,
    nt_any,
    q_any,
    k_any,
    v_any,
    xbuf,
    wbuf,
    wt,
    nt,
    qkv,
    send,
    recv,
    wsem,
    osem,
    xsem,
):
    tok, width = xbuf.shape[1:]
    dp = lax.axis_index("dp")
    blk = lax.axis_index("blk")
    own = pltpu.make_async_copy(x_any.at[blk], xbuf.at[0], xsem)
    own.start()
    loads = [
        pltpu.make_async_copy(w, wbuf.at[i], wsem.at[i]) for i, w in enumerate((wq_any, wk_any, wv_any))
    ]
    for load in loads:
        load.start()
    greet([(dp, blk ^ s) for s in range(1, n_blk)])
    order = list(range(n_blk - 1, 0, -1))
    copies = {}
    for s in order:
        copies[s] = pltpu.make_async_remote_copy(
            src_ref=x_any.at[blk ^ s],
            dst_ref=xbuf.at[s],
            send_sem=send.at[s - 1],
            recv_sem=recv.at[s - 1],
            device_id=(dp, blk ^ s),
            device_id_type=MESH,
        )
        if s != 2:
            copies[s].start()
    for i, load in enumerate(loads):
        load.wait()
        wt[i] = wbuf[i].T
    cols = jnp.concatenate([as_row(bq), as_row(bv), jnp.zeros((6, width), F32)], axis=0).T
    writes = []
    for s in (0, 1, 3, 2):
        if s == 0:
            own.wait()
        else:
            if s == 3:
                copies[3].wait_send()
                copies[2].start()
            copies[s].wait_recv()
        sl = slice(s * tok, (s + 1) * tok)
        n, _ = center(xbuf[s].astype(F32))
        n = (n * as_row(gain) + as_row(bias)).astype(BF16).T
        nt[:, sl] = n
        qkv[0, :, sl] = ((dot(wt[0], n) + cols[:, :1]) * scale).astype(BF16)
        qkv[1, :, sl] = dot(wt[1], n).astype(BF16)
        qkv[2, :, sl] = (dot(wt[2], n) + cols[:, 1:2]).astype(BF16)
        for i, (src, dst) in enumerate(
            (
                (xbuf.at[s], xs_any.at[s]),
                (nt.at[:, sl], nt_any.at[:, sl]),
                (qkv.at[0, :, sl], q_any.at[:, sl]),
                (qkv.at[1, :, sl], k_any.at[:, sl]),
                (qkv.at[2, :, sl], v_any.at[:, sl]),
            )
        ):
            write = pltpu.make_async_copy(src, dst, osem.at[s, i])
            write.start()
            writes.append(write)
    for s in (1, 2):
        copies[s].wait_send()
    for write in writes:
        write.wait()


def attend_spread_kernel(n_blk, len_ref, q_ref, k_ref, v_ref, g_any, c_ref, p_ref, il_ref, f_ref, gs_any, send, recv, osem):
    h = pl.program_id(0)
    dp = lax.axis_index("dp")
    blk = lax.axis_index("blk")

    def copy(s):
        return pltpu.make_async_remote_copy(
            src_ref=g_any.at[blk ^ s],
            dst_ref=gs_any.at[s],
            send_sem=send.at[s - 1],
            recv_sem=recv.at[s - 1],
            device_id=(dp, blk ^ s),
            device_id_type=MESH,
        )

    own = pltpu.make_async_copy(g_any.at[blk], gs_any.at[0], osem)

    @pl.when(h == 0)
    def _():
        greet([(dp, blk ^ s) for s in range(1, n_blk)])
        own.start()
        for s in range(1, n_blk):
            copy(s).start()

    attend_kernel(n_blk, len_ref, q_ref, k_ref, v_ref, c_ref, p_ref, il_ref, f_ref)

    @pl.when(h == pl.num_programs(0) - 1)
    def _():
        own.wait()
        for s in range(1, n_blk):
            copy(s).wait()


def regroup(v, share):
    def slab(c, x, y):
        at = [(z * 8 + y * 4 + x * 2 + c) * share for z in range(4)]
        return jnp.concatenate([v[a : a + share] for a in at], axis=0)

    return [[[slab(c, x, y) for y in range(2)] for x in range(2)] for c in range(2)]


CXY = [(c, x, y) for c in range(2) for x in range(2) for y in range(2)]


class Scatter:
    def __init__(self, source, cols, share, first, out, bufs, place):
        self.source, self.cols, self.share, self.out = source, cols, share, out
        self.b = bufs
        dp, blk = place
        self.c, self.x, self.y, self.z = blk & 1, blk >> 1, dp & 1, dp >> 1
        self.first = first
        ids = {"x": (dp, blk ^ 2), "y": (dp ^ 1, blk)}
        self.mp = self.x if first == "x" else self.y
        self.mq = self.y if first == "x" else self.x
        self.core_id = (dp, blk ^ 1)
        self.p_id = ids[first]
        self.q_id = ids["y" if first == "x" else "x"]
        self.z_ids = [(((self.z + d) & 3) * 2 + self.y, blk) for d in (1, 2, 3)]
        self.chunk = share if share % 16 == 0 else 2 * share

    def remote(self, src, dst, i, where):
        return pltpu.make_async_remote_copy(
            src_ref=src,
            dst_ref=dst,
            send_sem=self.b["send"].at[i],
            recv_sem=self.b["recv"].at[i],
            device_id=where,
            device_id_type=MESH,
        )

    def part(self, c):
        if self.cols is None:
            return self.source.at[c]
        return self.source.at[c, :, :, :, self.cols]

    def core_copy(self):
        return self.remote(self.part(1 - self.c), self.b["r0"], 0, self.core_id)

    def load(self):
        return pltpu.make_async_copy(self.part(self.c), self.b["keep"], self.b["load"])

    def p_copy(self):
        return self.remote(self.b["t1"], self.b["r1"], 1, self.p_id)

    def q_copy(self):
        return self.remote(self.b["t2"], self.b["r2"], 2, self.q_id)

    def z_copies(self):
        return [self.remote(self.b["t3"].at[d], self.b["r3"].at[d], 3 + d, self.z_ids[d]) for d in range(3)]

    def pick(self, ref, a, b, rows):
        return (ref[a, b, rows] if self.first == "x" else ref[b, a, rows]).astype(F32)

    def two(self, a, b, rows):
        own = self.b["keep"] if "keep" in self.b else self.source.at[self.c]
        a, b = (a, b) if self.first == "x" else (b, a)
        return own[a, b, rows] + self.b["r0"][a, b, rows]

    def base(self, a, b, rows):
        if "keep" in self.b:
            own = self.pick(self.b["keep"], a, b, rows)
        else:
            own = (
                self.source[self.c, a, b, rows] if self.first == "x" else self.source[self.c, b, a, rows]
            ).astype(F32)
        return own + self.pick(self.b["r0"], a, b, rows)

    def each(self, fn):
        rows = 4 * self.share

        def step(i, carry):
            fn(i, pl.ds(pl.multiple_of(i * self.chunk, self.chunk), self.chunk))
            return carry

        lax.fori_loop(0, rows // self.chunk, step, 0)

    def stage0(self):
        self.core_copy().start()
        if "keep" in self.b:
            self.load().start()

    def stage1(self):
        if "keep" in self.b:
            self.load().wait()
        self.core_copy().wait()
        for b in range(2):

            def fn(i, rows):
                self.b["t1"][b, rows] = self.two(1 - self.mp, b, rows)

            self.each(fn)
        self.p_copy().start()

    def stage2(self):
        self.p_copy().wait()

        def fn(i, rows):
            v = self.base(self.mp, 1 - self.mq, rows) + self.b["r1"][1 - self.mq, rows].astype(F32)
            self.b["t2"][rows] = v.astype(BF16)

        self.each(fn)
        self.q_copy().start()

    def stage3(self):
        self.q_copy().wait()
        share = self.share
        per = self.chunk // share
        f = self.b["f"]

        def fn(i, rows):
            v = self.base(self.mp, self.mq, rows)
            v = v + self.b["r1"][self.mq, rows].astype(F32) + self.b["r2"][rows].astype(F32)
            for k in range(per):
                f[i * per + k] = v[k * share : (k + 1) * share]

        self.each(fn)
        half = f.shape[2] // 2
        for d in range(3):
            v = f[(self.z + d + 1) & 3]
            if per > 1:
                v = jnp.concatenate([v[:, :half], v[:, half:]], axis=0)
            self.b["t3"][d] = v.astype(BF16)
        for copy in self.z_copies():
            copy.start()

    def stage4(self):
        for copy in self.z_copies():
            copy.wait()
        v = self.b["f"][self.z]
        for d in range(3):
            w = self.b["r3"][d].astype(F32)
            if self.chunk > self.share:
                w = jnp.concatenate([w[: self.share], w[self.share :]], axis=1)
            v = v + w
        self.out(v)


class ScatterLate(Scatter):
    def x_copy(self):
        return self.remote(self.b["f2"].at[1 - self.x], self.b["rx"], 2, self.q_id)

    def stage2(self):
        self.p_copy().wait()
        share = self.share
        per = self.chunk // share
        f = self.b["f"]
        for x in range(2):

            def fn(i, rows, x=x):
                v = self.base(self.mp, x, rows) + self.b["r1"][x, rows].astype(F32)
                for k in range(per):
                    f[x, i * per + k] = v[k * share : (k + 1) * share]

            self.each(fn)
        for d in range(3):
            at = (self.z + d + 1) & 3
            self.b["t3"][d] = jnp.concatenate([f[0, at], f[1, at]], axis=0).astype(BF16)
        for copy in self.z_copies():
            copy.start()

    def stage3(self):
        for copy in self.z_copies():
            copy.wait()
        for x in range(2):
            v = self.b["f"][x, self.z]
            for d in range(3):
                v = v + self.b["r3"][d].astype(F32)[x * self.share : (x + 1) * self.share]
            self.b["f2"][x] = v
        self.x_copy().start()

    def stage4(self):
        self.x_copy().wait()
        self.out(self.b["f2"][self.x] + self.b["rx"][...])


def scatter_scratch(share, cols, in_hbm, late):
    rows = 4 * share
    slab = (share, cols) if share % 16 == 0 else (2 * share, cols // 2)
    bufs = {
        "r0": pltpu.VMEM((2, 2, rows, cols), BF16),
        "t1": pltpu.VMEM((2, rows, cols), BF16),
        "r1": pltpu.VMEM((2, rows, cols), BF16),
        "t2": pltpu.VMEM((rows, cols), BF16),
        "r2": pltpu.VMEM((rows, cols), BF16),
        "t3": pltpu.VMEM((3,) + slab, BF16),
        "r3": pltpu.VMEM((3,) + slab, BF16),
        "f": pltpu.VMEM((4, share, cols), F32),
        "send": pltpu.SemaphoreType.DMA((6,)),
        "recv": pltpu.SemaphoreType.DMA((6,)),
    }
    if late:
        del bufs["t2"], bufs["r2"]
        bufs["t3"] = pltpu.VMEM((3, 2 * share, cols), BF16)
        bufs["r3"] = pltpu.VMEM((3, 2 * share, cols), BF16)
        bufs["f"] = pltpu.VMEM((2, 4, share, cols), F32)
        bufs["f2"] = pltpu.VMEM((2, share, cols), F32)
        bufs["rx"] = pltpu.VMEM((share, cols), F32)
    if in_hbm:
        bufs["keep"] = pltpu.VMEM((2, 2, rows, cols), BF16)
        bufs["load"] = pltpu.SemaphoreType.DMA
    return bufs


def ffn_kernel(n_blk, *refs):
    x_ref, g = refs[:2]
    (ct_ref, il_ref, wo_ref, bo_ref, gain_ref, bias_ref, win_ref, bin_ref, wout_ref, bout_ref) = refs[2:12]
    rest = refs[12:]
    outs = rest[:n_blk]
    (gwout_ref, gwin_ref, gbin_ref, dmid_ref, dot_ref, gwo_ref, vec_ref) = rest[n_blk : n_blk + 7]
    mid, n2, n2t, acc_o, acc_d, act, dpre = rest[n_blk + 7 :]
    tok = outs[0].shape[0]
    j = pl.program_id(0)

    @pl.when(j == 0)
    def _():
        for s in range(n_blk):
            sl = slice(s * tok, (s + 1) * tok)
            m = x_ref[sl].astype(F32) + dot(ct_ref[:, sl], wo_ref[...], TN) + bo_ref[...]
            mid[sl] = m
            acc_o[sl] = m + bout_ref[...]
            acc_d[sl] = jnp.zeros_like(m)
            n, _ = center(m)
            nb = (n * gain_ref[...] + bias_ref[...]).astype(BF16)
            n2[sl] = nb
            n2t[:, sl] = nb.T

    bin_grad = None
    for s in range(n_blk):
        sl = slice(s * tok, (s + 1) * tok)
        pre = dot(n2[sl], win_ref[...]) + bin_ref[...]
        phi, slope = gate(pre)
        a = (pre * phi).astype(BF16)
        dact = dot(g[sl], wout_ref[...], NT)
        dp = (dact * (phi + slope)).astype(BF16)
        act[sl] = a
        dpre[sl] = dp
        col = jnp.sum(dp.astype(F32), axis=0, keepdims=True)
        bin_grad = col if bin_grad is None else bin_grad + col
        acc_o[sl] += dot(a, wout_ref[...])
        acc_d[sl] += dot(dp, win_ref[...], NT)
    gbin_ref[...] = bin_grad
    gwout_ref[...] = dot(act[...], g[...], TN).astype(BF16)
    gwin_ref[...] = dot(n2t[...], dpre[...]).astype(BF16)

    @pl.when(j == pl.num_programs(0) - 1)
    def _():
        head = wo_ref.shape[0] // H
        sums = [None] * 4
        for s in range(n_blk):
            sl = slice(s * tok, (s + 1) * tok)
            outs[s][...] = acc_o[sl].astype(BF16)
            n, rstd = center(mid[sl])
            e = acc_d[sl]
            gf = g[sl].astype(F32)
            f = e * gain_ref[...]
            dm = gf + rstd * (
                f - jnp.mean(f, axis=-1, keepdims=True) - n * jnp.mean(f * n, axis=-1, keepdims=True)
            )
            dmid_ref[sl] = dm
            db = dm.astype(BF16)
            n2[sl] = db
            for i, term in enumerate((gf, e * n, e, db.astype(F32))):
                col = jnp.sum(term, axis=0, keepdims=True)
                sums[i] = col if sums[i] is None else sums[i] + col
            dc = dot(wo_ref[...], db, NT)
            for h in range(H):
                hs = slice(h * head, (h + 1) * head)
                dot_ref[hs, sl] = (dc[hs] * il_ref[h, :, sl]).astype(BF16)
        for i in range(4):
            vec_ref[i : i + 1] = sums[i]
        gwo_ref[...] = dot(ct_ref[...], n2[...]).astype(BF16)


def attend_back_kernel(
    scale, n_blk, p_ref, q_ref, k_ref, v_ref, do_ref, c_ref, f_ref, dq_ref, dk_ref, dv_ref, ds, doi
):
    dq_ref[...], dk_ref[...], dv_ref[...] = attend_back_head(
        scale, n_blk, p_ref, q_ref[...], k_ref[...], v_ref[...], do_ref[...], c_ref[...], f_ref, ds, doi
    )


def input_kernel(n_blk, x_ref, dmid_ref, gain_ref, dq_ref, dk_ref, dv_ref, wq_ref, wk_ref, wv_ref, *rest):
    outs = rest[:n_blk]
    vec_ref = rest[n_blk]
    tok = outs[0].shape[0]
    sums = [None] * 2
    for s in range(n_blk):
        sl = slice(s * tok, (s + 1) * tok)
        et = dot(wq_ref[...], dq_ref[:, sl]) + dot(wk_ref[...], dk_ref[:, sl]) + dot(wv_ref[...], dv_ref[:, sl])
        e = et.T
        n, rstd = center(x_ref[sl].astype(F32))
        f = e * gain_ref[...]
        dx = dmid_ref[sl] + rstd * (
            f - jnp.mean(f, axis=-1, keepdims=True) - n * jnp.mean(f * n, axis=-1, keepdims=True)
        )
        outs[s][...] = dx.astype(BF16)
        for i, term in enumerate((e * n, e)):
            col = jnp.sum(term, axis=0, keepdims=True)
            sums[i] = col if sums[i] is None else sums[i] + col
    for i in range(2):
        vec_ref[i : i + 1] = sums[i]


def qkv_grad_kernel(nt_ref, dq_ref, dk_ref, dv_ref, gq_ref, gk_ref, gv_ref, vec_ref):
    nt = nt_ref[...]
    ones = jnp.ones((8, nt.shape[1]), BF16)
    gq_ref[...] = dot(nt, dq_ref[...], NT).astype(BF16)
    gk_ref[...] = dot(nt, dk_ref[...], NT).astype(BF16)
    gv_ref[...] = dot(nt, dv_ref[...], NT).astype(BF16)
    vec_ref[0:1] = dot(ones, dq_ref[...], NT)[:1]
    vec_ref[1:2] = dot(ones, dv_ref[...], NT)[:1]


def ffn_host_kernel(names, n_blk, *refs):
    r = dict(zip(names, refs))
    i = pl.program_id(0)
    j = i & 3
    dp = lax.axis_index("dp")
    blk = lax.axis_index("blk")
    core, y = blk & 1, dp & 1
    mid, acc, n2, n2t, act, gp, gw, r0, t1, r1 = [
        r[k] for k in ("mid", "acc", "n2", "n2t", "act", "gp", "gw", "r0", "t1", "r1")
    ]
    g, win, wout, ct = r["gbuf"], r["win"], r["wout"], r["ct"]
    g_load = pltpu.make_async_copy(r["g"], g, r["lsem"].at[3])
    seq, width = mid.shape
    tok = seq // n_blk
    tile = act.shape[1]
    share_f = gw.shape[4]
    rows = [slice(s * tok, (s + 1) * tok) for s in range(n_blk)]

    def core_copy(plane):
        return pltpu.make_async_remote_copy(
            src_ref=gw.at[1 - core, :, :, plane],
            dst_ref=r0.at[:, :, plane],
            send_sem=r["csend"].at[plane],
            recv_sem=r["crecv"].at[plane],
            device_id=(dp, blk ^ 1),
            device_id_type=MESH,
        )

    def y_copy(plane):
        return pltpu.make_async_remote_copy(
            src_ref=t1.at[:, plane],
            dst_ref=r1.at[:, plane],
            send_sem=r["ysend"].at[plane],
            recv_sem=r["yrecv"].at[plane],
            device_id=(dp ^ 1, blk),
            device_id_type=MESH,
        )

    def y_start(plane):
        core_copy(plane).wait()
        for x in range(2):
            t1[x, plane] = gw[core, x, 1 - y, plane] + r0[x, 1 - y, plane]
        y_copy(plane).start()

    def out_copy(s):
        src, dst = r["obuf"].at[s], r["output"].at[blk]
        if s == 0:
            return pltpu.make_async_copy(src, dst, r["lsem"].at[0])
        return pltpu.make_async_remote_copy(
            src_ref=src,
            dst_ref=dst,
            send_sem=r["osend"].at[s - 1],
            recv_sem=r["orecv"].at[s - 1],
            device_id=(dp, blk ^ s),
            device_id_type=MESH,
        )

    @pl.when(i == 0)
    def _():
        g_load.start()
        greet([(dp, blk ^ 1), (dp, blk ^ 2), (dp, blk ^ 3), (dp ^ 1, blk)])
        bins = as_row(r["bin"])
        for k in range(4):
            r["bins"][k] = bins[:, k * tile : (k + 1) * tile]
        for sl in rows:
            m = r["x"][sl].astype(F32) + dot(ct[:, sl], r["wo"][...], TN) + as_row(r["bo"])
            mid[sl] = m
            acc[sl] = m + as_row(r["bout"])
            n, _ = center(m)
            nb = (n * as_row(r["gain"]) + as_row(r["bias"])).astype(BF16)
            n2[sl] = nb
            n2t[:, sl] = nb.T

    @pl.when(i < 4)
    def _():
        ahead = dot(n2[rows[0]], win[...])
        for s, sl in enumerate(rows):
            pre = ahead + r["bins"][j]
            if s + 1 < n_blk:
                ahead = dot(n2[rows[s + 1]], win[...])
            phi, slope = gate(pre)
            a = (pre * phi).astype(BF16)
            act[sl] = a
            gp[j, sl] = (phi + slope).astype(BF16)
            acc[sl] += dot(a, wout[...])

        @pl.when(i > 0)
        def _():
            y_start(j - 1)

        @pl.when(i == 0)
        def _():
            g_load.wait()

        v = dot(act[...], g[...], TN)
        for c, x, yy in CXY:
            at = (yy * 4 + x * 2 + c) * share_f
            gw[c, x, yy, j] = v[at : at + share_f].astype(BF16)
        core_copy(j).start()

    @pl.when(i == 4)
    def _():
        for s in range(n_blk - 1, -1, -1):
            r["obuf"][s] = acc[rows[s]].astype(BF16)
            out_copy(s).start()
            acc[rows[s]] = jnp.zeros((tok, width), F32)

    @pl.when(i >= 4)
    def _():
        total = None
        ahead = dot(g[rows[0]], wout[...], NT)
        for s, sl in enumerate(rows):
            d = (ahead * gp[j, sl].astype(F32)).astype(BF16)
            if s + 1 < n_blk:
                ahead = dot(g[rows[s + 1]], wout[...], NT)
            act[sl] = d
            col = jnp.sum(d.astype(F32), axis=0, keepdims=True)
            total = col if total is None else total + col
            acc[sl] += dot(d, win[...], NT)
        r["bing"][j] = total

        @pl.when(i == 4)
        def _():
            y_start(3)

        v = regroup(dot(n2t[...], act[...]), width // 32)
        for c, x, yy in CXY:
            r["gwin"][c, x, yy] = v[c][x][yy].astype(BF16)

    @pl.when(i == 7)
    def _():
        head = width // H
        sums = [None] * 4
        for sl in rows:
            n, rstd = center(mid[sl])
            e = acc[sl]
            gf = g[sl].astype(F32)
            f = e * as_row(r["gain"])
            dm = gf + rstd * (
                f - jnp.mean(f, axis=-1, keepdims=True) - n * jnp.mean(f * n, axis=-1, keepdims=True)
            )
            mid[sl] = dm
            db = dm.astype(BF16)
            n2[sl] = db
            for k, term in enumerate((gf, e * n, e, db.astype(F32))):
                col = jnp.sum(term, axis=0, keepdims=True)
                sums[k] = col if sums[k] is None else sums[k] + col
            dc = dot(r["wo"][...], db, NT)
            for h in range(H):
                hs = slice(h * head, (h + 1) * head)
                r["dot"][hs, sl] = (dc[hs] * r["il"][h, :, sl]).astype(BF16)
        save = pltpu.make_async_copy(mid, r["dmid"], r["lsem"].at[1])
        save.start()
        vec = r["vec"]
        for k in range(4):
            vec[k : k + 1] = sums[k]
            vec[4 + k : 5 + k] = r["bing"][k]
        v = regroup(dot(ct[...], n2[...]), width // 32)
        for c, x, yy in CXY:
            r["gwo"][c, x, yy] = v[c][x][yy].astype(BF16)
        for k in range(4):
            y_copy(k).wait()

        def step(k, carry):
            for x in range(2):
                v = gw[core, x, y, k].astype(F32) + r0[x, y, k].astype(F32) + r1[x, k].astype(F32)
                t1[x, k] = v.astype(BF16)
            return carry

        lax.fori_loop(0, 4, step, 0)
        part = pltpu.make_async_copy(t1, r["part"], r["lsem"].at[2])
        part.start()
        for s in range(n_blk):
            out_copy(s).wait()
        save.wait()
        part.wait()


class Resume:
    def __init__(self, r, place):
        dp, blk = place
        self.r = r
        self.x, self.y, self.z = blk >> 1, dp & 1, dp >> 1
        self.ids = [(((self.z + d) & 3) * 2 + self.y, blk) for d in (1, 2, 3)] + [(dp, blk ^ 2)]

    def remote(self, src, dst, i):
        return pltpu.make_async_remote_copy(
            src_ref=src,
            dst_ref=dst,
            send_sem=self.r["w_send"].at[i],
            recv_sem=self.r["w_recv"].at[i],
            device_id=self.ids[i],
            device_id_type=MESH,
        )

    def z_copies(self):
        return [
            self.remote(self.r["part"].at[:, (self.z + d + 1) & 3], self.r["w_rz"].at[d], d) for d in range(3)
        ]

    def load(self):
        return pltpu.make_async_copy(self.r["part"].at[:, self.z], self.r["w_keep"], self.r["lsem"].at[0])

    def x_copy(self):
        return self.remote(self.r["w_t"], self.r["w_rx"], 3)

    def stage0(self):
        for copy in self.z_copies():
            copy.start()
        self.load().start()

    def stage1(self):
        self.load().wait()
        for copy in self.z_copies():
            copy.wait()
        for k in range(2):
            v = self.r["w_keep"][k].astype(F32)
            for d in range(3):
                v = v + self.r["w_rz"][d, k].astype(F32)
            self.r["w_f"][k] = v
        self.r["w_t"][...] = self.r["w_f"][1 - self.x].astype(BF16)
        self.x_copy().start()

    def stage2(self):
        self.x_copy().wait()
        self.r["s_wout"][...] = self.r["w_f"][self.x] + self.r["w_rx"][...].astype(F32)


def finish_kernel(n_big, *refs):
    src, va, vb = refs[:n_big], refs[n_big], refs[n_big + 1]
    dst, small = refs[n_big + 2 : 2 * n_big + 2], refs[2 * n_big + 2 :]
    for a, b in zip(src[:2], dst[:2]):
        b[...] = a[...]

    @pl.when(pl.program_id(0) == 0)
    def _():
        for a, b in zip(src[2:], dst[2:]):
            b[...] = a[...]
        me = lax.axis_index("dp") * lax.axis_size("blk") + lax.axis_index("blk")
        share = small[0].shape[0]
        wide = small[8].shape[0]
        width = va.shape[1]
        shift = lax.rem(width - me * share, width)
        moved = pltpu.roll(va[...], shift, 1)
        for k in range(4):
            small[k][...] = moved[k, :share]
        lines = vb[...]
        moved = pltpu.roll(lines, shift, 1)
        for i, k in enumerate((3, 1, 2, 0)):
            small[4 + i][...] = moved[k, :share]
        each = width // wide
        moved = pltpu.roll(lines, lax.rem(width - lax.rem(me, each) * wide, width), 1)
        row = 4 + lax.div(me, each)
        pick = lax.broadcasted_iota(jnp.int32, moved.shape, 0) == row
        small[8][...] = jnp.sum(jnp.where(pick, moved, 0.0), axis=0)[:wide]


def back_kernel(scale, names, tasks, plan, *refs):
    r = dict(zip(names, refs))
    h = pl.program_id(0)
    dp = lax.axis_index("dp")
    blk = lax.axis_index("blk")
    place = (dp, blk)
    n_blk, tok, width = r["xs"].shape
    seq = n_blk * tok
    head = width // H
    dcat, wcat, gq, vec = r["dcat"], r["wcat"], r["gq"], r["va"]

    def put(ref, cols):
        def out(v):
            if cols is None:
                ref[...] = v
            else:
                ref[:, cols] = v

        return out

    jobs = {}
    for name, source, index, cols, share, first, out, out_cols in tasks:
        ref = r[source] if index is None else r[source].at[index]
        bufs = {k: r[name + "_" + k] for k in SCATTER_KEYS if name + "_" + k in r}
        if isinstance(out, tuple):
            outs = [put(r[o], out_cols) for o in out]

            def sink(v, outs=outs):
                each = v.shape[1] // len(outs)
                for i, o in enumerate(outs):
                    o(v[:, i * each : (i + 1) * each])

        else:
            sink = put(r[out], out_cols)
        kind = ScatterLate if first == "late" else Scatter
        jobs[name] = kind(ref, cols, share, "y" if first == "late" else first, sink, bufs, place)

    jobs["wout"] = Resume(r, place)

    def spread(src, dst, sems, s):
        return pltpu.make_async_remote_copy(
            src_ref=src.at[s],
            dst_ref=dst.at[blk],
            send_sem=sems[0].at[s - 1],
            recv_sem=sems[1].at[s - 1],
            device_id=(dp, blk ^ s),
            device_id_type=MESH,
        )

    def in_copy(s):
        if s == 0:
            return pltpu.make_async_copy(r["dx"].at[0], r["input_grad"].at[blk], r["lsem"].at[1])
        return spread(r["dx"], r["input_grad"], (r["isend"], r["irecv"]), s)

    def nt_load():
        return pltpu.make_async_copy(r["nt"], r["ntbuf"], r["lsem"].at[7])

    def loads():
        pairs = [(r["xs"], r["xbuf"]), (r["dmid"], r["dmbuf"])]
        pairs += [(r[w], wcat.at[:, i * width : (i + 1) * width]) for i, w in enumerate(("wq", "wk", "wv"))]
        return [pltpu.make_async_copy(a, b, r["lsem"].at[2 + i]) for i, (a, b) in enumerate(pairs)]

    z, y = dp >> 1, dp & 1
    z_ids = [(((z + d) & 3) * 2 + y, blk) for d in (1, 2, 3)]
    vec_ids = [z_ids, [(dp ^ 1, blk)], [(dp, blk ^ 1), (dp, blk ^ 2), (dp, blk ^ 3)]]

    def vec_copies(name, stage):
        at = (0, 3, 4)[stage]
        return [
            pltpu.make_async_remote_copy(
                src_ref=r[name],
                dst_ref=r[name + "_r"].at[at + d],
                send_sem=r[name + "_send"].at[at + d],
                recv_sem=r[name + "_recv"].at[at + d],
                device_id=where,
                device_id_type=MESH,
            )
            for d, where in enumerate(vec_ids[stage])
        ]

    def vec_step(name, stage):
        if stage > 0:
            copies = vec_copies(name, stage - 1)
            for copy in copies:
                copy.wait()
            at = (0, 3, 4)[stage - 1]
            r[name][...] += sum(r[name + "_r"][at + d] for d in range(len(copies)))
        if stage < 3:
            for copy in vec_copies(name, stage):
                copy.start()

    def input_piece(s, sums):
        sl = slice(s * tok, (s + 1) * tok)
        e = r["ebuf"][s & 1].T
        n, rstd = center(r["xbuf"][s].astype(F32))
        f = e * as_row(r["gain"])
        dx = r["dmbuf"][sl] + rstd * (
            f - jnp.mean(f, axis=-1, keepdims=True) - n * jnp.mean(f * n, axis=-1, keepdims=True)
        )
        r["dx"][s] = dx.astype(BF16)
        in_copy(s).start()
        new = [jnp.sum(t, axis=0, keepdims=True) for t in (e * n, e)]
        return new if sums is None else [a + b for a, b in zip(sums, new)]

    @pl.when(h == 0)
    def _():
        greet(
            [(dp, blk ^ 1), (dp, blk ^ 2), (dp, blk ^ 3), (dp ^ 1, blk)]
            + [(((z + d) & 3) * 2 + y, blk) for d in (1, 2, 3)]
        )
        nt_load().start()
        for load in loads():
            load.start()
        vec[...] = jnp.zeros_like(vec)
        r["vb"][...] = r["vec_in"][...]

    def act(item):
        kind, what = item
        if kind in ("va", "vb"):
            vec_step(kind, what)
        else:
            getattr(jobs[kind], "stage%d" % what)()

    for at in range(H):
        if plan.get(at):

            @pl.when(h == at)
            def _(at=at):
                for item in plan[at]:
                    act(item)

    @pl.when(h < H)
    def _():
        base = pl.multiple_of(h * head, head)
        dq, dk, dv = attend_back_head(
            scale,
            n_blk,
            r["p"],
            r["q"][...],
            r["k"][...],
            r["v"][...],
            r["do"][...],
            r["ct"][...],
            r["tops"],
            r["ds"],
            r["doi"],
        )
        dcat[pl.ds(base, head)] = dq
        dcat[pl.ds(base + width, head)] = dk
        dcat[pl.ds(base + 2 * width, head)] = dv

    n_group = gq.shape[0]
    cols = width // n_group
    for gi in range(n_group):

        @pl.when(h == (gi + 1) * (H // n_group) - 1)
        def _(gi=gi):
            if gi == 0:
                nt_load().wait()
            nt = r["ntbuf"][...]
            ones = jnp.ones((8, seq), BF16)
            for t in range(3):
                part = dcat[t * width + gi * cols : t * width + (gi + 1) * cols]
                v = regroup(dot(nt, part, NT), width // 32)
                for c, x, y in CXY:
                    gq[gi, c, x, y, :, t * cols : (t + 1) * cols] = v[c][x][y].astype(BF16)
                if t != 1:
                    row = 2 if t == 0 else 3
                    vec[row : row + 1, gi * cols : (gi + 1) * cols] = dot(ones, part, NT)[:1]
            jobs["q%d" % gi].stage0()

    @pl.when(h == H)
    def _():
        sums = None
        for load in loads():
            load.wait()
        for item in plan["tail"]:
            kind, what = item
            if kind == "mul":
                r["ebuf"][what & 1] = dot(wcat[...], dcat[:, what * tok : (what + 1) * tok])
            elif kind == "piece":
                sums = input_piece(what, sums)
                if what == 0:
                    vec[0:1] = sums[0]
                    vec[1:2] = sums[1]
            else:
                act(item)
        r["va_out"][...] = vec[...]
        r["vb_out"][...] = r["vb"][...]
        for s in range(n_blk):
            in_copy(s).wait()


PLAN = {
    0: [("wout", 0), ("a2", 0), ("b2", 0), ("wo", 0)],
    2: [("a2", 1), ("b2", 1)],
    3: [("wo", 1)],
    5: [("q0", 1)],
    7: [("a2", 2), ("b2", 2)],
    9: [("q1", 1)],
    10: [("q0", 2), ("wo", 2)],
    11: [("a2", 3), ("b2", 3), ("wout", 1)],
    "tail": [
        ("mul", 3),
        ("mul", 2),
        ("piece", 3),
        ("q2", 1),
        ("mul", 1),
        ("piece", 2),
        ("mul", 0),
        ("piece", 1),
        ("piece", 0),
        ("vb", 0),
        ("va", 0),
        ("q2", 2),
        ("q1", 2),
        ("wo", 3),
        ("q0", 3),
        ("vb", 1),
        ("va", 1),
        ("wout", 2),
        ("a2", 4),
        ("vb", 2),
        ("va", 2),
        ("q1", 3),
        ("b2", 4),
        ("q2", 3),
        ("vb", 3),
        ("va", 3),
        ("wo", 4),
        ("q0", 4),
        ("q1", 4),
        ("q2", 4),
    ],
}

SCATTER_KEYS = ("f2", "rx", "r0", "t1", "r1", "t2", "r2", "t3", "r3", "f", "send", "recv", "keep", "load")


def body(
    inputs,
    lengths,
    out_grad,
    ln1_gain,
    ln1_bias,
    w_query,
    b_query,
    w_key,
    w_value,
    b_value,
    w_output,
    b_output,
    ln2_gain,
    ln2_bias,
    w_in,
    b_in,
    w_out,
    b_out,
):
    n_seq, tok, width = inputs.shape
    n_blk = lax.axis_size("blk")
    n_dp = lax.axis_size("dp")
    n_dev = n_blk * n_dp
    assert n_seq == n_blk
    seq = tok * n_blk
    hidden = w_in.shape[1]
    head = width // H
    scale = head ** (-0.5)
    blk = lax.axis_index("blk")
    me = lax.axis_index("dp") * n_blk + blk

    def swap(v, s):
        return lax.ppermute(v, "blk", [(i, i ^ s) for i in range(n_blk)])

    def collect(pieces):
        back = [pieces[0]] + [swap(pieces[s], s) for s in range(1, n_blk)]
        out = jnp.zeros((n_seq, tok, width), BF16)
        for s in range(n_blk):
            out = lax.dynamic_update_index_in_dim(out, back[s], blk ^ s, 0)
        return out

    row = lambda v: v.astype(F32).reshape(1, -1)


    sds = jax.ShapeDtypeStruct
    piece = full((tok, width))
    wide = full((width, seq))
    n_col = 3
    cols = width // n_col
    strip = pl.BlockSpec((cols, seq), lambda j: (j, 0))
    anywhere = pl.BlockSpec(memory_space=pl.ANY)
    vmem = pl.BlockSpec(memory_space=pltpu.VMEM)
    xs, nt, qt, kt, vt = pl.pallas_call(
        functools.partial(qkv_spread_kernel, scale * LOG2E, n_blk),
        in_specs=[anywhere, vmem, vmem, anywhere, vmem, anywhere, anywhere, vmem],
        out_specs=[anywhere] * 5,
        out_shape=[sds((n_blk, tok, width), BF16)] + [sds((width, seq), BF16)] * 4,
        scratch_shapes=[
            pltpu.VMEM((n_blk, tok, width), BF16),
            pltpu.VMEM((3, width, width), BF16),
            pltpu.VMEM((3, width, width), BF16),
            pltpu.VMEM((width, seq), BF16),
            pltpu.VMEM((3, width, seq), BF16),
            pltpu.SemaphoreType.DMA((n_blk - 1,)),
            pltpu.SemaphoreType.DMA((n_blk - 1,)),
            pltpu.SemaphoreType.DMA((3,)),
            pltpu.SemaphoreType.DMA((n_blk, 5)),
            pltpu.SemaphoreType.DMA,
        ],
        compiler_params=params(collective_id=0, has_side_effects=True),
        cost_estimate=cost(3 * seq * width * width, 14 * seq * width),
        name="qkv",
    )(inputs, ln1_gain, ln1_bias, w_query, b_query, w_key, w_value, b_value)

    per_head = pl.BlockSpec((head, seq), lambda h: (h, 0))
    per_square = pl.BlockSpec((1, seq, seq), lambda h: (h, 0, 0))
    per_block = pl.BlockSpec((1, n_blk, seq), lambda h: (h, 0, 0))
    ct, probs, inv_total, tops, gs = pl.pallas_call(
        functools.partial(attend_spread_kernel, n_blk),
        grid=(H,),
        in_specs=[pl.BlockSpec(memory_space=pltpu.SMEM), per_head, per_head, per_head, anywhere],
        out_specs=[per_head, per_square, pl.BlockSpec((1, 1, seq), lambda h: (h, 0, 0)), per_block, anywhere],
        out_shape=[
            sds((width, seq), BF16),
            sds((H, seq, seq), BF16),
            sds((H, 1, seq), F32),
            sds((H, n_blk, seq), F32),
            sds((n_blk, tok, width), BF16),
        ],
        scratch_shapes=[
            pltpu.SemaphoreType.DMA((n_blk - 1,)),
            pltpu.SemaphoreType.DMA((n_blk - 1,)),
            pltpu.SemaphoreType.DMA,
        ],
        compiler_params=params(collective_id=1, has_side_effects=True),
        cost_estimate=cost(8 * seq * seq * width, 2 * H * seq * seq, H * seq * seq),
        name="attend",
    )(lengths, qt, kt, vt, out_grad)

    if n_dp == 8 and n_blk == 4 and width % 768 == 0 and hidden == 4 * width:
        share, share_f = width // n_dev, hidden // n_dev
        tile = hidden // 4
        once = lambda shape: pl.BlockSpec(shape, lambda i: (0,) * len(shape), pipeline_mode=pl.Buffered(1))
        vec_rows = 8
        ins = {
            "x": (xs.reshape(seq, width), once((seq, width))),
            "g": (gs.reshape(seq, width), anywhere),
            "ct": (ct, once((width, seq))),
            "il": (inv_total, once((H, 1, seq))),
            "wo": (w_output, once((width, width))),
            "bo": (b_output, once((width,))),
            "gain": (ln2_gain, once((width,))),
            "bias": (ln2_bias, once((width,))),
            "bout": (b_out, once((width,))),
            "bin": (b_in, once((hidden,))),
            "win": (w_in, pl.BlockSpec((width, tile), lambda i: (0, i % 4))),
            "wout": (w_out, pl.BlockSpec((tile, width), lambda i: (i % 4, 0))),
        }
        outs = {
            "output": (sds((n_seq, tok, width), BF16), anywhere),
            "dmid": (sds((seq, width), F32), anywhere),
            "dot": (sds((width, seq), BF16), once((width, seq))),
            "gwin": (
                sds((2, 2, 2, 4 * share, hidden), BF16),
                pl.BlockSpec((2, 2, 2, 4 * share, tile), lambda i: (0, 0, 0, 0, jnp.maximum(i - 4, 0))),
            ),
            "gwo": (sds((2, 2, 2, 4 * share, width), BF16), once((2, 2, 2, 4 * share, width))),
            "part": (sds((2, 4, share_f, width), BF16), anywhere),
            "vec": (sds((vec_rows, width), F32), once((vec_rows, width))),
        }
        scratch = {
            "gbuf": pltpu.VMEM((seq, width), BF16),
            "mid": pltpu.VMEM((seq, width), F32),
            "acc": pltpu.VMEM((seq, width), F32),
            "n2": pltpu.VMEM((seq, width), BF16),
            "n2t": pltpu.VMEM((width, seq), BF16),
            "act": pltpu.VMEM((seq, tile), BF16),
            "gp": pltpu.VMEM((4, seq, tile), BF16),
            "bins": pltpu.VMEM((4, 1, tile), F32),
            "bing": pltpu.VMEM((4, 1, tile), F32),
            "obuf": pltpu.VMEM((n_blk, tok, width), BF16),
            "gw": pltpu.VMEM((2, 2, 2, 4, share_f, width), BF16),
            "r0": pltpu.VMEM((2, 2, 4, share_f, width), BF16),
            "t1": pltpu.VMEM((2, 4, share_f, width), BF16),
            "r1": pltpu.VMEM((2, 4, share_f, width), BF16),
            "csend": pltpu.SemaphoreType.DMA((4,)),
            "crecv": pltpu.SemaphoreType.DMA((4,)),
            "ysend": pltpu.SemaphoreType.DMA((4,)),
            "yrecv": pltpu.SemaphoreType.DMA((4,)),
            "osend": pltpu.SemaphoreType.DMA((n_blk - 1,)),
            "orecv": pltpu.SemaphoreType.DMA((n_blk - 1,)),
            "lsem": pltpu.SemaphoreType.DMA((4,)),
        }
        names = tuple(ins) + tuple(outs) + tuple(scratch)
        ffn = pl.pallas_call(
            functools.partial(ffn_host_kernel, names, n_blk),
            grid=(8,),
            in_specs=[v[1] for v in ins.values()],
            out_specs=[v[1] for v in outs.values()],
            out_shape=[v[0] for v in outs.values()],
            scratch_shapes=list(scratch.values()),
            compiler_params=pltpu.CompilerParams(
                vmem_limit_bytes=62 * 2**20, collective_id=3, has_side_effects=True
            ),
            name="ffn",
        )(*[v[0] for v in ins.values()])
        ffn = dict(zip(outs, ffn))
        tasks = (
            ("a2", "gwin", None, slice(0, hidden // 2), share, "x", "s_win", slice(0, hidden // 2)),
            ("b2", "gwin", None, slice(hidden // 2, hidden), share, "y", "s_win", slice(hidden // 2, hidden)),
            ("wo", "gwo", None, None, share, "x", "s_wo", None),
        ) + tuple(
            (
                "q%d" % i,
                "gq",
                i,
                None,
                share,
                ("y", "x", "late")[i],
                ("s_wq", "s_wk", "s_wv"),
                slice(i * cols, (i + 1) * cols),
            )
            for i in range(n_col)
        )
        sizes = {"a2": hidden // 2, "b2": hidden // 2, "wo": width}
        plan = PLAN
        last = lambda shape: pl.BlockSpec(shape, lambda h: (jnp.minimum(h, H - 1),) + (0,) * (len(shape) - 1))
        strip_h = last((head, seq))
        ins = {
            "p": (probs, last((1, seq, seq))),
            "q": (qt, strip_h),
            "k": (kt, strip_h),
            "v": (vt, strip_h),
            "do": (ffn["dot"], strip_h),
            "ct": (ct, strip_h),
            "tops": (tops, last((1, n_blk, seq))),
            "nt": (nt, anywhere),
            "gain": (ln1_gain, full((width,))),
            "vec_in": (ffn["vec"], full((vec_rows, width))),
            "xs": (xs, anywhere),
            "dmid": (ffn["dmid"], anywhere),
            "wq": (w_query, anywhere),
            "wk": (w_key, anywhere),
            "wv": (w_value, anywhere),
            "part": (ffn["part"], anywhere),
            "gwin": (ffn["gwin"], anywhere),
            "gwo": (ffn["gwo"], anywhere),
        }
        outs = {
            "input_grad": (sds((n_seq, tok, width), BF16), anywhere),
            "s_wq": (sds((share, width), F32), full((share, width))),
            "s_wk": (sds((share, width), F32), full((share, width))),
            "s_wv": (sds((share, width), F32), full((share, width))),
            "s_wo": (sds((share, width), F32), full((share, width))),
            "s_win": (sds((share, hidden), F32), full((share, hidden))),
            "s_wout": (sds((share_f, width), F32), full((share_f, width))),
            "va_out": (sds((8, width), F32), full((8, width))),
            "vb_out": (sds((8, width), F32), full((8, width))),
        }
        scratch = {
            "ds": pltpu.VMEM((seq, seq), BF16),
            "doi": pltpu.VMEM((n_blk, head, seq), BF16),
            "dcat": pltpu.VMEM((3 * width, seq), BF16),
            "wcat": pltpu.VMEM((width, 3 * width), BF16),
            "gq": pltpu.VMEM((n_col, 2, 2, 2, 4 * share, 3 * cols), BF16),
            "va": pltpu.VMEM((8, width), F32),
            "vb": pltpu.VMEM((8, width), F32),
            "va_r": pltpu.VMEM((7, 8, width), F32),
            "vb_r": pltpu.VMEM((7, 8, width), F32),
            "ebuf": pltpu.VMEM((2, width, tok), F32),
            "ntbuf": pltpu.VMEM((width, seq), BF16),
            "xbuf": pltpu.VMEM((n_blk, tok, width), BF16),
            "dmbuf": pltpu.VMEM((seq, width), F32),
            "dx": pltpu.VMEM((n_blk, tok, width), BF16),
            "lsem": pltpu.SemaphoreType.DMA((8,)),
            "va_send": pltpu.SemaphoreType.DMA((7,)),
            "va_recv": pltpu.SemaphoreType.DMA((7,)),
            "vb_send": pltpu.SemaphoreType.DMA((7,)),
            "vb_recv": pltpu.SemaphoreType.DMA((7,)),
            "w_keep": pltpu.VMEM((2, share_f, width), BF16),
            "w_rz": pltpu.VMEM((3, 2, share_f, width), BF16),
            "w_f": pltpu.VMEM((2, share_f, width), F32),
            "w_t": pltpu.VMEM((share_f, width), BF16),
            "w_rx": pltpu.VMEM((share_f, width), BF16),
            "w_send": pltpu.SemaphoreType.DMA((4,)),
            "w_recv": pltpu.SemaphoreType.DMA((4,)),
            "isend": pltpu.SemaphoreType.DMA((n_blk - 1,)),
            "irecv": pltpu.SemaphoreType.DMA((n_blk - 1,)),
        }
        for name, source, _, _, task_share, first, _, _ in tasks:
            for k, v in scatter_scratch(task_share, sizes.get(name, width), source != "gq", first == "late").items():
                scratch[name + "_" + k] = v
        names = tuple(ins) + tuple(outs) + tuple(scratch)
        got = pl.pallas_call(
            functools.partial(back_kernel, scale, names, tasks, plan),
            grid=(H + 1,),
            in_specs=[v[1] for v in ins.values()],
            out_specs=[v[1] for v in outs.values()],
            out_shape=[v[0] for v in outs.values()],
            scratch_shapes=list(scratch.values()),
            compiler_params=pltpu.CompilerParams(
                vmem_limit_bytes=60 * 2**20, collective_id=2, has_side_effects=True
            ),
            name="back",
        )(*[v[0] for v in ins.values()])
        got = dict(zip(outs, got))
        big = [ffn["output"], got["input_grad"]] + [
            got[k] for k in ("s_wq", "s_wk", "s_wv", "s_wo", "s_win", "s_wout")
        ]
        part = pl.BlockSpec((n_blk // 2, tok, width), lambda i: (i, 0, 0))
        flat = [sds(v.shape, v.dtype) for v in big]
        fin = pl.pallas_call(
            functools.partial(finish_kernel, len(big)),
            grid=(2,),
            in_specs=[part] * 2 + [full(v.shape) for v in big[2:]] + [full((8, width))] * 2,
            out_specs=[part] * 2 + [full(v.shape) for v in big[2:]] + [full((share,))] * 8 + [full((share_f,))],
            out_shape=flat + [sds((share,), F32)] * 8 + [sds((share_f,), F32)],
            name="finish",
        )(*big, got["va_out"], got["vb_out"])
        output, input_grad, s_wq, s_wk, s_wv, s_wo, s_win, s_wout = fin[: len(big)]
        g1, b1, bq, bv, bo_sum, g2, b2, bout_sum, bin_sum = fin[len(big) :]
        return (
            output,
            input_grad,
            g1,
            b1,
            s_wq,
            bq,
            s_wk,
            s_wv,
            bv,
            s_wo,
            bo_sum,
            g2,
            b2,
            s_win,
            bin_sum,
            s_wout,
            bout_sum,
        )

    n_tile = 4
    tile = hidden // n_tile
    result = pl.pallas_call(
        functools.partial(ffn_kernel, n_blk),
        grid=(n_tile,),
        in_specs=[full((seq, width))] * 2
        + [
            wide,
            full((H, 1, seq)),
            full((width, width)),
            full((1, width)),
            full((1, width)),
            full((1, width)),
            pl.BlockSpec((width, tile), lambda j: (0, j)),
            pl.BlockSpec((1, tile), lambda j: (0, j)),
            pl.BlockSpec((tile, width), lambda j: (j, 0)),
            full((1, width)),
        ],
        out_specs=[piece] * n_blk
        + [
            pl.BlockSpec((tile, width), lambda j: (j, 0)),
            pl.BlockSpec((width, tile), lambda j: (0, j)),
            pl.BlockSpec((1, tile), lambda j: (0, j)),
            full((seq, width)),
            wide,
            full((width, width)),
            full((8, width)),
        ],
        out_shape=[sds((tok, width), BF16)] * n_blk
        + [
            sds((hidden, width), BF16),
            sds((width, hidden), BF16),
            sds((1, hidden), F32),
            sds((seq, width), F32),
            sds((width, seq), BF16),
            sds((width, width), BF16),
            sds((8, width), F32),
        ],
        scratch_shapes=[
            pltpu.VMEM((seq, width), F32),
            pltpu.VMEM((seq, width), BF16),
            pltpu.VMEM((width, seq), BF16),
            pltpu.VMEM((seq, width), F32),
            pltpu.VMEM((seq, width), F32),
            pltpu.VMEM((seq, tile), BF16),
            pltpu.VMEM((seq, tile), BF16),
        ],
        compiler_params=params(),
        cost_estimate=cost(8 * seq * width * hidden, 8 * width * hidden),
        name="ffn",
    )(
        xs.reshape(seq, width),
        gs.reshape(seq, width),
        ct,
        inv_total,
        w_output,
        row(b_output),
        row(ln2_gain),
        row(ln2_bias),
        w_in,
        row(b_in),
        w_out,
        row(b_out),
    )
    out_pieces = result[:n_blk]
    g_wout, g_win, g_bin, dmid, dct, g_wo, vec2 = result[n_blk:]

    bits = (n_dev - 1).bit_length()
    assert n_dev == 1 << bits

    def scatter(grad, order, wire):
        share = grad.shape[0] // n_dev
        order = list(order) + [b for b in range(bits) if b not in order]
        axes = list(range(bits - 1, -1, -1))
        terms = [grad.reshape((2,) * bits + (share,) + grad.shape[1:])]
        for b in order:
            at = axes.index(b)
            axes.pop(at)
            mine = (me >> b) & 1
            send = None
            keep = []
            for t in terms:
                other = lax.dynamic_index_in_dim(t, 1 - mine, at, keepdims=False)
                send = other.astype(F32) if send is None else send + other.astype(F32)
                keep.append(lax.dynamic_index_in_dim(t, mine, at, keepdims=False))
            got = lax.ppermute(send.astype(wire), ("dp", "blk"), [(i, i ^ (1 << b)) for i in range(n_dev)])
            terms = keep + [got]
        total = terms[0].astype(F32)
        for t in terms[1:]:
            total = total + t.astype(F32)
        return total

    s_wout = scatter(g_wout, (0, 1, 2, 3, 4), BF16)
    s_win = scatter(g_win, (0, 2, 1, 3, 4), BF16)
    s_wo = scatter(g_wo, (0, 3, 4, 1, 2), BF16)
    output = collect(out_pieces)

    dqt, dkt, dvt = pl.pallas_call(
        functools.partial(attend_back_kernel, scale, n_blk),
        grid=(H,),
        in_specs=[per_square] + [per_head] * 5 + [per_block],
        out_specs=[per_head] * 3,
        out_shape=[sds((width, seq), BF16)] * 3,
        scratch_shapes=[pltpu.VMEM((seq, seq), BF16), pltpu.VMEM((n_blk, head, seq), BF16)],
        compiler_params=params(),
        cost_estimate=cost(10 * seq * seq * width, 2 * H * seq * seq),
        name="attend_back",
    )(probs, qt, kt, vt, dct, ct, tops)

    result = pl.pallas_call(
        functools.partial(input_kernel, n_blk),
        in_specs=[full((seq, width))] * 2
        + [full((1, width)), wide, wide, wide]
        + [full((width, width))] * 3,
        out_specs=[piece] * n_blk + [full((8, width))],
        out_shape=[sds((tok, width), BF16)] * n_blk + [sds((8, width), F32)],
        compiler_params=params(),
        cost_estimate=cost(3 * seq * width * width, 14 * seq * width),
        name="input_grad",
    )(xs.reshape(seq, width), dmid, row(ln1_gain), dqt, dkt, dvt, w_query, w_key, w_value)
    input_grad = collect(result[:n_blk])
    vec1 = result[n_blk]

    col = pl.BlockSpec((width, cols), lambda j: (0, j))
    g_wq, g_wk, g_wv, vecq = pl.pallas_call(
        qkv_grad_kernel,
        grid=(n_col,),
        in_specs=[wide, strip, strip, strip],
        out_specs=[col, col, col, pl.BlockSpec((8, cols), lambda j: (0, j))],
        out_shape=[sds((width, width), BF16)] * 3 + [sds((8, width), F32)],
        compiler_params=params(),
        cost_estimate=cost(3 * seq * width * width, 14 * seq * width),
        name="qkv_grad",
    )(nt, dqt, dkt, dvt)
    s_wq = scatter(g_wq, (0, 1, 2, 3, 4), BF16)
    s_wk = scatter(g_wk, (0, 2, 3, 4, 1), BF16)
    s_wv = scatter(g_wv, (0, 3, 4, 1, 2), BF16)

    vectors = [vec1[0], vec1[1], vecq[0], vecq[1], vec2[3], vec2[1], vec2[2], g_bin[0], vec2[0]]
    packed = jnp.concatenate([v.reshape(n_dev, -1) for v in vectors], axis=1)
    packed = scatter(packed, (0, 1, 2, 3, 4), F32).reshape(-1)
    parts = []
    at = 0
    for v in vectors:
        size = v.shape[0] // n_dev
        parts.append(packed[at : at + size])
        at += size
    p_ln1g, p_ln1b, p_bq, p_bv, p_bo, p_ln2g, p_ln2b, p_bin, p_bout = parts
    return (
        output,
        input_grad,
        p_ln1g,
        p_ln1b,
        s_wq,
        p_bq,
        s_wk,
        s_wv,
        p_bv,
        s_wo,
        p_bo,
        p_ln2g,
        p_ln2b,
        s_win,
        p_bin,
        s_wout,
        p_bout,
    )


def solution(mesh):
    whole = P(("dp", "blk"))
    rows = P(("dp", "blk"), None)
    tokens = P("dp", "blk", None)
    in_specs = (tokens, P("dp"), tokens) + (P(),) * 15
    out_specs = (
        tokens,
        tokens,
        whole,
        whole,
        rows,
        whole,
        rows,
        rows,
        whole,
        rows,
        whole,
        whole,
        whole,
        rows,
        whole,
        rows,
        whole,
    )
    return jax.shard_map(body, mesh=mesh, in_specs=in_specs, out_specs=out_specs, check_vma=False)
```

```python
import functools

import jax
import jax.numpy as jnp
from jax import lax
from jax.experimental import pallas as pl
from jax.experimental.pallas import tpu as pltpu
from jax.sharding import PartitionSpec as P

H = 12
EPS = 1e-05
LOG2E = 1.4426950408889634
LN2 = 0.6931471805599453
INV_SQRT_2PI = 0.3989422804014327
SQRT_HALF = 0.7071067811865476
F32 = jnp.float32
BF16 = jnp.bfloat16
VMEM_LIMIT = 56 * 2**20

NN = (((1,), (0,)), ((), ()))
NT = (((1,), (1,)), ((), ()))
TN = (((0,), (0,)), ((), ()))

def dot(left, right, dims=NN):
    return lax.dot_general(left, right, dims, preferred_element_type=F32)


def params(**kw):
    return pltpu.CompilerParams(vmem_limit_bytes=VMEM_LIMIT, **kw)


def cost(macs, nbytes, exps=0):
    return pl.CostEstimate(flops=2 * macs, bytes_accessed=nbytes, transcendentals=exps)


def full(shape):
    return pl.BlockSpec(shape, lambda *_: (0,) * len(shape))


def as_row(ref):
    return ref[...].astype(F32)[None, :]


def center(v):
    mean = jnp.mean(v, axis=-1, keepdims=True)
    cent = v - mean
    var = jnp.mean(cent * cent, axis=-1, keepdims=True)
    rstd = lax.rsqrt(var + EPS)
    return cent * rstd, rstd


def gate(u):
    phi = 0.5 + 0.5 * lax.erf(u * SQRT_HALF)
    e = jnp.exp2(u * u * (-0.5 * LOG2E))
    return phi, u * e * INV_SQRT_2PI


def attend_kernel(n_blk, len_ref, q_ref, k_ref, v_ref, c_ref, p_ref, il_ref, f_ref):
    seq = q_ref.shape[1]
    tok = seq // n_blk
    blk = lax.axis_index("blk")
    length = len_ref[blk]
    live = [(blk ^ i) * tok < length for i in range(n_blk)]
    keys, q, v = k_ref[...].T, q_ref[...], v_ref[...]
    m = jnp.full((1, seq), -1e30, F32)
    total = summed = None
    tops = []
    ahead = dot(keys[:tok], q)
    for i in range(n_blk):
        s = ahead
        if i + 1 < n_blk:
            ahead = dot(keys[(i + 1) * tok : (i + 2) * tok], q)
        new = jnp.maximum(m, jnp.where(live[i], jnp.max(s, axis=0, keepdims=True), -1e30))
        p = jnp.exp2(s - jnp.where(live[i], new, 1e30))
        part = jnp.sum(p, axis=0, keepdims=True)
        p = p.astype(BF16)
        p_ref[0, i * tok : (i + 1) * tok] = p
        o = dot(v[:, i * tok : (i + 1) * tok], p)
        if i == 0:
            summed, total = o, part
        else:
            shrink = jnp.exp2(m - new)
            summed, total = summed * shrink + o, total * shrink + part
        m = new
        tops.append(m)
    inv = 1.0 / total
    c_ref[...] = (summed * inv).astype(BF16)
    il_ref[0] = inv
    for i in range(n_blk):
        f_ref[0, i : i + 1] = jnp.exp2(tops[i] - m)


def attend_back_head(scale, n_blk, p_ref, q, k, v, do, ct, f_ref, ds, doi):
    seq = q.shape[1]
    tok = seq // n_blk
    vh = v.T
    do = do.astype(F32)
    delta = jnp.sum(do * ct.astype(F32), axis=0, keepdims=True)
    for i in range(n_blk):
        sl = slice(i * tok, (i + 1) * tok)
        f = f_ref[0, i : i + 1]
        d = (do * f).astype(BF16)
        doi[i] = d
        ds[sl] = (p_ref[0, sl].astype(F32) * (dot(vh[sl], d) - delta * f)).astype(BF16)
    dq = (dot(k, ds[...]) * scale).astype(BF16)
    dv = [dot(p_ref[0, i * tok : (i + 1) * tok], doi[i], NT).T.astype(BF16) for i in range(n_blk)]
    dk = (dot(ds[...], q, NT) * LN2).T.astype(BF16)
    return dq, dk, jnp.concatenate(dv, axis=1)


MESH = pl.DeviceIdType.MESH


def greet(partners):
    barrier = pltpu.get_barrier_semaphore()
    for where in partners:
        pl.semaphore_signal(barrier, inc=1, device_id=where, device_id_type=MESH)
    pl.semaphore_wait(barrier, len(partners))


def qkv_spread_kernel(
    scale,
    n_blk,
    x_any,
    gain,
    bias,
    wq_any,
    bq,
    wk_any,
    wv_any,
    bv,
    xs_any,
    nt_any,
    q_any,
    k_any,
    v_any,
    xbuf,
    wbuf,
    wt,
    nt,
    qkv,
    send,
    recv,
    wsem,
    osem,
    xsem,
):
    tok, width = xbuf.shape[1:]
    dp = lax.axis_index("dp")
    blk = lax.axis_index("blk")
    own = pltpu.make_async_copy(x_any.at[blk], xbuf.at[0], xsem)
    own.start()
    loads = [
        pltpu.make_async_copy(w, wbuf.at[i], wsem.at[i]) for i, w in enumerate((wq_any, wk_any, wv_any))
    ]
    for load in loads:
        load.start()
    greet([(dp, blk ^ s) for s in range(1, n_blk)])
    order = list(range(n_blk - 1, 0, -1))
    copies = {}
    for s in order:
        copies[s] = pltpu.make_async_remote_copy(
            src_ref=x_any.at[blk ^ s],
            dst_ref=xbuf.at[s],
            send_sem=send.at[s - 1],
            recv_sem=recv.at[s - 1],
            device_id=(dp, blk ^ s),
            device_id_type=MESH,
        )
        if s != 2:
            copies[s].start()
    for i, load in enumerate(loads):
        load.wait()
        wt[i] = wbuf[i].T
    cols = jnp.concatenate([as_row(bq), as_row(bv), jnp.zeros((6, width), F32)], axis=0).T
    writes = []
    for s in (0, 1, 3, 2):
        if s == 0:
            own.wait()
        else:
            if s == 3:
                copies[3].wait_send()
                copies[2].start()
            copies[s].wait_recv()
        sl = slice(s * tok, (s + 1) * tok)
        n, _ = center(xbuf[s].astype(F32))
        n = (n * as_row(gain) + as_row(bias)).astype(BF16).T
        nt[:, sl] = n
        qkv[0, :, sl] = ((dot(wt[0], n) + cols[:, :1]) * scale).astype(BF16)
        qkv[1, :, sl] = dot(wt[1], n).astype(BF16)
        qkv[2, :, sl] = (dot(wt[2], n) + cols[:, 1:2]).astype(BF16)
        for i, (src, dst) in enumerate(
            (
                (xbuf.at[s], xs_any.at[s]),
                (nt.at[:, sl], nt_any.at[:, sl]),
                (qkv.at[0, :, sl], q_any.at[:, sl]),
                (qkv.at[1, :, sl], k_any.at[:, sl]),
                (qkv.at[2, :, sl], v_any.at[:, sl]),
            )
        ):
            write = pltpu.make_async_copy(src, dst, osem.at[s, i])
            write.start()
            writes.append(write)
    for s in (1, 2):
        copies[s].wait_send()
    for write in writes:
        write.wait()


def attend_spread_kernel(n_blk, len_ref, q_ref, k_ref, v_ref, g_any, c_ref, p_ref, il_ref, f_ref, gs_any, send, recv, osem):
    h = pl.program_id(0)
    dp = lax.axis_index("dp")
    blk = lax.axis_index("blk")

    def copy(s):
        return pltpu.make_async_remote_copy(
            src_ref=g_any.at[blk ^ s],
            dst_ref=gs_any.at[s],
            send_sem=send.at[s - 1],
            recv_sem=recv.at[s - 1],
            device_id=(dp, blk ^ s),
            device_id_type=MESH,
        )

    own = pltpu.make_async_copy(g_any.at[blk], gs_any.at[0], osem)

    @pl.when(h == 0)
    def _():
        greet([(dp, blk ^ s) for s in range(1, n_blk)])
        own.start()
        for s in range(1, n_blk):
            copy(s).start()

    pack = p_ref.shape[0]
    head = q_ref.shape[0] // pack
    for g in range(pack):
        rows, one = slice(g * head, (g + 1) * head), slice(g, g + 1)
        attend_kernel(
            n_blk,
            len_ref,
            q_ref.at[rows],
            k_ref.at[rows],
            v_ref.at[rows],
            c_ref.at[rows],
            p_ref.at[one],
            il_ref.at[one],
            f_ref.at[one],
        )

    @pl.when(h == pl.num_programs(0) - 1)
    def _():
        own.wait()
        for s in range(1, n_blk):
            copy(s).wait()


def regroup(v, share):
    def slab(c, x, y):
        at = [(z * 8 + y * 4 + x * 2 + c) * share for z in range(4)]
        return jnp.concatenate([v[a : a + share] for a in at], axis=0)

    return [[[slab(c, x, y) for y in range(2)] for x in range(2)] for c in range(2)]


CXY = [(c, x, y) for c in range(2) for x in range(2) for y in range(2)]


class Scatter:
    def __init__(self, source, cols, share, first, out, bufs, place):
        self.source, self.cols, self.share, self.out = source, cols, share, out
        self.b = bufs
        dp, blk = place
        self.c, self.x, self.y, self.z = blk & 1, blk >> 1, dp & 1, dp >> 1
        self.first = first
        ids = {"x": (dp, blk ^ 2), "y": (dp ^ 1, blk)}
        self.mp = self.x if first == "x" else self.y
        self.mq = self.y if first == "x" else self.x
        self.core_id = (dp, blk ^ 1)
        self.p_id = ids[first]
        self.q_id = ids["y" if first == "x" else "x"]
        self.z_ids = [(((self.z + d) & 3) * 2 + self.y, blk) for d in (1, 2, 3)]
        self.chunk = share if share % 16 == 0 else 2 * share

    def remote(self, src, dst, i, where):
        return pltpu.make_async_remote_copy(
            src_ref=src,
            dst_ref=dst,
            send_sem=self.b["send"].at[i],
            recv_sem=self.b["recv"].at[i],
            device_id=where,
            device_id_type=MESH,
        )

    def part(self, c):
        if self.cols is None:
            return self.source.at[c]
        return self.source.at[c, :, :, :, self.cols]

    def core_copy(self):
        return self.remote(self.part(1 - self.c), self.b["r0"], 0, self.core_id)

    def load(self):
        return pltpu.make_async_copy(self.part(self.c), self.b["keep"], self.b["load"])

    def p_copy(self):
        return self.remote(self.b["t1"], self.b["r1"], 1, self.p_id)

    def q_copy(self):
        return self.remote(self.b["t2"], self.b["r2"], 2, self.q_id)

    def z_copies(self):
        return [self.remote(self.b["t3"].at[d], self.b["r3"].at[d], 3 + d, self.z_ids[d]) for d in range(3)]

    def pick(self, ref, a, b, rows):
        return (ref[a, b, rows] if self.first == "x" else ref[b, a, rows]).astype(F32)

    def two(self, a, b, rows):
        own = self.b["keep"] if "keep" in self.b else self.source.at[self.c]
        a, b = (a, b) if self.first == "x" else (b, a)
        return own[a, b, rows] + self.b["r0"][a, b, rows]

    def base(self, a, b, rows):
        if "keep" in self.b:
            own = self.pick(self.b["keep"], a, b, rows)
        else:
            own = (
                self.source[self.c, a, b, rows] if self.first == "x" else self.source[self.c, b, a, rows]
            ).astype(F32)
        return own + self.pick(self.b["r0"], a, b, rows)

    def each(self, fn):
        rows = 4 * self.share

        def step(i, carry):
            fn(i, pl.ds(pl.multiple_of(i * self.chunk, self.chunk), self.chunk))
            return carry

        lax.fori_loop(0, rows // self.chunk, step, 0)

    def stage0(self):
        self.core_copy().start()
        if "keep" in self.b:
            self.load().start()

    def stage1(self):
        if "keep" in self.b:
            self.load().wait()
        self.core_copy().wait()
        for b in range(2):

            def fn(i, rows):
                self.b["t1"][b, rows] = self.two(1 - self.mp, b, rows)

            self.each(fn)
        self.p_copy().start()

    def stage2(self):
        self.p_copy().wait()

        def fn(i, rows):
            v = self.base(self.mp, 1 - self.mq, rows) + self.b["r1"][1 - self.mq, rows].astype(F32)
            self.b["t2"][rows] = v.astype(BF16)

        self.each(fn)
        self.q_copy().start()

    def stage3(self):
        self.q_copy().wait()
        share = self.share
        per = self.chunk // share
        f = self.b["f"]

        def fn(i, rows):
            v = self.base(self.mp, self.mq, rows)
            v = v + self.b["r1"][self.mq, rows].astype(F32) + self.b["r2"][rows].astype(F32)
            for k in range(per):
                f[i * per + k] = v[k * share : (k + 1) * share]

        self.each(fn)
        half = f.shape[2] // 2
        for d in range(3):
            v = f[(self.z + d + 1) & 3]
            if per > 1:
                v = jnp.concatenate([v[:, :half], v[:, half:]], axis=0)
            self.b["t3"][d] = v.astype(BF16)
        for copy in self.z_copies():
            copy.start()

    def stage4(self):
        for copy in self.z_copies():
            copy.wait()
        v = self.b["f"][self.z]
        for d in range(3):
            w = self.b["r3"][d].astype(F32)
            if self.chunk > self.share:
                w = jnp.concatenate([w[: self.share], w[self.share :]], axis=1)
            v = v + w
        self.out(v)


class ScatterLate(Scatter):
    def x_copy(self):
        return self.remote(self.b["f2"].at[1 - self.x], self.b["rx"], 2, self.q_id)

    def stage2(self):
        self.p_copy().wait()
        share = self.share
        per = self.chunk // share
        f = self.b["f"]
        for x in range(2):

            def fn(i, rows, x=x):
                v = self.base(self.mp, x, rows) + self.b["r1"][x, rows].astype(F32)
                for k in range(per):
                    f[x, i * per + k] = v[k * share : (k + 1) * share]

            self.each(fn)
        for d in range(3):
            at = (self.z + d + 1) & 3
            self.b["t3"][d] = jnp.concatenate([f[0, at], f[1, at]], axis=0).astype(BF16)
        for copy in self.z_copies():
            copy.start()

    def stage3(self):
        for copy in self.z_copies():
            copy.wait()
        for x in range(2):
            v = self.b["f"][x, self.z]
            for d in range(3):
                v = v + self.b["r3"][d].astype(F32)[x * self.share : (x + 1) * self.share]
            self.b["f2"][x] = v
        self.x_copy().start()

    def stage4(self):
        self.x_copy().wait()
        self.out(self.b["f2"][self.x] + self.b["rx"][...])


def scatter_scratch(share, cols, in_hbm, late):
    rows = 4 * share
    slab = (share, cols) if share % 16 == 0 else (2 * share, cols // 2)
    bufs = {
        "r0": pltpu.VMEM((2, 2, rows, cols), BF16),
        "t1": pltpu.VMEM((2, rows, cols), BF16),
        "r1": pltpu.VMEM((2, rows, cols), BF16),
        "t2": pltpu.VMEM((rows, cols), BF16),
        "r2": pltpu.VMEM((rows, cols), BF16),
        "t3": pltpu.VMEM((3,) + slab, BF16),
        "r3": pltpu.VMEM((3,) + slab, BF16),
        "f": pltpu.VMEM((4, share, cols), F32),
        "send": pltpu.SemaphoreType.DMA((6,)),
        "recv": pltpu.SemaphoreType.DMA((6,)),
    }
    if late:
        del bufs["t2"], bufs["r2"]
        bufs["t3"] = pltpu.VMEM((3, 2 * share, cols), BF16)
        bufs["r3"] = pltpu.VMEM((3, 2 * share, cols), BF16)
        bufs["f"] = pltpu.VMEM((2, 4, share, cols), F32)
        bufs["f2"] = pltpu.VMEM((2, share, cols), F32)
        bufs["rx"] = pltpu.VMEM((share, cols), F32)
    if in_hbm:
        bufs["keep"] = pltpu.VMEM((2, 2, rows, cols), BF16)
        bufs["load"] = pltpu.SemaphoreType.DMA
    return bufs


def ffn_kernel(n_blk, *refs):
    x_ref, g = refs[:2]
    (ct_ref, il_ref, wo_ref, bo_ref, gain_ref, bias_ref, win_ref, bin_ref, wout_ref, bout_ref) = refs[2:12]
    rest = refs[12:]
    outs = rest[:n_blk]
    (gwout_ref, gwin_ref, gbin_ref, dmid_ref, dot_ref, gwo_ref, vec_ref) = rest[n_blk : n_blk + 7]
    mid, n2, n2t, acc_o, acc_d, act, dpre = rest[n_blk + 7 :]
    tok = outs[0].shape[0]
    j = pl.program_id(0)

    @pl.when(j == 0)
    def _():
        for s in range(n_blk):
            sl = slice(s * tok, (s + 1) * tok)
            m = x_ref[sl].astype(F32) + dot(ct_ref[:, sl], wo_ref[...], TN) + bo_ref[...]
            mid[sl] = m
            acc_o[sl] = m + bout_ref[...]
            acc_d[sl] = jnp.zeros_like(m)
            n, _ = center(m)
            nb = (n * gain_ref[...] + bias_ref[...]).astype(BF16)
            n2[sl] = nb
            n2t[:, sl] = nb.T

    bin_grad = None
    for s in range(n_blk):
        sl = slice(s * tok, (s + 1) * tok)
        pre = dot(n2[sl], win_ref[...]) + bin_ref[...]
        phi, slope = gate(pre)
        a = (pre * phi).astype(BF16)
        dact = dot(g[sl], wout_ref[...], NT)
        dp = (dact * (phi + slope)).astype(BF16)
        act[sl] = a
        dpre[sl] = dp
        col = jnp.sum(dp.astype(F32), axis=0, keepdims=True)
        bin_grad = col if bin_grad is None else bin_grad + col
        acc_o[sl] += dot(a, wout_ref[...])
        acc_d[sl] += dot(dp, win_ref[...], NT)
    gbin_ref[...] = bin_grad
    gwout_ref[...] = dot(act[...], g[...], TN).astype(BF16)
    gwin_ref[...] = dot(n2t[...], dpre[...]).astype(BF16)

    @pl.when(j == pl.num_programs(0) - 1)
    def _():
        head = wo_ref.shape[0] // H
        sums = [None] * 4
        for s in range(n_blk):
            sl = slice(s * tok, (s + 1) * tok)
            outs[s][...] = acc_o[sl].astype(BF16)
            n, rstd = center(mid[sl])
            e = acc_d[sl]
            gf = g[sl].astype(F32)
            f = e * gain_ref[...]
            dm = gf + rstd * (
                f - jnp.mean(f, axis=-1, keepdims=True) - n * jnp.mean(f * n, axis=-1, keepdims=True)
            )
            dmid_ref[sl] = dm
            db = dm.astype(BF16)
            n2[sl] = db
            for i, term in enumerate((gf, e * n, e, db.astype(F32))):
                col = jnp.sum(term, axis=0, keepdims=True)
                sums[i] = col if sums[i] is None else sums[i] + col
            dc = dot(wo_ref[...], db, NT)
            for h in range(H):
                hs = slice(h * head, (h + 1) * head)
                dot_ref[hs, sl] = (dc[hs] * il_ref[h, :, sl]).astype(BF16)
        for i in range(4):
            vec_ref[i : i + 1] = sums[i]
        gwo_ref[...] = dot(ct_ref[...], n2[...]).astype(BF16)


def attend_back_kernel(
    scale, n_blk, p_ref, q_ref, k_ref, v_ref, do_ref, c_ref, f_ref, dq_ref, dk_ref, dv_ref, ds, doi
):
    dq_ref[...], dk_ref[...], dv_ref[...] = attend_back_head(
        scale, n_blk, p_ref, q_ref[...], k_ref[...], v_ref[...], do_ref[...], c_ref[...], f_ref, ds, doi
    )


def input_kernel(n_blk, x_ref, dmid_ref, gain_ref, dq_ref, dk_ref, dv_ref, wq_ref, wk_ref, wv_ref, *rest):
    outs = rest[:n_blk]
    vec_ref = rest[n_blk]
    tok = outs[0].shape[0]
    sums = [None] * 2
    for s in range(n_blk):
        sl = slice(s * tok, (s + 1) * tok)
        et = dot(wq_ref[...], dq_ref[:, sl]) + dot(wk_ref[...], dk_ref[:, sl]) + dot(wv_ref[...], dv_ref[:, sl])
        e = et.T
        n, rstd = center(x_ref[sl].astype(F32))
        f = e * gain_ref[...]
        dx = dmid_ref[sl] + rstd * (
            f - jnp.mean(f, axis=-1, keepdims=True) - n * jnp.mean(f * n, axis=-1, keepdims=True)
        )
        outs[s][...] = dx.astype(BF16)
        for i, term in enumerate((e * n, e)):
            col = jnp.sum(term, axis=0, keepdims=True)
            sums[i] = col if sums[i] is None else sums[i] + col
    for i in range(2):
        vec_ref[i : i + 1] = sums[i]


def qkv_grad_kernel(nt_ref, dq_ref, dk_ref, dv_ref, gq_ref, gk_ref, gv_ref, vec_ref):
    nt = nt_ref[...]
    ones = jnp.ones((8, nt.shape[1]), BF16)
    gq_ref[...] = dot(nt, dq_ref[...], NT).astype(BF16)
    gk_ref[...] = dot(nt, dk_ref[...], NT).astype(BF16)
    gv_ref[...] = dot(nt, dv_ref[...], NT).astype(BF16)
    vec_ref[0:1] = dot(ones, dq_ref[...], NT)[:1]
    vec_ref[1:2] = dot(ones, dv_ref[...], NT)[:1]


def ffn_host_kernel(names, n_blk, *refs):
    r = dict(zip(names, refs))
    i = pl.program_id(0)
    j = i & 3
    dp = lax.axis_index("dp")
    blk = lax.axis_index("blk")
    core, y = blk & 1, dp & 1
    mid, acc, n2, n2t, act, gp, gw, r0, t1, r1 = [
        r[k] for k in ("mid", "acc", "n2", "n2t", "act", "gp", "gw", "r0", "t1", "r1")
    ]
    g, win, wout, ct = r["gbuf"], r["win"], r["wout"], r["ct"]
    g_load = pltpu.make_async_copy(r["g"], g, r["lsem"].at[3])
    seq, width = mid.shape
    tok = seq // n_blk
    tile = act.shape[1]
    share_f = gw.shape[4]
    rows = [slice(s * tok, (s + 1) * tok) for s in range(n_blk)]

    def core_copy(plane):
        return pltpu.make_async_remote_copy(
            src_ref=gw.at[1 - core, :, :, plane],
            dst_ref=r0.at[:, :, plane],
            send_sem=r["csend"].at[plane],
            recv_sem=r["crecv"].at[plane],
            device_id=(dp, blk ^ 1),
            device_id_type=MESH,
        )

    def y_copy(plane):
        return pltpu.make_async_remote_copy(
            src_ref=t1.at[:, plane],
            dst_ref=r1.at[:, plane],
            send_sem=r["ysend"].at[plane],
            recv_sem=r["yrecv"].at[plane],
            device_id=(dp ^ 1, blk),
            device_id_type=MESH,
        )

    def y_start(plane):
        core_copy(plane).wait()
        for x in range(2):
            t1[x, plane] = gw[core, x, 1 - y, plane] + r0[x, 1 - y, plane]
        y_copy(plane).start()

    def out_copy(s):
        src, dst = r["obuf"].at[s], r["output"].at[blk]
        if s == 0:
            return pltpu.make_async_copy(src, dst, r["lsem"].at[0])
        return pltpu.make_async_remote_copy(
            src_ref=src,
            dst_ref=dst,
            send_sem=r["osend"].at[s - 1],
            recv_sem=r["orecv"].at[s - 1],
            device_id=(dp, blk ^ s),
            device_id_type=MESH,
        )

    @pl.when(i == 0)
    def _():
        g_load.start()
        greet([(dp, blk ^ 1), (dp, blk ^ 2), (dp, blk ^ 3), (dp ^ 1, blk)])
        bins = as_row(r["bin"])
        for k in range(4):
            r["bins"][k] = bins[:, k * tile : (k + 1) * tile]
        for sl in rows:
            m = r["x"][sl].astype(F32) + dot(ct[:, sl], r["wo"][...], TN) + as_row(r["bo"])
            mid[sl] = m
            acc[sl] = m + as_row(r["bout"])
            n, _ = center(m)
            nb = (n * as_row(r["gain"]) + as_row(r["bias"])).astype(BF16)
            n2[sl] = nb
            n2t[:, sl] = nb.T

    @pl.when(i < 4)
    def _():
        ahead = dot(n2[rows[0]], win[...])
        for s, sl in enumerate(rows):
            pre = ahead + r["bins"][j]
            if s + 1 < n_blk:
                ahead = dot(n2[rows[s + 1]], win[...])
            phi, slope = gate(pre)
            a = (pre * phi).astype(BF16)
            act[sl] = a
            gp[j, sl] = (phi + slope).astype(BF16)
            acc[sl] += dot(a, wout[...])

        @pl.when(i > 0)
        def _():
            y_start(j - 1)

        @pl.when(i == 0)
        def _():
            g_load.wait()

        v = dot(act[...], g[...], TN)
        for c, x, yy in CXY:
            at = (yy * 4 + x * 2 + c) * share_f
            gw[c, x, yy, j] = v[at : at + share_f].astype(BF16)
        core_copy(j).start()

    @pl.when(i == 4)
    def _():
        for s in range(n_blk - 1, -1, -1):
            r["obuf"][s] = acc[rows[s]].astype(BF16)
            out_copy(s).start()
            acc[rows[s]] = jnp.zeros((tok, width), F32)

    @pl.when(i >= 4)
    def _():
        total = None
        ahead = dot(g[rows[0]], wout[...], NT)
        for s, sl in enumerate(rows):
            d = (ahead * gp[j, sl].astype(F32)).astype(BF16)
            if s + 1 < n_blk:
                ahead = dot(g[rows[s + 1]], wout[...], NT)
            act[sl] = d
            col = jnp.sum(d.astype(F32), axis=0, keepdims=True)
            total = col if total is None else total + col
            acc[sl] += dot(d, win[...], NT)
        r["bing"][j] = total

        @pl.when(i == 4)
        def _():
            y_start(3)

        v = regroup(dot(n2t[...], act[...]), width // 32)
        for c, x, yy in CXY:
            r["gwin"][c, x, yy] = v[c][x][yy].astype(BF16)

    @pl.when(i == 7)
    def _():
        head = width // H
        sums = [None] * 4
        for sl in rows:
            n, rstd = center(mid[sl])
            e = acc[sl]
            gf = g[sl].astype(F32)
            f = e * as_row(r["gain"])
            dm = gf + rstd * (
                f - jnp.mean(f, axis=-1, keepdims=True) - n * jnp.mean(f * n, axis=-1, keepdims=True)
            )
            mid[sl] = dm
            db = dm.astype(BF16)
            n2[sl] = db
            for k, term in enumerate((gf, e * n, e, db.astype(F32))):
                col = jnp.sum(term, axis=0, keepdims=True)
                sums[k] = col if sums[k] is None else sums[k] + col
            dc = dot(r["wo"][...], db, NT)
            for h in range(H):
                hs = slice(h * head, (h + 1) * head)
                r["dot"][hs, sl] = (dc[hs] * r["il"][h, :, sl]).astype(BF16)
        save = pltpu.make_async_copy(mid, r["dmid"], r["lsem"].at[1])
        save.start()
        vec = r["vec"]
        for k in range(4):
            vec[k : k + 1] = sums[k]
            vec[4 + k : 5 + k] = r["bing"][k]
        v = regroup(dot(ct[...], n2[...]), width // 32)
        for c, x, yy in CXY:
            r["gwo"][c, x, yy] = v[c][x][yy].astype(BF16)
        for k in range(4):
            y_copy(k).wait()

        def step(k, carry):
            for x in range(2):
                v = gw[core, x, y, k].astype(F32) + r0[x, y, k].astype(F32) + r1[x, k].astype(F32)
                t1[x, k] = v.astype(BF16)
            return carry

        lax.fori_loop(0, 4, step, 0)
        part = pltpu.make_async_copy(t1, r["part"], r["lsem"].at[2])
        part.start()
        for s in range(n_blk):
            out_copy(s).wait()
        save.wait()
        part.wait()


class Resume:
    def __init__(self, r, place):
        dp, blk = place
        self.r = r
        self.x, self.y, self.z = blk >> 1, dp & 1, dp >> 1
        self.ids = [(((self.z + d) & 3) * 2 + self.y, blk) for d in (1, 2, 3)] + [(dp, blk ^ 2)]

    def remote(self, src, dst, i):
        return pltpu.make_async_remote_copy(
            src_ref=src,
            dst_ref=dst,
            send_sem=self.r["w_send"].at[i],
            recv_sem=self.r["w_recv"].at[i],
            device_id=self.ids[i],
            device_id_type=MESH,
        )

    def z_copies(self):
        return [
            self.remote(self.r["part"].at[:, (self.z + d + 1) & 3], self.r["w_rz"].at[d], d) for d in range(3)
        ]

    def load(self):
        return pltpu.make_async_copy(self.r["part"].at[:, self.z], self.r["w_keep"], self.r["lsem"].at[0])

    def x_copy(self):
        return self.remote(self.r["w_t"], self.r["w_rx"], 3)

    def stage0(self):
        for copy in self.z_copies():
            copy.start()
        self.load().start()

    def stage1(self):
        self.load().wait()
        for copy in self.z_copies():
            copy.wait()
        for k in range(2):
            v = self.r["w_keep"][k].astype(F32)
            for d in range(3):
                v = v + self.r["w_rz"][d, k].astype(F32)
            self.r["w_f"][k] = v
        self.r["w_t"][...] = self.r["w_f"][1 - self.x].astype(BF16)
        self.x_copy().start()

    def stage2(self):
        self.x_copy().wait()
        self.r["s_wout"][...] = self.r["w_f"][self.x] + self.r["w_rx"][...].astype(F32)


def finish_kernel(n_big, *refs):
    src, va, vb = refs[:n_big], refs[n_big], refs[n_big + 1]
    dst, small = refs[n_big + 2 : 2 * n_big + 2], refs[2 * n_big + 2 :]
    for a, b in zip(src[:2], dst[:2]):
        b[...] = a[...]

    @pl.when(pl.program_id(0) == 0)
    def _():
        for a, b in zip(src[2:], dst[2:]):
            b[...] = a[...]
        me = lax.axis_index("dp") * lax.axis_size("blk") + lax.axis_index("blk")
        share = small[0].shape[0]
        wide = small[8].shape[0]
        width = va.shape[1]
        shift = lax.rem(width - me * share, width)
        moved = pltpu.roll(va[...], shift, 1)
        for k in range(4):
            small[k][...] = moved[k, :share]
        lines = vb[...]
        moved = pltpu.roll(lines, shift, 1)
        for i, k in enumerate((3, 1, 2, 0)):
            small[4 + i][...] = moved[k, :share]
        each = width // wide
        moved = pltpu.roll(lines, lax.rem(width - lax.rem(me, each) * wide, width), 1)
        row = 4 + lax.div(me, each)
        pick = lax.broadcasted_iota(jnp.int32, moved.shape, 0) == row
        small[8][...] = jnp.sum(jnp.where(pick, moved, 0.0), axis=0)[:wide]


def back_kernel(scale, names, tasks, plan, *refs):
    r = dict(zip(names, refs))
    h = pl.program_id(0)
    dp = lax.axis_index("dp")
    blk = lax.axis_index("blk")
    place = (dp, blk)
    n_blk, tok, width = r["xs"].shape
    seq = n_blk * tok
    head = width // H
    dcat, wcat, gq, vec = r["dcat"], r["wcat"], r["gq"], r["va"]

    def put(ref, cols):
        def out(v):
            if cols is None:
                ref[...] = v
            else:
                ref[:, cols] = v

        return out

    jobs = {}
    for name, source, index, cols, share, first, out, out_cols in tasks:
        ref = r[source] if index is None else r[source].at[index]
        bufs = {k: r[name + "_" + k] for k in SCATTER_KEYS if name + "_" + k in r}
        if isinstance(out, tuple):
            outs = [put(r[o], out_cols) for o in out]

            def sink(v, outs=outs):
                each = v.shape[1] // len(outs)
                for i, o in enumerate(outs):
                    o(v[:, i * each : (i + 1) * each])

        else:
            sink = put(r[out], out_cols)
        kind = ScatterLate if first == "late" else Scatter
        jobs[name] = kind(ref, cols, share, "y" if first == "late" else first, sink, bufs, place)

    jobs["wout"] = Resume(r, place)

    def spread(src, dst, sems, s):
        return pltpu.make_async_remote_copy(
            src_ref=src.at[s],
            dst_ref=dst.at[blk],
            send_sem=sems[0].at[s - 1],
            recv_sem=sems[1].at[s - 1],
            device_id=(dp, blk ^ s),
            device_id_type=MESH,
        )

    def in_copy(s):
        if s == 0:
            return pltpu.make_async_copy(r["dx"].at[0], r["input_grad"].at[blk], r["lsem"].at[1])
        return spread(r["dx"], r["input_grad"], (r["isend"], r["irecv"]), s)

    def nt_load():
        return pltpu.make_async_copy(r["nt"], r["ntbuf"], r["lsem"].at[7])

    def loads():
        pairs = [(r["xs"], r["xbuf"]), (r["dmid"], r["dmbuf"])]
        pairs += [(r[w], wcat.at[:, i * width : (i + 1) * width]) for i, w in enumerate(("wq", "wk", "wv"))]
        return [pltpu.make_async_copy(a, b, r["lsem"].at[2 + i]) for i, (a, b) in enumerate(pairs)]

    z, y = dp >> 1, dp & 1
    z_ids = [(((z + d) & 3) * 2 + y, blk) for d in (1, 2, 3)]
    vec_ids = [z_ids, [(dp ^ 1, blk)], [(dp, blk ^ 1), (dp, blk ^ 2), (dp, blk ^ 3)]]

    def vec_copies(name, stage):
        at = (0, 3, 4)[stage]
        return [
            pltpu.make_async_remote_copy(
                src_ref=r[name],
                dst_ref=r[name + "_r"].at[at + d],
                send_sem=r[name + "_send"].at[at + d],
                recv_sem=r[name + "_recv"].at[at + d],
                device_id=where,
                device_id_type=MESH,
            )
            for d, where in enumerate(vec_ids[stage])
        ]

    def vec_step(name, stage):
        if stage > 0:
            copies = vec_copies(name, stage - 1)
            for copy in copies:
                copy.wait()
            at = (0, 3, 4)[stage - 1]
            r[name][...] += sum(r[name + "_r"][at + d] for d in range(len(copies)))
        if stage < 3:
            for copy in vec_copies(name, stage):
                copy.start()

    def input_piece(s, sums):
        sl = slice(s * tok, (s + 1) * tok)
        e = r["ebuf"][s & 1].T
        n, rstd = center(r["xbuf"][s].astype(F32))
        f = e * as_row(r["gain"])
        dx = r["dmbuf"][sl] + rstd * (
            f - jnp.mean(f, axis=-1, keepdims=True) - n * jnp.mean(f * n, axis=-1, keepdims=True)
        )
        r["dx"][s] = dx.astype(BF16)
        in_copy(s).start()
        new = [jnp.sum(t, axis=0, keepdims=True) for t in (e * n, e)]
        return new if sums is None else [a + b for a, b in zip(sums, new)]

    @pl.when(h == 0)
    def _():
        greet(
            [(dp, blk ^ 1), (dp, blk ^ 2), (dp, blk ^ 3), (dp ^ 1, blk)]
            + [(((z + d) & 3) * 2 + y, blk) for d in (1, 2, 3)]
        )
        nt_load().start()
        for load in loads():
            load.start()
        vec[...] = jnp.zeros_like(vec)
        r["vb"][...] = r["vec_in"][...]

    def act(item):
        kind, what = item
        if kind in ("va", "vb"):
            vec_step(kind, what)
        else:
            getattr(jobs[kind], "stage%d" % what)()

    for at in range(H):
        if plan.get(at):

            @pl.when(h == at)
            def _(at=at):
                for item in plan[at]:
                    act(item)

    @pl.when(h < H)
    def _():
        base = pl.multiple_of(h * head, head)
        dq, dk, dv = attend_back_head(
            scale,
            n_blk,
            r["p"],
            r["q"][...],
            r["k"][...],
            r["v"][...],
            r["do"][...],
            r["ct"][...],
            r["tops"],
            r["ds"],
            r["doi"],
        )
        dcat[pl.ds(base, head)] = dq
        dcat[pl.ds(base + width, head)] = dk
        dcat[pl.ds(base + 2 * width, head)] = dv

    n_group = gq.shape[0]
    cols = width // n_group
    for gi in range(n_group):

        @pl.when(h == (gi + 1) * (H // n_group) - 1)
        def _(gi=gi):
            if gi == 0:
                nt_load().wait()
            nt = r["ntbuf"][...]
            ones = jnp.ones((8, seq), BF16)
            for t in range(3):
                part = dcat[t * width + gi * cols : t * width + (gi + 1) * cols]
                v = regroup(dot(nt, part, NT), width // 32)
                for c, x, y in CXY:
                    gq[gi, c, x, y, :, t * cols : (t + 1) * cols] = v[c][x][y].astype(BF16)
                if t != 1:
                    row = 2 if t == 0 else 3
                    vec[row : row + 1, gi * cols : (gi + 1) * cols] = dot(ones, part, NT)[:1]
            jobs["q%d" % gi].stage0()

    @pl.when(h == H)
    def _():
        sums = None
        for load in loads():
            load.wait()
        for item in plan["tail"]:
            kind, what = item
            if kind == "mul":
                r["ebuf"][what & 1] = dot(wcat[...], dcat[:, what * tok : (what + 1) * tok])
            elif kind == "piece":
                sums = input_piece(what, sums)
                if what == 0:
                    vec[0:1] = sums[0]
                    vec[1:2] = sums[1]
            else:
                act(item)
        r["va_out"][...] = vec[...]
        r["vb_out"][...] = r["vb"][...]
        for s in range(n_blk):
            in_copy(s).wait()


PLAN = {
    0: [("wout", 0), ("a2", 0), ("b2", 0), ("wo", 0)],
    2: [("a2", 1), ("b2", 1)],
    3: [("wo", 1)],
    5: [("q0", 1)],
    7: [("a2", 2), ("b2", 2)],
    9: [("q1", 1)],
    10: [("q0", 2), ("wo", 2)],
    11: [("a2", 3), ("b2", 3), ("wout", 1)],
    "tail": [
        ("mul", 3),
        ("mul", 2),
        ("piece", 3),
        ("q2", 1),
        ("mul", 1),
        ("piece", 2),
        ("mul", 0),
        ("piece", 1),
        ("piece", 0),
        ("vb", 0),
        ("va", 0),
        ("q2", 2),
        ("q1", 2),
        ("wo", 3),
        ("q0", 3),
        ("vb", 1),
        ("va", 1),
        ("wout", 2),
        ("a2", 4),
        ("vb", 2),
        ("va", 2),
        ("q1", 3),
        ("b2", 4),
        ("q2", 3),
        ("vb", 3),
        ("va", 3),
        ("wo", 4),
        ("q0", 4),
        ("q1", 4),
        ("q2", 4),
    ],
}

SCATTER_KEYS = ("f2", "rx", "r0", "t1", "r1", "t2", "r2", "t3", "r3", "f", "send", "recv", "keep", "load")


def body(
    inputs,
    lengths,
    out_grad,
    ln1_gain,
    ln1_bias,
    w_query,
    b_query,
    w_key,
    w_value,
    b_value,
    w_output,
    b_output,
    ln2_gain,
    ln2_bias,
    w_in,
    b_in,
    w_out,
    b_out,
):
    n_seq, tok, width = inputs.shape
    n_blk = lax.axis_size("blk")
    n_dp = lax.axis_size("dp")
    n_dev = n_blk * n_dp
    assert n_seq == n_blk
    seq = tok * n_blk
    hidden = w_in.shape[1]
    head = width // H
    scale = head ** (-0.5)
    blk = lax.axis_index("blk")
    me = lax.axis_index("dp") * n_blk + blk

    def swap(v, s):
        return lax.ppermute(v, "blk", [(i, i ^ s) for i in range(n_blk)])

    def collect(pieces):
        back = [pieces[0]] + [swap(pieces[s], s) for s in range(1, n_blk)]
        out = jnp.zeros((n_seq, tok, width), BF16)
        for s in range(n_blk):
            out = lax.dynamic_update_index_in_dim(out, back[s], blk ^ s, 0)
        return out

    row = lambda v: v.astype(F32).reshape(1, -1)


    sds = jax.ShapeDtypeStruct
    piece = full((tok, width))
    wide = full((width, seq))
    n_col = 3
    cols = width // n_col
    strip = pl.BlockSpec((cols, seq), lambda j: (j, 0))
    anywhere = pl.BlockSpec(memory_space=pl.ANY)
    vmem = pl.BlockSpec(memory_space=pltpu.VMEM)
    xs, nt, qt, kt, vt = pl.pallas_call(
        functools.partial(qkv_spread_kernel, scale * LOG2E, n_blk),
        in_specs=[anywhere, vmem, vmem, anywhere, vmem, anywhere, anywhere, vmem],
        out_specs=[anywhere] * 5,
        out_shape=[sds((n_blk, tok, width), BF16)] + [sds((width, seq), BF16)] * 4,
        scratch_shapes=[
            pltpu.VMEM((n_blk, tok, width), BF16),
            pltpu.VMEM((3, width, width), BF16),
            pltpu.VMEM((3, width, width), BF16),
            pltpu.VMEM((width, seq), BF16),
            pltpu.VMEM((3, width, seq), BF16),
            pltpu.SemaphoreType.DMA((n_blk - 1,)),
            pltpu.SemaphoreType.DMA((n_blk - 1,)),
            pltpu.SemaphoreType.DMA((3,)),
            pltpu.SemaphoreType.DMA((n_blk, 5)),
            pltpu.SemaphoreType.DMA,
        ],
        compiler_params=params(collective_id=0, has_side_effects=True),
        cost_estimate=cost(3 * seq * width * width, 14 * seq * width),
        name="qkv",
    )(inputs, ln1_gain, ln1_bias, w_query, b_query, w_key, w_value, b_value)

    per_head = pl.BlockSpec((head, seq), lambda h: (h, 0))
    per_square = pl.BlockSpec((1, seq, seq), lambda h: (h, 0, 0))
    per_block = pl.BlockSpec((1, n_blk, seq), lambda h: (h, 0, 0))
    pack = 2
    heads = lambda *shape: pl.BlockSpec(shape, lambda h: (h,) + (0,) * (len(shape) - 1))
    strips = heads(pack * head, seq)
    ct, probs, inv_total, tops, gs = pl.pallas_call(
        functools.partial(attend_spread_kernel, n_blk),
        grid=(H // pack,),
        in_specs=[pl.BlockSpec(memory_space=pltpu.SMEM), strips, strips, strips, anywhere],
        out_specs=[strips, heads(pack, seq, seq), heads(pack, 1, seq), heads(pack, n_blk, seq), anywhere],
        out_shape=[
            sds((width, seq), BF16),
            sds((H, seq, seq), BF16),
            sds((H, 1, seq), F32),
            sds((H, n_blk, seq), F32),
            sds((n_blk, tok, width), BF16),
        ],
        scratch_shapes=[
            pltpu.SemaphoreType.DMA((n_blk - 1,)),
            pltpu.SemaphoreType.DMA((n_blk - 1,)),
            pltpu.SemaphoreType.DMA,
        ],
        compiler_params=params(collective_id=1, has_side_effects=True),
        cost_estimate=cost(8 * seq * seq * width, 2 * H * seq * seq, H * seq * seq),
        name="attend",
    )(lengths, qt, kt, vt, out_grad)

    if n_dp == 8 and n_blk == 4 and width % 768 == 0 and hidden == 4 * width:
        share, share_f = width // n_dev, hidden // n_dev
        tile = hidden // 4
        once = lambda shape: pl.BlockSpec(shape, lambda i: (0,) * len(shape), pipeline_mode=pl.Buffered(1))
        vec_rows = 8
        ins = {
            "x": (xs.reshape(seq, width), once((seq, width))),
            "g": (gs.reshape(seq, width), anywhere),
            "ct": (ct, once((width, seq))),
            "il": (inv_total, once((H, 1, seq))),
            "wo": (w_output, once((width, width))),
            "bo": (b_output, once((width,))),
            "gain": (ln2_gain, once((width,))),
            "bias": (ln2_bias, once((width,))),
            "bout": (b_out, once((width,))),
            "bin": (b_in, once((hidden,))),
            "win": (w_in, pl.BlockSpec((width, tile), lambda i: (0, i % 4))),
            "wout": (w_out, pl.BlockSpec((tile, width), lambda i: (i % 4, 0))),
        }
        outs = {
            "output": (sds((n_seq, tok, width), BF16), anywhere),
            "dmid": (sds((seq, width), F32), anywhere),
            "dot": (sds((width, seq), BF16), once((width, seq))),
            "gwin": (
                sds((2, 2, 2, 4 * share, hidden), BF16),
                pl.BlockSpec((2, 2, 2, 4 * share, tile), lambda i: (0, 0, 0, 0, jnp.maximum(i - 4, 0))),
            ),
            "gwo": (sds((2, 2, 2, 4 * share, width), BF16), once((2, 2, 2, 4 * share, width))),
            "part": (sds((2, 4, share_f, width), BF16), anywhere),
            "vec": (sds((vec_rows, width), F32), once((vec_rows, width))),
        }
        scratch = {
            "gbuf": pltpu.VMEM((seq, width), BF16),
            "mid": pltpu.VMEM((seq, width), F32),
            "acc": pltpu.VMEM((seq, width), F32),
            "n2": pltpu.VMEM((seq, width), BF16),
            "n2t": pltpu.VMEM((width, seq), BF16),
            "act": pltpu.VMEM((seq, tile), BF16),
            "gp": pltpu.VMEM((4, seq, tile), BF16),
            "bins": pltpu.VMEM((4, 1, tile), F32),
            "bing": pltpu.VMEM((4, 1, tile), F32),
            "obuf": pltpu.VMEM((n_blk, tok, width), BF16),
            "gw": pltpu.VMEM((2, 2, 2, 4, share_f, width), BF16),
            "r0": pltpu.VMEM((2, 2, 4, share_f, width), BF16),
            "t1": pltpu.VMEM((2, 4, share_f, width), BF16),
            "r1": pltpu.VMEM((2, 4, share_f, width), BF16),
            "csend": pltpu.SemaphoreType.DMA((4,)),
            "crecv": pltpu.SemaphoreType.DMA((4,)),
            "ysend": pltpu.SemaphoreType.DMA((4,)),
            "yrecv": pltpu.SemaphoreType.DMA((4,)),
            "osend": pltpu.SemaphoreType.DMA((n_blk - 1,)),
            "orecv": pltpu.SemaphoreType.DMA((n_blk - 1,)),
            "lsem": pltpu.SemaphoreType.DMA((4,)),
        }
        names = tuple(ins) + tuple(outs) + tuple(scratch)
        ffn = pl.pallas_call(
            functools.partial(ffn_host_kernel, names, n_blk),
            grid=(8,),
            in_specs=[v[1] for v in ins.values()],
            out_specs=[v[1] for v in outs.values()],
            out_shape=[v[0] for v in outs.values()],
            scratch_shapes=list(scratch.values()),
            compiler_params=pltpu.CompilerParams(
                vmem_limit_bytes=62 * 2**20, collective_id=3, has_side_effects=True
            ),
            name="ffn",
        )(*[v[0] for v in ins.values()])
        ffn = dict(zip(outs, ffn))
        tasks = (
            ("a2", "gwin", None, slice(0, hidden // 2), share, "x", "s_win", slice(0, hidden // 2)),
            ("b2", "gwin", None, slice(hidden // 2, hidden), share, "y", "s_win", slice(hidden // 2, hidden)),
            ("wo", "gwo", None, None, share, "x", "s_wo", None),
        ) + tuple(
            (
                "q%d" % i,
                "gq",
                i,
                None,
                share,
                ("y", "x", "late")[i],
                ("s_wq", "s_wk", "s_wv"),
                slice(i * cols, (i + 1) * cols),
            )
            for i in range(n_col)
        )
        sizes = {"a2": hidden // 2, "b2": hidden // 2, "wo": width}
        plan = PLAN
        last = lambda shape: pl.BlockSpec(shape, lambda h: (jnp.minimum(h, H - 1),) + (0,) * (len(shape) - 1))
        strip_h = last((head, seq))
        ins = {
            "p": (probs, last((1, seq, seq))),
            "q": (qt, strip_h),
            "k": (kt, strip_h),
            "v": (vt, strip_h),
            "do": (ffn["dot"], strip_h),
            "ct": (ct, strip_h),
            "tops": (tops, last((1, n_blk, seq))),
            "nt": (nt, anywhere),
            "gain": (ln1_gain, full((width,))),
            "vec_in": (ffn["vec"], full((vec_rows, width))),
            "xs": (xs, anywhere),
            "dmid": (ffn["dmid"], anywhere),
            "wq": (w_query, anywhere),
            "wk": (w_key, anywhere),
            "wv": (w_value, anywhere),
            "part": (ffn["part"], anywhere),
            "gwin": (ffn["gwin"], anywhere),
            "gwo": (ffn["gwo"], anywhere),
        }
        outs = {
            "input_grad": (sds((n_seq, tok, width), BF16), anywhere),
            "s_wq": (sds((share, width), F32), full((share, width))),
            "s_wk": (sds((share, width), F32), full((share, width))),
            "s_wv": (sds((share, width), F32), full((share, width))),
            "s_wo": (sds((share, width), F32), full((share, width))),
            "s_win": (sds((share, hidden), F32), full((share, hidden))),
            "s_wout": (sds((share_f, width), F32), full((share_f, width))),
            "va_out": (sds((8, width), F32), full((8, width))),
            "vb_out": (sds((8, width), F32), full((8, width))),
        }
        scratch = {
            "ds": pltpu.VMEM((seq, seq), BF16),
            "doi": pltpu.VMEM((n_blk, head, seq), BF16),
            "dcat": pltpu.VMEM((3 * width, seq), BF16),
            "wcat": pltpu.VMEM((width, 3 * width), BF16),
            "gq": pltpu.VMEM((n_col, 2, 2, 2, 4 * share, 3 * cols), BF16),
            "va": pltpu.VMEM((8, width), F32),
            "vb": pltpu.VMEM((8, width), F32),
            "va_r": pltpu.VMEM((7, 8, width), F32),
            "vb_r": pltpu.VMEM((7, 8, width), F32),
            "ebuf": pltpu.VMEM((2, width, tok), F32),
            "ntbuf": pltpu.VMEM((width, seq), BF16),
            "xbuf": pltpu.VMEM((n_blk, tok, width), BF16),
            "dmbuf": pltpu.VMEM((seq, width), F32),
            "dx": pltpu.VMEM((n_blk, tok, width), BF16),
            "lsem": pltpu.SemaphoreType.DMA((8,)),
            "va_send": pltpu.SemaphoreType.DMA((7,)),
            "va_recv": pltpu.SemaphoreType.DMA((7,)),
            "vb_send": pltpu.SemaphoreType.DMA((7,)),
            "vb_recv": pltpu.SemaphoreType.DMA((7,)),
            "w_keep": pltpu.VMEM((2, share_f, width), BF16),
            "w_rz": pltpu.VMEM((3, 2, share_f, width), BF16),
            "w_f": pltpu.VMEM((2, share_f, width), F32),
            "w_t": pltpu.VMEM((share_f, width), BF16),
            "w_rx": pltpu.VMEM((share_f, width), BF16),
            "w_send": pltpu.SemaphoreType.DMA((4,)),
            "w_recv": pltpu.SemaphoreType.DMA((4,)),
            "isend": pltpu.SemaphoreType.DMA((n_blk - 1,)),
            "irecv": pltpu.SemaphoreType.DMA((n_blk - 1,)),
        }
        for name, source, _, _, task_share, first, _, _ in tasks:
            for k, v in scatter_scratch(task_share, sizes.get(name, width), source != "gq", first == "late").items():
                scratch[name + "_" + k] = v
        names = tuple(ins) + tuple(outs) + tuple(scratch)
        got = pl.pallas_call(
            functools.partial(back_kernel, scale, names, tasks, plan),
            grid=(H + 1,),
            in_specs=[v[1] for v in ins.values()],
            out_specs=[v[1] for v in outs.values()],
            out_shape=[v[0] for v in outs.values()],
            scratch_shapes=list(scratch.values()),
            compiler_params=pltpu.CompilerParams(
                vmem_limit_bytes=60 * 2**20, collective_id=2, has_side_effects=True
            ),
            name="back",
        )(*[v[0] for v in ins.values()])
        got = dict(zip(outs, got))
        big = [ffn["output"], got["input_grad"]] + [
            got[k] for k in ("s_wq", "s_wk", "s_wv", "s_wo", "s_win", "s_wout")
        ]
        part = pl.BlockSpec((n_blk // 2, tok, width), lambda i: (i, 0, 0))
        flat = [sds(v.shape, v.dtype) for v in big]
        fin = pl.pallas_call(
            functools.partial(finish_kernel, len(big)),
            grid=(2,),
            in_specs=[part] * 2 + [full(v.shape) for v in big[2:]] + [full((8, width))] * 2,
            out_specs=[part] * 2 + [full(v.shape) for v in big[2:]] + [full((share,))] * 8 + [full((share_f,))],
            out_shape=flat + [sds((share,), F32)] * 8 + [sds((share_f,), F32)],
            name="finish",
        )(*big, got["va_out"], got["vb_out"])
        output, input_grad, s_wq, s_wk, s_wv, s_wo, s_win, s_wout = fin[: len(big)]
        g1, b1, bq, bv, bo_sum, g2, b2, bout_sum, bin_sum = fin[len(big) :]
        return (
            output,
            input_grad,
            g1,
            b1,
            s_wq,
            bq,
            s_wk,
            s_wv,
            bv,
            s_wo,
            bo_sum,
            g2,
            b2,
            s_win,
            bin_sum,
            s_wout,
            bout_sum,
        )

    n_tile = 4
    tile = hidden // n_tile
    result = pl.pallas_call(
        functools.partial(ffn_kernel, n_blk),
        grid=(n_tile,),
        in_specs=[full((seq, width))] * 2
        + [
            wide,
            full((H, 1, seq)),
            full((width, width)),
            full((1, width)),
            full((1, width)),
            full((1, width)),
            pl.BlockSpec((width, tile), lambda j: (0, j)),
            pl.BlockSpec((1, tile), lambda j: (0, j)),
            pl.BlockSpec((tile, width), lambda j: (j, 0)),
            full((1, width)),
        ],
        out_specs=[piece] * n_blk
        + [
            pl.BlockSpec((tile, width), lambda j: (j, 0)),
            pl.BlockSpec((width, tile), lambda j: (0, j)),
            pl.BlockSpec((1, tile), lambda j: (0, j)),
            full((seq, width)),
            wide,
            full((width, width)),
            full((8, width)),
        ],
        out_shape=[sds((tok, width), BF16)] * n_blk
        + [
            sds((hidden, width), BF16),
            sds((width, hidden), BF16),
            sds((1, hidden), F32),
            sds((seq, width), F32),
            sds((width, seq), BF16),
            sds((width, width), BF16),
            sds((8, width), F32),
        ],
        scratch_shapes=[
            pltpu.VMEM((seq, width), F32),
            pltpu.VMEM((seq, width), BF16),
            pltpu.VMEM((width, seq), BF16),
            pltpu.VMEM((seq, width), F32),
            pltpu.VMEM((seq, width), F32),
            pltpu.VMEM((seq, tile), BF16),
            pltpu.VMEM((seq, tile), BF16),
        ],
        compiler_params=params(),
        cost_estimate=cost(8 * seq * width * hidden, 8 * width * hidden),
        name="ffn",
    )(
        xs.reshape(seq, width),
        gs.reshape(seq, width),
        ct,
        inv_total,
        w_output,
        row(b_output),
        row(ln2_gain),
        row(ln2_bias),
        w_in,
        row(b_in),
        w_out,
        row(b_out),
    )
    out_pieces = result[:n_blk]
    g_wout, g_win, g_bin, dmid, dct, g_wo, vec2 = result[n_blk:]

    bits = (n_dev - 1).bit_length()
    assert n_dev == 1 << bits

    def scatter(grad, order, wire):
        share = grad.shape[0] // n_dev
        order = list(order) + [b for b in range(bits) if b not in order]
        axes = list(range(bits - 1, -1, -1))
        terms = [grad.reshape((2,) * bits + (share,) + grad.shape[1:])]
        for b in order:
            at = axes.index(b)
            axes.pop(at)
            mine = (me >> b) & 1
            send = None
            keep = []
            for t in terms:
                other = lax.dynamic_index_in_dim(t, 1 - mine, at, keepdims=False)
                send = other.astype(F32) if send is None else send + other.astype(F32)
                keep.append(lax.dynamic_index_in_dim(t, mine, at, keepdims=False))
            got = lax.ppermute(send.astype(wire), ("dp", "blk"), [(i, i ^ (1 << b)) for i in range(n_dev)])
            terms = keep + [got]
        total = terms[0].astype(F32)
        for t in terms[1:]:
            total = total + t.astype(F32)
        return total

    s_wout = scatter(g_wout, (0, 1, 2, 3, 4), BF16)
    s_win = scatter(g_win, (0, 2, 1, 3, 4), BF16)
    s_wo = scatter(g_wo, (0, 3, 4, 1, 2), BF16)
    output = collect(out_pieces)

    dqt, dkt, dvt = pl.pallas_call(
        functools.partial(attend_back_kernel, scale, n_blk),
        grid=(H,),
        in_specs=[per_square] + [per_head] * 5 + [per_block],
        out_specs=[per_head] * 3,
        out_shape=[sds((width, seq), BF16)] * 3,
        scratch_shapes=[pltpu.VMEM((seq, seq), BF16), pltpu.VMEM((n_blk, head, seq), BF16)],
        compiler_params=params(),
        cost_estimate=cost(10 * seq * seq * width, 2 * H * seq * seq),
        name="attend_back",
    )(probs, qt, kt, vt, dct, ct, tops)

    result = pl.pallas_call(
        functools.partial(input_kernel, n_blk),
        in_specs=[full((seq, width))] * 2
        + [full((1, width)), wide, wide, wide]
        + [full((width, width))] * 3,
        out_specs=[piece] * n_blk + [full((8, width))],
        out_shape=[sds((tok, width), BF16)] * n_blk + [sds((8, width), F32)],
        compiler_params=params(),
        cost_estimate=cost(3 * seq * width * width, 14 * seq * width),
        name="input_grad",
    )(xs.reshape(seq, width), dmid, row(ln1_gain), dqt, dkt, dvt, w_query, w_key, w_value)
    input_grad = collect(result[:n_blk])
    vec1 = result[n_blk]

    col = pl.BlockSpec((width, cols), lambda j: (0, j))
    g_wq, g_wk, g_wv, vecq = pl.pallas_call(
        qkv_grad_kernel,
        grid=(n_col,),
        in_specs=[wide, strip, strip, strip],
        out_specs=[col, col, col, pl.BlockSpec((8, cols), lambda j: (0, j))],
        out_shape=[sds((width, width), BF16)] * 3 + [sds((8, width), F32)],
        compiler_params=params(),
        cost_estimate=cost(3 * seq * width * width, 14 * seq * width),
        name="qkv_grad",
    )(nt, dqt, dkt, dvt)
    s_wq = scatter(g_wq, (0, 1, 2, 3, 4), BF16)
    s_wk = scatter(g_wk, (0, 2, 3, 4, 1), BF16)
    s_wv = scatter(g_wv, (0, 3, 4, 1, 2), BF16)

    vectors = [vec1[0], vec1[1], vecq[0], vecq[1], vec2[3], vec2[1], vec2[2], g_bin[0], vec2[0]]
    packed = jnp.concatenate([v.reshape(n_dev, -1) for v in vectors], axis=1)
    packed = scatter(packed, (0, 1, 2, 3, 4), F32).reshape(-1)
    parts = []
    at = 0
    for v in vectors:
        size = v.shape[0] // n_dev
        parts.append(packed[at : at + size])
        at += size
    p_ln1g, p_ln1b, p_bq, p_bv, p_bo, p_ln2g, p_ln2b, p_bin, p_bout = parts
    return (
        output,
        input_grad,
        p_ln1g,
        p_ln1b,
        s_wq,
        p_bq,
        s_wk,
        s_wv,
        p_bv,
        s_wo,
        p_bo,
        p_ln2g,
        p_ln2b,
        s_win,
        p_bin,
        s_wout,
        p_bout,
    )


def solution(mesh):
    whole = P(("dp", "blk"))
    rows = P(("dp", "blk"), None)
    tokens = P("dp", "blk", None)
    in_specs = (tokens, P("dp"), tokens) + (P(),) * 15
    out_specs = (
        tokens,
        tokens,
        whole,
        whole,
        rows,
        whole,
        rows,
        rows,
        whole,
        rows,
        whole,
        whole,
        whole,
        rows,
        whole,
        rows,
        whole,
    )
    return jax.shard_map(body, mesh=mesh, in_specs=in_specs, out_specs=out_specs, check_vma=False)
```

```python
import functools

import jax
import jax.numpy as jnp
from jax import lax
from jax.experimental import pallas as pl
from jax.experimental.pallas import tpu as pltpu
from jax.sharding import PartitionSpec as P

H = 12
EPS = 1e-05
LOG2E = 1.4426950408889634
LN2 = 0.6931471805599453
INV_SQRT_2PI = 0.3989422804014327
SQRT_HALF = 0.7071067811865476
F32 = jnp.float32
BF16 = jnp.bfloat16
VMEM_LIMIT = 56 * 2**20

NN = (((1,), (0,)), ((), ()))
NT = (((1,), (1,)), ((), ()))
TN = (((0,), (0,)), ((), ()))

def dot(left, right, dims=NN):
    return lax.dot_general(left, right, dims, preferred_element_type=F32)


def params(**kw):
    return pltpu.CompilerParams(vmem_limit_bytes=VMEM_LIMIT, **kw)


def cost(macs, nbytes, exps=0):
    return pl.CostEstimate(flops=2 * macs, bytes_accessed=nbytes, transcendentals=exps)


def full(shape):
    return pl.BlockSpec(shape, lambda *_: (0,) * len(shape))


def as_row(ref):
    return ref[...].astype(F32)[None, :]


def center(v):
    mean = jnp.mean(v, axis=-1, keepdims=True)
    cent = v - mean
    var = jnp.mean(cent * cent, axis=-1, keepdims=True)
    rstd = lax.rsqrt(var + EPS)
    return cent * rstd, rstd


def gate(u):
    phi = 0.5 + 0.5 * lax.erf(u * SQRT_HALF)
    e = jnp.exp2(u * u * (-0.5 * LOG2E))
    return phi, u * e * INV_SQRT_2PI


def attend_kernel(n_blk, len_ref, q_ref, k_ref, v_ref, c_ref, p_ref, il_ref, f_ref):
    seq = q_ref.shape[1]
    tok = seq // n_blk
    blk = lax.axis_index("blk")
    length = len_ref[blk]
    live = [(blk ^ i) * tok < length for i in range(n_blk)]
    keys, q, v = k_ref[...].T, q_ref[...], v_ref[...]
    m = jnp.full((1, seq), -1e30, F32)
    total = summed = None
    tops = []
    ahead = dot(keys[:tok], q)
    for i in range(n_blk):
        s = ahead
        if i + 1 < n_blk:
            ahead = dot(keys[(i + 1) * tok : (i + 2) * tok], q)
        new = jnp.maximum(m, jnp.where(live[i], jnp.max(s, axis=0, keepdims=True), -1e30))
        p = jnp.exp2(s - jnp.where(live[i], new, 1e30))
        part = jnp.sum(p, axis=0, keepdims=True)
        p = p.astype(BF16)
        p_ref[0, i * tok : (i + 1) * tok] = p
        o = dot(v[:, i * tok : (i + 1) * tok], p)
        if i == 0:
            summed, total = o, part
        else:
            shrink = jnp.exp2(m - new)
            summed, total = summed * shrink + o, total * shrink + part
        m = new
        tops.append(m)
    inv = 1.0 / total
    c_ref[...] = (summed * inv).astype(BF16)
    il_ref[0] = inv
    for i in range(n_blk):
        f_ref[0, i : i + 1] = jnp.exp2(tops[i] - m)


def attend_back_head(scale, n_blk, p_ref, q, k, v, do, ct, f_ref, ds, doi):
    seq = q.shape[1]
    tok = seq // n_blk
    vh = v.T
    do = do.astype(F32)
    delta = jnp.sum(do * ct.astype(F32), axis=0, keepdims=True)
    for i in range(n_blk):
        sl = slice(i * tok, (i + 1) * tok)
        f = f_ref[0, i : i + 1]
        d = (do * f).astype(BF16)
        doi[i] = d
        ds[sl] = (p_ref[0, sl].astype(F32) * (dot(vh[sl], d) - delta * f)).astype(BF16)
    dq = (dot(k, ds[...]) * scale).astype(BF16)
    dv = [dot(p_ref[0, i * tok : (i + 1) * tok], doi[i], NT).T.astype(BF16) for i in range(n_blk)]
    dk = (dot(ds[...], q, NT) * LN2).T.astype(BF16)
    return dq, dk, jnp.concatenate(dv, axis=1)


MESH = pl.DeviceIdType.MESH


def greet(partners):
    barrier = pltpu.get_barrier_semaphore()
    for where in partners:
        pl.semaphore_signal(barrier, inc=1, device_id=where, device_id_type=MESH)
    pl.semaphore_wait(barrier, len(partners))


def qkv_spread_kernel(
    scale,
    n_blk,
    x_any,
    gain,
    bias,
    wq_any,
    bq,
    wk_any,
    wv_any,
    bv,
    xs_any,
    nt_any,
    q_any,
    k_any,
    v_any,
    xbuf,
    wbuf,
    wt,
    nt,
    qkv,
    send,
    recv,
    wsem,
    osem,
    xsem,
):
    tok, width = xbuf.shape[1:]
    dp = lax.axis_index("dp")
    blk = lax.axis_index("blk")
    own = pltpu.make_async_copy(x_any.at[blk], xbuf.at[0], xsem)
    own.start()
    loads = [
        pltpu.make_async_copy(w, wbuf.at[i], wsem.at[i]) for i, w in enumerate((wq_any, wk_any, wv_any))
    ]
    for load in loads:
        load.start()
    greet([(dp, blk ^ s) for s in range(1, n_blk)])
    order = list(range(n_blk - 1, 0, -1))
    copies = {}
    for s in order:
        copies[s] = pltpu.make_async_remote_copy(
            src_ref=x_any.at[blk ^ s],
            dst_ref=xbuf.at[s],
            send_sem=send.at[s - 1],
            recv_sem=recv.at[s - 1],
            device_id=(dp, blk ^ s),
            device_id_type=MESH,
        )
        if s != 2:
            copies[s].start()
    for i, load in enumerate(loads):
        load.wait()
        wt[i] = wbuf[i].T
    cols = jnp.concatenate([as_row(bq), as_row(bv), jnp.zeros((6, width), F32)], axis=0).T
    writes = []
    for s in (0, 1, 3, 2):
        if s == 0:
            own.wait()
        else:
            if s == 3:
                copies[3].wait_send()
                copies[2].start()
            copies[s].wait_recv()
        sl = slice(s * tok, (s + 1) * tok)
        n, _ = center(xbuf[s].astype(F32))
        n = (n * as_row(gain) + as_row(bias)).astype(BF16).T
        nt[:, sl] = n
        qkv[0, :, sl] = ((dot(wt[0], n) + cols[:, :1]) * scale).astype(BF16)
        qkv[1, :, sl] = dot(wt[1], n).astype(BF16)
        qkv[2, :, sl] = (dot(wt[2], n) + cols[:, 1:2]).astype(BF16)
        for i, (src, dst) in enumerate(
            (
                (xbuf.at[s], xs_any.at[s]),
                (nt.at[:, sl], nt_any.at[:, sl]),
                (qkv.at[0, :, sl], q_any.at[:, sl]),
                (qkv.at[1, :, sl], k_any.at[:, sl]),
                (qkv.at[2, :, sl], v_any.at[:, sl]),
            )
        ):
            write = pltpu.make_async_copy(src, dst, osem.at[s, i])
            write.start()
            writes.append(write)
    for s in (1, 2):
        copies[s].wait_send()
    for write in writes:
        write.wait()


def attend_spread_kernel(n_blk, len_ref, q_ref, k_ref, v_ref, g_any, c_ref, p_ref, il_ref, f_ref, gs_any, send, recv, osem):
    h = pl.program_id(0)
    dp = lax.axis_index("dp")
    blk = lax.axis_index("blk")

    def copy(s):
        return pltpu.make_async_remote_copy(
            src_ref=g_any.at[blk ^ s],
            dst_ref=gs_any.at[s],
            send_sem=send.at[s - 1],
            recv_sem=recv.at[s - 1],
            device_id=(dp, blk ^ s),
            device_id_type=MESH,
        )

    own = pltpu.make_async_copy(g_any.at[blk], gs_any.at[0], osem)

    @pl.when(h == 0)
    def _():
        greet([(dp, blk ^ s) for s in range(1, n_blk)])
        own.start()
        for s in range(1, n_blk):
            copy(s).start()

    pack = p_ref.shape[0]
    head = q_ref.shape[0] // pack
    for g in range(pack):
        rows, one = slice(g * head, (g + 1) * head), slice(g, g + 1)
        attend_kernel(
            n_blk,
            len_ref,
            q_ref.at[rows],
            k_ref.at[rows],
            v_ref.at[rows],
            c_ref.at[rows],
            p_ref.at[one],
            il_ref.at[one],
            f_ref.at[one],
        )

    @pl.when(h == pl.num_programs(0) - 1)
    def _():
        own.wait()
        for s in range(1, n_blk):
            copy(s).wait()


def regroup(v, share):
    def slab(c, x, y):
        at = [(z * 8 + y * 4 + x * 2 + c) * share for z in range(4)]
        return jnp.concatenate([v[a : a + share] for a in at], axis=0)

    return [[[slab(c, x, y) for y in range(2)] for x in range(2)] for c in range(2)]


CXY = [(c, x, y) for c in range(2) for x in range(2) for y in range(2)]


class Scatter:
    def __init__(self, source, cols, share, first, out, bufs, place):
        self.source, self.cols, self.share, self.out = source, cols, share, out
        self.b = bufs
        dp, blk = place
        self.c, self.x, self.y, self.z = blk & 1, blk >> 1, dp & 1, dp >> 1
        self.first = first
        ids = {"x": (dp, blk ^ 2), "y": (dp ^ 1, blk)}
        self.mp = self.x if first == "x" else self.y
        self.mq = self.y if first == "x" else self.x
        self.core_id = (dp, blk ^ 1)
        self.p_id = ids[first]
        self.q_id = ids["y" if first == "x" else "x"]
        self.z_ids = [(((self.z + d) & 3) * 2 + self.y, blk) for d in (1, 2, 3)]
        self.chunk = share if share % 16 == 0 else 2 * share

    def remote(self, src, dst, i, where):
        return pltpu.make_async_remote_copy(
            src_ref=src,
            dst_ref=dst,
            send_sem=self.b["send"].at[i],
            recv_sem=self.b["recv"].at[i],
            device_id=where,
            device_id_type=MESH,
        )

    def part(self, c):
        if self.cols is None:
            return self.source.at[c]
        return self.source.at[c, :, :, :, self.cols]

    def core_copy(self):
        return self.remote(self.part(1 - self.c), self.b["r0"], 0, self.core_id)

    def load(self):
        return pltpu.make_async_copy(self.part(self.c), self.b["keep"], self.b["load"])

    def p_copy(self):
        return self.remote(self.b["t1"], self.b["r1"], 1, self.p_id)

    def q_copy(self):
        return self.remote(self.b["t2"], self.b["r2"], 2, self.q_id)

    def z_copies(self):
        return [self.remote(self.b["t3"].at[d], self.b["r3"].at[d], 3 + d, self.z_ids[d]) for d in range(3)]

    def pick(self, ref, a, b, rows):
        return (ref[a, b, rows] if self.first == "x" else ref[b, a, rows]).astype(F32)

    def two(self, a, b, rows):
        own = self.b["keep"] if "keep" in self.b else self.source.at[self.c]
        a, b = (a, b) if self.first == "x" else (b, a)
        return own[a, b, rows] + self.b["r0"][a, b, rows]

    def base(self, a, b, rows):
        if "keep" in self.b:
            own = self.pick(self.b["keep"], a, b, rows)
        else:
            own = (
                self.source[self.c, a, b, rows] if self.first == "x" else self.source[self.c, b, a, rows]
            ).astype(F32)
        return own + self.pick(self.b["r0"], a, b, rows)

    def each(self, fn):
        rows = 4 * self.share

        def step(i, carry):
            fn(i, pl.ds(pl.multiple_of(i * self.chunk, self.chunk), self.chunk))
            return carry

        lax.fori_loop(0, rows // self.chunk, step, 0)

    def stage0(self):
        self.core_copy().start()
        if "keep" in self.b:
            self.load().start()

    def stage1(self):
        if "keep" in self.b:
            self.load().wait()
        self.core_copy().wait()
        for b in range(2):

            def fn(i, rows):
                self.b["t1"][b, rows] = self.two(1 - self.mp, b, rows)

            self.each(fn)
        self.p_copy().start()

    def stage2(self):
        self.p_copy().wait()

        def fn(i, rows):
            v = self.base(self.mp, 1 - self.mq, rows) + self.b["r1"][1 - self.mq, rows].astype(F32)
            self.b["t2"][rows] = v.astype(BF16)

        self.each(fn)
        self.q_copy().start()

    def stage3(self):
        self.q_copy().wait()
        share = self.share
        per = self.chunk // share
        f = self.b["f"]

        def fn(i, rows):
            v = self.base(self.mp, self.mq, rows)
            v = v + self.b["r1"][self.mq, rows].astype(F32) + self.b["r2"][rows].astype(F32)
            for k in range(per):
                f[i * per + k] = v[k * share : (k + 1) * share]

        self.each(fn)
        half = f.shape[2] // 2
        for d in range(3):
            v = f[(self.z + d + 1) & 3]
            if per > 1:
                v = jnp.concatenate([v[:, :half], v[:, half:]], axis=0)
            self.b["t3"][d] = v.astype(BF16)
        for copy in self.z_copies():
            copy.start()

    def stage4(self):
        for copy in self.z_copies():
            copy.wait()
        v = self.b["f"][self.z]
        for d in range(3):
            w = self.b["r3"][d].astype(F32)
            if self.chunk > self.share:
                w = jnp.concatenate([w[: self.share], w[self.share :]], axis=1)
            v = v + w
        self.out(v)


class ScatterLate(Scatter):
    def x_copy(self):
        return self.remote(self.b["f2"].at[1 - self.x], self.b["rx"], 2, self.q_id)

    def stage2(self):
        self.p_copy().wait()
        share = self.share
        per = self.chunk // share
        f = self.b["f"]
        for x in range(2):

            def fn(i, rows, x=x):
                v = self.base(self.mp, x, rows) + self.b["r1"][x, rows].astype(F32)
                for k in range(per):
                    f[x, i * per + k] = v[k * share : (k + 1) * share]

            self.each(fn)
        for d in range(3):
            at = (self.z + d + 1) & 3
            self.b["t3"][d] = jnp.concatenate([f[0, at], f[1, at]], axis=0).astype(BF16)
        for copy in self.z_copies():
            copy.start()

    def stage3(self):
        for copy in self.z_copies():
            copy.wait()
        for x in range(2):
            v = self.b["f"][x, self.z]
            for d in range(3):
                v = v + self.b["r3"][d].astype(F32)[x * self.share : (x + 1) * self.share]
            self.b["f2"][x] = v
        self.x_copy().start()

    def stage4(self):
        self.x_copy().wait()
        self.out(self.b["f2"][self.x] + self.b["rx"][...])


def scatter_scratch(share, cols, in_hbm, late):
    rows = 4 * share
    slab = (share, cols) if share % 16 == 0 else (2 * share, cols // 2)
    bufs = {
        "r0": pltpu.VMEM((2, 2, rows, cols), BF16),
        "t1": pltpu.VMEM((2, rows, cols), BF16),
        "r1": pltpu.VMEM((2, rows, cols), BF16),
        "t2": pltpu.VMEM((rows, cols), BF16),
        "r2": pltpu.VMEM((rows, cols), BF16),
        "t3": pltpu.VMEM((3,) + slab, BF16),
        "r3": pltpu.VMEM((3,) + slab, BF16),
        "f": pltpu.VMEM((4, share, cols), F32),
        "send": pltpu.SemaphoreType.DMA((6,)),
        "recv": pltpu.SemaphoreType.DMA((6,)),
    }
    if late:
        del bufs["t2"], bufs["r2"]
        bufs["t3"] = pltpu.VMEM((3, 2 * share, cols), BF16)
        bufs["r3"] = pltpu.VMEM((3, 2 * share, cols), BF16)
        bufs["f"] = pltpu.VMEM((2, 4, share, cols), F32)
        bufs["f2"] = pltpu.VMEM((2, share, cols), F32)
        bufs["rx"] = pltpu.VMEM((share, cols), F32)
    if in_hbm:
        bufs["keep"] = pltpu.VMEM((2, 2, rows, cols), BF16)
        bufs["load"] = pltpu.SemaphoreType.DMA
    return bufs


def ffn_kernel(n_blk, *refs):
    x_ref, g = refs[:2]
    (ct_ref, il_ref, wo_ref, bo_ref, gain_ref, bias_ref, win_ref, bin_ref, wout_ref, bout_ref) = refs[2:12]
    rest = refs[12:]
    outs = rest[:n_blk]
    (gwout_ref, gwin_ref, gbin_ref, dmid_ref, dot_ref, gwo_ref, vec_ref) = rest[n_blk : n_blk + 7]
    mid, n2, n2t, acc_o, acc_d, act, dpre = rest[n_blk + 7 :]
    tok = outs[0].shape[0]
    j = pl.program_id(0)

    @pl.when(j == 0)
    def _():
        for s in range(n_blk):
            sl = slice(s * tok, (s + 1) * tok)
            m = x_ref[sl].astype(F32) + dot(ct_ref[:, sl], wo_ref[...], TN) + bo_ref[...]
            mid[sl] = m
            acc_o[sl] = m + bout_ref[...]
            acc_d[sl] = jnp.zeros_like(m)
            n, _ = center(m)
            nb = (n * gain_ref[...] + bias_ref[...]).astype(BF16)
            n2[sl] = nb
            n2t[:, sl] = nb.T

    bin_grad = None
    for s in range(n_blk):
        sl = slice(s * tok, (s + 1) * tok)
        pre = dot(n2[sl], win_ref[...]) + bin_ref[...]
        phi, slope = gate(pre)
        a = (pre * phi).astype(BF16)
        dact = dot(g[sl], wout_ref[...], NT)
        dp = (dact * (phi + slope)).astype(BF16)
        act[sl] = a
        dpre[sl] = dp
        col = jnp.sum(dp.astype(F32), axis=0, keepdims=True)
        bin_grad = col if bin_grad is None else bin_grad + col
        acc_o[sl] += dot(a, wout_ref[...])
        acc_d[sl] += dot(dp, win_ref[...], NT)
    gbin_ref[...] = bin_grad
    gwout_ref[...] = dot(act[...], g[...], TN).astype(BF16)
    gwin_ref[...] = dot(n2t[...], dpre[...]).astype(BF16)

    @pl.when(j == pl.num_programs(0) - 1)
    def _():
        head = wo_ref.shape[0] // H
        sums = [None] * 4
        for s in range(n_blk):
            sl = slice(s * tok, (s + 1) * tok)
            outs[s][...] = acc_o[sl].astype(BF16)
            n, rstd = center(mid[sl])
            e = acc_d[sl]
            gf = g[sl].astype(F32)
            f = e * gain_ref[...]
            dm = gf + rstd * (
                f - jnp.mean(f, axis=-1, keepdims=True) - n * jnp.mean(f * n, axis=-1, keepdims=True)
            )
            dmid_ref[sl] = dm
            db = dm.astype(BF16)
            n2[sl] = db
            for i, term in enumerate((gf, e * n, e, db.astype(F32))):
                col = jnp.sum(term, axis=0, keepdims=True)
                sums[i] = col if sums[i] is None else sums[i] + col
            dc = dot(wo_ref[...], db, NT)
            for h in range(H):
                hs = slice(h * head, (h + 1) * head)
                dot_ref[hs, sl] = (dc[hs] * il_ref[h, :, sl]).astype(BF16)
        for i in range(4):
            vec_ref[i : i + 1] = sums[i]
        gwo_ref[...] = dot(ct_ref[...], n2[...]).astype(BF16)


def attend_back_kernel(
    scale, n_blk, p_ref, q_ref, k_ref, v_ref, do_ref, c_ref, f_ref, dq_ref, dk_ref, dv_ref, ds, doi
):
    dq_ref[...], dk_ref[...], dv_ref[...] = attend_back_head(
        scale, n_blk, p_ref, q_ref[...], k_ref[...], v_ref[...], do_ref[...], c_ref[...], f_ref, ds, doi
    )


def input_kernel(n_blk, x_ref, dmid_ref, gain_ref, dq_ref, dk_ref, dv_ref, wq_ref, wk_ref, wv_ref, *rest):
    outs = rest[:n_blk]
    vec_ref = rest[n_blk]
    tok = outs[0].shape[0]
    sums = [None] * 2
    for s in range(n_blk):
        sl = slice(s * tok, (s + 1) * tok)
        et = dot(wq_ref[...], dq_ref[:, sl]) + dot(wk_ref[...], dk_ref[:, sl]) + dot(wv_ref[...], dv_ref[:, sl])
        e = et.T
        n, rstd = center(x_ref[sl].astype(F32))
        f = e * gain_ref[...]
        dx = dmid_ref[sl] + rstd * (
            f - jnp.mean(f, axis=-1, keepdims=True) - n * jnp.mean(f * n, axis=-1, keepdims=True)
        )
        outs[s][...] = dx.astype(BF16)
        for i, term in enumerate((e * n, e)):
            col = jnp.sum(term, axis=0, keepdims=True)
            sums[i] = col if sums[i] is None else sums[i] + col
    for i in range(2):
        vec_ref[i : i + 1] = sums[i]


def qkv_grad_kernel(nt_ref, dq_ref, dk_ref, dv_ref, gq_ref, gk_ref, gv_ref, vec_ref):
    nt = nt_ref[...]
    ones = jnp.ones((8, nt.shape[1]), BF16)
    gq_ref[...] = dot(nt, dq_ref[...], NT).astype(BF16)
    gk_ref[...] = dot(nt, dk_ref[...], NT).astype(BF16)
    gv_ref[...] = dot(nt, dv_ref[...], NT).astype(BF16)
    vec_ref[0:1] = dot(ones, dq_ref[...], NT)[:1]
    vec_ref[1:2] = dot(ones, dv_ref[...], NT)[:1]


def ffn_host_kernel(names, n_blk, *refs):
    r = dict(zip(names, refs))
    i = pl.program_id(0)
    j = i & 3
    dp = lax.axis_index("dp")
    blk = lax.axis_index("blk")
    core, y = blk & 1, dp & 1
    mid, acc, n2, n2t, act, gp, gw, r0, t1, r1 = [
        r[k] for k in ("mid", "acc", "n2", "n2t", "act", "gp", "gw", "r0", "t1", "r1")
    ]
    g, win, wout, ct = r["gbuf"], r["win"], r["wout"], r["ct"]
    g_load = pltpu.make_async_copy(r["g"], g, r["lsem"].at[3])
    seq, width = mid.shape
    tok = seq // n_blk
    tile = act.shape[1]
    share_f = gw.shape[4]
    rows = [slice(s * tok, (s + 1) * tok) for s in range(n_blk)]

    def core_copy(plane):
        return pltpu.make_async_remote_copy(
            src_ref=gw.at[1 - core, :, :, plane],
            dst_ref=r0.at[:, :, plane],
            send_sem=r["csend"].at[plane],
            recv_sem=r["crecv"].at[plane],
            device_id=(dp, blk ^ 1),
            device_id_type=MESH,
        )

    def y_copy(plane):
        return pltpu.make_async_remote_copy(
            src_ref=t1.at[:, plane],
            dst_ref=r1.at[:, plane],
            send_sem=r["ysend"].at[plane],
            recv_sem=r["yrecv"].at[plane],
            device_id=(dp ^ 1, blk),
            device_id_type=MESH,
        )

    def y_start(plane):
        core_copy(plane).wait()
        for x in range(2):
            t1[x, plane] = gw[core, x, 1 - y, plane] + r0[x, 1 - y, plane]
        y_copy(plane).start()

    def out_copy(s):
        src, dst = r["obuf"].at[s], r["output"].at[blk]
        if s == 0:
            return pltpu.make_async_copy(src, dst, r["lsem"].at[0])
        return pltpu.make_async_remote_copy(
            src_ref=src,
            dst_ref=dst,
            send_sem=r["osend"].at[s - 1],
            recv_sem=r["orecv"].at[s - 1],
            device_id=(dp, blk ^ s),
            device_id_type=MESH,
        )

    @pl.when(i == 0)
    def _():
        g_load.start()
        greet([(dp, blk ^ 1), (dp, blk ^ 2), (dp, blk ^ 3), (dp ^ 1, blk)])
        bins = as_row(r["bin"])
        for k in range(4):
            r["bins"][k] = bins[:, k * tile : (k + 1) * tile]
        for sl in rows:
            m = r["x"][sl].astype(F32) + dot(ct[:, sl], r["wo"][...], TN) + as_row(r["bo"])
            mid[sl] = m
            acc[sl] = m + as_row(r["bout"])
            n, _ = center(m)
            nb = (n * as_row(r["gain"]) + as_row(r["bias"])).astype(BF16)
            n2[sl] = nb
            n2t[:, sl] = nb.T

    @pl.when(i < 4)
    def _():
        ahead = dot(n2[rows[0]], win[...])
        for s, sl in enumerate(rows):
            pre = ahead + r["bins"][j]
            if s + 1 < n_blk:
                ahead = dot(n2[rows[s + 1]], win[...])
            phi, slope = gate(pre)
            a = (pre * phi).astype(BF16)
            act[sl] = a
            gp[j, sl] = (phi + slope).astype(BF16)
            acc[sl] += dot(a, wout[...])

        @pl.when(i > 0)
        def _():
            y_start(j - 1)

        @pl.when(i == 0)
        def _():
            g_load.wait()

        v = dot(act[...], g[...], TN)
        for c, x, yy in CXY:
            at = (yy * 4 + x * 2 + c) * share_f
            gw[c, x, yy, j] = v[at : at + share_f].astype(BF16)
        core_copy(j).start()

    @pl.when(i == 4)
    def _():
        for s in range(n_blk - 1, -1, -1):
            r["obuf"][s] = acc[rows[s]].astype(BF16)
            out_copy(s).start()
            acc[rows[s]] = jnp.zeros((tok, width), F32)

    @pl.when(i >= 4)
    def _():
        total = None
        ahead = dot(g[rows[0]], wout[...], NT)
        for s, sl in enumerate(rows):
            d = (ahead * gp[j, sl].astype(F32)).astype(BF16)
            if s + 1 < n_blk:
                ahead = dot(g[rows[s + 1]], wout[...], NT)
            act[sl] = d
            col = jnp.sum(d.astype(F32), axis=0, keepdims=True)
            total = col if total is None else total + col
            acc[sl] += dot(d, win[...], NT)
        r["bing"][j] = total

        @pl.when(i == 4)
        def _():
            y_start(3)

        v = regroup(dot(n2t[...], act[...]), width // 32)
        for c, x, yy in CXY:
            r["gwin"][c, x, yy] = v[c][x][yy].astype(BF16)

    @pl.when(i == 7)
    def _():
        head = width // H
        sums = [None] * 4
        for sl in rows:
            n, rstd = center(mid[sl])
            e = acc[sl]
            gf = g[sl].astype(F32)
            f = e * as_row(r["gain"])
            dm = gf + rstd * (
                f - jnp.mean(f, axis=-1, keepdims=True) - n * jnp.mean(f * n, axis=-1, keepdims=True)
            )
            mid[sl] = dm
            db = dm.astype(BF16)
            n2[sl] = db
            for k, term in enumerate((gf, e * n, e, db.astype(F32))):
                col = jnp.sum(term, axis=0, keepdims=True)
                sums[k] = col if sums[k] is None else sums[k] + col
            dc = dot(r["wo"][...], db, NT)
            for h in range(H):
                hs = slice(h * head, (h + 1) * head)
                r["dot"][hs, sl] = (dc[hs] * r["il"][h, :, sl]).astype(BF16)
        save = pltpu.make_async_copy(mid, r["dmid"], r["lsem"].at[1])
        save.start()
        vec = r["vec"]
        for k in range(4):
            vec[k : k + 1] = sums[k]
            vec[4 + k : 5 + k] = r["bing"][k]
        v = regroup(dot(ct[...], n2[...]), width // 32)
        for c, x, yy in CXY:
            r["gwo"][c, x, yy] = v[c][x][yy].astype(BF16)
        for k in range(4):
            y_copy(k).wait()

        def step(k, carry):
            for x in range(2):
                v = gw[core, x, y, k].astype(F32) + r0[x, y, k].astype(F32) + r1[x, k].astype(F32)
                t1[x, k] = v.astype(BF16)
            return carry

        lax.fori_loop(0, 4, step, 0)
        part = pltpu.make_async_copy(t1, r["part"], r["lsem"].at[2])
        part.start()
        for s in range(n_blk):
            out_copy(s).wait()
        save.wait()
        part.wait()


class Resume:
    def __init__(self, r, place):
        dp, blk = place
        self.r = r
        self.x, self.y, self.z = blk >> 1, dp & 1, dp >> 1
        self.ids = [(((self.z + d) & 3) * 2 + self.y, blk) for d in (1, 2, 3)] + [(dp, blk ^ 2)]

    def remote(self, src, dst, i):
        return pltpu.make_async_remote_copy(
            src_ref=src,
            dst_ref=dst,
            send_sem=self.r["w_send"].at[i],
            recv_sem=self.r["w_recv"].at[i],
            device_id=self.ids[i],
            device_id_type=MESH,
        )

    def z_copies(self):
        return [
            self.remote(self.r["part"].at[:, (self.z + d + 1) & 3], self.r["w_rz"].at[d], d) for d in range(3)
        ]

    def load(self):
        return pltpu.make_async_copy(self.r["part"].at[:, self.z], self.r["w_keep"], self.r["lsem"].at[0])

    def x_copy(self):
        return self.remote(self.r["w_t"], self.r["w_rx"], 3)

    def stage0(self):
        for copy in self.z_copies():
            copy.start()
        self.load().start()

    def stage1(self):
        self.load().wait()
        for copy in self.z_copies():
            copy.wait()
        for k in range(2):
            v = self.r["w_keep"][k].astype(F32)
            for d in range(3):
                v = v + self.r["w_rz"][d, k].astype(F32)
            self.r["w_f"][k] = v
        self.r["w_t"][...] = self.r["w_f"][1 - self.x].astype(BF16)
        self.x_copy().start()

    def stage2(self):
        self.x_copy().wait()
        self.r["s_wout"][...] = self.r["w_f"][self.x] + self.r["w_rx"][...].astype(F32)


def finish_kernel(n_big, *refs):
    src, va, vb = refs[:n_big], refs[n_big], refs[n_big + 1]
    dst, small = refs[n_big + 2 : 2 * n_big + 2], refs[2 * n_big + 2 :]
    for a, b in zip(src[:2], dst[:2]):
        b[...] = a[...]

    @pl.when(pl.program_id(0) == 0)
    def _():
        for a, b in zip(src[2:], dst[2:]):
            b[...] = a[...]
        me = lax.axis_index("dp") * lax.axis_size("blk") + lax.axis_index("blk")
        share = small[0].shape[0]
        wide = small[8].shape[0]
        width = va.shape[1]
        shift = lax.rem(width - me * share, width)
        moved = pltpu.roll(va[...], shift, 1)
        for k in range(4):
            small[k][...] = moved[k, :share]
        lines = vb[...]
        moved = pltpu.roll(lines, shift, 1)
        for i, k in enumerate((3, 1, 2, 0)):
            small[4 + i][...] = moved[k, :share]
        each = width // wide
        moved = pltpu.roll(lines, lax.rem(width - lax.rem(me, each) * wide, width), 1)
        row = 4 + lax.div(me, each)
        pick = lax.broadcasted_iota(jnp.int32, moved.shape, 0) == row
        small[8][...] = jnp.sum(jnp.where(pick, moved, 0.0), axis=0)[:wide]


def back_kernel(scale, names, tasks, plan, *refs):
    r = dict(zip(names, refs))
    h = pl.program_id(0)
    dp = lax.axis_index("dp")
    blk = lax.axis_index("blk")
    place = (dp, blk)
    n_blk, tok, width = r["xs"].shape
    seq = n_blk * tok
    head = width // H
    dcat, wcat, gq, vec = r["dcat"], r["wcat"], r["gq"], r["va"]

    def put(ref, cols):
        def out(v):
            if cols is None:
                ref[...] = v
            else:
                ref[:, cols] = v

        return out

    jobs = {}
    for name, source, index, cols, share, first, out, out_cols in tasks:
        ref = r[source] if index is None else r[source].at[index]
        bufs = {k: r[name + "_" + k] for k in SCATTER_KEYS if name + "_" + k in r}
        if isinstance(out, tuple):
            outs = [put(r[o], out_cols) for o in out]

            def sink(v, outs=outs):
                each = v.shape[1] // len(outs)
                for i, o in enumerate(outs):
                    o(v[:, i * each : (i + 1) * each])

        else:
            sink = put(r[out], out_cols)
        kind = ScatterLate if first == "late" else Scatter
        jobs[name] = kind(ref, cols, share, "y" if first == "late" else first, sink, bufs, place)

    jobs["wout"] = Resume(r, place)

    def spread(src, dst, sems, s):
        return pltpu.make_async_remote_copy(
            src_ref=src.at[s],
            dst_ref=dst.at[blk],
            send_sem=sems[0].at[s - 1],
            recv_sem=sems[1].at[s - 1],
            device_id=(dp, blk ^ s),
            device_id_type=MESH,
        )

    def in_copy(s):
        if s == 0:
            return pltpu.make_async_copy(r["dx"].at[0], r["input_grad"].at[blk], r["lsem"].at[1])
        return spread(r["dx"], r["input_grad"], (r["isend"], r["irecv"]), s)

    def nt_load():
        return pltpu.make_async_copy(r["nt"], r["ntbuf"], r["lsem"].at[7])

    def loads():
        pairs = [(r["xs"], r["xbuf"]), (r["dmid"], r["dmbuf"])]
        pairs += [(r[w], wcat.at[:, i * width : (i + 1) * width]) for i, w in enumerate(("wq", "wk", "wv"))]
        return [pltpu.make_async_copy(a, b, r["lsem"].at[2 + i]) for i, (a, b) in enumerate(pairs)]

    z, y = dp >> 1, dp & 1
    z_ids = [(((z + d) & 3) * 2 + y, blk) for d in (1, 2, 3)]
    vec_ids = [z_ids, [(dp ^ 1, blk)], [(dp, blk ^ 1), (dp, blk ^ 2), (dp, blk ^ 3)]]

    def vec_copies(name, stage):
        at = (0, 3, 4)[stage]
        return [
            pltpu.make_async_remote_copy(
                src_ref=r[name],
                dst_ref=r[name + "_r"].at[at + d],
                send_sem=r[name + "_send"].at[at + d],
                recv_sem=r[name + "_recv"].at[at + d],
                device_id=where,
                device_id_type=MESH,
            )
            for d, where in enumerate(vec_ids[stage])
        ]

    def vec_step(name, stage):
        if stage > 0:
            copies = vec_copies(name, stage - 1)
            for copy in copies:
                copy.wait()
            at = (0, 3, 4)[stage - 1]
            r[name][...] += sum(r[name + "_r"][at + d] for d in range(len(copies)))
        if stage < 3:
            for copy in vec_copies(name, stage):
                copy.start()

    def input_piece(s, sums):
        sl = slice(s * tok, (s + 1) * tok)
        e = r["ebuf"][s & 1].T
        n, rstd = center(r["xbuf"][s].astype(F32))
        f = e * as_row(r["gain"])
        dx = r["dmbuf"][sl] + rstd * (
            f - jnp.mean(f, axis=-1, keepdims=True) - n * jnp.mean(f * n, axis=-1, keepdims=True)
        )
        r["dx"][s] = dx.astype(BF16)
        in_copy(s).start()
        new = [jnp.sum(t, axis=0, keepdims=True) for t in (e * n, e)]
        return new if sums is None else [a + b for a, b in zip(sums, new)]

    @pl.when(h == 0)
    def _():
        greet(
            [(dp, blk ^ 1), (dp, blk ^ 2), (dp, blk ^ 3), (dp ^ 1, blk)]
            + [(((z + d) & 3) * 2 + y, blk) for d in (1, 2, 3)]
        )
        nt_load().start()
        for load in loads():
            load.start()
        vec[...] = jnp.zeros_like(vec)
        r["vb"][...] = r["vec_in"][...]

    def act(item):
        kind, what = item
        if kind in ("va", "vb"):
            vec_step(kind, what)
        else:
            getattr(jobs[kind], "stage%d" % what)()

    for at in range(H):
        if plan.get(at):

            @pl.when(h == at)
            def _(at=at):
                for item in plan[at]:
                    act(item)

    @pl.when(h < H)
    def _():
        base = pl.multiple_of(h * head, head)
        dq, dk, dv = attend_back_head(
            scale,
            n_blk,
            r["p"],
            r["q"][...],
            r["k"][...],
            r["v"][...],
            r["do"][...],
            r["ct"][...],
            r["tops"],
            r["ds"],
            r["doi"],
        )
        dcat[pl.ds(base, head)] = dq
        dcat[pl.ds(base + width, head)] = dk
        dcat[pl.ds(base + 2 * width, head)] = dv

    n_group = gq.shape[0]
    cols = width // n_group
    for gi in range(n_group):

        @pl.when(h == (gi + 1) * (H // n_group) - 1)
        def _(gi=gi):
            if gi == 0:
                nt_load().wait()
            nt = r["ntbuf"][...]
            ones = jnp.ones((8, seq), BF16)
            for t in range(3):
                part = dcat[t * width + gi * cols : t * width + (gi + 1) * cols]
                v = regroup(dot(nt, part, NT), width // 32)
                for c, x, y in CXY:
                    gq[gi, c, x, y, :, t * cols : (t + 1) * cols] = v[c][x][y].astype(BF16)
                if t != 1:
                    row = 2 if t == 0 else 3
                    vec[row : row + 1, gi * cols : (gi + 1) * cols] = dot(ones, part, NT)[:1]
            jobs["q%d" % gi].stage0()

    @pl.when(h == H)
    def _():
        sums = None
        for load in loads():
            load.wait()
        for item in plan["tail"]:
            kind, what = item
            if kind == "mul":
                r["ebuf"][what & 1] = dot(wcat[...], dcat[:, what * tok : (what + 1) * tok])
            elif kind == "piece":
                sums = input_piece(what, sums)
                if what == 0:
                    vec[0:1] = sums[0]
                    vec[1:2] = sums[1]
            else:
                act(item)
        r["va_out"][...] = vec[...]
        r["vb_out"][...] = r["vb"][...]
        for s in range(n_blk):
            in_copy(s).wait()


PLAN = {
    0: [("wout", 0), ("a2", 0), ("b2", 0), ("wo", 0)],
    2: [("a2", 1), ("b2", 1)],
    3: [("wo", 1)],
    5: [("q0", 1)],
    7: [("a2", 2), ("b2", 2)],
    9: [("q1", 1)],
    10: [("q0", 2), ("wo", 2)],
    11: [("a2", 3), ("b2", 3), ("wout", 1)],
    "tail": [
        ("mul", 3),
        ("mul", 2),
        ("piece", 3),
        ("q2", 1),
        ("mul", 1),
        ("piece", 2),
        ("mul", 0),
        ("piece", 1),
        ("piece", 0),
        ("vb", 0),
        ("va", 0),
        ("q2", 2),
        ("q1", 2),
        ("wo", 3),
        ("q0", 3),
        ("vb", 1),
        ("va", 1),
        ("wout", 2),
        ("a2", 4),
        ("vb", 2),
        ("va", 2),
        ("q1", 3),
        ("b2", 4),
        ("q2", 3),
        ("vb", 3),
        ("va", 3),
        ("wo", 4),
        ("q0", 4),
        ("q1", 4),
        ("q2", 4),
    ],
}

SCATTER_KEYS = ("f2", "rx", "r0", "t1", "r1", "t2", "r2", "t3", "r3", "f", "send", "recv", "keep", "load")


def body(
    inputs,
    lengths,
    out_grad,
    ln1_gain,
    ln1_bias,
    w_query,
    b_query,
    w_key,
    w_value,
    b_value,
    w_output,
    b_output,
    ln2_gain,
    ln2_bias,
    w_in,
    b_in,
    w_out,
    b_out,
):
    n_seq, tok, width = inputs.shape
    n_blk = lax.axis_size("blk")
    n_dp = lax.axis_size("dp")
    n_dev = n_blk * n_dp
    assert n_seq == n_blk
    seq = tok * n_blk
    hidden = w_in.shape[1]
    head = width // H
    scale = head ** (-0.5)
    blk = lax.axis_index("blk")
    me = lax.axis_index("dp") * n_blk + blk

    def swap(v, s):
        return lax.ppermute(v, "blk", [(i, i ^ s) for i in range(n_blk)])

    def collect(pieces):
        back = [pieces[0]] + [swap(pieces[s], s) for s in range(1, n_blk)]
        out = jnp.zeros((n_seq, tok, width), BF16)
        for s in range(n_blk):
            out = lax.dynamic_update_index_in_dim(out, back[s], blk ^ s, 0)
        return out

    row = lambda v: v.astype(F32).reshape(1, -1)


    sds = jax.ShapeDtypeStruct
    piece = full((tok, width))
    wide = full((width, seq))
    n_col = 3
    cols = width // n_col
    strip = pl.BlockSpec((cols, seq), lambda j: (j, 0))
    anywhere = pl.BlockSpec(memory_space=pl.ANY)
    vmem = pl.BlockSpec(memory_space=pltpu.VMEM)
    xs, nt, qt, kt, vt = pl.pallas_call(
        functools.partial(qkv_spread_kernel, scale * LOG2E, n_blk),
        in_specs=[anywhere, vmem, vmem, anywhere, vmem, anywhere, anywhere, vmem],
        out_specs=[anywhere] * 5,
        out_shape=[sds((n_blk, tok, width), BF16)] + [sds((width, seq), BF16)] * 4,
        scratch_shapes=[
            pltpu.VMEM((n_blk, tok, width), BF16),
            pltpu.VMEM((3, width, width), BF16),
            pltpu.VMEM((3, width, width), BF16),
            pltpu.VMEM((width, seq), BF16),
            pltpu.VMEM((3, width, seq), BF16),
            pltpu.SemaphoreType.DMA((n_blk - 1,)),
            pltpu.SemaphoreType.DMA((n_blk - 1,)),
            pltpu.SemaphoreType.DMA((3,)),
            pltpu.SemaphoreType.DMA((n_blk, 5)),
            pltpu.SemaphoreType.DMA,
        ],
        compiler_params=params(collective_id=0, has_side_effects=True),
        cost_estimate=cost(3 * seq * width * width, 14 * seq * width),
        name="qkv",
    )(inputs, ln1_gain, ln1_bias, w_query, b_query, w_key, w_value, b_value)

    per_head = pl.BlockSpec((head, seq), lambda h: (h, 0))
    per_square = pl.BlockSpec((1, seq, seq), lambda h: (h, 0, 0))
    per_block = pl.BlockSpec((1, n_blk, seq), lambda h: (h, 0, 0))
    pack = 3
    heads = lambda *shape: pl.BlockSpec(shape, lambda h: (h,) + (0,) * (len(shape) - 1))
    strips = heads(pack * head, seq)
    ct, probs, inv_total, tops, gs = pl.pallas_call(
        functools.partial(attend_spread_kernel, n_blk),
        grid=(H // pack,),
        in_specs=[pl.BlockSpec(memory_space=pltpu.SMEM), strips, strips, strips, anywhere],
        out_specs=[strips, heads(pack, seq, seq), heads(pack, 1, seq), heads(pack, n_blk, seq), anywhere],
        out_shape=[
            sds((width, seq), BF16),
            sds((H, seq, seq), BF16),
            sds((H, 1, seq), F32),
            sds((H, n_blk, seq), F32),
            sds((n_blk, tok, width), BF16),
        ],
        scratch_shapes=[
            pltpu.SemaphoreType.DMA((n_blk - 1,)),
            pltpu.SemaphoreType.DMA((n_blk - 1,)),
            pltpu.SemaphoreType.DMA,
        ],
        compiler_params=params(collective_id=1, has_side_effects=True),
        cost_estimate=cost(8 * seq * seq * width, 2 * H * seq * seq, H * seq * seq),
        name="attend",
    )(lengths, qt, kt, vt, out_grad)

    if n_dp == 8 and n_blk == 4 and width % 768 == 0 and hidden == 4 * width:
        share, share_f = width // n_dev, hidden // n_dev
        tile = hidden // 4
        once = lambda shape: pl.BlockSpec(shape, lambda i: (0,) * len(shape), pipeline_mode=pl.Buffered(1))
        vec_rows = 8
        ins = {
            "x": (xs.reshape(seq, width), once((seq, width))),
            "g": (gs.reshape(seq, width), anywhere),
            "ct": (ct, once((width, seq))),
            "il": (inv_total, once((H, 1, seq))),
            "wo": (w_output, once((width, width))),
            "bo": (b_output, once((width,))),
            "gain": (ln2_gain, once((width,))),
            "bias": (ln2_bias, once((width,))),
            "bout": (b_out, once((width,))),
            "bin": (b_in, once((hidden,))),
            "win": (w_in, pl.BlockSpec((width, tile), lambda i: (0, i % 4))),
            "wout": (w_out, pl.BlockSpec((tile, width), lambda i: (i % 4, 0))),
        }
        outs = {
            "output": (sds((n_seq, tok, width), BF16), anywhere),
            "dmid": (sds((seq, width), F32), anywhere),
            "dot": (sds((width, seq), BF16), once((width, seq))),
            "gwin": (
                sds((2, 2, 2, 4 * share, hidden), BF16),
                pl.BlockSpec((2, 2, 2, 4 * share, tile), lambda i: (0, 0, 0, 0, jnp.maximum(i - 4, 0))),
            ),
            "gwo": (sds((2, 2, 2, 4 * share, width), BF16), once((2, 2, 2, 4 * share, width))),
            "part": (sds((2, 4, share_f, width), BF16), anywhere),
            "vec": (sds((vec_rows, width), F32), once((vec_rows, width))),
        }
        scratch = {
            "gbuf": pltpu.VMEM((seq, width), BF16),
            "mid": pltpu.VMEM((seq, width), F32),
            "acc": pltpu.VMEM((seq, width), F32),
            "n2": pltpu.VMEM((seq, width), BF16),
            "n2t": pltpu.VMEM((width, seq), BF16),
            "act": pltpu.VMEM((seq, tile), BF16),
            "gp": pltpu.VMEM((4, seq, tile), BF16),
            "bins": pltpu.VMEM((4, 1, tile), F32),
            "bing": pltpu.VMEM((4, 1, tile), F32),
            "obuf": pltpu.VMEM((n_blk, tok, width), BF16),
            "gw": pltpu.VMEM((2, 2, 2, 4, share_f, width), BF16),
            "r0": pltpu.VMEM((2, 2, 4, share_f, width), BF16),
            "t1": pltpu.VMEM((2, 4, share_f, width), BF16),
            "r1": pltpu.VMEM((2, 4, share_f, width), BF16),
            "csend": pltpu.SemaphoreType.DMA((4,)),
            "crecv": pltpu.SemaphoreType.DMA((4,)),
            "ysend": pltpu.SemaphoreType.DMA((4,)),
            "yrecv": pltpu.SemaphoreType.DMA((4,)),
            "osend": pltpu.SemaphoreType.DMA((n_blk - 1,)),
            "orecv": pltpu.SemaphoreType.DMA((n_blk - 1,)),
            "lsem": pltpu.SemaphoreType.DMA((4,)),
        }
        names = tuple(ins) + tuple(outs) + tuple(scratch)
        ffn = pl.pallas_call(
            functools.partial(ffn_host_kernel, names, n_blk),
            grid=(8,),
            in_specs=[v[1] for v in ins.values()],
            out_specs=[v[1] for v in outs.values()],
            out_shape=[v[0] for v in outs.values()],
            scratch_shapes=list(scratch.values()),
            compiler_params=pltpu.CompilerParams(
                vmem_limit_bytes=62 * 2**20, collective_id=3, has_side_effects=True
            ),
            name="ffn",
        )(*[v[0] for v in ins.values()])
        ffn = dict(zip(outs, ffn))
        tasks = (
            ("a2", "gwin", None, slice(0, hidden // 2), share, "x", "s_win", slice(0, hidden // 2)),
            ("b2", "gwin", None, slice(hidden // 2, hidden), share, "y", "s_win", slice(hidden // 2, hidden)),
            ("wo", "gwo", None, None, share, "x", "s_wo", None),
        ) + tuple(
            (
                "q%d" % i,
                "gq",
                i,
                None,
                share,
                ("y", "x", "late")[i],
                ("s_wq", "s_wk", "s_wv"),
                slice(i * cols, (i + 1) * cols),
            )
            for i in range(n_col)
        )
        sizes = {"a2": hidden // 2, "b2": hidden // 2, "wo": width}
        plan = PLAN
        last = lambda shape: pl.BlockSpec(shape, lambda h: (jnp.minimum(h, H - 1),) + (0,) * (len(shape) - 1))
        strip_h = last((head, seq))
        ins = {
            "p": (probs, last((1, seq, seq))),
            "q": (qt, strip_h),
            "k": (kt, strip_h),
            "v": (vt, strip_h),
            "do": (ffn["dot"], strip_h),
            "ct": (ct, strip_h),
            "tops": (tops, last((1, n_blk, seq))),
            "nt": (nt, anywhere),
            "gain": (ln1_gain, full((width,))),
            "vec_in": (ffn["vec"], full((vec_rows, width))),
            "xs": (xs, anywhere),
            "dmid": (ffn["dmid"], anywhere),
            "wq": (w_query, anywhere),
            "wk": (w_key, anywhere),
            "wv": (w_value, anywhere),
            "part": (ffn["part"], anywhere),
            "gwin": (ffn["gwin"], anywhere),
            "gwo": (ffn["gwo"], anywhere),
        }
        outs = {
            "input_grad": (sds((n_seq, tok, width), BF16), anywhere),
            "s_wq": (sds((share, width), F32), full((share, width))),
            "s_wk": (sds((share, width), F32), full((share, width))),
            "s_wv": (sds((share, width), F32), full((share, width))),
            "s_wo": (sds((share, width), F32), full((share, width))),
            "s_win": (sds((share, hidden), F32), full((share, hidden))),
            "s_wout": (sds((share_f, width), F32), full((share_f, width))),
            "va_out": (sds((8, width), F32), full((8, width))),
            "vb_out": (sds((8, width), F32), full((8, width))),
        }
        scratch = {
            "ds": pltpu.VMEM((seq, seq), BF16),
            "doi": pltpu.VMEM((n_blk, head, seq), BF16),
            "dcat": pltpu.VMEM((3 * width, seq), BF16),
            "wcat": pltpu.VMEM((width, 3 * width), BF16),
            "gq": pltpu.VMEM((n_col, 2, 2, 2, 4 * share, 3 * cols), BF16),
            "va": pltpu.VMEM((8, width), F32),
            "vb": pltpu.VMEM((8, width), F32),
            "va_r": pltpu.VMEM((7, 8, width), F32),
            "vb_r": pltpu.VMEM((7, 8, width), F32),
            "ebuf": pltpu.VMEM((2, width, tok), F32),
            "ntbuf": pltpu.VMEM((width, seq), BF16),
            "xbuf": pltpu.VMEM((n_blk, tok, width), BF16),
            "dmbuf": pltpu.VMEM((seq, width), F32),
            "dx": pltpu.VMEM((n_blk, tok, width), BF16),
            "lsem": pltpu.SemaphoreType.DMA((8,)),
            "va_send": pltpu.SemaphoreType.DMA((7,)),
            "va_recv": pltpu.SemaphoreType.DMA((7,)),
            "vb_send": pltpu.SemaphoreType.DMA((7,)),
            "vb_recv": pltpu.SemaphoreType.DMA((7,)),
            "w_keep": pltpu.VMEM((2, share_f, width), BF16),
            "w_rz": pltpu.VMEM((3, 2, share_f, width), BF16),
            "w_f": pltpu.VMEM((2, share_f, width), F32),
            "w_t": pltpu.VMEM((share_f, width), BF16),
            "w_rx": pltpu.VMEM((share_f, width), BF16),
            "w_send": pltpu.SemaphoreType.DMA((4,)),
            "w_recv": pltpu.SemaphoreType.DMA((4,)),
            "isend": pltpu.SemaphoreType.DMA((n_blk - 1,)),
            "irecv": pltpu.SemaphoreType.DMA((n_blk - 1,)),
        }
        for name, source, _, _, task_share, first, _, _ in tasks:
            for k, v in scatter_scratch(task_share, sizes.get(name, width), source != "gq", first == "late").items():
                scratch[name + "_" + k] = v
        names = tuple(ins) + tuple(outs) + tuple(scratch)
        got = pl.pallas_call(
            functools.partial(back_kernel, scale, names, tasks, plan),
            grid=(H + 1,),
            in_specs=[v[1] for v in ins.values()],
            out_specs=[v[1] for v in outs.values()],
            out_shape=[v[0] for v in outs.values()],
            scratch_shapes=list(scratch.values()),
            compiler_params=pltpu.CompilerParams(
                vmem_limit_bytes=60 * 2**20, collective_id=2, has_side_effects=True
            ),
            name="back",
        )(*[v[0] for v in ins.values()])
        got = dict(zip(outs, got))
        big = [ffn["output"], got["input_grad"]] + [
            got[k] for k in ("s_wq", "s_wk", "s_wv", "s_wo", "s_win", "s_wout")
        ]
        part = pl.BlockSpec((n_blk // 2, tok, width), lambda i: (i, 0, 0))
        flat = [sds(v.shape, v.dtype) for v in big]
        fin = pl.pallas_call(
            functools.partial(finish_kernel, len(big)),
            grid=(2,),
            in_specs=[part] * 2 + [full(v.shape) for v in big[2:]] + [full((8, width))] * 2,
            out_specs=[part] * 2 + [full(v.shape) for v in big[2:]] + [full((share,))] * 8 + [full((share_f,))],
            out_shape=flat + [sds((share,), F32)] * 8 + [sds((share_f,), F32)],
            name="finish",
        )(*big, got["va_out"], got["vb_out"])
        output, input_grad, s_wq, s_wk, s_wv, s_wo, s_win, s_wout = fin[: len(big)]
        g1, b1, bq, bv, bo_sum, g2, b2, bout_sum, bin_sum = fin[len(big) :]
        return (
            output,
            input_grad,
            g1,
            b1,
            s_wq,
            bq,
            s_wk,
            s_wv,
            bv,
            s_wo,
            bo_sum,
            g2,
            b2,
            s_win,
            bin_sum,
            s_wout,
            bout_sum,
        )

    n_tile = 4
    tile = hidden // n_tile
    result = pl.pallas_call(
        functools.partial(ffn_kernel, n_blk),
        grid=(n_tile,),
        in_specs=[full((seq, width))] * 2
        + [
            wide,
            full((H, 1, seq)),
            full((width, width)),
            full((1, width)),
            full((1, width)),
            full((1, width)),
            pl.BlockSpec((width, tile), lambda j: (0, j)),
            pl.BlockSpec((1, tile), lambda j: (0, j)),
            pl.BlockSpec((tile, width), lambda j: (j, 0)),
            full((1, width)),
        ],
        out_specs=[piece] * n_blk
        + [
            pl.BlockSpec((tile, width), lambda j: (j, 0)),
            pl.BlockSpec((width, tile), lambda j: (0, j)),
            pl.BlockSpec((1, tile), lambda j: (0, j)),
            full((seq, width)),
            wide,
            full((width, width)),
            full((8, width)),
        ],
        out_shape=[sds((tok, width), BF16)] * n_blk
        + [
            sds((hidden, width), BF16),
            sds((width, hidden), BF16),
            sds((1, hidden), F32),
            sds((seq, width), F32),
            sds((width, seq), BF16),
            sds((width, width), BF16),
            sds((8, width), F32),
        ],
        scratch_shapes=[
            pltpu.VMEM((seq, width), F32),
            pltpu.VMEM((seq, width), BF16),
            pltpu.VMEM((width, seq), BF16),
            pltpu.VMEM((seq, width), F32),
            pltpu.VMEM((seq, width), F32),
            pltpu.VMEM((seq, tile), BF16),
            pltpu.VMEM((seq, tile), BF16),
        ],
        compiler_params=params(),
        cost_estimate=cost(8 * seq * width * hidden, 8 * width * hidden),
        name="ffn",
    )(
        xs.reshape(seq, width),
        gs.reshape(seq, width),
        ct,
        inv_total,
        w_output,
        row(b_output),
        row(ln2_gain),
        row(ln2_bias),
        w_in,
        row(b_in),
        w_out,
        row(b_out),
    )
    out_pieces = result[:n_blk]
    g_wout, g_win, g_bin, dmid, dct, g_wo, vec2 = result[n_blk:]

    bits = (n_dev - 1).bit_length()
    assert n_dev == 1 << bits

    def scatter(grad, order, wire):
        share = grad.shape[0] // n_dev
        order = list(order) + [b for b in range(bits) if b not in order]
        axes = list(range(bits - 1, -1, -1))
        terms = [grad.reshape((2,) * bits + (share,) + grad.shape[1:])]
        for b in order:
            at = axes.index(b)
            axes.pop(at)
            mine = (me >> b) & 1
            send = None
            keep = []
            for t in terms:
                other = lax.dynamic_index_in_dim(t, 1 - mine, at, keepdims=False)
                send = other.astype(F32) if send is None else send + other.astype(F32)
                keep.append(lax.dynamic_index_in_dim(t, mine, at, keepdims=False))
            got = lax.ppermute(send.astype(wire), ("dp", "blk"), [(i, i ^ (1 << b)) for i in range(n_dev)])
            terms = keep + [got]
        total = terms[0].astype(F32)
        for t in terms[1:]:
            total = total + t.astype(F32)
        return total

    s_wout = scatter(g_wout, (0, 1, 2, 3, 4), BF16)
    s_win = scatter(g_win, (0, 2, 1, 3, 4), BF16)
    s_wo = scatter(g_wo, (0, 3, 4, 1, 2), BF16)
    output = collect(out_pieces)

    dqt, dkt, dvt = pl.pallas_call(
        functools.partial(attend_back_kernel, scale, n_blk),
        grid=(H,),
        in_specs=[per_square] + [per_head] * 5 + [per_block],
        out_specs=[per_head] * 3,
        out_shape=[sds((width, seq), BF16)] * 3,
        scratch_shapes=[pltpu.VMEM((seq, seq), BF16), pltpu.VMEM((n_blk, head, seq), BF16)],
        compiler_params=params(),
        cost_estimate=cost(10 * seq * seq * width, 2 * H * seq * seq),
        name="attend_back",
    )(probs, qt, kt, vt, dct, ct, tops)

    result = pl.pallas_call(
        functools.partial(input_kernel, n_blk),
        in_specs=[full((seq, width))] * 2
        + [full((1, width)), wide, wide, wide]
        + [full((width, width))] * 3,
        out_specs=[piece] * n_blk + [full((8, width))],
        out_shape=[sds((tok, width), BF16)] * n_blk + [sds((8, width), F32)],
        compiler_params=params(),
        cost_estimate=cost(3 * seq * width * width, 14 * seq * width),
        name="input_grad",
    )(xs.reshape(seq, width), dmid, row(ln1_gain), dqt, dkt, dvt, w_query, w_key, w_value)
    input_grad = collect(result[:n_blk])
    vec1 = result[n_blk]

    col = pl.BlockSpec((width, cols), lambda j: (0, j))
    g_wq, g_wk, g_wv, vecq = pl.pallas_call(
        qkv_grad_kernel,
        grid=(n_col,),
        in_specs=[wide, strip, strip, strip],
        out_specs=[col, col, col, pl.BlockSpec((8, cols), lambda j: (0, j))],
        out_shape=[sds((width, width), BF16)] * 3 + [sds((8, width), F32)],
        compiler_params=params(),
        cost_estimate=cost(3 * seq * width * width, 14 * seq * width),
        name="qkv_grad",
    )(nt, dqt, dkt, dvt)
    s_wq = scatter(g_wq, (0, 1, 2, 3, 4), BF16)
    s_wk = scatter(g_wk, (0, 2, 3, 4, 1), BF16)
    s_wv = scatter(g_wv, (0, 3, 4, 1, 2), BF16)

    vectors = [vec1[0], vec1[1], vecq[0], vecq[1], vec2[3], vec2[1], vec2[2], g_bin[0], vec2[0]]
    packed = jnp.concatenate([v.reshape(n_dev, -1) for v in vectors], axis=1)
    packed = scatter(packed, (0, 1, 2, 3, 4), F32).reshape(-1)
    parts = []
    at = 0
    for v in vectors:
        size = v.shape[0] // n_dev
        parts.append(packed[at : at + size])
        at += size
    p_ln1g, p_ln1b, p_bq, p_bv, p_bo, p_ln2g, p_ln2b, p_bin, p_bout = parts
    return (
        output,
        input_grad,
        p_ln1g,
        p_ln1b,
        s_wq,
        p_bq,
        s_wk,
        s_wv,
        p_bv,
        s_wo,
        p_bo,
        p_ln2g,
        p_ln2b,
        s_win,
        p_bin,
        s_wout,
        p_bout,
    )


def solution(mesh):
    whole = P(("dp", "blk"))
    rows = P(("dp", "blk"), None)
    tokens = P("dp", "blk", None)
    in_specs = (tokens, P("dp"), tokens) + (P(),) * 15
    out_specs = (
        tokens,
        tokens,
        whole,
        whole,
        rows,
        whole,
        rows,
        rows,
        whole,
        rows,
        whole,
        whole,
        whole,
        rows,
        whole,
        rows,
        whole,
    )
    return jax.shard_map(body, mesh=mesh, in_specs=in_specs, out_specs=out_specs, check_vma=False)
```
